32 devices in a mesh: group: 2 (over y), gx: 4 (over z), gy: 2 (over x), gz: 2 (over core).
Axes of the slice: x: 2, y: 2, z: 4, core: 2. Of those that a mesh axis runs over, the one named last changes fastest.
Arguments:
- node_latent: bfloat16 [16, 4, 2, 128, 128], P(('group', 'gx'), 'gy', 'gz'), parts along dimension 0, may hold values from -6 to 6
- edge_latent: bfloat16 [16, 4, 2, 12, 128, 128], P(('group', 'gx'), 'gy', 'gz'), parts along dimension 0, may hold values from -6 to 6
- positions: float32 [3, 16, 4, 2, 128], P(None, ('group', 'gx'), 'gy', 'gz'), parts along dimension 1, may hold values from 0 to 8, as said below
- velocity: float32 [3, 16, 4, 2, 128], P(None, ('group', 'gx'), 'gy', 'gz'), parts along dimension 1, may hold values from -2 to 2
- fill: int32 [16, 4, 2], P(('group', 'gx'), 'gy', 'gz'), parts along dimension 0, may hold values from 64 to 128, as said below
- neighbours: int32 [16, 4, 2, 12, 128], P(('group', 'gx'), 'gy', 'gz'), parts along dimension 0, may hold values from 0 to 6143, as said below
- owners: int32 [16, 4, 2, 128], P(('group', 'gx'), 'gy', 'gz'), parts along dimension 0, may hold values from 0 to 15, as said below
- edge_weights: bfloat16 [5, 128, 128], replicated, may hold values from -0.5 to 0.5
- node_in: bfloat16 [256, 128], replicated, may hold values from -0.375 to 0.375
- node_weights: bfloat16 [2, 128, 128], replicated, may hold values from -0.5 to 0.5
- decoder_weights: bfloat16 [2, 128, 128], replicated, may hold values from -0.5 to 0.5
- decoder_out: bfloat16 [3, 128], replicated, may hold values from -0.5 to 0.5
- encoder_in: bfloat16 [12, 128], replicated, may hold values from -1.75 to 1.75
- encoder_weights: bfloat16 [2, 128, 128], replicated, may hold values from -0.5 to 0.5
Outputs:
- kept_latent: bfloat16 [16, 4, 2, 128, 128], P(('group', 'gx'), 'gy', 'gz'), parts along dimension 0
- kept_state: float32 [9, 16, 4, 2, 128], P(None, ('group', 'gx'), 'gy', 'gz'), parts along dimension 1
- arrived_latent: bfloat16 [8, 2, 2, 208, 128], P(('group', 'gx'), 'gy', 'gz'), parts along dimension 0
- arrived_state: float32 [9, 8, 2, 2, 208], P(None, ('group', 'gx'), 'gy', 'gz'), parts along dimension 1
The draws below stay inside these ranges and needn't reach their ends.
There are 2 independent parts, one for each index of `group`. The reference program is written for one: setup_inputs(seed, part) draws one part's arguments, and reference() takes and returns one part's arrays. A program takes and returns all parts, laid end to end along the dimension named above; an argument that names none is the same for every part. Nothing has to cross between parts.
Inputs may be any that keep to these rules, and one draw needn't show every extreme that they name: live particles fill the first fill slots of their cell; in every draw some cell is full. `neighbours`: every entry of a live particle names a live slot of its own cell or of a cell beside it (faces, edges or corners) inside the domain. `owners`: the owner of a live particle is its own device or one whose block of cells touches it; from one device at most 8 live particles go to any one other device, and in every draw each device sends exactly 8 to some other; slots without a particle name their own device. `positions`: each position lies within its own cell, cell (X, Y, Z) covering [X, X + 1) x [Y, Y + 1) x [Z, Z + 1).
All inputs are finite; a program needn't handle non-finite values.
Results may differ from the reference program's by a relative error of at most 0.0077.
Values may be sent and summed in bfloat16 or wider, within the bound.
No kernel may reach another device: no remote copies, remote signals or barrier semaphores. Data moves between devices by JAX's collectives and lax.ppermute only.
A program may use at most 64 MiB of HBM per device.

```python
import jax
import jax.numpy as jnp
from jax import lax

H = 128
SLOT = 128
K = 12
CX = 2
CY = 2
CZ = 1
CAP = 8
NX = 8
NY = 4
NZ = 2
N_GX = 4
N_GY = 2
N_GZ = 2


def cell_fill(key):
    counts = jax.random.randint(jax.random.fold_in(key, 11), (NX, NY, NZ), SLOT // 2, SLOT + 1)
    corner = jax.random.randint(jax.random.fold_in(key, 12), (3,), 0, jnp.array([NX, NY, NZ], dtype=jnp.int32))
    return counts.at[corner[0], corner[1], corner[2]].set(SLOT)


def draw_fill(key, part):
    return cell_fill(key)


def draw_owners(key, part):
    counts = cell_fill(key)
    key = jax.random.fold_in(key, 2)
    blocks_x = NX // CX
    blocks_y = NY // CY
    blocks_z = NZ // CZ
    block_total = blocks_x * blocks_y * blocks_z
    block_rows = CX * CY * CZ * SLOT
    block_ids = jnp.arange(block_total, dtype=jnp.int32)
    home_x = block_ids // (blocks_y * blocks_z)
    home_y = block_ids // blocks_z % blocks_y
    home_z = block_ids % blocks_z
    directs = jnp.arange(27, dtype=jnp.int32)
    step_x = directs // 9 - 1
    step_y = directs // 3 % 3 - 1
    step_z = directs % 3 - 1
    target_x = home_x[:, None] + step_x[None, :]
    target_y = home_y[:, None] + step_y[None, :]
    target_z = home_z[:, None] + step_z[None, :]
    inside = (target_x >= 0) & (target_x < blocks_x) & (target_y >= 0) & (target_y < blocks_y)
    inside = inside & (target_z >= 0) & (target_z < blocks_z) & (directs[None, :] != 13)
    movers = jax.random.randint(jax.random.fold_in(key, 1), (block_total, 27), 0, CAP + 1) * inside.astype(jnp.int32)
    score = jnp.where(inside, jax.random.randint(jax.random.fold_in(key, 2), (block_total, 27), 0, 1 << 20) * 32 + directs[None, :], -1)
    chosen = jnp.argmax(score, axis=1)
    movers = movers.at[block_ids, chosen].set(CAP)
    alive = jnp.arange(SLOT, dtype=jnp.int32)[None, None, None, :] < counts[..., None]
    alive_blocks = alive.reshape(blocks_x, CX, blocks_y, CY, blocks_z, CZ, SLOT).transpose(0, 2, 4, 1, 3, 5, 6).reshape(block_total, block_rows)
    slot_ids = jnp.arange(block_rows, dtype=jnp.int32)
    noise = jax.random.randint(jax.random.fold_in(key, 3), (block_total, block_rows), 0, 1 << 13)
    score_rows = alive_blocks.astype(jnp.int32) * (1 << 26) + noise * block_rows + slot_ids[None, :]
    order = jnp.argsort(-score_rows, axis=1)
    position = jnp.argsort(order, axis=1)
    bounds = jnp.cumsum(movers, axis=1)
    direction = jnp.sum((position[:, :, None] >= bounds[:, None, :]).astype(jnp.int32), axis=2)
    moving = direction < 27
    picked = jnp.minimum(direction, 26)
    target = ((home_x[:, None] + step_x[picked]) * blocks_y + home_y[:, None] + step_y[picked]) * blocks_z + home_z[:, None] + step_z[picked]
    owner_blocks = jnp.where(moving, target, block_ids[:, None])
    shaped = owner_blocks.reshape(blocks_x, blocks_y, blocks_z, CX, CY, CZ, SLOT).transpose(0, 3, 1, 4, 2, 5, 6)
    return shaped.reshape(NX, NY, NZ, SLOT).astype(jnp.int32)


def draw_neighbours(key, part):
    counts = cell_fill(key)
    key = jax.random.fold_in(key, 3)
    shape_all = (NX, NY, NZ, K, SLOT)
    offsets = jax.random.randint(jax.random.fold_in(key, 1), (3,) + shape_all, -1, 2)
    cell_x = jnp.arange(NX, dtype=jnp.int32)[:, None, None, None, None]
    cell_y = jnp.arange(NY, dtype=jnp.int32)[None, :, None, None, None]
    cell_z = jnp.arange(NZ, dtype=jnp.int32)[None, None, :, None, None]
    target_x = jnp.clip(cell_x + offsets[0], 0, NX - 1)
    target_y = jnp.clip(cell_y + offsets[1], 0, NY - 1)
    target_z = jnp.clip(cell_z + offsets[2], 0, NZ - 1)
    target_slot = jax.random.randint(jax.random.fold_in(key, 2), shape_all, 0, counts[target_x, target_y, target_z])
    outer_x = target_x - (cell_x - cell_x % CX) + 1
    outer_y = target_y - (cell_y - cell_y % CY) + 1
    outer_z = target_z - (cell_z - cell_z % CZ) + 1
    return (((outer_x * (CY + 2) + outer_y) * (CZ + 2) + outer_z) * SLOT + target_slot).astype(jnp.int32)


def draw_positions(key, part):
    key = jax.random.fold_in(key, 4)
    offset = jax.random.uniform(key, (3, NX, NY, NZ, SLOT), jnp.float32)
    grid_x = jnp.broadcast_to(jnp.arange(NX, dtype=jnp.float32)[:, None, None, None], (NX, NY, NZ, SLOT))
    grid_y = jnp.broadcast_to(jnp.arange(NY, dtype=jnp.float32)[None, :, None, None], (NX, NY, NZ, SLOT))
    grid_z = jnp.broadcast_to(jnp.arange(NZ, dtype=jnp.float32)[None, None, :, None], (NX, NY, NZ, SLOT))
    return jnp.stack([grid_x, grid_y, grid_z], axis=0) + offset


def block_levels(key, shape, shards, smallest, largest):
    def one(dim, blocks):
        heights = jax.random.uniform(jax.random.fold_in(jax.random.fold_in(key, 6), dim), (blocks,), jnp.float32, smallest / len(shards), largest / len(shards))
        return jnp.repeat(jnp.exp(heights), shape[dim] // blocks).reshape((-1,) + (1,) * (len(shape) - dim - 1))

    gain = one(*shards[0])
    for cut in shards[1:]:
        gain = gain * one(*cut)
    return gain


def bell_draw(stream_key, dims, deviation, most, cuts=(), kind=jnp.bfloat16):
    loudness = block_levels(stream_key, dims, cuts, -0.22, 0.18) if cuts else 1.0
    result = jax.random.normal(stream_key, dims, jnp.float32) * deviation * loudness
    return jnp.minimum(jnp.maximum(result, -most), most).astype(kind)


def setup_inputs(seed: int = 0, part: int = 0) -> dict:
    seeds = jax.random.split(jax.random.key(seed), 15)
    own_keys = jax.random.split(jax.random.fold_in(seeds[14], part), 15)
    node_latent = bell_draw(own_keys[0], (NX, NY, NZ, SLOT, H), 1.0, 6.0, ((0, 4), (1, 2), (2, 2)))
    edge_latent = bell_draw(own_keys[1], (NX, NY, NZ, K, SLOT, H), 1.0, 6.0, ((0, 4), (1, 2), (2, 2)))
    positions = draw_positions(jax.random.fold_in(jax.random.fold_in(seeds[14], part), 71), part)
    velocity = bell_draw(own_keys[3], (3, NX, NY, NZ, SLOT), 0.3, 2.0, ((1, 4), (2, 2), (3, 2)), jnp.float32)
    fill = draw_fill(jax.random.fold_in(jax.random.fold_in(seeds[14], part), 71), part)
    neighbours = draw_neighbours(jax.random.fold_in(jax.random.fold_in(seeds[14], part), 71), part)
    owners = draw_owners(jax.random.fold_in(jax.random.fold_in(seeds[14], part), 71), part)
    edge_weights = bell_draw(seeds[7], (5, H, H), H ** -0.5, 0.5)
    node_in = bell_draw(seeds[8], (2 * H, H), (2 * H) ** -0.5, 0.375)
    node_weights = bell_draw(seeds[9], (2, H, H), H ** -0.5, 0.5)
    decoder_weights = bell_draw(seeds[10], (2, H, H), H ** -0.5, 0.5)
    decoder_out = bell_draw(seeds[11], (3, H), H ** -0.5, 0.5)
    encoder_in = bell_draw(seeds[12], (12, H), 12 ** -0.5, 1.75)
    encoder_weights = bell_draw(seeds[13], (2, H, H), H ** -0.5, 0.5)
    return dict(node_latent=node_latent, edge_latent=edge_latent, positions=positions, velocity=velocity, fill=fill, neighbours=neighbours, owners=owners, edge_weights=edge_weights, node_in=node_in, node_weights=node_weights, decoder_weights=decoder_weights, decoder_out=decoder_out, encoder_in=encoder_in, encoder_weights=encoder_weights)


def layer_norm(values):
    centred = values - lax.optimization_barrier(jnp.mean(values, axis=-1, keepdims=True))
    spread = lax.optimization_barrier(jnp.mean(centred * centred, axis=-1, keepdims=True))
    return centred * lax.rsqrt(spread + 1e-05)

def mlp_tail(pre_act, middle_w, final_w):
    hidden = jax.nn.relu(pre_act).astype(jnp.bfloat16)
    hidden = jax.nn.relu(jnp.dot(hidden, middle_w, preferred_element_type=jnp.float32)).astype(jnp.bfloat16)
    return layer_norm(jnp.dot(hidden, final_w, preferred_element_type=jnp.float32))

def decode_step(updated, decoder_weights, decoder_out):
    hidden = jax.nn.relu(jnp.dot(updated, decoder_weights[0], preferred_element_type=jnp.float32)).astype(jnp.bfloat16)
    hidden = jax.nn.relu(jnp.dot(hidden, decoder_weights[1], preferred_element_type=jnp.float32)).astype(jnp.bfloat16)
    return jnp.dot(hidden, decoder_out.T, preferred_element_type=jnp.float32).T

def encode(new_state, alive_mask, encoder_in, encoder_weights, extent):
    position = new_state[0:3]
    features = jnp.concatenate([new_state[3:9], jnp.clip(position, -1.0, 1.0), jnp.clip(extent - position, -1.0, 1.0)], axis=0)
    pre_act = jnp.dot(features.T, encoder_in.astype(jnp.float32), precision=lax.Precision.HIGHEST)
    latent = mlp_tail(pre_act, encoder_weights[0], encoder_weights[1]) * alive_mask[:, None]
    return latent.astype(jnp.bfloat16)

def to_blocks(values):
    leading = values.shape[0]
    shaped = values.reshape(leading, N_GX, CX, N_GY, CY, N_GZ, CZ, SLOT)
    shaped = shaped.transpose(0, 1, 3, 5, 2, 4, 6, 7)
    return shaped.reshape(leading, N_GX * N_GY * N_GZ, CX * CY * CZ * SLOT)

def block_coords(block_ids):
    return (block_ids // (N_GY * N_GZ), block_ids // N_GZ % N_GY, block_ids % N_GZ)

def reference(node_latent, edge_latent, positions, velocity, fill, neighbours, owners, edge_weights, node_in, node_weights, decoder_weights, decoder_out, encoder_in, encoder_weights):
    occupied = jnp.arange(SLOT, dtype=jnp.int32)[None, None, None, :] < fill[..., None]
    flat_latent = node_latent.reshape(-1, H)
    near_term = jnp.dot(flat_latent, edge_weights[1], preferred_element_type=jnp.float32).reshape(NX, NY, NZ, SLOT, H)
    far_term = jnp.dot(flat_latent, edge_weights[2], preferred_element_type=jnp.float32).astype(jnp.bfloat16)
    cell_x = jnp.arange(NX, dtype=jnp.int32)[:, None, None, None, None]
    cell_y = jnp.arange(NY, dtype=jnp.int32)[None, :, None, None, None]
    cell_z = jnp.arange(NZ, dtype=jnp.int32)[None, None, :, None, None]
    outer_cell = neighbours // SLOT
    target_slot = neighbours % SLOT
    outer_z = outer_cell % (CZ + 2)
    outer_y = outer_cell // (CZ + 2) % (CY + 2)
    outer_x = outer_cell // ((CY + 2) * (CZ + 2))
    target_x = cell_x - cell_x % CX + outer_x - 1
    target_y = cell_y - cell_y % CY + outer_y - 1
    target_z = cell_z - cell_z % CZ + outer_z - 1
    global_row = (((target_x * NY + target_y) * NZ + target_z) * SLOT + target_slot).astype(jnp.int32)

    def slab_messages(pieces):
        edge_rows, row_ids, receiver, alive_mask = pieces
        pre_act = jnp.dot(edge_rows.reshape(-1, H), edge_weights[0], preferred_element_type=jnp.float32).reshape(edge_rows.shape)
        pre_act = pre_act + receiver[:, :, None] + far_term[row_ids].astype(jnp.float32)
        message = mlp_tail(pre_act.reshape(-1, H), edge_weights[3], edge_weights[4]).reshape(edge_rows.shape)
        message = message * alive_mask[:, :, None, :, None]
        return lax.optimization_barrier(jnp.sum(message, axis=2))
    aggregate = lax.map(slab_messages, (edge_latent, global_row, near_term, occupied.astype(jnp.float32)))
    aggregate = aggregate.astype(jnp.bfloat16).reshape(-1, H)
    pre_node = jnp.dot(flat_latent, node_in[:H], preferred_element_type=jnp.float32) + jnp.dot(aggregate, node_in[H:], preferred_element_type=jnp.float32)
    updated = (flat_latent.astype(jnp.float32) + mlp_tail(pre_node, node_weights[0], node_weights[1])).astype(jnp.bfloat16)
    acceleration = decode_step(updated, decoder_weights, decoder_out)
    flat_velocity = velocity.reshape(3, -1)
    new_velocity = flat_velocity + acceleration
    new_position = positions.reshape(3, -1) + new_velocity
    new_state = jnp.concatenate([new_position, new_velocity, flat_velocity], axis=0)
    extent = jnp.array([NX, NY, NZ], dtype=jnp.float32)[:, None]
    flat_alive = occupied.reshape(-1).astype(jnp.float32)
    latent = encode(new_state, flat_alive, encoder_in, encoder_weights, extent)
    home_block = (cell_x[..., 0] // CX * N_GY + cell_y[..., 0] // CY) * N_GZ + cell_z[..., 0] // CZ
    staying = occupied & (owners == home_block)
    stay_mask = staying.reshape(-1).astype(jnp.float32)
    kept_latent = (latent * stay_mask[:, None].astype(jnp.bfloat16)).reshape(NX, NY, NZ, SLOT, H)
    kept_state = (new_state * stay_mask[None, :]).reshape(9, NX, NY, NZ, SLOT)
    block_total = N_GX * N_GY * N_GZ
    owner_blocks = to_blocks(owners[None])[0]
    alive_blocks = to_blocks(occupied[None])[0]
    state_blocks = to_blocks(new_state.reshape(9, NX, NY, NZ, SLOT))
    latent_blocks = to_blocks(latent.reshape(NX, NY, NZ, SLOT, H).transpose(4, 0, 1, 2, 3)).transpose(1, 2, 0)
    source = jnp.arange(block_total, dtype=jnp.int32)[:, None]
    moving = alive_blocks & (owner_blocks != source)

    def block_rank(pieces):
        owner_row, moving_row = pieces
        member = ((owner_row[:, None] == jnp.arange(block_total, dtype=jnp.int32)[None, :]) & moving_row[:, None]).astype(jnp.int32)
        return lax.optimization_barrier(jnp.sum(jnp.cumsum(member, axis=0) * member, axis=1)) - 1
    order_rank = lax.map(block_rank, (owner_blocks, moving))
    source_x, source_y, source_z = block_coords(source)
    owner_x, owner_y, owner_z = block_coords(owner_blocks)
    direction = (source_x - owner_x + 1) * 9 + (source_y - owner_y + 1) * 3 + (source_z - owner_z + 1)
    column = (jnp.where(direction > 13, direction - 1, direction) * CAP + jnp.maximum(order_rank, 0)).astype(jnp.int32)
    receiver = jnp.where(moving, owner_blocks, block_total).astype(jnp.int32)
    arrived_latent = jnp.zeros((block_total, 26 * CAP, H), jnp.bfloat16).at[receiver, column].set(latent_blocks, mode='drop')
    arrived_state = jnp.zeros((9, block_total, 26 * CAP), jnp.float32).at[:, receiver, column].set(state_blocks, mode='drop')
    arrived_latent = arrived_latent.reshape(N_GX, N_GY, N_GZ, 26 * CAP, H)
    arrived_state = arrived_state.reshape(9, N_GX, N_GY, N_GZ, 26 * CAP)
    return (kept_latent, kept_state, arrived_latent, arrived_state)
```

```python
import functools

import jax
import jax.numpy as jnp
from jax import lax
from jax.experimental import pallas as pl
from jax.experimental.pallas import tpu as pltpu
from jax.sharding import PartitionSpec as P

CAP = 8
F32 = jnp.float32
BF16 = jnp.bfloat16
ROWS = 16


def dot(left, right):
    return jnp.dot(left, right, preferred_element_type=F32)


def dot_nt(left, right):
    return lax.dot_general(
        left, right, (((1,), (1,)), ((), ())), preferred_element_type=F32
    )


def relu16(values):
    return jnp.maximum(values, 0.0).astype(BF16)


def norm_rows(values):
    scale = 1.0 / values.shape[0]
    centred = values - jnp.sum(values, axis=0, keepdims=True) * scale
    spread = jnp.sum(centred * centred, axis=0, keepdims=True) * scale
    return centred * lax.rsqrt(spread + 1e-05)


def thirds(values):
    high = values.astype(BF16)
    rest = values - high.astype(F32)
    middle = rest.astype(BF16)
    low = (rest - middle.astype(F32)).astype(BF16)
    return high, middle, low


def quotient(values, count):
    if count & (count - 1) == 0:
        return values >> (count.bit_length() - 1)
    return lax.div(values, jnp.full_like(values, count))


def flip(weights):
    return weights.astype(F32).T.astype(BF16)


def encode(state, encoder_in, first, second, extent):
    width = state.shape[1]
    position = state[0:3]
    row = lax.broadcasted_iota(jnp.int32, (3, width), 0)
    size = jnp.where(row == 0, extent[0], jnp.where(row == 1, extent[1], extent[2]))
    features = jnp.concatenate(
        [
            state[3:9],
            jnp.clip(position, -1.0, 1.0),
            jnp.clip(size - position, -1.0, 1.0),
            jnp.zeros((4, width), F32),
        ],
        axis=0,
    )
    inward = jnp.concatenate([encoder_in.astype(F32), jnp.zeros((4, encoder_in.shape[1]), F32)], axis=0)
    inward = jnp.concatenate([inward, inward, inward], axis=0).T.astype(BF16)
    hidden = relu16(dot(inward, jnp.concatenate(thirds(features), axis=0)))
    hidden = relu16(dot(first, hidden))
    return norm_rows(dot(second, hidden))


def step_kernel(
    sizes,
    fill_ref,
    own_ref,
    zed_ref,
    side_refs,
    left_ref,
    right_ref,
    edge_ref,
    positions_ref,
    velocity_ref,
    neighbours_ref,
    owners_ref,
    edge_w_ref,
    node_in_ref,
    node_w_ref,
    decoder_w_ref,
    decoder_out_ref,
    encoder_in_ref,
    encoder_w_ref,
    kept_latent_ref,
    kept_state_ref,
    bucket_ref,
    far_ref,
    gather_ref,
):
    count_x, count_y, count_z = sizes
    fold_y = count_y == 2
    index_x = lax.axis_index("gx")
    index_y = lax.axis_index("gy")
    index_z = lax.axis_index("gz")
    slots, width = own_ref.shape[-2:]
    neighbour_count = edge_ref.shape[3]
    middle_t = flip(edge_w_ref[3])
    final_t = flip(edge_w_ref[4])
    edge_t = flip(edge_w_ref[0])
    near_t = flip(edge_w_ref[1])
    far_t = flip(edge_w_ref[2])

    if fold_y:
        row_count = 3
        own_rows = (0, 1)
        outer = {2: 0}
    else:
        row_count = 4
        own_rows = (1, 2)
        outer = {0: 0, 3: 1}
    for ex in range(4):
        for row in range(row_count):
            if ex == 0:
                pair = (left_ref[0, row], left_ref[1, row])
            elif ex == 3:
                pair = (right_ref[0, row], right_ref[1, row])
            elif row in own_rows:
                b = own_rows.index(row)
                pair = (own_ref[ex - 1, b, 0], zed_ref[ex - 1, b, 0])
            else:
                side = side_refs[outer[row]]
                pair = (side[0, ex - 1], side[1, ex - 1])
            far_ref[ex * row_count + row] = dot_nt(
                far_t, jnp.concatenate(pair, axis=0)
            ).astype(BF16)

    lane = lax.broadcasted_iota(jnp.int32, (1, slots), 1)
    key_rows = lax.broadcasted_iota(jnp.int32, (2 * slots, 2 * slots), 0)
    chunk = 32
    for a in range(2):
        for bt in range(2):
            if fold_y:
                b = index_y if bt == 0 else 1 - index_y
                rows = (0, 1) if bt == 0 else (0, 1, 2)
            else:
                b = bt
                rows = (bt, bt + 1, bt + 2)
            columns = [(ex, row) for ex in range(a, a + 3) for row in rows]
            near = dot_nt(near_t, own_ref[a, b, 0])
            near = jnp.concatenate([near, near], axis=1)
            total = jnp.zeros((width, slots), F32)
            window = jnp.concatenate(
                [
                    far_ref[ex * row_count + row, f : f + chunk]
                    for f in range(0, width, chunk)
                    for ex, row in columns
                ],
                axis=0,
            )
            for k in range(0, neighbour_count, 2):
                ids = jnp.concatenate(
                    [neighbours_ref[a, b, k], neighbours_ref[a, b, k + 1]], axis=1
                )
                cell = ids >> 7
                plane = (cell * 43) >> 7
                ez = cell - plane * 3
                ey = plane & 3
                ex = plane >> 2
                if fold_y:
                    row = jnp.where(ey == 1, 0, jnp.where(ey == 2, 1, 2))
                else:
                    row = ey
                place = ex * 4 + row
                key = (ids & 127) + jnp.where(ez == 1, 0, slots)
                picker = (key_rows == key).astype(F32).astype(BF16)
                found = dot(window, picker)
                edges = jnp.concatenate([edge_ref[a, b, 0, k], edge_ref[a, b, 0, k + 1]], axis=0)
                pre = dot_nt(edge_t, edges) + near
                parts = []
                at = 0
                for f in range(0, width, chunk):
                    part = jnp.zeros((chunk, 2 * slots), F32)
                    for ex_at, row_at in columns:
                        part = jnp.where(
                            place == ex_at * 4 + row_at, found[at : at + chunk], part
                        )
                        at += chunk
                    parts.append(part)
                hidden = relu16(pre + jnp.concatenate(parts, axis=0))
                hidden = relu16(dot(middle_t, hidden))
                message = norm_rows(dot(final_t, hidden))
                total = total + message[:, :slots] + message[:, slots:]
            total = jnp.where(lane < fill_ref[a * 2 + b], total, 0.0)
            gather_ref[a * 2 + b] = total.astype(BF16)

    cells = [(a, b) for a in range(2) for b in range(2)]
    aggregate = jnp.concatenate([gather_ref[i] for i in range(4)], axis=1)
    latent = jnp.concatenate([own_ref[a, b, 0] for a, b in cells], axis=0)
    pre = dot_nt(flip(node_in_ref[:width]), latent) + dot(flip(node_in_ref[width:]), aggregate)
    hidden = relu16(dot(flip(node_w_ref[0]), relu16(pre)))
    updated = (latent.astype(F32).T + norm_rows(dot(flip(node_w_ref[1]), hidden))).astype(BF16)
    hidden = relu16(dot(flip(decoder_w_ref[0]), updated))
    hidden = relu16(dot(flip(decoder_w_ref[1]), hidden))
    acceleration = dot(decoder_out_ref[...], hidden)

    def flat(ref, i):
        return jnp.concatenate([ref[i, a, b] for a, b in cells], axis=1)

    old = jnp.concatenate([flat(velocity_ref, i) for i in range(3)], axis=0)
    new_velocity = old + acceleration
    new_position = jnp.concatenate([flat(positions_ref, i) for i in range(3)], axis=0) + new_velocity
    state = jnp.concatenate([new_position, new_velocity, old], axis=0)

    owner = jnp.concatenate([owners_ref[a, b] for a, b in cells], axis=1)
    alive = jnp.concatenate(
        [(lane < fill_ref[i]).astype(jnp.int32) for i in range(4)], axis=1
    )
    own_block = (index_x * count_y + index_y) * count_z + index_z
    stays = jnp.where((alive == 1) & (owner == own_block), 1.0, 0.0)
    moving = jnp.where((alive == 1) & (owner != own_block), 1, 0)

    extent = (2.0 * count_x, 2.0 * count_y, 1.0 * count_z)
    latents = encode(
        state, encoder_in_ref[...], flip(encoder_w_ref[0]), flip(encoder_w_ref[1]), extent
    )
    latents = (latents * stays).T.astype(BF16)
    kept = state * stays
    for i, (a, b) in enumerate(cells):
        kept_latent_ref[a, b, 0] = latents[i * slots : (i + 1) * slots]
        for j in range(9):
            kept_state_ref[j, a, b] = kept[j : j + 1, i * slots : (i + 1) * slots]

    owner_x = quotient(owner, count_y * count_z)
    rest = owner - owner_x * (count_y * count_z)
    owner_y = quotient(rest, count_z)
    owner_z = rest - owner_y * count_z
    step_y = owner_y - index_y
    side_y = jnp.where(step_y == 0, 0, 1) if fold_y else jnp.where(step_y < 0, 1, 2 * step_y)
    options_y = 2 if fold_y else 3
    group = ((owner_x - index_x + 1) * options_y + side_y) * 2 + jnp.where(owner_z == index_z, 0, 1)
    groups = 3 * options_y * 2
    group_rows = (groups + 15) // 16 * 16
    particles = owner.shape[1]
    member = jnp.where(
        (lax.broadcasted_iota(jnp.int32, (group_rows, particles), 0) == group) & (moving == 1),
        1.0,
        0.0,
    )
    triangle = jnp.where(
        lax.broadcasted_iota(jnp.int32, (slots, slots), 0)
        <= lax.broadcasted_iota(jnp.int32, (slots, slots), 1),
        1.0,
        0.0,
    ).astype(BF16)
    counted = []
    before = jnp.zeros((group_rows, 1), F32)
    for i in range(4):
        inside = member[:, i * slots : (i + 1) * slots]
        counted.append(dot(inside.astype(BF16), triangle) + before)
        before = before + jnp.sum(inside, axis=1, keepdims=True)
    counted = jnp.concatenate(counted, axis=1)
    rank = (jnp.sum(counted * member, axis=0, keepdims=True) - 1.0).astype(jnp.int32)
    column = jnp.where(moving == 1, group * CAP + rank, -1)
    placer = (
        (lax.broadcasted_iota(jnp.int32, (groups * CAP, particles), 0) == column)
        .astype(F32)
        .astype(BF16)
    )
    payload = jnp.concatenate(
        [state, moving.astype(F32), jnp.zeros((ROWS - 10, particles), F32)], axis=0
    )
    placed = dot_nt(jnp.concatenate(thirds(payload), axis=0), placer)
    bucket_ref[...] = placed[:ROWS] + placed[ROWS : 2 * ROWS] + placed[2 * ROWS :]


def arrive_kernel(
    sizes,
    middle_ref,
    left_ref,
    right_ref,
    encoder_in_ref,
    encoder_w_ref,
    arrived_latent_ref,
    arrived_state_ref,
):
    count_x, count_y, count_z = sizes
    fold_y = count_y == 2
    index_y = lax.axis_index("gy")
    index_z = lax.axis_index("gz")
    options_y = 2 if fold_y else 3
    lanes = middle_ref.shape[-1]
    group = lax.broadcasted_iota(jnp.int32, (ROWS, lanes), 1) >> 3
    found = jnp.zeros((ROWS, lanes), F32)
    for source_x, ref in ((-1, left_ref), (0, middle_ref), (1, right_ref)):
        for from_y in range(options_y):
            for from_z in range(2):
                if source_x == 0 and from_y == 0 and from_z == 0:
                    continue
                side_y = from_y if fold_y or from_y == 0 else 3 - from_y
                target = ((1 - source_x) * options_y + side_y) * 2 + from_z
                found = jnp.where(group == target, ref[from_y * 2 + from_z], found)
    out_lanes = arrived_state_ref.shape[-1]
    spread_shape = (lanes, out_lanes)
    line = lax.broadcasted_iota(jnp.int32, spread_shape, 0)
    from_group = line >> 3
    plane = quotient(from_group, 2)
    from_x = 1 - quotient(plane, options_y) if fold_y else 1 - ((plane * 43) >> 7)
    side_y = plane - (1 - from_x) * options_y
    if fold_y:
        from_y = jnp.where(side_y == 0, 0, jnp.where(index_y == 0, 1, -1))
    else:
        from_y = jnp.where(side_y == 0, 0, jnp.where(side_y == 1, 1, -1))
    from_z = jnp.where((from_group & 1) == 0, 0, jnp.where(index_z == 0, 1, -1))
    direction = (from_x + 1) * 9 + (from_y + 1) * 3 + from_z + 1
    direction = direction - jnp.where(direction > 13, 1, 0)
    column = direction * CAP + (line & 7)
    valid = (lax.broadcasted_iota(jnp.int32, spread_shape, 1) == column) & (
        (from_x != 0) | (from_y != 0) | (from_z != 0)
    )
    spread = jnp.where(valid, 1.0, 0.0).astype(BF16)
    arrived = dot(jnp.concatenate(thirds(found), axis=0), spread)
    arrived = arrived[:ROWS] + arrived[ROWS : 2 * ROWS] + arrived[2 * ROWS :]
    for j in range(9):
        arrived_state_ref[j, 0, 0] = arrived[j : j + 1]
    extent = (2.0 * count_x, 2.0 * count_y, 1.0 * count_z)
    latents = encode(
        arrived[:9], encoder_in_ref[...], flip(encoder_w_ref[0]), flip(encoder_w_ref[1]), extent
    )
    arrived_latent_ref[0, 0, 0] = (latents * arrived[9:10]).T.astype(BF16)


def along(count):
    up = [(i, i + 1) for i in range(count - 1)]
    return up, [(j, i) for i, j in up]


def swap(values, axis):
    return lax.ppermute(values, axis, [(0, 1), (1, 0)])


def shift(values, axis, way):
    return lax.ppermute(values, axis, along(lax.axis_size(axis))[way])


def body(
    node_latent,
    edge_latent,
    positions,
    velocity,
    fill,
    neighbours,
    owners,
    edge_weights,
    node_in,
    node_weights,
    decoder_weights,
    decoder_out,
    encoder_in,
    encoder_weights,
):
    sizes = tuple(lax.axis_size(axis) for axis in ("gx", "gy", "gz"))
    fold_y = sizes[1] == 2
    slots, width = node_latent.shape[-2:]
    zed = swap(node_latent, "gz")
    both = jnp.stack([node_latent[:, :, 0], zed[:, :, 0]], axis=0)
    if fold_y:
        inner = 1 - lax.axis_index("gy")
        sides = [swap(lax.dynamic_index_in_dim(both, inner, 2, keepdims=False), "gy")]
        layers = jnp.concatenate([both, sides[0][:, :, None]], axis=2)
    else:
        sides = [shift(both[:, :, 1], "gy", 0), shift(both[:, :, 0], "gy", 1)]
        layers = jnp.concatenate([sides[0][:, :, None], both, sides[1][:, :, None]], axis=2)
    left = shift(layers[:, 1], "gx", 0)
    right = shift(layers[:, 0], "gx", 1)

    options_y = 2 if fold_y else 3
    lanes = 3 * options_y * 2 * CAP
    rows = layers.shape[2]
    vmem = pl.BlockSpec(memory_space=pltpu.VMEM)
    smem = pl.BlockSpec(memory_space=pltpu.SMEM)
    side_count = len(sides)

    def step(fill_ref, own_ref, zed_ref, *refs):
        step_kernel(sizes, fill_ref, own_ref, zed_ref, refs[:side_count], *refs[side_count:])

    kept_latent, kept_state, bucket = pl.pallas_call(
        step,
        out_shape=(
            jax.ShapeDtypeStruct(node_latent.shape, BF16),
            jax.ShapeDtypeStruct((9,) + node_latent.shape[:4], F32),
            jax.ShapeDtypeStruct((ROWS, lanes), F32),
        ),
        in_specs=[smem] + [vmem] * (17 + side_count - 1),
        out_specs=(vmem, vmem, vmem),
        scratch_shapes=[
            pltpu.VMEM((4 * rows, width, 2 * slots), BF16),
            pltpu.VMEM((4, width, slots), BF16),
        ],
        compiler_params=pltpu.CompilerParams(vmem_limit_bytes=40 * 1024 * 1024),
        name="step",
    )(
        fill.reshape(-1),
        node_latent,
        zed,
        *sides,
        left,
        right,
        edge_latent,
        positions,
        velocity,
        neighbours.reshape(2, 2, neighbours.shape[3], 1, slots),
        owners,
        edge_weights,
        node_in,
        node_weights,
        decoder_weights,
        decoder_out,
        encoder_in,
        encoder_weights,
    )

    tiles = jnp.stack([bucket, swap(bucket, "gz")], axis=0)
    if fold_y:
        tiles = jnp.concatenate([tiles, swap(tiles, "gy")], axis=0)
    else:
        tiles = jnp.concatenate([tiles, shift(tiles, "gy", 0), shift(tiles, "gy", 1)], axis=0)
    tiles_left = shift(tiles, "gx", 0)
    tiles_right = shift(tiles, "gx", 1)
    arrived_latent, arrived_state = pl.pallas_call(
        functools.partial(arrive_kernel, sizes),
        out_shape=(
            jax.ShapeDtypeStruct((1, 1, 1, 26 * CAP, width), BF16),
            jax.ShapeDtypeStruct((9, 1, 1, 1, 26 * CAP), F32),
        ),
        in_specs=[vmem] * 5,
        out_specs=(vmem, vmem),
        name="arrive",
    )(tiles, tiles_left, tiles_right, encoder_in, encoder_weights)
    return kept_latent, kept_state, arrived_latent, arrived_state


def solution(mesh):
    placed = (
        P(("group", "gx"), "gy", "gz", None, None),
        P(("group", "gx"), "gy", "gz", None, None, None),
        P(None, ("group", "gx"), "gy", "gz", None),
        P(None, ("group", "gx"), "gy", "gz", None),
        P(("group", "gx"), "gy", "gz"),
        P(("group", "gx"), "gy", "gz", None, None),
        P(("group", "gx"), "gy", "gz", None),
        P(),
        P(),
        P(),
        P(),
        P(),
        P(),
        P(),
    )
    return jax.shard_map(
        body,
        mesh=mesh,
        in_specs=placed,
        out_specs=(
            P(("group", "gx"), "gy", "gz", None, None),
            P(None, ("group", "gx"), "gy", "gz", None),
            P(("group", "gx"), "gy", "gz", None, None),
            P(None, ("group", "gx"), "gy", "gz", None),
        ),
        check_vma=False,
    )
```

```python
import functools

import jax
import jax.numpy as jnp
from jax import lax
from jax.experimental import pallas as pl
from jax.experimental.pallas import tpu as pltpu
from jax.sharding import PartitionSpec as P

CAP = 8
F32 = jnp.float32
BF16 = jnp.bfloat16
ROWS = 16


def dot(left, right):
    return jnp.dot(left, right, preferred_element_type=F32)


def dot_nt(left, right):
    return lax.dot_general(
        left, right, (((1,), (1,)), ((), ())), preferred_element_type=F32
    )


def dot_tn(left, right):
    return lax.dot_general(
        left, right, (((0,), (0,)), ((), ())), preferred_element_type=F32
    )


def relu16(values):
    return jnp.maximum(values, 0.0).astype(BF16)


def norm_rows(values):
    scale = 1.0 / values.shape[0]
    centred = values - jnp.sum(values, axis=0, keepdims=True) * scale
    spread = jnp.sum(centred * centred, axis=0, keepdims=True) * scale
    return centred * lax.rsqrt(spread + 1e-05)


def thirds(values):
    high = values.astype(BF16)
    rest = values - high.astype(F32)
    middle = rest.astype(BF16)
    low = (rest - middle.astype(F32)).astype(BF16)
    return high, middle, low


def quotient(values, count):
    if count & (count - 1) == 0:
        return values >> (count.bit_length() - 1)
    return lax.div(values, jnp.full_like(values, count))


def flip(weights):
    return weights.astype(F32).T.astype(BF16)


def norm_lanes(values):
    scale = 1.0 / values.shape[1]
    centred = values - jnp.sum(values, axis=1, keepdims=True) * scale
    spread = jnp.sum(centred * centred, axis=1, keepdims=True) * scale
    return centred * lax.rsqrt(spread + 1e-05)


def encode(state, mask, encoder_in, encoder_w, extent):
    width = state.shape[1]
    position = state[0:3]
    row = lax.broadcasted_iota(jnp.int32, (3, width), 0)
    size = jnp.where(row == 0, extent[0], jnp.where(row == 1, extent[1], extent[2]))
    features = jnp.concatenate(
        [
            state[3:9],
            jnp.clip(position, -1.0, 1.0),
            jnp.clip(size - position, -1.0, 1.0),
            jnp.zeros((4, width), F32),
        ],
        axis=0,
    )
    inward = jnp.concatenate(
        [encoder_in.astype(F32), jnp.zeros((4, encoder_in.shape[1]), F32)], axis=0
    ).astype(BF16)
    inward = jnp.concatenate([inward, inward, inward], axis=0)
    hidden = relu16(dot_tn(jnp.concatenate(thirds(features), axis=0), inward))
    hidden = relu16(dot(hidden, encoder_w[0]))
    column = jnp.broadcast_to(mask, (8, width)).T[:, 0:1]
    return (norm_lanes(dot(hidden, encoder_w[1])) * column).astype(BF16)


def step_kernel(
    sizes,
    fill_ref,
    own_ref,
    side_refs,
    even_ref,
    odd_ref,
    zed_refs,
    edge_ref,
    positions_ref,
    velocity_ref,
    neighbours_ref,
    owners_ref,
    edge_w_ref,
    node_in_ref,
    node_w_ref,
    decoder_w_ref,
    decoder_out_ref,
    encoder_in_ref,
    encoder_w_ref,
    kept_latent_ref,
    kept_state_ref,
    bucket_ref,
    far_ref,
    gather_ref,
):
    count_x, count_y, count_z = sizes
    fold_y = count_y == 2
    index_x = lax.axis_index("gx")
    index_y = lax.axis_index("gy")
    index_z = lax.axis_index("gz")
    slots, width = own_ref.shape[-2:]
    neighbour_count = edge_ref.shape[3]
    middle_t = flip(edge_w_ref[3])
    final_t = flip(edge_w_ref[4])
    edge_t = flip(edge_w_ref[0])
    near_t = flip(edge_w_ref[1])
    far_t = flip(edge_w_ref[2])

    if fold_y:
        row_count = 3
        own_rows = (0, 1)
        outer = {2: 0}
    else:
        row_count = 4
        own_rows = (1, 2)
        outer = {0: 0, 3: 1}
    own_zed, side_zeds, even_zed, odd_zed = zed_refs
    parity = index_x & 1

    def far(place, here, beside):
        pair = jnp.concatenate([here, beside], axis=0)
        far_ref[place] = dot_nt(far_t, pair).astype(BF16)

    for row in range(row_count):
        for ex in (1, 2):
            if row in own_rows:
                b = own_rows.index(row)
                far(ex * row_count + row, own_ref[ex - 1, b, 0], own_zed[ex - 1, b, 0])
            else:
                side = outer[row]
                far(ex * row_count + row, side_refs[side][ex - 1], side_zeds[side][ex - 1])
        far(3 * (1 - parity) * row_count + row, even_ref[row], even_zed[row])
        far(3 * parity * row_count + row, odd_ref[row], odd_zed[row])

    lane = lax.broadcasted_iota(jnp.int32, (1, slots), 1)
    key_rows = lax.broadcasted_iota(jnp.int32, (2 * slots, 2 * slots), 0)
    chunk = 32
    for a in range(2):
        for bt in range(2):
            if fold_y:
                b = index_y if bt == 0 else 1 - index_y
                rows = (0, 1) if bt == 0 else (0, 1, 2)
            else:
                b = bt
                rows = (bt, bt + 1, bt + 2)
            columns = [(ex, row) for ex in range(a, a + 3) for row in rows]
            near = dot_nt(near_t, own_ref[a, b, 0])
            near = jnp.concatenate([near, near], axis=1)
            total = jnp.zeros((width, slots), F32)
            window = jnp.concatenate(
                [
                    far_ref[ex * row_count + row, f : f + chunk]
                    for f in range(0, width, chunk)
                    for ex, row in columns
                ],
                axis=0,
            )
            for k in range(0, neighbour_count, 2):
                ids = jnp.concatenate(
                    [neighbours_ref[a, b, k], neighbours_ref[a, b, k + 1]], axis=1
                )
                cell = ids >> 7
                plane = (cell * 43) >> 7
                ez = cell - plane * 3
                ey = plane & 3
                ex = plane >> 2
                if fold_y:
                    row = jnp.where(ey == 1, 0, jnp.where(ey == 2, 1, 2))
                else:
                    row = ey
                place = ex * 4 + row
                key = (ids & 127) + jnp.where(ez == 1, 0, slots)
                picker = (key_rows == key).astype(F32).astype(BF16)
                found = dot(window, picker)
                edges = jnp.concatenate([edge_ref[a, b, 0, k], edge_ref[a, b, 0, k + 1]], axis=0)
                pre = dot_nt(edge_t, edges) + near
                parts = []
                at = 0
                for f in range(0, width, chunk):
                    part = jnp.zeros((chunk, 2 * slots), F32)
                    for ex_at, row_at in columns:
                        part = jnp.where(
                            place == ex_at * 4 + row_at, found[at : at + chunk], part
                        )
                        at += chunk
                    parts.append(part)
                hidden = relu16(pre + jnp.concatenate(parts, axis=0))
                hidden = relu16(dot(middle_t, hidden))
                message = norm_rows(dot(final_t, hidden))
                total = total + message[:, :slots] + message[:, slots:]
            total = jnp.where(lane < fill_ref[a, 0, b], total, 0.0)
            gather_ref[a * 2 + b] = total.astype(BF16)

    cells = [(a, b) for a in range(2) for b in range(2)]
    aggregate = jnp.concatenate([gather_ref[i] for i in range(4)], axis=1)
    latent = jnp.concatenate([own_ref[a, b, 0] for a, b in cells], axis=0)
    pre = dot_nt(flip(node_in_ref[:width]), latent) + dot(flip(node_in_ref[width:]), aggregate)
    hidden = relu16(dot(flip(node_w_ref[0]), relu16(pre)))
    updated = (latent.astype(F32).T + norm_rows(dot(flip(node_w_ref[1]), hidden))).astype(BF16)
    hidden = relu16(dot(flip(decoder_w_ref[0]), updated))
    hidden = relu16(dot(flip(decoder_w_ref[1]), hidden))
    acceleration = dot(decoder_out_ref[...], hidden)

    def flat(ref, i):
        return jnp.concatenate([ref[i, a, b] for a, b in cells], axis=1)

    old = jnp.concatenate([flat(velocity_ref, i) for i in range(3)], axis=0)
    new_velocity = old + acceleration
    new_position = jnp.concatenate([flat(positions_ref, i) for i in range(3)], axis=0) + new_velocity
    state = jnp.concatenate([new_position, new_velocity, old], axis=0)

    owner = jnp.concatenate([owners_ref[a, b] for a, b in cells], axis=1)
    alive = jnp.concatenate(
        [(lane < fill_ref[a, 0, b]).astype(jnp.int32) for a, b in cells], axis=1
    )
    own_block = (index_x * count_y + index_y) * count_z + index_z
    stays = jnp.where((alive == 1) & (owner == own_block), 1.0, 0.0)
    moving = jnp.where((alive == 1) & (owner != own_block), 1, 0)

    extent = (2.0 * count_x, 2.0 * count_y, 1.0 * count_z)
    latents = encode(state, stays, encoder_in_ref[...], encoder_w_ref[...], extent)
    kept = state * stays
    for i, (a, b) in enumerate(cells):
        kept_latent_ref[a, b, 0] = latents[i * slots : (i + 1) * slots]
        for j in range(9):
            kept_state_ref[j, a, b] = kept[j : j + 1, i * slots : (i + 1) * slots]

    owner_x = quotient(owner, count_y * count_z)
    rest = owner - owner_x * (count_y * count_z)
    owner_y = quotient(rest, count_z)
    owner_z = rest - owner_y * count_z
    step_y = owner_y - index_y
    side_y = jnp.where(step_y == 0, 0, 1) if fold_y else jnp.where(step_y < 0, 1, 2 * step_y)
    options_y = 2 if fold_y else 3
    group = ((owner_x - index_x + 1) * options_y + side_y) * 2 + jnp.where(owner_z == index_z, 0, 1)
    groups = 3 * options_y * 2
    group_rows = (groups + 15) // 16 * 16
    particles = owner.shape[1]
    member = jnp.where(
        (lax.broadcasted_iota(jnp.int32, (group_rows, particles), 0) == group) & (moving == 1),
        1.0,
        0.0,
    )
    triangle = jnp.where(
        lax.broadcasted_iota(jnp.int32, (slots, slots), 0)
        <= lax.broadcasted_iota(jnp.int32, (slots, slots), 1),
        1.0,
        0.0,
    ).astype(BF16)
    counted = []
    before = jnp.zeros((group_rows, 1), F32)
    for i in range(4):
        inside = member[:, i * slots : (i + 1) * slots]
        counted.append(dot(inside.astype(BF16), triangle) + before)
        before = before + jnp.sum(inside, axis=1, keepdims=True)
    counted = jnp.concatenate(counted, axis=1)
    rank = (jnp.sum(counted * member, axis=0, keepdims=True) - 1.0).astype(jnp.int32)
    column = jnp.where(moving == 1, group * CAP + rank, -1)
    placer = (
        (lax.broadcasted_iota(jnp.int32, (groups * CAP, particles), 0) == column)
        .astype(F32)
        .astype(BF16)
    )
    payload = jnp.concatenate(
        [state, moving.astype(F32), jnp.zeros((ROWS - 10, particles), F32)], axis=0
    )
    placed = dot_nt(jnp.concatenate(thirds(payload), axis=0), placer)
    bucket_ref[...] = placed[:ROWS] + placed[ROWS : 2 * ROWS] + placed[2 * ROWS :]


def arrive_kernel(
    sizes,
    own_ref,
    even_ref,
    odd_ref,
    own_zed,
    even_zed,
    odd_zed,
    encoder_in_ref,
    encoder_w_ref,
    arrived_latent_ref,
    arrived_state_ref,
):
    count_x, count_y, count_z = sizes
    fold_y = count_y == 2
    index_x = lax.axis_index("gx")
    index_y = lax.axis_index("gy")
    index_z = lax.axis_index("gz")
    options_y = 2 if fold_y else 3
    lanes = own_ref.shape[-1]
    group = lax.broadcasted_iota(jnp.int32, (ROWS, lanes), 1) >> 3
    even = (index_x & 1) == 0
    found = jnp.zeros((ROWS, lanes), F32)
    for source_x in (-1, 0, 1):
        for from_y in range(options_y):
            for from_z in range(2):
                if source_x == 0 and from_y == 0 and from_z == 0:
                    continue
                own, first, second = (own_ref, even_ref, odd_ref) if from_z == 0 else (own_zed, even_zed, odd_zed)
                side_y = from_y if fold_y or from_y == 0 else 3 - from_y
                target = ((1 - source_x) * options_y + side_y) * 2 + from_z
                if source_x == 0:
                    tile = own[from_y]
                    there = group == target
                elif source_x == -1:
                    tile = jnp.where(even, second[from_y], first[from_y])
                    there = (group == target) & (index_x > 0)
                else:
                    tile = jnp.where(even, first[from_y], second[from_y])
                    there = (group == target) & (index_x < count_x - 1)
                found = jnp.where(there, tile, found)
    out_lanes = arrived_state_ref.shape[-1]
    spread_shape = (lanes, out_lanes)
    line = lax.broadcasted_iota(jnp.int32, spread_shape, 0)
    from_group = line >> 3
    plane = quotient(from_group, 2)
    from_x = 1 - quotient(plane, options_y) if fold_y else 1 - ((plane * 43) >> 7)
    side_y = plane - (1 - from_x) * options_y
    if fold_y:
        from_y = jnp.where(side_y == 0, 0, jnp.where(index_y == 0, 1, -1))
    else:
        from_y = jnp.where(side_y == 0, 0, jnp.where(side_y == 1, 1, -1))
    from_z = jnp.where((from_group & 1) == 0, 0, jnp.where(index_z == 0, 1, -1))
    direction = (from_x + 1) * 9 + (from_y + 1) * 3 + from_z + 1
    direction = direction - jnp.where(direction > 13, 1, 0)
    column = direction * CAP + (line & 7)
    valid = (lax.broadcasted_iota(jnp.int32, spread_shape, 1) == column) & (
        (from_x != 0) | (from_y != 0) | (from_z != 0)
    )
    spread = jnp.where(valid, 1.0, 0.0).astype(BF16)
    arrived = dot(jnp.concatenate(thirds(found), axis=0), spread)
    arrived = arrived[:ROWS] + arrived[ROWS : 2 * ROWS] + arrived[2 * ROWS :]
    for j in range(9):
        arrived_state_ref[j, 0, 0] = arrived[j : j + 1]
    extent = (2.0 * count_x, 2.0 * count_y, 1.0 * count_z)
    arrived_latent_ref[0, 0, 0] = encode(
        arrived[:9], arrived[9:10], encoder_in_ref[...], encoder_w_ref[...], extent
    )


def along(count):
    up = [(i, i + 1) for i in range(count - 1)]
    return up, [(j, i) for i, j in up]


def swap(values, axis):
    return lax.ppermute(values, axis, [(0, 1), (1, 0)])


def shift(values, axis, way):
    return lax.ppermute(values, axis, along(lax.axis_size(axis))[way])


def swap_x(values, first):
    count = lax.axis_size("gx")
    pairs = []
    for x in range(count):
        partner = x + 1 if (x - first) % 2 == 0 else x - 1
        for z in range(2):
            if 0 <= partner < count:
                pairs.append((x * 2 + z, partner * 2 + z))
            else:
                pairs.append((x * 2 + z, x * 2 + 1 - z))
    return lax.ppermute(values, ("gx", "gz"), pairs)


def body(
    node_latent,
    edge_latent,
    positions,
    velocity,
    fill,
    neighbours,
    owners,
    edge_weights,
    node_in,
    node_weights,
    decoder_weights,
    decoder_out,
    encoder_in,
    encoder_weights,
):
    sizes = tuple(lax.axis_size(axis) for axis in ("gx", "gy", "gz"))
    fold_y = sizes[1] == 2
    slots, width = node_latent.shape[-2:]
    parity = lax.axis_index("gx") & 1
    cells = node_latent[:, :, 0]
    if fold_y:
        inner = 1 - lax.axis_index("gy")
        sides = [swap(lax.dynamic_index_in_dim(cells, inner, 1, keepdims=False), "gy")]
        layers = [cells, sides[0][:, None]]
    else:
        sides = [shift(cells[:, 1], "gy", 0), shift(cells[:, 0], "gy", 1)]
        layers = [sides[0][:, None], cells, sides[1][:, None]]

    def layer(a):
        return jnp.concatenate(
            [lax.dynamic_index_in_dim(part, a, 0, keepdims=False) for part in layers], axis=0
        )

    even = swap_x(layer(1 - parity), 0)
    odd = swap_x(layer(parity), 1)
    halo = [node_latent, *sides, even, odd]
    halo = halo + [swap(part, "gz") for part in halo]

    options_y = 2 if fold_y else 3
    lanes = 3 * options_y * 2 * CAP
    rows = 3 if fold_y else 4
    vmem = pl.BlockSpec(memory_space=pltpu.VMEM)
    smem = pl.BlockSpec(memory_space=pltpu.SMEM)
    count = len(sides)

    def step(fill_ref, *refs):
        own_ref, *side_refs, even_ref, odd_ref = refs[: count + 3]
        own_zed, *side_zeds, even_zed, odd_zed = refs[count + 3 : 2 * count + 6]
        step_kernel(
            sizes,
            fill_ref,
            own_ref,
            side_refs,
            even_ref,
            odd_ref,
            (own_zed, side_zeds, even_zed, odd_zed),
            *refs[2 * count + 6 :],
        )

    kept_latent, kept_state, bucket = pl.pallas_call(
        step,
        out_shape=(
            jax.ShapeDtypeStruct(node_latent.shape, BF16),
            jax.ShapeDtypeStruct((9,) + node_latent.shape[:4], F32),
            jax.ShapeDtypeStruct((ROWS, lanes), F32),
        ),
        in_specs=[smem] + [vmem] * (len(halo) + 12),
        out_specs=(vmem, vmem, vmem),
        scratch_shapes=[
            pltpu.VMEM((4 * rows, width, 2 * slots), BF16),
            pltpu.VMEM((4, width, slots), BF16),
        ],
        compiler_params=pltpu.CompilerParams(vmem_limit_bytes=40 * 1024 * 1024),
        name="step",
    )(
        jnp.transpose(fill, (0, 2, 1)),
        *halo,
        edge_latent,
        positions,
        velocity,
        neighbours.reshape(2, 2, neighbours.shape[3], 1, slots),
        owners,
        edge_weights,
        node_in,
        node_weights,
        decoder_weights,
        decoder_out,
        encoder_in,
        encoder_weights,
    )

    if fold_y:
        tiles = jnp.stack([bucket, swap(bucket, "gy")], axis=0)
    else:
        tiles = jnp.stack([bucket, shift(bucket, "gy", 0), shift(bucket, "gy", 1)], axis=0)
    tiles = [tiles, swap_x(tiles, 0), swap_x(tiles, 1)]
    tiles = tiles + [swap(part, "gz") for part in tiles]
    arrived_latent, arrived_state = pl.pallas_call(
        functools.partial(arrive_kernel, sizes),
        out_shape=(
            jax.ShapeDtypeStruct((1, 1, 1, 26 * CAP, width), BF16),
            jax.ShapeDtypeStruct((9, 1, 1, 1, 26 * CAP), F32),
        ),
        in_specs=[vmem] * 8,
        out_specs=(vmem, vmem),
        name="arrive",
    )(*tiles, encoder_in, encoder_weights)
    return kept_latent, kept_state, arrived_latent, arrived_state


def solution(mesh):
    placed = (
        P(("group", "gx"), "gy", "gz", None, None),
        P(("group", "gx"), "gy", "gz", None, None, None),
        P(None, ("group", "gx"), "gy", "gz", None),
        P(None, ("group", "gx"), "gy", "gz", None),
        P(("group", "gx"), "gy", "gz"),
        P(("group", "gx"), "gy", "gz", None, None),
        P(("group", "gx"), "gy", "gz", None),
        P(),
        P(),
        P(),
        P(),
        P(),
        P(),
        P(),
    )
    return jax.shard_map(
        body,
        mesh=mesh,
        in_specs=placed,
        out_specs=(
            P(("group", "gx"), "gy", "gz", None, None),
            P(None, ("group", "gx"), "gy", "gz", None),
            P(("group", "gx"), "gy", "gz", None, None),
            P(None, ("group", "gx"), "gy", "gz", None),
        ),
        check_vma=False,
    )
```

```python
import functools

import jax
import jax.numpy as jnp
from jax import lax
from jax.experimental import pallas as pl
from jax.experimental.pallas import tpu as pltpu
from jax.sharding import PartitionSpec as P

CAP = 8
F32 = jnp.float32
BF16 = jnp.bfloat16
I32 = jnp.int32
ROWS = 16
TILE = 256
CELLS = [(a, b) for a in range(2) for b in range(2)]
EDGE, NEAR, FAR, MIDDLE, FINAL, NODE_OLD, NODE_NEW, NODE_0, NODE_1, DECODE_0, DECODE_1 = range(11)

VMEM = pl.BlockSpec(memory_space=pltpu.VMEM)
SMEM = pl.BlockSpec(memory_space=pltpu.SMEM)
ANY = pl.BlockSpec(memory_space=pl.ANY)


def dot(left, right):
    return jnp.dot(left, right, preferred_element_type=F32)


def dot_nt(left, right):
    return lax.dot_general(left, right, (((1,), (1,)), ((), ())), preferred_element_type=F32)


def dot_tn(left, right):
    return lax.dot_general(left, right, (((0,), (0,)), ((), ())), preferred_element_type=F32)


def relu16(values):
    return jnp.maximum(values, 0.0).astype(BF16)


def norm(values, axis):
    scale = 1.0 / values.shape[axis]
    centred = values - jnp.sum(values, axis=axis, keepdims=True) * scale
    spread = jnp.sum(centred * centred, axis=axis, keepdims=True) * scale
    return centred * lax.rsqrt(spread + 1e-05)


def thirds(values):
    high = values.astype(BF16)
    rest = values - high.astype(F32)
    middle = rest.astype(BF16)
    low = (rest - middle.astype(F32)).astype(BF16)
    return jnp.concatenate([high, middle, low], axis=0)


def joined(values):
    rows = values.shape[0] // 3
    return values[:rows] + values[rows : 2 * rows] + values[2 * rows :]


def quotient(values, count):
    if count & (count - 1) == 0:
        return values >> (count.bit_length() - 1)
    return lax.div(values, jnp.full_like(values, count))


def flip(weights):
    return weights.astype(F32).T.astype(BF16)


def fetch(pairs, sems):
    copies = [pltpu.make_async_copy(src, dst, sems.at[i]) for i, (src, dst) in enumerate(pairs)]
    for copy in copies:
        copy.start()
    return copies


def encode(state, mask, inward, encoder_w, extent):
    width = state.shape[1]
    position = state[0:3]
    row = lax.broadcasted_iota(I32, (3, width), 0)
    size = jnp.where(row == 0, extent[0], jnp.where(row == 1, extent[1], extent[2]))
    features = jnp.concatenate(
        [
            state[3:9],
            jnp.clip(position, -1.0, 1.0),
            jnp.clip(size - position, -1.0, 1.0),
            jnp.zeros((4, width), F32),
        ],
        axis=0,
    )
    hidden = relu16(dot_tn(thirds(features), inward))
    hidden = relu16(dot(hidden, encoder_w[0]))
    column = jnp.broadcast_to(mask, (8, width)).T[:, 0:1]
    return (norm(dot(hidden, encoder_w[1]), 1) * column).astype(BF16)


def places(ids_low, ids_high, fold_y):
    plane = (ids_high * 43) >> 7
    ez = ids_high - plane * 3
    ey = plane & 3
    ex = plane >> 2
    if fold_y:
        row = jnp.where(ey == 1, 0, jnp.where(ey == 2, 1, 2))
    else:
        row = ey
    return ex * 4 + row, ids_low + jnp.where(ez == 1, 0, 128)


def messages(far_ref, columns, row_count, place, key, pre, middle_t, final_t, hidden_ref):
    width = far_ref.shape[1]
    chunk = 32
    window = jnp.concatenate(
        [
            far_ref[ex * row_count + row, f : f + chunk]
            for f in range(0, width, chunk)
            for ex, row in columns
        ],
        axis=0,
    )
    key_rows = lax.broadcasted_iota(I32, (TILE, TILE), 0)
    lanes = place.shape[1]
    for tile in range(lanes // TILE):
        at = slice(tile * TILE, (tile + 1) * TILE)
        picker = jnp.where(key_rows == key[:, at], 1.0, 0.0).astype(BF16)
        found = dot(window, picker).reshape(width // chunk, len(columns), chunk // 8, 8, TILE)
        where = jnp.broadcast_to(place[:, at], (8, TILE))
        parts = []
        for f in range(width // chunk):
            part = jnp.zeros((chunk // 8, 8, TILE), F32)
            for i, (ex, row) in enumerate(columns):
                part = jnp.where((where == ex * 4 + row)[None], found[f, i], part)
            parts.append(part.reshape(chunk, TILE))
        hidden_ref[:, at] = relu16(pre(tile) + jnp.concatenate(parts, axis=0))
    hidden = relu16(dot(middle_t, hidden_ref[...]))
    return norm(dot(final_t, hidden), 0)


def slot_sum(message, step):
    total = message[:, :step]
    for at in range(step, message.shape[1], step):
        total = total + message[:, at : at + step]
    return total


def advance(pre, aggregate, latent_t, weights_ref, decoder_out):
    pre = pre + dot(weights_ref[NODE_NEW], aggregate)
    hidden = relu16(dot(weights_ref[NODE_0], relu16(pre)))
    updated = (latent_t + norm(dot(weights_ref[NODE_1], hidden), 0)).astype(BF16)
    hidden = relu16(dot(weights_ref[DECODE_0], updated))
    hidden = relu16(dot(weights_ref[DECODE_1], hidden))
    return dot(decoder_out, hidden)


def moved(position, velocity, acceleration):
    new_velocity = velocity + acceleration
    return jnp.concatenate([position + new_velocity, new_velocity, velocity], axis=0)


def prepare_kernel(
    sizes,
    fill_ref,
    latent_any,
    edge_any,
    positions_any,
    velocity_any,
    neighbours_any,
    owners_any,
    edge_w_any,
    node_in_any,
    node_w_any,
    decoder_w_any,
    decoder_out_any,
    encoder_in_any,
    encoder_w_any,
    weights_ref,
    decoder_out_ref,
    inward_ref,
    encoder_w_ref,
    latent_t_ref,
    node_pre_ref,
    state_ref,
    mover_pre_ref,
    mover_place_ref,
    mover_key_ref,
    mover_node_pre_ref,
    mover_latent_ref,
    mover_state_ref,
    latent_ref,
    edge_ref,
    positions_ref,
    velocity_ref,
    neighbours_ref,
    owners_ref,
    edge_w_ref,
    node_in_ref,
    node_w_ref,
    decoder_w_ref,
    encoder_in_ref,
    sems,
):
    count_x, count_y, count_z = sizes
    fold_y = count_y == 2
    copies = fetch(
        [
            (owners_any, owners_ref),
            (edge_w_any, edge_w_ref),
            (neighbours_any, neighbours_ref),
            (positions_any, positions_ref),
            (velocity_any, velocity_ref),
            (latent_any, latent_ref),
            (edge_any, edge_ref),
            (node_in_any, node_in_ref),
            (node_w_any, node_w_ref),
            (decoder_w_any, decoder_w_ref),
            (decoder_out_any, decoder_out_ref),
            (encoder_in_any, encoder_in_ref),
            (encoder_w_any, encoder_w_ref),
        ],
        sems,
    )
    for copy in copies:
        copy.wait()
    index_x = lax.axis_index("gx")
    index_y = lax.axis_index("gy")
    index_z = lax.axis_index("gz")
    slots, width = latent_ref.shape[-2:]
    neighbour_count = edge_ref.shape[3]

    lane = lax.broadcasted_iota(I32, (1, slots), 1)
    owner = jnp.concatenate([owners_ref[a, b] for a, b in CELLS], axis=1)
    alive = jnp.concatenate([jnp.where(lane < fill_ref[a, 0, b], 1, 0) for a, b in CELLS], axis=1)
    own_block = (index_x * count_y + index_y) * count_z + index_z
    stays = jnp.where((alive == 1) & (owner == own_block), 1.0, 0.0)
    moving = jnp.where((alive == 1) & (owner != own_block), 1, 0)
    owner_x = quotient(owner, count_y * count_z)
    rest = owner - owner_x * (count_y * count_z)
    owner_y = quotient(rest, count_z)
    owner_z = rest - owner_y * count_z
    step_y = owner_y - index_y
    side_y = jnp.where(step_y == 0, 0, 1) if fold_y else jnp.where(step_y < 0, 1, 2 * step_y)
    options_y = 2 if fold_y else 3
    group = ((owner_x - index_x + 1) * options_y + side_y) * 2 + jnp.where(owner_z == index_z, 0, 1)
    group_rows = (3 * options_y * 2 + 15) // 16 * 16
    particles = owner.shape[1]
    member = jnp.where(
        (lax.broadcasted_iota(I32, (group_rows, particles), 0) == group) & (moving == 1), 1.0, 0.0
    )
    triangle = jnp.where(
        lax.broadcasted_iota(I32, (slots, slots), 0) <= lax.broadcasted_iota(I32, (slots, slots), 1),
        1.0,
        0.0,
    ).astype(BF16)
    counted = []
    before = jnp.zeros((group_rows, 1), F32)
    for i in range(4):
        inside = member[:, i * slots : (i + 1) * slots]
        counted.append(dot(inside.astype(BF16), triangle) + before)
        before = before + jnp.sum(inside, axis=1, keepdims=True)
    counted = jnp.concatenate(counted, axis=1)
    rank = (jnp.sum(counted * member, axis=0, keepdims=True) - 1.0).astype(I32)
    column = jnp.where(moving == 1, group * CAP + rank, -1)
    movers = mover_state_ref.shape[1]
    placer = jnp.where(
        lax.broadcasted_iota(I32, (movers, particles), 0) == column, 1.0, 0.0
    ).astype(BF16)

    for i in range(5):
        weights_ref[i] = flip(edge_w_ref[i])
    weights_ref[NODE_OLD] = flip(node_in_ref[:width])
    weights_ref[NODE_NEW] = flip(node_in_ref[width:])
    for i in range(2):
        weights_ref[NODE_0 + i] = flip(node_w_ref[i])
        weights_ref[DECODE_0 + i] = flip(decoder_w_ref[i])
    inward = jnp.concatenate([encoder_in_ref[...].astype(F32), jnp.zeros((4, width), F32)], axis=0)
    inward = inward.astype(BF16)
    inward_ref[...] = jnp.concatenate([inward, inward, inward], axis=0)

    latent = jnp.concatenate([latent_ref[a, b, 0] for a, b in CELLS], axis=0)
    latent_t_ref[...] = latent.astype(F32).T
    node_pre_ref[...] = dot_nt(weights_ref[NODE_OLD], latent)

    def flat(ref, i):
        return jnp.concatenate([ref[i, a, b] for a, b in CELLS], axis=1)

    state = [flat(positions_ref, i) for i in range(3)] + [flat(velocity_ref, i) for i in range(3)]
    state_ref[...] = jnp.concatenate(state + [stays, jnp.zeros_like(stays)], axis=0)

    mover_latent = dot(placer, latent).astype(BF16)
    mover_latent_ref[...] = mover_latent.astype(F32).T
    mover_node_pre_ref[...] = dot_nt(weights_ref[NODE_OLD], mover_latent)
    near = dot_nt(weights_ref[NEAR], mover_latent)
    state = jnp.concatenate(state + [moving.astype(F32), jnp.zeros_like(stays)], axis=0)
    mover_state_ref[...] = joined(dot_nt(thirds(state), placer))
    ids = jnp.concatenate(
        [
            jnp.concatenate([neighbours_ref[a, b, k] for a, b in CELLS], axis=1)
            for k in range(neighbour_count)
        ],
        axis=0,
    )
    ids = jnp.concatenate([ids & 127, ids >> 7, jnp.zeros((8, particles), I32)], axis=0)
    ids = dot_nt(ids.astype(F32).astype(BF16), placer).astype(I32)
    place, key = places(ids[:neighbour_count], ids[neighbour_count : 2 * neighbour_count], fold_y)
    mover_place_ref[...] = place
    mover_key_ref[...] = key
    for k in range(neighbour_count):
        edges = jnp.concatenate([edge_ref[a, b, 0, k] for a, b in CELLS], axis=0)
        edges = dot(placer, edges).astype(BF16)
        mover_pre_ref[:, k * movers : (k + 1) * movers] = dot_nt(weights_ref[EDGE], edges) + near


def movers_kernel(
    sizes,
    side_count,
    latent_any,
    *refs,
):
    count_x, count_y, _ = sizes
    fold_y = count_y == 2
    side_refs, refs = refs[:side_count], refs[side_count:]
    even_ref, odd_ref, own_zed, refs = refs[0], refs[1], refs[2], refs[3:]
    side_zeds, refs = refs[:side_count], refs[side_count:]
    even_zed, odd_zed, refs = refs[0], refs[1], refs[2:]
    (
        weights_ref,
        decoder_out_ref,
        pre_ref,
        place_ref,
        key_ref,
        node_pre_ref,
        latent_t_ref,
        state_ref,
        far_ref,
        bucket_ref,
        own_ref,
        hidden_ref,
        sems,
    ) = refs
    copies = fetch([(latent_any, own_ref)], sems)
    row_count = 3 if fold_y else 4
    own_rows = (0, 1) if fold_y else (1, 2)
    outer = {2: 0} if fold_y else {0: 0, 3: 1}
    parity = lax.axis_index("gx") & 1
    far_t = weights_ref[FAR]

    def far(at, here, beside):
        pair = jnp.concatenate([here, beside], axis=0)
        far_ref[at] = dot_nt(far_t, pair).astype(BF16)

    copies[0].wait()
    for row in range(row_count):
        for ex in (1, 2):
            if row in own_rows:
                b = own_rows.index(row)
                far(ex * row_count + row, own_ref[ex - 1, b, 0], own_zed[ex - 1, b, 0])
            else:
                side = outer[row]
                far(ex * row_count + row, side_refs[side][ex - 1], side_zeds[side][ex - 1])
        far(3 * (1 - parity) * row_count + row, even_ref[row], even_zed[row])
        far(3 * parity * row_count + row, odd_ref[row], odd_zed[row])

    movers = state_ref.shape[1]
    neighbour_count = place_ref.shape[0]
    place = jnp.concatenate([place_ref[k : k + 1] for k in range(neighbour_count)], axis=1)
    key = jnp.concatenate([key_ref[k : k + 1] for k in range(neighbour_count)], axis=1)
    columns = [(ex, row) for ex in range(4) for row in range(row_count)]
    message = messages(
        far_ref,
        columns,
        row_count,
        place,
        key,
        lambda tile: pre_ref[:, tile * TILE : (tile + 1) * TILE],
        weights_ref[MIDDLE],
        weights_ref[FINAL],
        hidden_ref,
    )
    aggregate = slot_sum(message, movers).astype(BF16)
    acceleration = advance(
        node_pre_ref[...], aggregate, latent_t_ref[...], weights_ref, decoder_out_ref[...]
    )
    mask = state_ref[6:7]
    state = moved(state_ref[0:3], state_ref[3:6], acceleration) * mask
    bucket_ref[...] = jnp.concatenate([state, mask, jnp.zeros((ROWS - 10, movers), F32)], axis=0)


def edges_kernel(
    sizes,
    a,
    fill_ref,
    latent_any,
    edge_any,
    neighbours_any,
    far_ref,
    weights_ref,
    total_ref,
    latent_ref,
    edge_ref,
    neighbours_ref,
    hidden_ref,
    sems,
):
    fold_y = sizes[1] == 2
    row_count = 3 if fold_y else 4
    index_y = lax.axis_index("gy")
    copies = fetch(
        [
            (neighbours_any.at[a], neighbours_ref),
            (latent_any.at[a], latent_ref),
            (edge_any.at[a], edge_ref),
        ],
        sems,
    )
    for copy in copies:
        copy.wait()
    slots, width = latent_ref.shape[-2:]
    neighbour_count = edge_ref.shape[2]
    lane = lax.broadcasted_iota(I32, (1, slots), 1)
    for bt in range(2):
        if fold_y:
            b = index_y if bt == 0 else 1 - index_y
            rows = (0, 1) if bt == 0 else (0, 1, 2)
        else:
            b = bt
            rows = (bt, bt + 1, bt + 2)
        columns = [(ex, row) for ex in range(a, a + 3) for row in rows]
        near = dot_nt(weights_ref[NEAR], latent_ref[b, 0])
        near = jnp.concatenate([near, near], axis=1)
        ids = jnp.concatenate([neighbours_ref[b, k] for k in range(neighbour_count)], axis=1)
        place, key = places(ids & 127, ids >> 7, fold_y)

        def pre(tile, b=b, near=near):
            edges = jnp.concatenate([edge_ref[b, 0, 2 * tile], edge_ref[b, 0, 2 * tile + 1]], axis=0)
            return dot_nt(weights_ref[EDGE], edges) + near

        message = messages(
            far_ref,
            columns,
            row_count,
            place,
            key,
            pre,
            weights_ref[MIDDLE],
            weights_ref[FINAL],
            hidden_ref.at[bt],
        )
        total = jnp.where(lane < fill_ref[a, 0, b], slot_sum(message, slots), 0.0)
        total_ref[b] = total.astype(BF16)


def nodes_kernel(
    sizes,
    first_ref,
    second_ref,
    node_pre_ref,
    latent_t_ref,
    state_ref,
    weights_ref,
    decoder_out_ref,
    inward_ref,
    encoder_w_ref,
    kept_latent_ref,
    kept_state_ref,
):
    slots = first_ref.shape[-1]
    aggregate = jnp.concatenate([first_ref[0], first_ref[1], second_ref[0], second_ref[1]], axis=1)
    acceleration = advance(
        node_pre_ref[...], aggregate, latent_t_ref[...], weights_ref, decoder_out_ref[...]
    )
    stays = state_ref[6:7]
    state = moved(state_ref[0:3], state_ref[3:6], acceleration)
    extent = (2.0 * sizes[0], 2.0 * sizes[1], 1.0 * sizes[2])
    latents = encode(state, stays, inward_ref[...], encoder_w_ref[...], extent)
    kept = state * stays
    for i, (a, b) in enumerate(CELLS):
        kept_latent_ref[a, b, 0] = latents[i * slots : (i + 1) * slots]
        for j in range(9):
            kept_state_ref[j, a, b] = kept[j : j + 1, i * slots : (i + 1) * slots]


def arrive_kernel(
    sizes,
    own_ref,
    even_ref,
    odd_ref,
    own_zed,
    even_zed,
    odd_zed,
    inward_ref,
    encoder_w_ref,
    arrived_latent_ref,
    arrived_state_ref,
):
    count_x, count_y, count_z = sizes
    fold_y = count_y == 2
    index_x = lax.axis_index("gx")
    index_y = lax.axis_index("gy")
    index_z = lax.axis_index("gz")
    options_y = 2 if fold_y else 3
    lanes = own_ref.shape[-1]
    group = lax.broadcasted_iota(I32, (ROWS, lanes), 1) >> 3
    even = (index_x & 1) == 0
    found = jnp.zeros((ROWS, lanes), F32)
    for source_x in (-1, 0, 1):
        for from_y in range(options_y):
            for from_z in range(2):
                if source_x == 0 and from_y == 0 and from_z == 0:
                    continue
                if from_z == 0:
                    own, first, second = own_ref, even_ref, odd_ref
                else:
                    own, first, second = own_zed, even_zed, odd_zed
                side_y = from_y if fold_y or from_y == 0 else 3 - from_y
                target = ((1 - source_x) * options_y + side_y) * 2 + from_z
                if source_x == 0:
                    tile = own[from_y]
                    there = group == target
                elif source_x == -1:
                    tile = jnp.where(even, second[from_y], first[from_y])
                    there = (group == target) & (index_x > 0)
                else:
                    tile = jnp.where(even, first[from_y], second[from_y])
                    there = (group == target) & (index_x < count_x - 1)
                found = jnp.where(there, tile, found)
    out_lanes = arrived_state_ref.shape[-1]
    spread_shape = (lanes, out_lanes)
    line = lax.broadcasted_iota(I32, spread_shape, 0)
    from_group = line >> 3
    plane = from_group >> 1
    from_x = 1 - ((plane >> 1) if fold_y else ((plane * 43) >> 7))
    side_y = plane - (1 - from_x) * options_y
    if fold_y:
        from_y = jnp.where(side_y == 0, 0, jnp.where(index_y == 0, 1, -1))
    else:
        from_y = jnp.where(side_y == 0, 0, jnp.where(side_y == 1, 1, -1))
    from_z = jnp.where((from_group & 1) == 0, 0, jnp.where(index_z == 0, 1, -1))
    direction = (from_x + 1) * 9 + (from_y + 1) * 3 + from_z + 1
    direction = direction - jnp.where(direction > 13, 1, 0)
    column = direction * CAP + (line & 7)
    valid = (lax.broadcasted_iota(I32, spread_shape, 1) == column) & (
        (from_x != 0) | (from_y != 0) | (from_z != 0)
    )
    spread = jnp.where(valid, 1.0, 0.0).astype(BF16)
    arrived = joined(dot(thirds(found), spread))
    for j in range(9):
        arrived_state_ref[j, 0, 0] = arrived[j : j + 1]
    extent = (2.0 * count_x, 2.0 * count_y, 1.0 * count_z)
    arrived_latent_ref[0, 0, 0] = encode(
        arrived[:9], arrived[9:10], inward_ref[...], encoder_w_ref[...], extent
    )


def swap(values, axis):
    return lax.ppermute(values, axis, [(0, 1), (1, 0)])


def shift(values, axis, way):
    pairs = [(i, i + 1) for i in range(lax.axis_size(axis) - 1)]
    return lax.ppermute(values, axis, [(j, i) for i, j in pairs] if way else pairs)


def swap_x(values, first):
    count = lax.axis_size("gx")
    pairs = []
    for x in range(count):
        partner = x + 1 if (x - first) % 2 == 0 else x - 1
        for z in range(2):
            if 0 <= partner < count:
                pairs.append((x * 2 + z, partner * 2 + z))
            else:
                pairs.append((x * 2 + z, x * 2 + 1 - z))
    return lax.ppermute(values, ("gx", "gz"), pairs)


def call(kernel, name, in_specs, outs, scratch, operands, flops):
    return pl.pallas_call(
        kernel,
        out_shape=tuple(jax.ShapeDtypeStruct(shape, kind) for shape, kind in outs),
        in_specs=in_specs,
        out_specs=tuple(VMEM for _ in outs),
        scratch_shapes=scratch,
        compiler_params=pltpu.CompilerParams(vmem_limit_bytes=32 * 1024 * 1024),
        cost_estimate=pl.CostEstimate(flops=flops, bytes_accessed=0, transcendentals=0),
        name=name,
    )(*operands)


def like(array):
    return pltpu.VMEM(array.shape, array.dtype)


def body(
    node_latent,
    edge_latent,
    positions,
    velocity,
    fill,
    neighbours,
    owners,
    edge_weights,
    node_in,
    node_weights,
    decoder_weights,
    decoder_out,
    encoder_in,
    encoder_weights,
):
    sizes = tuple(lax.axis_size(axis) for axis in ("gx", "gy", "gz"))
    fold_y = sizes[1] == 2
    slots, width = node_latent.shape[-2:]
    neighbour_count = neighbours.shape[3]
    particles = 4 * slots
    options_y = 2 if fold_y else 3
    movers = (3 * options_y * 2 * CAP + 127) // 128 * 128
    rows = 3 if fold_y else 4
    fill = jnp.transpose(fill, (0, 2, 1))
    neighbours = neighbours.reshape(2, 2, neighbour_count, 1, slots)

    parity = lax.axis_index("gx") & 1
    cells = node_latent[:, :, 0]
    if fold_y:
        inner = 1 - lax.axis_index("gy")
        sides = [swap(lax.dynamic_index_in_dim(cells, inner, 1, keepdims=False), "gy")]
    else:
        sides = [shift(cells[:, 1], "gy", 0), shift(cells[:, 0], "gy", 1)]

    prepared = call(
        functools.partial(prepare_kernel, sizes),
        "prepare",
        [SMEM] + [ANY] * 13,
        [
            ((11, width, width), BF16),
            (decoder_out.shape, BF16),
            ((48, width), BF16),
            (encoder_weights.shape, BF16),
            ((width, particles), F32),
            ((width, particles), F32),
            ((8, particles), F32),
            ((width, neighbour_count * movers), F32),
            ((neighbour_count, movers), I32),
            ((neighbour_count, movers), I32),
            ((width, movers), F32),
            ((width, movers), F32),
            ((8, movers), F32),
        ],
        [
            like(node_latent),
            like(edge_latent),
            like(positions),
            like(velocity),
            like(neighbours),
            like(owners),
            like(edge_weights),
            like(node_in),
            like(node_weights),
            like(decoder_weights),
            like(encoder_in),
            pltpu.SemaphoreType.DMA((13,)),
        ],
        (
            fill,
            node_latent,
            edge_latent,
            positions,
            velocity,
            neighbours,
            owners,
            edge_weights,
            node_in,
            node_weights,
            decoder_weights,
            decoder_out,
            encoder_in,
            encoder_weights,
        ),
        2_000_000_000,
    )
    sides, prepared = lax.optimization_barrier((sides, prepared))
    (
        weights,
        decoder_out,
        inward,
        encoder_weights,
        latent_t,
        node_pre,
        state,
        mover_pre,
        mover_place,
        mover_key,
        mover_node_pre,
        mover_latent,
        mover_state,
    ) = prepared

    if fold_y:
        layers = [cells, sides[0][:, None]]
    else:
        layers = [sides[0][:, None], cells, sides[1][:, None]]

    def layer(a):
        return jnp.concatenate(
            [lax.dynamic_index_in_dim(part, a, 0, keepdims=False) for part in layers], axis=0
        )

    halo = [*sides, swap_x(layer(1 - parity), 0), swap_x(layer(parity), 1)]
    halo = halo + [swap(part, "gz") for part in [node_latent] + halo]

    far, bucket = call(
        functools.partial(movers_kernel, sizes, len(sides)),
        "movers",
        [ANY] + [VMEM] * (len(halo) + 8),
        [((4 * rows, width, 2 * slots), BF16), ((ROWS, movers), F32)],
        [
            like(node_latent),
            pltpu.VMEM((width, neighbour_count * movers), BF16),
            pltpu.SemaphoreType.DMA((1,)),
        ],
        (
            node_latent,
            *halo,
            weights,
            decoder_out,
            mover_pre,
            mover_place,
            mover_key,
            mover_node_pre,
            mover_latent,
            mover_state,
        ),
        3_000_000_000,
    )

    def edges(a):
        return call(
            functools.partial(edges_kernel, sizes, a),
            "edges",
            [SMEM] + [ANY] * 3 + [VMEM] * 2,
            [((2, width, slots), BF16)],
            [
                pltpu.VMEM(node_latent.shape[1:], BF16),
                pltpu.VMEM(edge_latent.shape[1:], BF16),
                pltpu.VMEM(neighbours.shape[1:], I32),
                pltpu.VMEM((2, width, neighbour_count * slots), BF16),
                pltpu.SemaphoreType.DMA((3,)),
            ],
            (fill, node_latent, edge_latent, neighbours, far, weights),
            4_000_000_000,
        )[0]

    first = edges(0)
    if fold_y:
        tiles = [swap(bucket, "gy")]
    else:
        tiles = [shift(bucket, "gy", 0), shift(bucket, "gy", 1)]
    tiles, first = lax.optimization_barrier((tiles, first))
    tiles = jnp.stack([bucket, *tiles], axis=0)
    second = edges(1)
    sided = [swap_x(tiles, 0), swap_x(tiles, 1)]
    sided, second = lax.optimization_barrier((sided, second))
    tiles = [tiles, *sided]
    tiles = tiles + [swap(part, "gz") for part in tiles]
    kept_latent, kept_state = call(
        functools.partial(nodes_kernel, sizes),
        "nodes",
        [VMEM] * 9,
        [(node_latent.shape, BF16), ((9,) + node_latent.shape[:4], F32)],
        [],
        (
            first,
            second,
            node_pre,
            latent_t,
            state,
            weights,
            decoder_out,
            inward,
            encoder_weights,
        ),
        2_000_000_000,
    )
    arrived_latent, arrived_state = call(
        functools.partial(arrive_kernel, sizes),
        "arrive",
        [VMEM] * 8,
        [((1, 1, 1, 26 * CAP, width), BF16), ((9, 1, 1, 1, 26 * CAP), F32)],
        [],
        (*tiles, inward, encoder_weights),
        1_000_000_000,
    )
    return kept_latent, kept_state, arrived_latent, arrived_state


def solution(mesh):
    placed = (
        P(("group", "gx"), "gy", "gz", None, None),
        P(("group", "gx"), "gy", "gz", None, None, None),
        P(None, ("group", "gx"), "gy", "gz", None),
        P(None, ("group", "gx"), "gy", "gz", None),
        P(("group", "gx"), "gy", "gz"),
        P(("group", "gx"), "gy", "gz", None, None),
        P(("group", "gx"), "gy", "gz", None),
        P(),
        P(),
        P(),
        P(),
        P(),
        P(),
        P(),
    )
    return jax.shard_map(
        body,
        mesh=mesh,
        in_specs=placed,
        out_specs=(
            P(("group", "gx"), "gy", "gz", None, None),
            P(None, ("group", "gx"), "gy", "gz", None),
            P(("group", "gx"), "gy", "gz", None, None),
            P(None, ("group", "gx"), "gy", "gz", None),
        ),
        check_vma=False,
    )
```

```python
import functools

import jax
import jax.numpy as jnp
from jax import lax
from jax.experimental import pallas as pl
from jax.experimental.pallas import tpu as pltpu
from jax.sharding import PartitionSpec as P

CAP = 8
F32 = jnp.float32
BF16 = jnp.bfloat16
I32 = jnp.int32
ROWS = 16
TILE = 256
CELLS = [(a, b) for a in range(2) for b in range(2)]
EDGE, NEAR, FAR, MIDDLE, FINAL, NODE_OLD, NODE_NEW, NODE_0, NODE_1, DECODE_0, DECODE_1 = range(11)

VMEM = pl.BlockSpec(memory_space=pltpu.VMEM)
SMEM = pl.BlockSpec(memory_space=pltpu.SMEM)
ANY = pl.BlockSpec(memory_space=pl.ANY)


def dot(left, right):
    return jnp.dot(left, right, preferred_element_type=F32)


def dot_nt(left, right):
    return lax.dot_general(left, right, (((1,), (1,)), ((), ())), preferred_element_type=F32)


def dot_tn(left, right):
    return lax.dot_general(left, right, (((0,), (0,)), ((), ())), preferred_element_type=F32)


def relu16(values):
    return jnp.maximum(values, 0.0).astype(BF16)


def norm(values, axis):
    scale = 1.0 / values.shape[axis]
    centred = values - jnp.sum(values, axis=axis, keepdims=True) * scale
    spread = jnp.sum(centred * centred, axis=axis, keepdims=True) * scale
    return centred * lax.rsqrt(spread + 1e-05)


def thirds(values):
    high = values.astype(BF16)
    rest = values - high.astype(F32)
    middle = rest.astype(BF16)
    low = (rest - middle.astype(F32)).astype(BF16)
    return jnp.concatenate([high, middle, low], axis=0)


def joined(values):
    rows = values.shape[0] // 3
    return values[:rows] + values[rows : 2 * rows] + values[2 * rows :]


def quotient(values, count):
    if count & (count - 1) == 0:
        return values >> (count.bit_length() - 1)
    return lax.div(values, jnp.full_like(values, count))


def flip(weights):
    return weights.astype(F32).T.astype(BF16)


def fetch(pairs, sems):
    copies = [pltpu.make_async_copy(src, dst, sems.at[i]) for i, (src, dst) in enumerate(pairs)]
    for copy in copies:
        copy.start()
    return copies


def encode(state, mask, inward, encoder_w, extent):
    width = state.shape[1]
    position = state[0:3]
    row = lax.broadcasted_iota(I32, (3, width), 0)
    size = jnp.where(row == 0, extent[0], jnp.where(row == 1, extent[1], extent[2]))
    features = jnp.concatenate(
        [
            state[3:9],
            jnp.clip(position, -1.0, 1.0),
            jnp.clip(size - position, -1.0, 1.0),
            jnp.zeros((4, width), F32),
        ],
        axis=0,
    )
    hidden = relu16(dot_tn(thirds(features), inward))
    hidden = relu16(dot(hidden, encoder_w[0]))
    column = jnp.broadcast_to(mask, (8, width)).T[:, 0:1]
    return (norm(dot(hidden, encoder_w[1]), 1) * column).astype(BF16)


def places(ids_low, ids_high, fold_y):
    plane = (ids_high * 43) >> 7
    ez = ids_high - plane * 3
    ey = plane & 3
    ex = plane >> 2
    if fold_y:
        row = jnp.where(ey == 1, 0, jnp.where(ey == 2, 1, 2))
    else:
        row = ey
    return ex * 4 + row, ids_low + jnp.where(ez == 1, 0, 128)


def messages(far_ref, columns, row_count, place, key, pre, middle_t, final_t, hidden_ref):
    width = far_ref.shape[1]
    chunk = 32
    window = jnp.concatenate(
        [
            far_ref[ex * row_count + row, f : f + chunk]
            for f in range(0, width, chunk)
            for ex, row in columns
        ],
        axis=0,
    )
    key_rows = lax.broadcasted_iota(I32, (TILE, TILE), 0)
    lanes = place.shape[1]
    for tile in range(lanes // TILE):
        at = slice(tile * TILE, (tile + 1) * TILE)
        picker = jnp.where(key_rows == key[:, at], 1.0, 0.0).astype(BF16)
        found = dot(window, picker).reshape(width // chunk, len(columns), chunk // 8, 8, TILE)
        where = jnp.broadcast_to(place[:, at], (8, TILE))
        parts = []
        for f in range(width // chunk):
            part = jnp.zeros((chunk // 8, 8, TILE), F32)
            for i, (ex, row) in enumerate(columns):
                part = jnp.where((where == ex * 4 + row)[None], found[f, i], part)
            parts.append(part.reshape(chunk, TILE))
        hidden_ref[:, at] = relu16(pre(tile) + jnp.concatenate(parts, axis=0))
    hidden = relu16(dot(middle_t, hidden_ref[...]))
    return norm(dot(final_t, hidden), 0)


def slot_sum(message, step):
    total = message[:, :step]
    for at in range(step, message.shape[1], step):
        total = total + message[:, at : at + step]
    return total


def advance(pre, aggregate, latent_t, weights_ref, decoder_out):
    pre = pre + dot(weights_ref[NODE_NEW], aggregate)
    hidden = relu16(dot(weights_ref[NODE_0], relu16(pre)))
    updated = (latent_t + norm(dot(weights_ref[NODE_1], hidden), 0)).astype(BF16)
    hidden = relu16(dot(weights_ref[DECODE_0], updated))
    hidden = relu16(dot(weights_ref[DECODE_1], hidden))
    return dot(decoder_out, hidden)


def moved(position, velocity, acceleration):
    new_velocity = velocity + acceleration
    return jnp.concatenate([position + new_velocity, new_velocity, velocity], axis=0)


def ranks_kernel(
    sizes,
    fill_ref,
    owners_any,
    edge_w_any,
    node_in_any,
    node_w_any,
    decoder_w_any,
    decoder_out_any,
    encoder_in_any,
    encoder_w_any,
    weights_ref,
    decoder_out_ref,
    inward_ref,
    encoder_w_ref,
    placer_ref,
    masks_ref,
    owners_ref,
    edge_w_ref,
    node_in_ref,
    node_w_ref,
    decoder_w_ref,
    encoder_in_ref,
    sems,
):
    count_x, count_y, count_z = sizes
    fold_y = count_y == 2
    copies = fetch(
        [
            (owners_any, owners_ref),
            (edge_w_any, edge_w_ref),
            (node_in_any, node_in_ref),
            (node_w_any, node_w_ref),
            (decoder_w_any, decoder_w_ref),
            (decoder_out_any, decoder_out_ref),
            (encoder_in_any, encoder_in_ref),
            (encoder_w_any, encoder_w_ref),
        ],
        sems,
    )
    for copy in copies:
        copy.wait()
    index_x = lax.axis_index("gx")
    index_y = lax.axis_index("gy")
    index_z = lax.axis_index("gz")
    slots = owners_ref.shape[-1]
    width = node_in_ref.shape[-1]

    lane = lax.broadcasted_iota(I32, (1, slots), 1)
    owner = jnp.concatenate([owners_ref[a, b] for a, b in CELLS], axis=1)
    alive = jnp.concatenate([jnp.where(lane < fill_ref[a, 0, b], 1, 0) for a, b in CELLS], axis=1)
    own_block = (index_x * count_y + index_y) * count_z + index_z
    stays = jnp.where((alive == 1) & (owner == own_block), 1.0, 0.0)
    moving = jnp.where((alive == 1) & (owner != own_block), 1, 0)
    owner_x = quotient(owner, count_y * count_z)
    rest = owner - owner_x * (count_y * count_z)
    owner_y = quotient(rest, count_z)
    owner_z = rest - owner_y * count_z
    step_y = owner_y - index_y
    side_y = jnp.where(step_y == 0, 0, 1) if fold_y else jnp.where(step_y < 0, 1, 2 * step_y)
    options_y = 2 if fold_y else 3
    group = ((owner_x - index_x + 1) * options_y + side_y) * 2 + jnp.where(owner_z == index_z, 0, 1)
    group_rows = (3 * options_y * 2 + 15) // 16 * 16
    particles = owner.shape[1]
    member = jnp.where(
        (lax.broadcasted_iota(I32, (group_rows, particles), 0) == group) & (moving == 1), 1.0, 0.0
    )
    triangle = jnp.where(
        lax.broadcasted_iota(I32, (slots, slots), 0) <= lax.broadcasted_iota(I32, (slots, slots), 1),
        1.0,
        0.0,
    ).astype(BF16)
    counted = []
    before = jnp.zeros((group_rows, 1), F32)
    for i in range(4):
        inside = member[:, i * slots : (i + 1) * slots]
        counted.append(dot(inside.astype(BF16), triangle) + before)
        before = before + jnp.sum(inside, axis=1, keepdims=True)
    counted = jnp.concatenate(counted, axis=1)
    rank = (jnp.sum(counted * member, axis=0, keepdims=True) - 1.0).astype(I32)
    column = jnp.where(moving == 1, group * CAP + rank, -1)
    movers = placer_ref.shape[0]
    placer_ref[...] = jnp.where(
        lax.broadcasted_iota(I32, (movers, particles), 0) == column, 1.0, 0.0
    ).astype(BF16)
    masks_ref[...] = jnp.concatenate(
        [stays, moving.astype(F32), jnp.zeros((6, particles), F32)], axis=0
    )

    for i in range(5):
        weights_ref[i] = flip(edge_w_ref[i])
    weights_ref[NODE_OLD] = flip(node_in_ref[:width])
    weights_ref[NODE_NEW] = flip(node_in_ref[width:])
    for i in range(2):
        weights_ref[NODE_0 + i] = flip(node_w_ref[i])
        weights_ref[DECODE_0 + i] = flip(decoder_w_ref[i])
    inward = jnp.concatenate([encoder_in_ref[...].astype(F32), jnp.zeros((4, width), F32)], axis=0)
    inward = inward.astype(BF16)
    inward_ref[...] = jnp.concatenate([inward, inward, inward], axis=0)


def prepare_kernel(
    sizes,
    latent_any,
    edge_any,
    positions_any,
    velocity_any,
    neighbours_any,
    weights_ref,
    placer_ref,
    masks_ref,
    latent_t_ref,
    node_pre_ref,
    state_ref,
    mover_pre_ref,
    mover_place_ref,
    mover_key_ref,
    mover_node_pre_ref,
    mover_latent_ref,
    mover_state_ref,
    latent_ref,
    edge_ref,
    positions_ref,
    velocity_ref,
    neighbours_ref,
    sems,
):
    fold_y = sizes[1] == 2
    copies = fetch(
        [
            (neighbours_any, neighbours_ref),
            (positions_any, positions_ref),
            (velocity_any, velocity_ref),
            (latent_any, latent_ref),
            (edge_any, edge_ref),
        ],
        sems,
    )
    for copy in copies[:4]:
        copy.wait()
    neighbour_count = edge_ref.shape[3]
    placer = placer_ref[...]
    movers, particles = placer.shape
    stays, moving = masks_ref[0:1], masks_ref[1:2]

    latent = jnp.concatenate([latent_ref[a, b, 0] for a, b in CELLS], axis=0)
    latent_t_ref[...] = latent.astype(F32).T
    node_pre_ref[...] = dot_nt(weights_ref[NODE_OLD], latent)

    def flat(ref, i):
        return jnp.concatenate([ref[i, a, b] for a, b in CELLS], axis=1)

    state = [flat(positions_ref, i) for i in range(3)] + [flat(velocity_ref, i) for i in range(3)]
    state_ref[...] = jnp.concatenate(state + [stays, jnp.zeros_like(stays)], axis=0)

    mover_latent = dot(placer, latent).astype(BF16)
    mover_latent_ref[...] = mover_latent.astype(F32).T
    mover_node_pre_ref[...] = dot_nt(weights_ref[NODE_OLD], mover_latent)
    near = dot_nt(weights_ref[NEAR], mover_latent)
    state = jnp.concatenate(state + [moving, jnp.zeros_like(stays)], axis=0)
    mover_state_ref[...] = joined(dot_nt(thirds(state), placer))
    ids = jnp.concatenate(
        [
            jnp.concatenate([neighbours_ref[a, b, k] for a, b in CELLS], axis=1)
            for k in range(neighbour_count)
        ],
        axis=0,
    )
    ids = jnp.concatenate([ids & 127, ids >> 7, jnp.zeros((8, particles), I32)], axis=0)
    ids = dot_nt(ids.astype(F32).astype(BF16), placer).astype(I32)
    place, key = places(ids[:neighbour_count], ids[neighbour_count : 2 * neighbour_count], fold_y)
    mover_place_ref[...] = place
    mover_key_ref[...] = key
    copies[4].wait()
    for k in range(neighbour_count):
        edges = jnp.concatenate([edge_ref[a, b, 0, k] for a, b in CELLS], axis=0)
        edges = dot(placer, edges).astype(BF16)
        mover_pre_ref[:, k * movers : (k + 1) * movers] = dot_nt(weights_ref[EDGE], edges) + near


def movers_kernel(
    sizes,
    side_count,
    latent_any,
    *refs,
):
    count_x, count_y, _ = sizes
    fold_y = count_y == 2
    side_refs, refs = refs[:side_count], refs[side_count:]
    even_ref, odd_ref, own_zed, refs = refs[0], refs[1], refs[2], refs[3:]
    side_zeds, refs = refs[:side_count], refs[side_count:]
    even_zed, odd_zed, refs = refs[0], refs[1], refs[2:]
    (
        weights_ref,
        decoder_out_ref,
        pre_ref,
        place_ref,
        key_ref,
        node_pre_ref,
        latent_t_ref,
        state_ref,
        far_ref,
        bucket_ref,
        own_ref,
        hidden_ref,
        sems,
    ) = refs
    copies = fetch([(latent_any, own_ref)], sems)
    row_count = 3 if fold_y else 4
    own_rows = (0, 1) if fold_y else (1, 2)
    outer = {2: 0} if fold_y else {0: 0, 3: 1}
    parity = lax.axis_index("gx") & 1
    far_t = weights_ref[FAR]

    def far(at, here, beside):
        pair = jnp.concatenate([here, beside], axis=0)
        far_ref[at] = dot_nt(far_t, pair).astype(BF16)

    copies[0].wait()
    for row in range(row_count):
        for ex in (1, 2):
            if row in own_rows:
                b = own_rows.index(row)
                far(ex * row_count + row, own_ref[ex - 1, b, 0], own_zed[ex - 1, b, 0])
            else:
                side = outer[row]
                far(ex * row_count + row, side_refs[side][ex - 1], side_zeds[side][ex - 1])
        far(3 * (1 - parity) * row_count + row, even_ref[row], even_zed[row])
        far(3 * parity * row_count + row, odd_ref[row], odd_zed[row])

    movers = state_ref.shape[1]
    neighbour_count = place_ref.shape[0]
    place = jnp.concatenate([place_ref[k : k + 1] for k in range(neighbour_count)], axis=1)
    key = jnp.concatenate([key_ref[k : k + 1] for k in range(neighbour_count)], axis=1)
    columns = [(ex, row) for ex in range(4) for row in range(row_count)]
    message = messages(
        far_ref,
        columns,
        row_count,
        place,
        key,
        lambda tile: pre_ref[:, tile * TILE : (tile + 1) * TILE],
        weights_ref[MIDDLE],
        weights_ref[FINAL],
        hidden_ref,
    )
    aggregate = slot_sum(message, movers).astype(BF16)
    acceleration = advance(
        node_pre_ref[...], aggregate, latent_t_ref[...], weights_ref, decoder_out_ref[...]
    )
    mask = state_ref[6:7]
    state = moved(state_ref[0:3], state_ref[3:6], acceleration) * mask
    bucket_ref[...] = jnp.concatenate([state, mask, jnp.zeros((ROWS - 10, movers), F32)], axis=0)


def edges_kernel(
    sizes,
    a,
    fill_ref,
    latent_any,
    edge_any,
    neighbours_any,
    far_ref,
    weights_ref,
    total_ref,
    latent_ref,
    edge_ref,
    neighbours_ref,
    hidden_ref,
    sems,
):
    fold_y = sizes[1] == 2
    row_count = 3 if fold_y else 4
    index_y = lax.axis_index("gy")
    copies = fetch(
        [
            (neighbours_any.at[a], neighbours_ref),
            (latent_any.at[a], latent_ref),
            (edge_any.at[a], edge_ref),
        ],
        sems,
    )
    for copy in copies:
        copy.wait()
    slots, width = latent_ref.shape[-2:]
    neighbour_count = edge_ref.shape[2]
    lane = lax.broadcasted_iota(I32, (1, slots), 1)
    for bt in range(2):
        if fold_y:
            b = index_y if bt == 0 else 1 - index_y
            rows = (0, 1) if bt == 0 else (0, 1, 2)
        else:
            b = bt
            rows = (bt, bt + 1, bt + 2)
        columns = [(ex, row) for ex in range(a, a + 3) for row in rows]
        near = dot_nt(weights_ref[NEAR], latent_ref[b, 0])
        near = jnp.concatenate([near, near], axis=1)
        ids = jnp.concatenate([neighbours_ref[b, k] for k in range(neighbour_count)], axis=1)
        place, key = places(ids & 127, ids >> 7, fold_y)

        def pre(tile, b=b, near=near):
            edges = jnp.concatenate([edge_ref[b, 0, 2 * tile], edge_ref[b, 0, 2 * tile + 1]], axis=0)
            return dot_nt(weights_ref[EDGE], edges) + near

        message = messages(
            far_ref,
            columns,
            row_count,
            place,
            key,
            pre,
            weights_ref[MIDDLE],
            weights_ref[FINAL],
            hidden_ref.at[bt],
        )
        total = jnp.where(lane < fill_ref[a, 0, b], slot_sum(message, slots), 0.0)
        total_ref[b] = total.astype(BF16)


def nodes_kernel(
    sizes,
    first_ref,
    second_ref,
    node_pre_ref,
    latent_t_ref,
    state_ref,
    weights_ref,
    decoder_out_ref,
    inward_ref,
    encoder_w_ref,
    kept_latent_ref,
    kept_state_ref,
):
    slots = first_ref.shape[-1]
    aggregate = jnp.concatenate([first_ref[0], first_ref[1], second_ref[0], second_ref[1]], axis=1)
    acceleration = advance(
        node_pre_ref[...], aggregate, latent_t_ref[...], weights_ref, decoder_out_ref[...]
    )
    stays = state_ref[6:7]
    state = moved(state_ref[0:3], state_ref[3:6], acceleration)
    extent = (2.0 * sizes[0], 2.0 * sizes[1], 1.0 * sizes[2])
    latents = encode(state, stays, inward_ref[...], encoder_w_ref[...], extent)
    kept = state * stays
    for i, (a, b) in enumerate(CELLS):
        kept_latent_ref[a, b, 0] = latents[i * slots : (i + 1) * slots]
        for j in range(9):
            kept_state_ref[j, a, b] = kept[j : j + 1, i * slots : (i + 1) * slots]


def arrive_kernel(
    sizes,
    own_ref,
    even_ref,
    odd_ref,
    own_zed,
    even_zed,
    odd_zed,
    inward_ref,
    encoder_w_ref,
    arrived_latent_ref,
    arrived_state_ref,
):
    count_x, count_y, count_z = sizes
    fold_y = count_y == 2
    index_x = lax.axis_index("gx")
    index_y = lax.axis_index("gy")
    index_z = lax.axis_index("gz")
    options_y = 2 if fold_y else 3
    lanes = own_ref.shape[-1]
    group = lax.broadcasted_iota(I32, (ROWS, lanes), 1) >> 3
    even = (index_x & 1) == 0
    found = jnp.zeros((ROWS, lanes), F32)
    for source_x in (-1, 0, 1):
        for from_y in range(options_y):
            for from_z in range(2):
                if source_x == 0 and from_y == 0 and from_z == 0:
                    continue
                if from_z == 0:
                    own, first, second = own_ref, even_ref, odd_ref
                else:
                    own, first, second = own_zed, even_zed, odd_zed
                side_y = from_y if fold_y or from_y == 0 else 3 - from_y
                target = ((1 - source_x) * options_y + side_y) * 2 + from_z
                if source_x == 0:
                    tile = own[from_y]
                    there = group == target
                elif source_x == -1:
                    tile = jnp.where(even, second[from_y], first[from_y])
                    there = (group == target) & (index_x > 0)
                else:
                    tile = jnp.where(even, first[from_y], second[from_y])
                    there = (group == target) & (index_x < count_x - 1)
                found = jnp.where(there, tile, found)
    out_lanes = arrived_state_ref.shape[-1]
    spread_shape = (lanes, out_lanes)
    line = lax.broadcasted_iota(I32, spread_shape, 0)
    from_group = line >> 3
    plane = from_group >> 1
    from_x = 1 - ((plane >> 1) if fold_y else ((plane * 43) >> 7))
    side_y = plane - (1 - from_x) * options_y
    if fold_y:
        from_y = jnp.where(side_y == 0, 0, jnp.where(index_y == 0, 1, -1))
    else:
        from_y = jnp.where(side_y == 0, 0, jnp.where(side_y == 1, 1, -1))
    from_z = jnp.where((from_group & 1) == 0, 0, jnp.where(index_z == 0, 1, -1))
    direction = (from_x + 1) * 9 + (from_y + 1) * 3 + from_z + 1
    direction = direction - jnp.where(direction > 13, 1, 0)
    column = direction * CAP + (line & 7)
    valid = (lax.broadcasted_iota(I32, spread_shape, 1) == column) & (
        (from_x != 0) | (from_y != 0) | (from_z != 0)
    )
    spread = jnp.where(valid, 1.0, 0.0).astype(BF16)
    arrived = joined(dot(thirds(found), spread))
    for j in range(9):
        arrived_state_ref[j, 0, 0] = arrived[j : j + 1]
    extent = (2.0 * count_x, 2.0 * count_y, 1.0 * count_z)
    arrived_latent_ref[0, 0, 0] = encode(
        arrived[:9], arrived[9:10], inward_ref[...], encoder_w_ref[...], extent
    )


def swap(values, axis):
    return lax.ppermute(values, axis, [(0, 1), (1, 0)])


def shift(values, axis, way):
    pairs = [(i, i + 1) for i in range(lax.axis_size(axis) - 1)]
    return lax.ppermute(values, axis, [(j, i) for i, j in pairs] if way else pairs)


def swap_x(values, first):
    count = lax.axis_size("gx")
    pairs = []
    for x in range(count):
        partner = x + 1 if (x - first) % 2 == 0 else x - 1
        for z in range(2):
            if 0 <= partner < count:
                pairs.append((x * 2 + z, partner * 2 + z))
            else:
                pairs.append((x * 2 + z, x * 2 + 1 - z))
    return lax.ppermute(values, ("gx", "gz"), pairs)


def call(kernel, name, in_specs, outs, scratch, operands, flops):
    return pl.pallas_call(
        kernel,
        out_shape=tuple(jax.ShapeDtypeStruct(shape, kind) for shape, kind in outs),
        in_specs=in_specs,
        out_specs=tuple(VMEM for _ in outs),
        scratch_shapes=scratch,
        compiler_params=pltpu.CompilerParams(vmem_limit_bytes=32 * 1024 * 1024),
        cost_estimate=pl.CostEstimate(flops=flops, bytes_accessed=0, transcendentals=0),
        name=name,
    )(*operands)


def in_hbm(array):
    return pltpu.with_memory_space_constraint(array, pltpu.HBM)


def like(array):
    return pltpu.VMEM(array.shape, array.dtype)


def body(
    node_latent,
    edge_latent,
    positions,
    velocity,
    fill,
    neighbours,
    owners,
    edge_weights,
    node_in,
    node_weights,
    decoder_weights,
    decoder_out,
    encoder_in,
    encoder_weights,
):
    sizes = tuple(lax.axis_size(axis) for axis in ("gx", "gy", "gz"))
    fold_y = sizes[1] == 2
    slots, width = node_latent.shape[-2:]
    neighbour_count = neighbours.shape[3]
    particles = 4 * slots
    options_y = 2 if fold_y else 3
    movers = (3 * options_y * 2 * CAP + 127) // 128 * 128
    rows = 3 if fold_y else 4
    fill = jnp.transpose(fill, (0, 2, 1))
    neighbours = neighbours.reshape(2, 2, neighbour_count, 1, slots)

    parity = lax.axis_index("gx") & 1
    cells = node_latent[:, :, 0]
    if fold_y:
        inner = 1 - lax.axis_index("gy")
        sides = [swap(lax.dynamic_index_in_dim(cells, inner, 1, keepdims=False), "gy")]
    else:
        sides = [shift(cells[:, 1], "gy", 0), shift(cells[:, 0], "gy", 1)]

    ranked = call(
        functools.partial(ranks_kernel, sizes),
        "ranks",
        [SMEM] + [ANY] * 8,
        [
            ((11, width, width), BF16),
            (decoder_out.shape, BF16),
            ((48, width), BF16),
            (encoder_weights.shape, BF16),
            ((movers, particles), BF16),
            ((8, particles), F32),
        ],
        [
            like(owners),
            like(edge_weights),
            like(node_in),
            like(node_weights),
            like(decoder_weights),
            like(encoder_in),
            pltpu.SemaphoreType.DMA((8,)),
        ],
        [
            in_hbm(array)
            for array in (
                fill,
                owners,
                edge_weights,
                node_in,
                node_weights,
                decoder_weights,
                decoder_out,
                encoder_in,
                encoder_weights,
            )
        ],
        500_000_000,
    )
    sides, ranked = lax.optimization_barrier((sides, ranked))
    weights, decoder_out, inward, encoder_weights, placer, masks = ranked

    if fold_y:
        layers = [cells, sides[0][:, None]]
    else:
        layers = [sides[0][:, None], cells, sides[1][:, None]]

    def layer(a):
        return jnp.concatenate(
            [lax.dynamic_index_in_dim(part, a, 0, keepdims=False) for part in layers], axis=0
        )

    ends = [swap_x(layer(1 - parity), 0), swap_x(layer(parity), 1)]
    prepared = call(
        functools.partial(prepare_kernel, sizes),
        "prepare",
        [ANY] * 5 + [VMEM] * 3,
        [
            ((width, particles), F32),
            ((width, particles), F32),
            ((8, particles), F32),
            ((width, neighbour_count * movers), F32),
            ((neighbour_count, movers), I32),
            ((neighbour_count, movers), I32),
            ((width, movers), F32),
            ((width, movers), F32),
            ((8, movers), F32),
        ],
        [
            like(node_latent),
            like(edge_latent),
            like(positions),
            like(velocity),
            like(neighbours),
            pltpu.SemaphoreType.DMA((5,)),
        ],
        [
            in_hbm(array)
            for array in (node_latent, edge_latent, positions, velocity, neighbours)
        ]
        + [weights, placer, masks],
        500_000_000,
    )
    ends, prepared = lax.optimization_barrier((ends, prepared))
    (
        latent_t,
        node_pre,
        state,
        mover_pre,
        mover_place,
        mover_key,
        mover_node_pre,
        mover_latent,
        mover_state,
    ) = prepared
    halo = [*sides, *ends]
    halo = halo + [swap(part, "gz") for part in [node_latent] + halo]

    far, bucket = call(
        functools.partial(movers_kernel, sizes, len(sides)),
        "movers",
        [ANY] + [VMEM] * (len(halo) + 8),
        [((4 * rows, width, 2 * slots), BF16), ((ROWS, movers), F32)],
        [
            like(node_latent),
            pltpu.VMEM((width, neighbour_count * movers), BF16),
            pltpu.SemaphoreType.DMA((1,)),
        ],
        (
            node_latent,
            *halo,
            weights,
            decoder_out,
            mover_pre,
            mover_place,
            mover_key,
            mover_node_pre,
            mover_latent,
            mover_state,
        ),
        3_000_000_000,
    )

    def edges(a):
        return call(
            functools.partial(edges_kernel, sizes, a),
            "edges",
            [SMEM] + [ANY] * 3 + [VMEM] * 2,
            [((2, width, slots), BF16)],
            [
                pltpu.VMEM(node_latent.shape[1:], BF16),
                pltpu.VMEM(edge_latent.shape[1:], BF16),
                pltpu.VMEM(neighbours.shape[1:], I32),
                pltpu.VMEM((2, width, neighbour_count * slots), BF16),
                pltpu.SemaphoreType.DMA((3,)),
            ],
            (in_hbm(fill), in_hbm(node_latent), in_hbm(edge_latent), in_hbm(neighbours), far, weights),
            4_000_000_000,
        )[0]

    first = edges(0)
    if fold_y:
        tiles = [swap(bucket, "gy")]
    else:
        tiles = [shift(bucket, "gy", 0), shift(bucket, "gy", 1)]
    tiles, first = lax.optimization_barrier((tiles, first))
    tiles = jnp.stack([bucket, *tiles], axis=0)
    second = edges(1)
    sided = [swap_x(tiles, 0), swap_x(tiles, 1)]
    sided, second = lax.optimization_barrier((sided, second))
    tiles = [tiles, *sided]
    tiles = tiles + [swap(part, "gz") for part in tiles]
    kept_latent, kept_state = call(
        functools.partial(nodes_kernel, sizes),
        "nodes",
        [VMEM] * 9,
        [(node_latent.shape, BF16), ((9,) + node_latent.shape[:4], F32)],
        [],
        (
            first,
            second,
            node_pre,
            latent_t,
            state,
            weights,
            decoder_out,
            inward,
            encoder_weights,
        ),
        2_000_000_000,
    )
    arrived_latent, arrived_state = call(
        functools.partial(arrive_kernel, sizes),
        "arrive",
        [VMEM] * 8,
        [((1, 1, 1, 26 * CAP, width), BF16), ((9, 1, 1, 1, 26 * CAP), F32)],
        [],
        (*tiles, inward, encoder_weights),
        1_000_000_000,
    )
    return kept_latent, kept_state, arrived_latent, arrived_state


def solution(mesh):
    placed = (
        P(("group", "gx"), "gy", "gz", None, None),
        P(("group", "gx"), "gy", "gz", None, None, None),
        P(None, ("group", "gx"), "gy", "gz", None),
        P(None, ("group", "gx"), "gy", "gz", None),
        P(("group", "gx"), "gy", "gz"),
        P(("group", "gx"), "gy", "gz", None, None),
        P(("group", "gx"), "gy", "gz", None),
        P(),
        P(),
        P(),
        P(),
        P(),
        P(),
        P(),
    )
    return jax.shard_map(
        body,
        mesh=mesh,
        in_specs=placed,
        out_specs=(
            P(("group", "gx"), "gy", "gz", None, None),
            P(None, ("group", "gx"), "gy", "gz", None),
            P(("group", "gx"), "gy", "gz", None, None),
            P(None, ("group", "gx"), "gy", "gz", None),
        ),
        check_vma=False,
    )
```

```python
import functools

import jax
import jax.numpy as jnp
from jax import lax
from jax.experimental import pallas as pl
from jax.experimental.pallas import tpu as pltpu
from jax.sharding import PartitionSpec as P

CAP = 8
F32 = jnp.float32
BF16 = jnp.bfloat16
I32 = jnp.int32
ROWS = 16
TILE = 256
CELLS = [(a, b) for a in range(2) for b in range(2)]
EDGE, NEAR, FAR, MIDDLE, FINAL, NODE_OLD, NODE_NEW, NODE_0, NODE_1, DECODE_0, DECODE_1 = range(11)

VMEM = pl.BlockSpec(memory_space=pltpu.VMEM)
SMEM = pl.BlockSpec(memory_space=pltpu.SMEM)
ANY = pl.BlockSpec(memory_space=pl.ANY)


def dot(left, right):
    return jnp.dot(left, right, preferred_element_type=F32)


def dot_nt(left, right):
    return lax.dot_general(left, right, (((1,), (1,)), ((), ())), preferred_element_type=F32)


def dot_tn(left, right):
    return lax.dot_general(left, right, (((0,), (0,)), ((), ())), preferred_element_type=F32)


def relu16(values):
    return jnp.maximum(values, 0.0).astype(BF16)


def norm(values, axis):
    scale = 1.0 / values.shape[axis]
    centred = values - jnp.sum(values, axis=axis, keepdims=True) * scale
    spread = jnp.sum(centred * centred, axis=axis, keepdims=True) * scale
    return centred * lax.rsqrt(spread + 1e-05)


def thirds(values):
    high = values.astype(BF16)
    rest = values - high.astype(F32)
    middle = rest.astype(BF16)
    low = (rest - middle.astype(F32)).astype(BF16)
    return jnp.concatenate([high, middle, low], axis=0)


def joined(values):
    rows = values.shape[0] // 3
    return values[:rows] + values[rows : 2 * rows] + values[2 * rows :]


def quotient(values, count):
    if count & (count - 1) == 0:
        return values >> (count.bit_length() - 1)
    return lax.div(values, jnp.full_like(values, count))


def flip(weights):
    return weights.astype(F32).T.astype(BF16)


def fetch(pairs, sems):
    copies = [pltpu.make_async_copy(src, dst, sems.at[i]) for i, (src, dst) in enumerate(pairs)]
    for copy in copies:
        copy.start()
    return copies


def encode(state, mask, inward, encoder_w, extent):
    width = state.shape[1]
    position = state[0:3]
    row = lax.broadcasted_iota(I32, (3, width), 0)
    size = jnp.where(row == 0, extent[0], jnp.where(row == 1, extent[1], extent[2]))
    features = jnp.concatenate(
        [
            state[3:9],
            jnp.clip(position, -1.0, 1.0),
            jnp.clip(size - position, -1.0, 1.0),
            jnp.zeros((4, width), F32),
        ],
        axis=0,
    )
    hidden = relu16(dot_tn(thirds(features), inward))
    hidden = relu16(dot(hidden, encoder_w[0]))
    column = jnp.broadcast_to(mask, (8, width)).T[:, 0:1]
    return (norm(dot(hidden, encoder_w[1]), 1) * column).astype(BF16)


def places(ids_low, ids_high, fold_y):
    plane = (ids_high * 43) >> 7
    ez = ids_high - plane * 3
    ey = plane & 3
    ex = plane >> 2
    if fold_y:
        row = jnp.where(ey == 1, 0, jnp.where(ey == 2, 1, 2))
    else:
        row = ey
    return ex * 4 + row, ids_low + jnp.where(ez == 1, 0, 128)


def messages(far_ref, columns, row_count, place, key, pre, middle_t, final_t, hidden_ref):
    width = far_ref.shape[1]
    chunk = 32
    window = jnp.concatenate(
        [
            far_ref[ex * row_count + row, f : f + chunk]
            for f in range(0, width, chunk)
            for ex, row in columns
        ],
        axis=0,
    )
    key_rows = lax.broadcasted_iota(I32, (TILE, TILE), 0)
    lanes = place.shape[1]
    for tile in range(lanes // TILE):
        at = slice(tile * TILE, (tile + 1) * TILE)
        picker = jnp.where(key_rows == key[:, at], 1.0, 0.0).astype(BF16)
        found = dot(window, picker).reshape(width // chunk, len(columns), chunk // 8, 8, TILE)
        where = jnp.broadcast_to(place[:, at], (8, TILE))
        parts = []
        for f in range(width // chunk):
            part = jnp.zeros((chunk // 8, 8, TILE), F32)
            for i, (ex, row) in enumerate(columns):
                part = jnp.where((where == ex * 4 + row)[None], found[f, i], part)
            parts.append(part.reshape(chunk, TILE))
        hidden_ref[:, at] = relu16(pre(tile) + jnp.concatenate(parts, axis=0))
    hidden = relu16(dot(middle_t, hidden_ref[...]))
    return norm(dot(final_t, hidden), 0)


def slot_sum(message, step):
    total = message[:, :step]
    for at in range(step, message.shape[1], step):
        total = total + message[:, at : at + step]
    return total


def advance(pre, aggregate, latent_t, weights_ref, decoder_out):
    pre = pre + dot(weights_ref[NODE_NEW], aggregate)
    hidden = relu16(dot(weights_ref[NODE_0], relu16(pre)))
    updated = (latent_t + norm(dot(weights_ref[NODE_1], hidden), 0)).astype(BF16)
    hidden = relu16(dot(weights_ref[DECODE_0], updated))
    hidden = relu16(dot(weights_ref[DECODE_1], hidden))
    return dot(decoder_out, hidden)


def moved(position, velocity, acceleration):
    new_velocity = velocity + acceleration
    return jnp.concatenate([position + new_velocity, new_velocity, velocity], axis=0)


def ranks_kernel(
    sizes,
    fill_ref,
    owners_any,
    edge_w_any,
    node_in_any,
    node_w_any,
    decoder_w_any,
    decoder_out_any,
    encoder_in_any,
    encoder_w_any,
    latent_any,
    neighbours_any,
    positions_any,
    velocity_any,
    edge_any,
    weights_ref,
    decoder_out_ref,
    inward_ref,
    encoder_w_ref,
    placer_ref,
    masks_ref,
    alive_ref,
    latent_ref,
    neighbours_ref,
    positions_ref,
    velocity_ref,
    edge_ref,
    first_end_ref,
    second_end_ref,
    owners_ref,
    edge_w_ref,
    node_in_ref,
    node_w_ref,
    decoder_w_ref,
    encoder_in_ref,
    sems,
):
    count_x, count_y, count_z = sizes
    fold_y = count_y == 2
    copies = fetch(
        [
            (owners_any, owners_ref),
            (edge_w_any, edge_w_ref),
            (node_in_any, node_in_ref),
            (node_w_any, node_w_ref),
            (decoder_w_any, decoder_w_ref),
            (decoder_out_any, decoder_out_ref),
            (encoder_in_any, encoder_in_ref),
            (encoder_w_any, encoder_w_ref),
            (latent_any, latent_ref),
            (neighbours_any, neighbours_ref),
            (positions_any, positions_ref),
            (velocity_any, velocity_ref),
            (edge_any, edge_ref),
        ],
        sems,
    )
    copies[0].wait()
    index_x = lax.axis_index("gx")
    index_y = lax.axis_index("gy")
    index_z = lax.axis_index("gz")
    slots = owners_ref.shape[-1]
    width = node_in_ref.shape[-1]
    for a, b in CELLS:
        alive_ref[a, b] = jnp.where(
            lax.broadcasted_iota(I32, (1, slots), 1) < fill_ref[a, 0, b], 1.0, 0.0
        )

    lane = lax.broadcasted_iota(I32, (1, slots), 1)
    owner = jnp.concatenate([owners_ref[a, b] for a, b in CELLS], axis=1)
    alive = jnp.concatenate([jnp.where(lane < fill_ref[a, 0, b], 1, 0) for a, b in CELLS], axis=1)
    own_block = (index_x * count_y + index_y) * count_z + index_z
    stays = jnp.where((alive == 1) & (owner == own_block), 1.0, 0.0)
    moving = jnp.where((alive == 1) & (owner != own_block), 1, 0)
    owner_x = quotient(owner, count_y * count_z)
    rest = owner - owner_x * (count_y * count_z)
    owner_y = quotient(rest, count_z)
    owner_z = rest - owner_y * count_z
    step_y = owner_y - index_y
    side_y = jnp.where(step_y == 0, 0, 1) if fold_y else jnp.where(step_y < 0, 1, 2 * step_y)
    options_y = 2 if fold_y else 3
    group = ((owner_x - index_x + 1) * options_y + side_y) * 2 + jnp.where(owner_z == index_z, 0, 1)
    group_rows = (3 * options_y * 2 + 15) // 16 * 16
    particles = owner.shape[1]
    member = jnp.where(
        (lax.broadcasted_iota(I32, (group_rows, particles), 0) == group) & (moving == 1), 1.0, 0.0
    )
    triangle = jnp.where(
        lax.broadcasted_iota(I32, (slots, slots), 0) <= lax.broadcasted_iota(I32, (slots, slots), 1),
        1.0,
        0.0,
    ).astype(BF16)
    counted = []
    before = jnp.zeros((group_rows, 1), F32)
    for i in range(4):
        inside = member[:, i * slots : (i + 1) * slots]
        counted.append(dot(inside.astype(BF16), triangle) + before)
        before = before + jnp.sum(inside, axis=1, keepdims=True)
    counted = jnp.concatenate(counted, axis=1)
    rank = (jnp.sum(counted * member, axis=0, keepdims=True) - 1.0).astype(I32)
    column = jnp.where(moving == 1, group * CAP + rank, -1)
    movers = placer_ref.shape[0]
    placer_ref[...] = jnp.where(
        lax.broadcasted_iota(I32, (movers, particles), 0) == column, 1.0, 0.0
    ).astype(BF16)
    masks_ref[...] = jnp.concatenate(
        [stays, moving.astype(F32), jnp.zeros((6, particles), F32)], axis=0
    )

    for copy in copies[1:]:
        copy.wait()
    for i in range(5):
        weights_ref[i] = flip(edge_w_ref[i])
    weights_ref[NODE_OLD] = flip(node_in_ref[:width])
    weights_ref[NODE_NEW] = flip(node_in_ref[width:])
    for i in range(2):
        weights_ref[NODE_0 + i] = flip(node_w_ref[i])
        weights_ref[DECODE_0 + i] = flip(decoder_w_ref[i])
    inward = jnp.concatenate([encoder_in_ref[...].astype(F32), jnp.zeros((4, width), F32)], axis=0)
    inward = inward.astype(BF16)
    inward_ref[...] = jnp.concatenate([inward, inward, inward], axis=0)
    parity = index_x & 1
    for b in range(2):
        first_end_ref[b] = latent_ref[1 - parity, b, 0]
        second_end_ref[b] = latent_ref[parity, b, 0]


def prepare_kernel(
    sizes,
    latent_ref,
    edge_ref,
    positions_ref,
    velocity_ref,
    neighbours_ref,
    weights_ref,
    placer_ref,
    masks_ref,
    latent_t_ref,
    node_pre_ref,
    state_ref,
    mover_pre_ref,
    mover_place_ref,
    mover_key_ref,
    mover_node_pre_ref,
    mover_latent_ref,
    mover_state_ref,
):
    fold_y = sizes[1] == 2
    neighbour_count = edge_ref.shape[3]
    placer = placer_ref[...]
    movers, particles = placer.shape
    stays, moving = masks_ref[0:1], masks_ref[1:2]

    latent = jnp.concatenate([latent_ref[a, b, 0] for a, b in CELLS], axis=0)
    latent_t_ref[...] = latent.astype(F32).T
    node_pre_ref[...] = dot_nt(weights_ref[NODE_OLD], latent)

    def flat(ref, i):
        return jnp.concatenate([ref[i, a, b] for a, b in CELLS], axis=1)

    state = [flat(positions_ref, i) for i in range(3)] + [flat(velocity_ref, i) for i in range(3)]
    state_ref[...] = jnp.concatenate(state + [stays, jnp.zeros_like(stays)], axis=0)

    mover_latent = dot(placer, latent).astype(BF16)
    mover_latent_ref[...] = mover_latent.astype(F32).T
    mover_node_pre_ref[...] = dot_nt(weights_ref[NODE_OLD], mover_latent)
    near = dot_nt(weights_ref[NEAR], mover_latent)
    state = jnp.concatenate(state + [moving, jnp.zeros_like(stays)], axis=0)
    mover_state_ref[...] = joined(dot_nt(thirds(state), placer))
    ids = jnp.concatenate(
        [
            jnp.concatenate([neighbours_ref[a, b, k] for a, b in CELLS], axis=1)
            for k in range(neighbour_count)
        ],
        axis=0,
    )
    ids = jnp.concatenate([ids & 127, ids >> 7, jnp.zeros((8, particles), I32)], axis=0)
    ids = dot_nt(ids.astype(F32).astype(BF16), placer).astype(I32)
    place, key = places(ids[:neighbour_count], ids[neighbour_count : 2 * neighbour_count], fold_y)
    mover_place_ref[...] = place
    mover_key_ref[...] = key
    for k in range(neighbour_count):
        edges = jnp.concatenate([edge_ref[a, b, 0, k] for a, b in CELLS], axis=0)
        edges = dot(placer, edges).astype(BF16)
        mover_pre_ref[:, k * movers : (k + 1) * movers] = dot_nt(weights_ref[EDGE], edges) + near


def movers_kernel(
    sizes,
    side_count,
    own_ref,
    *refs,
):
    count_x, count_y, count_z = sizes
    fold_y = count_y == 2
    side_refs, refs = refs[:side_count], refs[side_count:]
    even_ref, odd_ref, own_zed, refs = refs[0], refs[1], refs[2], refs[3:]
    side_zeds, refs = refs[:side_count], refs[side_count:]
    even_zed, odd_zed, refs = refs[0], refs[1], refs[2:]
    (
        weights_ref,
        decoder_out_ref,
        pre_ref,
        place_ref,
        key_ref,
        node_pre_ref,
        latent_t_ref,
        state_ref,
        far_ref,
        bucket_ref,
        hidden_ref,
    ) = refs
    row_count = 3 if fold_y else 4
    own_rows = (0, 1) if fold_y else (1, 2)
    outer = {2: 0} if fold_y else {0: 0, 3: 1}
    index_x = lax.axis_index("gx")
    index_y = lax.axis_index("gy")
    index_z = lax.axis_index("gz")
    parity = index_x & 1
    far_t = weights_ref[FAR]

    def far(at, here, beside):
        pair = jnp.concatenate([here, beside], axis=0)
        far_ref[at] = dot_nt(far_t, pair).astype(BF16)

    for row in range(row_count):
        for ex in (1, 2):
            if row in own_rows:
                b = own_rows.index(row)
                far(ex * row_count + row, own_ref[ex - 1, b, 0], own_zed[ex - 1, b, 0])
            else:
                side = outer[row]
                far(ex * row_count + row, side_refs[side][ex - 1], side_zeds[side][ex - 1])
        far(3 * (1 - parity) * row_count + row, even_ref[row], even_zed[row])
        far(3 * parity * row_count + row, odd_ref[row], odd_zed[row])

    movers = state_ref.shape[1]
    neighbour_count = place_ref.shape[0]
    place = jnp.concatenate([place_ref[k : k + 1] for k in range(neighbour_count)], axis=1)
    key = jnp.concatenate([key_ref[k : k + 1] for k in range(neighbour_count)], axis=1)
    columns = [(ex, row) for ex in range(4) for row in range(row_count)]
    message = messages(
        far_ref,
        columns,
        row_count,
        place,
        key,
        lambda tile: pre_ref[:, tile * TILE : (tile + 1) * TILE],
        weights_ref[MIDDLE],
        weights_ref[FINAL],
        hidden_ref,
    )
    aggregate = slot_sum(message, movers).astype(BF16)
    acceleration = advance(
        node_pre_ref[...], aggregate, latent_t_ref[...], weights_ref, decoder_out_ref[...]
    )
    mask = state_ref[6:7]
    state = moved(state_ref[0:3], state_ref[3:6], acceleration) * mask
    rows = jnp.concatenate([state, mask, jnp.zeros((118, movers), F32)], axis=0).T
    bucket_ref[...] = jnp.zeros_like(bucket_ref)
    options_y = 2 if fold_y else 3
    for step_x in (-1, 0, 1):
        for side_y in range(options_y):
            for side_z in range(2):
                if step_x == 0 and side_y == 0 and side_z == 0:
                    continue
                to_x = index_x + step_x
                if side_y == 0:
                    to_y = index_y
                elif fold_y:
                    to_y = 1 - index_y
                else:
                    to_y = index_y + (2 * side_y - 3)
                to_z = index_z if side_z == 0 else 1 - index_z
                at = (((step_x + 1) * options_y + side_y) * 2 + side_z) * CAP

                @pl.when((to_x >= 0) & (to_x < count_x) & (to_y >= 0) & (to_y < count_y))
                def _(to=(to_x * count_y + to_y) * count_z + to_z, at=at):
                    bucket_ref[to] = rows[at : at + CAP]


def edges_kernel(
    sizes,
    a,
    alive_ref,
    latent_ref,
    edge_ref,
    neighbours_ref,
    far_ref,
    weights_ref,
    total_ref,
    hidden_ref,
):
    fold_y = sizes[1] == 2
    row_count = 3 if fold_y else 4
    index_y = lax.axis_index("gy")
    alive_ref, latent_ref = alive_ref.at[a], latent_ref.at[a]
    edge_ref, neighbours_ref = edge_ref.at[a], neighbours_ref.at[a]
    slots, width = latent_ref.shape[-2:]
    neighbour_count = edge_ref.shape[2]
    for bt in range(2):
        if fold_y:
            b = index_y if bt == 0 else 1 - index_y
            rows = (0, 1) if bt == 0 else (0, 1, 2)
        else:
            b = bt
            rows = (bt, bt + 1, bt + 2)
        columns = [(ex, row) for ex in range(a, a + 3) for row in rows]
        near = dot_nt(weights_ref[NEAR], latent_ref[b, 0])
        near = jnp.concatenate([near, near], axis=1)
        ids = jnp.concatenate([neighbours_ref[b, k] for k in range(neighbour_count)], axis=1)
        place, key = places(ids & 127, ids >> 7, fold_y)

        def pre(tile, b=b, near=near):
            edges = jnp.concatenate([edge_ref[b, 0, 2 * tile], edge_ref[b, 0, 2 * tile + 1]], axis=0)
            return dot_nt(weights_ref[EDGE], edges) + near

        message = messages(
            far_ref,
            columns,
            row_count,
            place,
            key,
            pre,
            weights_ref[MIDDLE],
            weights_ref[FINAL],
            hidden_ref.at[bt],
        )
        total = jnp.where(alive_ref[b] > 0.5, slot_sum(message, slots), 0.0)
        total_ref[b] = total.astype(BF16)


def nodes_kernel(
    sizes,
    first_ref,
    second_ref,
    node_pre_ref,
    latent_t_ref,
    state_ref,
    weights_ref,
    decoder_out_ref,
    inward_ref,
    encoder_w_ref,
    kept_latent_ref,
    kept_state_ref,
):
    slots = first_ref.shape[-1]
    aggregate = jnp.concatenate([first_ref[0], first_ref[1], second_ref[0], second_ref[1]], axis=1)
    acceleration = advance(
        node_pre_ref[...], aggregate, latent_t_ref[...], weights_ref, decoder_out_ref[...]
    )
    stays = state_ref[6:7]
    state = moved(state_ref[0:3], state_ref[3:6], acceleration)
    extent = (2.0 * sizes[0], 2.0 * sizes[1], 1.0 * sizes[2])
    latents = encode(state, stays, inward_ref[...], encoder_w_ref[...], extent)
    kept = state * stays
    for i, (a, b) in enumerate(CELLS):
        kept_latent_ref[a, b, 0] = latents[i * slots : (i + 1) * slots]
        for j in range(9):
            kept_state_ref[j, a, b] = kept[j : j + 1, i * slots : (i + 1) * slots]


def arrive_kernel(
    sizes,
    received_ref,
    inward_ref,
    encoder_w_ref,
    arrived_latent_ref,
    arrived_state_ref,
):
    count_x, count_y, count_z = sizes
    index_x = lax.axis_index("gx")
    index_y = lax.axis_index("gy")
    index_z = lax.axis_index("gz")
    rows = []
    for direction in range(27):
        if direction == 13:
            continue
        x = index_x + (direction // 9 - 1)
        y = index_y + (direction // 3 % 3 - 1)
        z = index_z + (direction % 3 - 1)
        inside = (x >= 0) & (x < count_x) & (y >= 0) & (y < count_y) & (z >= 0) & (z < count_z)
        source = jnp.where(inside, (x * count_y + y) * count_z + z, 0)
        rows.append(jnp.where(inside, received_ref[source], 0.0))
    rows.append(jnp.zeros((256 - 26 * CAP, 128), F32))
    arrived = jnp.concatenate(rows, axis=0).T[:ROWS, : 26 * CAP]
    for j in range(9):
        arrived_state_ref[j, 0, 0] = arrived[j : j + 1]
    extent = (2.0 * count_x, 2.0 * count_y, 1.0 * count_z)
    arrived_latent_ref[0, 0, 0] = encode(
        arrived[:9], arrived[9:10], inward_ref[...], encoder_w_ref[...], extent
    )


def swap(values, axis):
    return lax.ppermute(values, axis, [(0, 1), (1, 0)])


def shift(values, axis, way):
    pairs = [(i, i + 1) for i in range(lax.axis_size(axis) - 1)]
    return lax.ppermute(values, axis, [(j, i) for i, j in pairs] if way else pairs)


def swap_x(values, first):
    count = lax.axis_size("gx")
    pairs = []
    for x in range(count):
        partner = x + 1 if (x - first) % 2 == 0 else x - 1
        for z in range(2):
            if 0 <= partner < count:
                pairs.append((x * 2 + z, partner * 2 + z))
            else:
                pairs.append((x * 2 + z, x * 2 + 1 - z))
    return lax.ppermute(values, ("gx", "gz"), pairs)


def call(kernel, name, in_specs, outs, scratch, operands, flops):
    return pl.pallas_call(
        kernel,
        out_shape=tuple(jax.ShapeDtypeStruct(shape, kind) for shape, kind in outs),
        in_specs=in_specs,
        out_specs=tuple(VMEM for _ in outs),
        scratch_shapes=scratch,
        compiler_params=pltpu.CompilerParams(vmem_limit_bytes=32 * 1024 * 1024),
        cost_estimate=pl.CostEstimate(flops=flops, bytes_accessed=0, transcendentals=0),
        name=name,
    )(*operands)


def in_hbm(array):
    return pltpu.with_memory_space_constraint(array, pltpu.HBM)


def like(array):
    return pltpu.VMEM(array.shape, array.dtype)


def body(
    node_latent,
    edge_latent,
    positions,
    velocity,
    fill,
    neighbours,
    owners,
    edge_weights,
    node_in,
    node_weights,
    decoder_weights,
    decoder_out,
    encoder_in,
    encoder_weights,
):
    sizes = tuple(lax.axis_size(axis) for axis in ("gx", "gy", "gz"))
    fold_y = sizes[1] == 2
    slots, width = node_latent.shape[-2:]
    neighbour_count = neighbours.shape[3]
    particles = 4 * slots
    options_y = 2 if fold_y else 3
    movers = (3 * options_y * 2 * CAP + 127) // 128 * 128
    rows = 3 if fold_y else 4
    fill = jnp.transpose(fill, (0, 2, 1))
    neighbours = neighbours.reshape(2, 2, neighbour_count, 1, slots)

    parity = lax.axis_index("gx") & 1
    cells = node_latent[:, :, 0]
    if fold_y:
        inner = 1 - lax.axis_index("gy")
        sides = [swap(lax.dynamic_index_in_dim(cells, inner, 1, keepdims=False), "gy")]
    else:
        sides = [shift(cells[:, 1], "gy", 0), shift(cells[:, 0], "gy", 1)]

    fetched = (node_latent, neighbours, positions, velocity, edge_latent)
    ranked = call(
        functools.partial(ranks_kernel, sizes),
        "ranks",
        [SMEM] + [ANY] * 13,
        [
            ((11, width, width), BF16),
            (decoder_out.shape, BF16),
            ((48, width), BF16),
            (encoder_weights.shape, BF16),
            ((movers, particles), BF16),
            ((8, particles), F32),
            ((2, 2, 1, slots), F32),
            *((array.shape, array.dtype) for array in fetched),
            ((2, slots, width), BF16),
            ((2, slots, width), BF16),
        ],
        [
            like(owners),
            like(edge_weights),
            like(node_in),
            like(node_weights),
            like(decoder_weights),
            like(encoder_in),
            pltpu.SemaphoreType.DMA((13,)),
        ],
        [
            in_hbm(array)
            for array in (
                fill,
                owners,
                edge_weights,
                node_in,
                node_weights,
                decoder_weights,
                decoder_out,
                encoder_in,
                encoder_weights,
                *fetched,
            )
        ],
        500_000_000,
    )
    sides, ranked = lax.optimization_barrier((sides, ranked))
    weights, decoder_out, inward, encoder_weights, placer, masks, alive, *ranked = ranked
    latent, neighbours, positions, velocity, edge_latent, *own_ends = ranked

    def layer(a, own):
        outer = [lax.dynamic_index_in_dim(side, a, 0) for side in sides]
        parts = [own, outer[0]] if fold_y else [outer[0], own, outer[1]]
        return jnp.concatenate(parts, axis=0)

    ends = [swap_x(layer(1 - parity, own_ends[0]), 0), swap_x(layer(parity, own_ends[1]), 1)]
    zeds = [swap(part, "gz") for part in [latent, *sides]]
    prepared = call(
        functools.partial(prepare_kernel, sizes),
        "prepare",
        [VMEM] * 8,
        [
            ((width, particles), F32),
            ((width, particles), F32),
            ((8, particles), F32),
            ((width, neighbour_count * movers), F32),
            ((neighbour_count, movers), I32),
            ((neighbour_count, movers), I32),
            ((width, movers), F32),
            ((width, movers), F32),
            ((8, movers), F32),
        ],
        [],
        (latent, edge_latent, positions, velocity, neighbours, weights, placer, masks),
        500_000_000,
    )
    ends, zeds, prepared = lax.optimization_barrier((ends, zeds, prepared))
    (
        latent_t,
        node_pre,
        state,
        mover_pre,
        mover_place,
        mover_key,
        mover_node_pre,
        mover_latent,
        mover_state,
    ) = prepared
    halo = [*sides, *ends, *zeds, *(swap(part, "gz") for part in ends)]

    far, bucket = call(
        functools.partial(movers_kernel, sizes, len(sides)),
        "movers",
        [VMEM] * (len(halo) + 9),
        [((4 * rows, width, 2 * slots), BF16), ((sizes[0] * sizes[1] * sizes[2], CAP, 128), F32)],
        [pltpu.VMEM((width, neighbour_count * movers), BF16)],
        (
            latent,
            *halo,
            weights,
            decoder_out,
            mover_pre,
            mover_place,
            mover_key,
            mover_node_pre,
            mover_latent,
            mover_state,
        ),
        3_000_000_000,
    )

    def edges(a):
        return call(
            functools.partial(edges_kernel, sizes, a),
            "edges",
            [VMEM] * 6,
            [((2, width, slots), BF16)],
            [pltpu.VMEM((2, width, neighbour_count * slots), BF16)],
            (alive, latent, edge_latent, neighbours, far, weights),
            4_000_000_000,
        )[0]

    received = lax.all_to_all(bucket, ("gx", "gy", "gz"), 0, 0, tiled=True)
    first, second = edges(0), edges(1)
    kept_latent, kept_state = call(
        functools.partial(nodes_kernel, sizes),
        "nodes",
        [VMEM] * 9,
        [(node_latent.shape, BF16), ((9,) + node_latent.shape[:4], F32)],
        [],
        (
            first,
            second,
            node_pre,
            latent_t,
            state,
            weights,
            decoder_out,
            inward,
            encoder_weights,
        ),
        2_000_000_000,
    )
    arrived_latent, arrived_state = call(
        functools.partial(arrive_kernel, sizes),
        "arrive",
        [VMEM] * 3,
        [((1, 1, 1, 26 * CAP, width), BF16), ((9, 1, 1, 1, 26 * CAP), F32)],
        [],
        (received, inward, encoder_weights),
        1_000_000_000,
    )
    return kept_latent, kept_state, arrived_latent, arrived_state


def solution(mesh):
    placed = (
        P(("group", "gx"), "gy", "gz", None, None),
        P(("group", "gx"), "gy", "gz", None, None, None),
        P(None, ("group", "gx"), "gy", "gz", None),
        P(None, ("group", "gx"), "gy", "gz", None),
        P(("group", "gx"), "gy", "gz"),
        P(("group", "gx"), "gy", "gz", None, None),
        P(("group", "gx"), "gy", "gz", None),
        P(),
        P(),
        P(),
        P(),
        P(),
        P(),
        P(),
    )
    return jax.shard_map(
        body,
        mesh=mesh,
        in_specs=placed,
        out_specs=(
            P(("group", "gx"), "gy", "gz", None, None),
            P(None, ("group", "gx"), "gy", "gz", None),
            P(("group", "gx"), "gy", "gz", None, None),
            P(None, ("group", "gx"), "gy", "gz", None),
        ),
        check_vma=False,
    )
```

```python
import functools

import jax
import jax.numpy as jnp
from jax import lax
from jax.experimental import pallas as pl
from jax.experimental.pallas import tpu as pltpu
from jax.sharding import PartitionSpec as P

CAP = 8
F32 = jnp.float32
BF16 = jnp.bfloat16
I32 = jnp.int32
ROWS = 16
TILE = 256
CELLS = [(a, b) for a in range(2) for b in range(2)]
EDGE, NEAR, FAR, MIDDLE, FINAL, NODE_OLD, NODE_NEW, NODE_0, NODE_1, DECODE_0, DECODE_1 = range(11)

VMEM = pl.BlockSpec(memory_space=pltpu.VMEM)
SMEM = pl.BlockSpec(memory_space=pltpu.SMEM)
ANY = pl.BlockSpec(memory_space=pl.ANY)


def dot(left, right):
    return jnp.dot(left, right, preferred_element_type=F32)


def dot_nt(left, right):
    return lax.dot_general(left, right, (((1,), (1,)), ((), ())), preferred_element_type=F32)


def dot_tn(left, right):
    return lax.dot_general(left, right, (((0,), (0,)), ((), ())), preferred_element_type=F32)


def relu16(values):
    return jnp.maximum(values, 0.0).astype(BF16)


def norm(values, axis):
    scale = 1.0 / values.shape[axis]
    centred = values - jnp.sum(values, axis=axis, keepdims=True) * scale
    spread = jnp.sum(centred * centred, axis=axis, keepdims=True) * scale
    return centred * lax.rsqrt(spread + 1e-05)


def thirds(values):
    high = values.astype(BF16)
    rest = values - high.astype(F32)
    middle = rest.astype(BF16)
    low = (rest - middle.astype(F32)).astype(BF16)
    return jnp.concatenate([high, middle, low], axis=0)


def joined(values):
    rows = values.shape[0] // 3
    return values[:rows] + values[rows : 2 * rows] + values[2 * rows :]


def quotient(values, count):
    if count & (count - 1) == 0:
        return values >> (count.bit_length() - 1)
    return lax.div(values, jnp.full_like(values, count))


def flip(weights):
    return weights.astype(F32).T.astype(BF16)


def fetch(pairs, sems):
    copies = [pltpu.make_async_copy(src, dst, sems.at[i]) for i, (src, dst) in enumerate(pairs)]
    for copy in copies:
        copy.start()
    return copies


def encode(state, mask, inward, encoder_w, extent):
    width = state.shape[1]
    position = state[0:3]
    row = lax.broadcasted_iota(I32, (3, width), 0)
    size = jnp.where(row == 0, extent[0], jnp.where(row == 1, extent[1], extent[2]))
    features = jnp.concatenate(
        [
            state[3:9],
            jnp.clip(position, -1.0, 1.0),
            jnp.clip(size - position, -1.0, 1.0),
            jnp.zeros((4, width), F32),
        ],
        axis=0,
    )
    hidden = relu16(dot_tn(thirds(features), inward))
    hidden = relu16(dot(hidden, encoder_w[0]))
    column = jnp.broadcast_to(mask, (8, width)).T[:, 0:1]
    return (norm(dot(hidden, encoder_w[1]), 1) * column).astype(BF16)


def places(ids_low, ids_high, fold_y):
    plane = (ids_high * 43) >> 7
    ez = ids_high - plane * 3
    ey = plane & 3
    ex = plane >> 2
    if fold_y:
        row = jnp.where(ey == 1, 0, jnp.where(ey == 2, 1, 2))
    else:
        row = ey
    return ex * 4 + row, ids_low + jnp.where(ez == 1, 0, 128)


def messages(far_ref, columns, row_count, place, key, pre, middle_t, final_t, hidden_ref):
    width = far_ref.shape[1]
    chunk = 32
    window = jnp.concatenate(
        [
            far_ref[ex * row_count + row, f : f + chunk]
            for f in range(0, width, chunk)
            for ex, row in columns
        ],
        axis=0,
    )
    key_rows = lax.broadcasted_iota(I32, (TILE, TILE), 0)
    lanes = place.shape[1]
    for tile in range(lanes // TILE):
        at = slice(tile * TILE, (tile + 1) * TILE)
        picker = jnp.where(key_rows == key[:, at], 1.0, 0.0).astype(BF16)
        found = dot(window, picker).reshape(width // chunk, len(columns), chunk // 8, 8, TILE)
        where = jnp.broadcast_to(place[:, at], (8, TILE))
        parts = []
        for f in range(width // chunk):
            part = jnp.zeros((chunk // 8, 8, TILE), F32)
            for i, (ex, row) in enumerate(columns):
                part = jnp.where((where == ex * 4 + row)[None], found[f, i], part)
            parts.append(part.reshape(chunk, TILE))
        hidden_ref[:, at] = relu16(pre(tile) + jnp.concatenate(parts, axis=0))
    hidden = relu16(dot(middle_t, hidden_ref[...]))
    return norm(dot(final_t, hidden), 0)


def slot_sum(message, step):
    total = message[:, :step]
    for at in range(step, message.shape[1], step):
        total = total + message[:, at : at + step]
    return total


def advance(pre, aggregate, latent_t, weights_ref, decoder_out):
    pre = pre + dot(weights_ref[NODE_NEW], aggregate)
    hidden = relu16(dot(weights_ref[NODE_0], relu16(pre)))
    updated = (latent_t + norm(dot(weights_ref[NODE_1], hidden), 0)).astype(BF16)
    hidden = relu16(dot(weights_ref[DECODE_0], updated))
    hidden = relu16(dot(weights_ref[DECODE_1], hidden))
    return dot(decoder_out, hidden)


def moved(position, velocity, acceleration):
    new_velocity = velocity + acceleration
    return jnp.concatenate([position + new_velocity, new_velocity, velocity], axis=0)


def ranks_kernel(
    sizes,
    fill_ref,
    owners_any,
    edge_w_any,
    node_in_any,
    node_w_any,
    decoder_w_any,
    decoder_out_any,
    encoder_in_any,
    encoder_w_any,
    latent_any,
    neighbours_any,
    positions_any,
    velocity_any,
    edge_any,
    weights_ref,
    decoder_out_ref,
    inward_ref,
    encoder_w_ref,
    placer_ref,
    masks_ref,
    alive_ref,
    latent_ref,
    neighbours_ref,
    positions_ref,
    velocity_ref,
    edge_ref,
    first_end_ref,
    second_end_ref,
    owners_ref,
    edge_w_ref,
    node_in_ref,
    node_w_ref,
    decoder_w_ref,
    encoder_in_ref,
    sems,
):
    count_x, count_y, count_z = sizes
    fold_y = count_y == 2
    copies = fetch(
        [
            (owners_any, owners_ref),
            (edge_w_any, edge_w_ref),
            (node_in_any, node_in_ref),
            (node_w_any, node_w_ref),
            (decoder_w_any, decoder_w_ref),
            (decoder_out_any, decoder_out_ref),
            (encoder_in_any, encoder_in_ref),
            (encoder_w_any, encoder_w_ref),
            (latent_any, latent_ref),
            (neighbours_any, neighbours_ref),
            (positions_any, positions_ref),
            (velocity_any, velocity_ref),
            (edge_any, edge_ref),
        ],
        sems,
    )
    copies[0].wait()
    index_x = lax.axis_index("gx")
    index_y = lax.axis_index("gy")
    index_z = lax.axis_index("gz")
    slots = owners_ref.shape[-1]
    width = node_in_ref.shape[-1]
    for a, b in CELLS:
        alive_ref[a, b] = jnp.where(
            lax.broadcasted_iota(I32, (1, slots), 1) < fill_ref[a, 0, b], 1.0, 0.0
        )

    lane = lax.broadcasted_iota(I32, (1, slots), 1)
    owner = jnp.concatenate([owners_ref[a, b] for a, b in CELLS], axis=1)
    alive = jnp.concatenate([jnp.where(lane < fill_ref[a, 0, b], 1, 0) for a, b in CELLS], axis=1)
    own_block = (index_x * count_y + index_y) * count_z + index_z
    stays = jnp.where((alive == 1) & (owner == own_block), 1.0, 0.0)
    moving = jnp.where((alive == 1) & (owner != own_block), 1, 0)
    owner_x = quotient(owner, count_y * count_z)
    rest = owner - owner_x * (count_y * count_z)
    owner_y = quotient(rest, count_z)
    owner_z = rest - owner_y * count_z
    step_y = owner_y - index_y
    side_y = jnp.where(step_y == 0, 0, 1) if fold_y else jnp.where(step_y < 0, 1, 2 * step_y)
    options_y = 2 if fold_y else 3
    group = ((owner_x - index_x + 1) * options_y + side_y) * 2 + jnp.where(owner_z == index_z, 0, 1)
    group_rows = (3 * options_y * 2 + 15) // 16 * 16
    particles = owner.shape[1]
    member = jnp.where(
        (lax.broadcasted_iota(I32, (group_rows, particles), 0) == group) & (moving == 1), 1.0, 0.0
    )
    triangle = jnp.where(
        lax.broadcasted_iota(I32, (slots, slots), 0) <= lax.broadcasted_iota(I32, (slots, slots), 1),
        1.0,
        0.0,
    ).astype(BF16)
    counted = []
    before = jnp.zeros((group_rows, 1), F32)
    for i in range(4):
        inside = member[:, i * slots : (i + 1) * slots]
        counted.append(dot(inside.astype(BF16), triangle) + before)
        before = before + jnp.sum(inside, axis=1, keepdims=True)
    counted = jnp.concatenate(counted, axis=1)
    rank = (jnp.sum(counted * member, axis=0, keepdims=True) - 1.0).astype(I32)
    column = jnp.where(moving == 1, group * CAP + rank, -1)
    movers = placer_ref.shape[0]
    placer_ref[...] = jnp.where(
        lax.broadcasted_iota(I32, (movers, particles), 0) == column, 1.0, 0.0
    ).astype(BF16)
    masks_ref[...] = jnp.concatenate(
        [stays, moving.astype(F32), jnp.zeros((6, particles), F32)], axis=0
    )

    for copy in copies[1:]:
        copy.wait()
    for i in range(5):
        weights_ref[i] = flip(edge_w_ref[i])
    weights_ref[NODE_OLD] = flip(node_in_ref[:width])
    weights_ref[NODE_NEW] = flip(node_in_ref[width:])
    for i in range(2):
        weights_ref[NODE_0 + i] = flip(node_w_ref[i])
        weights_ref[DECODE_0 + i] = flip(decoder_w_ref[i])
    inward = jnp.concatenate([encoder_in_ref[...].astype(F32), jnp.zeros((4, width), F32)], axis=0)
    inward = inward.astype(BF16)
    inward_ref[...] = jnp.concatenate([inward, inward, inward], axis=0)
    parity = index_x & 1
    for b in range(2):
        first_end_ref[b] = latent_ref[1 - parity, b, 0]
        second_end_ref[b] = latent_ref[parity, b, 0]


def prepare_kernel(
    sizes,
    latent_ref,
    edge_ref,
    positions_ref,
    velocity_ref,
    neighbours_ref,
    weights_ref,
    placer_ref,
    masks_ref,
    latent_t_ref,
    node_pre_ref,
    state_ref,
    mover_pre_ref,
    mover_place_ref,
    mover_key_ref,
    mover_node_pre_ref,
    mover_latent_ref,
    mover_state_ref,
):
    fold_y = sizes[1] == 2
    neighbour_count = edge_ref.shape[3]
    placer = placer_ref[...]
    movers, particles = placer.shape
    stays, moving = masks_ref[0:1], masks_ref[1:2]

    latent = jnp.concatenate([latent_ref[a, b, 0] for a, b in CELLS], axis=0)
    latent_t_ref[...] = latent.astype(F32).T
    node_pre_ref[...] = dot_nt(weights_ref[NODE_OLD], latent)

    def flat(ref, i):
        return jnp.concatenate([ref[i, a, b] for a, b in CELLS], axis=1)

    state = [flat(positions_ref, i) for i in range(3)] + [flat(velocity_ref, i) for i in range(3)]
    state_ref[...] = jnp.concatenate(state + [stays, jnp.zeros_like(stays)], axis=0)

    mover_latent = dot(placer, latent).astype(BF16)
    mover_latent_ref[...] = mover_latent.astype(F32).T
    mover_node_pre_ref[...] = dot_nt(weights_ref[NODE_OLD], mover_latent)
    near = dot_nt(weights_ref[NEAR], mover_latent)
    state = jnp.concatenate(state + [moving, jnp.zeros_like(stays)], axis=0)
    mover_state_ref[...] = joined(dot_nt(thirds(state), placer))
    ids = jnp.concatenate(
        [
            jnp.concatenate([neighbours_ref[a, b, k] for a, b in CELLS], axis=1)
            for k in range(neighbour_count)
        ],
        axis=0,
    )
    ids = jnp.concatenate([ids & 127, ids >> 7, jnp.zeros((8, particles), I32)], axis=0)
    ids = dot_nt(ids.astype(F32).astype(BF16), placer).astype(I32)
    place, key = places(ids[:neighbour_count], ids[neighbour_count : 2 * neighbour_count], fold_y)
    mover_place_ref[...] = place
    mover_key_ref[...] = key
    for k in range(neighbour_count):
        edges = jnp.concatenate([edge_ref[a, b, 0, k] for a, b in CELLS], axis=0)
        edges = dot(placer, edges).astype(BF16)
        mover_pre_ref[:, k * movers : (k + 1) * movers] = dot_nt(weights_ref[EDGE], edges) + near


def movers_kernel(
    sizes,
    side_count,
    own_ref,
    *refs,
):
    count_x, count_y, count_z = sizes
    fold_y = count_y == 2
    side_refs, refs = refs[:side_count], refs[side_count:]
    even_ref, odd_ref, own_zed, refs = refs[0], refs[1], refs[2], refs[3:]
    side_zeds, refs = refs[:side_count], refs[side_count:]
    even_zed, odd_zed, refs = refs[0], refs[1], refs[2:]
    (
        weights_ref,
        decoder_out_ref,
        pre_ref,
        place_ref,
        key_ref,
        node_pre_ref,
        latent_t_ref,
        state_ref,
        far_ref,
        bucket_ref,
        hidden_ref,
    ) = refs
    row_count = 3 if fold_y else 4
    own_rows = (0, 1) if fold_y else (1, 2)
    outer = {2: 0} if fold_y else {0: 0, 3: 1}
    parity = lax.axis_index("gx") & 1
    far_t = weights_ref[FAR]

    def far(at, here, beside):
        pair = jnp.concatenate([here, beside], axis=0)
        far_ref[at] = dot_nt(far_t, pair).astype(BF16)

    for row in range(row_count):
        for ex in (1, 2):
            if row in own_rows:
                b = own_rows.index(row)
                far(ex * row_count + row, own_ref[ex - 1, b, 0], own_zed[ex - 1, b, 0])
            else:
                side = outer[row]
                far(ex * row_count + row, side_refs[side][ex - 1], side_zeds[side][ex - 1])
        far(3 * (1 - parity) * row_count + row, even_ref[row], even_zed[row])
        far(3 * parity * row_count + row, odd_ref[row], odd_zed[row])

    movers = state_ref.shape[1]
    neighbour_count = place_ref.shape[0]
    place = jnp.concatenate([place_ref[k : k + 1] for k in range(neighbour_count)], axis=1)
    key = jnp.concatenate([key_ref[k : k + 1] for k in range(neighbour_count)], axis=1)
    columns = [(ex, row) for ex in range(4) for row in range(row_count)]
    message = messages(
        far_ref,
        columns,
        row_count,
        place,
        key,
        lambda tile: pre_ref[:, tile * TILE : (tile + 1) * TILE],
        weights_ref[MIDDLE],
        weights_ref[FINAL],
        hidden_ref,
    )
    aggregate = slot_sum(message, movers).astype(BF16)
    acceleration = advance(
        node_pre_ref[...], aggregate, latent_t_ref[...], weights_ref, decoder_out_ref[...]
    )
    mask = state_ref[6:7]
    state = moved(state_ref[0:3], state_ref[3:6], acceleration) * mask
    bucket_ref[...] = jnp.concatenate([state, mask, jnp.zeros((ROWS - 10, movers), F32)], axis=0)


def edges_kernel(
    sizes,
    a,
    alive_ref,
    latent_ref,
    edge_ref,
    neighbours_ref,
    far_ref,
    weights_ref,
    total_ref,
    hidden_ref,
):
    fold_y = sizes[1] == 2
    row_count = 3 if fold_y else 4
    index_y = lax.axis_index("gy")
    alive_ref, latent_ref = alive_ref.at[a], latent_ref.at[a]
    edge_ref, neighbours_ref = edge_ref.at[a], neighbours_ref.at[a]
    slots, width = latent_ref.shape[-2:]
    neighbour_count = edge_ref.shape[2]
    for bt in range(2):
        if fold_y:
            b = index_y if bt == 0 else 1 - index_y
            rows = (0, 1) if bt == 0 else (0, 1, 2)
        else:
            b = bt
            rows = (bt, bt + 1, bt + 2)
        columns = [(ex, row) for ex in range(a, a + 3) for row in rows]
        near = dot_nt(weights_ref[NEAR], latent_ref[b, 0])
        near = jnp.concatenate([near, near], axis=1)
        ids = jnp.concatenate([neighbours_ref[b, k] for k in range(neighbour_count)], axis=1)
        place, key = places(ids & 127, ids >> 7, fold_y)

        def pre(tile, b=b, near=near):
            edges = jnp.concatenate([edge_ref[b, 0, 2 * tile], edge_ref[b, 0, 2 * tile + 1]], axis=0)
            return dot_nt(weights_ref[EDGE], edges) + near

        message = messages(
            far_ref,
            columns,
            row_count,
            place,
            key,
            pre,
            weights_ref[MIDDLE],
            weights_ref[FINAL],
            hidden_ref.at[bt],
        )
        total = jnp.where(alive_ref[b] > 0.5, slot_sum(message, slots), 0.0)
        total_ref[b] = total.astype(BF16)


def nodes_kernel(
    first_ref,
    second_ref,
    node_pre_ref,
    latent_t_ref,
    state_ref,
    weights_ref,
    decoder_out_ref,
    moved_ref,
):
    aggregate = jnp.concatenate([first_ref[0], first_ref[1], second_ref[0], second_ref[1]], axis=1)
    acceleration = advance(
        node_pre_ref[...], aggregate, latent_t_ref[...], weights_ref, decoder_out_ref[...]
    )
    state = moved(state_ref[0:3], state_ref[3:6], acceleration)
    moved_ref[...] = jnp.concatenate(
        [state, state_ref[6:7], jnp.zeros((ROWS - 10, state.shape[1]), F32)], axis=0
    )


def finish_kernel(
    sizes,
    moved_ref,
    own_ref,
    even_ref,
    odd_ref,
    own_zed,
    even_zed,
    odd_zed,
    inward_ref,
    encoder_w_ref,
    kept_latent_ref,
    kept_state_ref,
    arrived_latent_ref,
    arrived_state_ref,
):
    count_x, count_y, count_z = sizes
    extent = (2.0 * count_x, 2.0 * count_y, 1.0 * count_z)
    slots = kept_latent_ref.shape[-2]
    stays = moved_ref[9:10]
    kept = moved_ref[:9] * stays
    latents = encode(moved_ref[:9], stays, inward_ref[...], encoder_w_ref[...], extent)
    for i, (a, b) in enumerate(CELLS):
        kept_latent_ref[a, b, 0] = latents[i * slots : (i + 1) * slots]
        for j in range(9):
            kept_state_ref[j, a, b] = kept[j : j + 1, i * slots : (i + 1) * slots]
    fold_y = count_y == 2
    index_x = lax.axis_index("gx")
    index_y = lax.axis_index("gy")
    index_z = lax.axis_index("gz")
    options_y = 2 if fold_y else 3
    lanes = own_ref.shape[-1]
    group = lax.broadcasted_iota(I32, (ROWS, lanes), 1) >> 3
    even = (index_x & 1) == 0
    found = jnp.zeros((ROWS, lanes), F32)
    for source_x in (-1, 0, 1):
        for from_y in range(options_y):
            for from_z in range(2):
                if source_x == 0 and from_y == 0 and from_z == 0:
                    continue
                if from_z == 0:
                    own, first, second = own_ref, even_ref, odd_ref
                else:
                    own, first, second = own_zed, even_zed, odd_zed
                side_y = from_y if fold_y or from_y == 0 else 3 - from_y
                target = ((1 - source_x) * options_y + side_y) * 2 + from_z
                if source_x == 0:
                    tile = own[from_y]
                    there = group == target
                elif source_x == -1:
                    tile = jnp.where(even, second[from_y], first[from_y])
                    there = (group == target) & (index_x > 0)
                else:
                    tile = jnp.where(even, first[from_y], second[from_y])
                    there = (group == target) & (index_x < count_x - 1)
                found = jnp.where(there, tile, found)
    out_lanes = arrived_state_ref.shape[-1]
    spread_shape = (lanes, out_lanes)
    line = lax.broadcasted_iota(I32, spread_shape, 0)
    from_group = line >> 3
    plane = from_group >> 1
    from_x = 1 - ((plane >> 1) if fold_y else ((plane * 43) >> 7))
    side_y = plane - (1 - from_x) * options_y
    if fold_y:
        from_y = jnp.where(side_y == 0, 0, jnp.where(index_y == 0, 1, -1))
    else:
        from_y = jnp.where(side_y == 0, 0, jnp.where(side_y == 1, 1, -1))
    from_z = jnp.where((from_group & 1) == 0, 0, jnp.where(index_z == 0, 1, -1))
    direction = (from_x + 1) * 9 + (from_y + 1) * 3 + from_z + 1
    direction = direction - jnp.where(direction > 13, 1, 0)
    column = direction * CAP + (line & 7)
    valid = (lax.broadcasted_iota(I32, spread_shape, 1) == column) & (
        (from_x != 0) | (from_y != 0) | (from_z != 0)
    )
    spread = jnp.where(valid, 1.0, 0.0).astype(BF16)
    arrived = joined(dot(thirds(found), spread))
    for j in range(9):
        arrived_state_ref[j, 0, 0] = arrived[j : j + 1]
    arrived_latent_ref[0, 0, 0] = encode(
        arrived[:9], arrived[9:10], inward_ref[...], encoder_w_ref[...], extent
    )


def swap(values, axis):
    return lax.ppermute(values, axis, [(0, 1), (1, 0)])


def shift(values, axis, way):
    pairs = [(i, i + 1) for i in range(lax.axis_size(axis) - 1)]
    return lax.ppermute(values, axis, [(j, i) for i, j in pairs] if way else pairs)


def swap_x(values, first):
    count = lax.axis_size("gx")
    pairs = []
    for x in range(count):
        partner = x + 1 if (x - first) % 2 == 0 else x - 1
        for z in range(2):
            if 0 <= partner < count:
                pairs.append((x * 2 + z, partner * 2 + z))
            else:
                pairs.append((x * 2 + z, x * 2 + 1 - z))
    return lax.ppermute(values, ("gx", "gz"), pairs)


def call(kernel, name, in_specs, outs, scratch, operands, flops):
    return pl.pallas_call(
        kernel,
        out_shape=tuple(jax.ShapeDtypeStruct(shape, kind) for shape, kind in outs),
        in_specs=in_specs,
        out_specs=tuple(VMEM for _ in outs),
        scratch_shapes=scratch,
        compiler_params=pltpu.CompilerParams(vmem_limit_bytes=32 * 1024 * 1024),
        cost_estimate=pl.CostEstimate(flops=flops, bytes_accessed=0, transcendentals=0),
        name=name,
    )(*operands)


def in_hbm(array):
    return pltpu.with_memory_space_constraint(array, pltpu.HBM)


def like(array):
    return pltpu.VMEM(array.shape, array.dtype)


def body(
    node_latent,
    edge_latent,
    positions,
    velocity,
    fill,
    neighbours,
    owners,
    edge_weights,
    node_in,
    node_weights,
    decoder_weights,
    decoder_out,
    encoder_in,
    encoder_weights,
):
    sizes = tuple(lax.axis_size(axis) for axis in ("gx", "gy", "gz"))
    fold_y = sizes[1] == 2
    slots, width = node_latent.shape[-2:]
    neighbour_count = neighbours.shape[3]
    particles = 4 * slots
    options_y = 2 if fold_y else 3
    movers = (3 * options_y * 2 * CAP + 127) // 128 * 128
    rows = 3 if fold_y else 4
    fill = jnp.transpose(fill, (0, 2, 1))
    neighbours = neighbours.reshape(2, 2, neighbour_count, 1, slots)

    parity = lax.axis_index("gx") & 1
    cells = node_latent[:, :, 0]
    if fold_y:
        inner = 1 - lax.axis_index("gy")
        sides = [swap(lax.dynamic_index_in_dim(cells, inner, 1, keepdims=False), "gy")]
    else:
        sides = [shift(cells[:, 1], "gy", 0), shift(cells[:, 0], "gy", 1)]

    fetched = (node_latent, neighbours, positions, velocity, edge_latent)
    ranked = call(
        functools.partial(ranks_kernel, sizes),
        "ranks",
        [SMEM] + [ANY] * 13,
        [
            ((11, width, width), BF16),
            (decoder_out.shape, BF16),
            ((48, width), BF16),
            (encoder_weights.shape, BF16),
            ((movers, particles), BF16),
            ((8, particles), F32),
            ((2, 2, 1, slots), F32),
            *((array.shape, array.dtype) for array in fetched),
            ((2, slots, width), BF16),
            ((2, slots, width), BF16),
        ],
        [
            like(owners),
            like(edge_weights),
            like(node_in),
            like(node_weights),
            like(decoder_weights),
            like(encoder_in),
            pltpu.SemaphoreType.DMA((13,)),
        ],
        [
            in_hbm(array)
            for array in (
                fill,
                owners,
                edge_weights,
                node_in,
                node_weights,
                decoder_weights,
                decoder_out,
                encoder_in,
                encoder_weights,
                *fetched,
            )
        ],
        500_000_000,
    )
    sides, ranked = lax.optimization_barrier((sides, ranked))
    weights, decoder_out, inward, encoder_weights, placer, masks, alive, *ranked = ranked
    latent, neighbours, positions, velocity, edge_latent, *own_ends = ranked

    def layer(a, own):
        outer = [lax.dynamic_index_in_dim(side, a, 0) for side in sides]
        parts = [own, outer[0]] if fold_y else [outer[0], own, outer[1]]
        return jnp.concatenate(parts, axis=0)

    ends = [swap_x(layer(1 - parity, own_ends[0]), 0), swap_x(layer(parity, own_ends[1]), 1)]
    zeds = [swap(part, "gz") for part in [latent, *sides]]
    prepared = call(
        functools.partial(prepare_kernel, sizes),
        "prepare",
        [VMEM] * 8,
        [
            ((width, particles), F32),
            ((width, particles), F32),
            ((8, particles), F32),
            ((width, neighbour_count * movers), F32),
            ((neighbour_count, movers), I32),
            ((neighbour_count, movers), I32),
            ((width, movers), F32),
            ((width, movers), F32),
            ((8, movers), F32),
        ],
        [],
        (latent, edge_latent, positions, velocity, neighbours, weights, placer, masks),
        500_000_000,
    )
    ends, zeds, prepared = lax.optimization_barrier((ends, zeds, prepared))
    (
        latent_t,
        node_pre,
        state,
        mover_pre,
        mover_place,
        mover_key,
        mover_node_pre,
        mover_latent,
        mover_state,
    ) = prepared
    halo = [*sides, *ends, *zeds, *(swap(part, "gz") for part in ends)]

    far, bucket = call(
        functools.partial(movers_kernel, sizes, len(sides)),
        "movers",
        [VMEM] * (len(halo) + 9),
        [((4 * rows, width, 2 * slots), BF16), ((ROWS, movers), F32)],
        [pltpu.VMEM((width, neighbour_count * movers), BF16)],
        (
            latent,
            *halo,
            weights,
            decoder_out,
            mover_pre,
            mover_place,
            mover_key,
            mover_node_pre,
            mover_latent,
            mover_state,
        ),
        3_000_000_000,
    )

    def edges(a):
        return call(
            functools.partial(edges_kernel, sizes, a),
            "edges",
            [VMEM] * 6,
            [((2, width, slots), BF16)],
            [pltpu.VMEM((2, width, neighbour_count * slots), BF16)],
            (alive, latent, edge_latent, neighbours, far, weights),
            4_000_000_000,
        )[0]

    first = edges(0)
    if fold_y:
        tiles = [swap(bucket, "gy")]
    else:
        tiles = [shift(bucket, "gy", 0), shift(bucket, "gy", 1)]
    tiles, first = lax.optimization_barrier((tiles, first))
    tiles = jnp.stack([bucket, *tiles], axis=0)
    second = edges(1)
    sided = [swap_x(tiles, 0), swap_x(tiles, 1)]
    sided, second = lax.optimization_barrier((sided, second))
    tiles = [tiles, *sided]
    zeds = [swap(part, "gz") for part in tiles]
    state = call(
        nodes_kernel,
        "nodes",
        [VMEM] * 7,
        [((ROWS, particles), F32)],
        [],
        (first, second, node_pre, latent_t, state, weights, decoder_out),
        1_000_000_000,
    )[0]
    zeds, state = lax.optimization_barrier((zeds, state))
    return call(
        functools.partial(finish_kernel, sizes),
        "finish",
        [VMEM] * 9,
        [
            (node_latent.shape, BF16),
            ((9,) + node_latent.shape[:4], F32),
            ((1, 1, 1, 26 * CAP, width), BF16),
            ((9, 1, 1, 1, 26 * CAP), F32),
        ],
        [],
        (state, *tiles, *zeds, inward, encoder_weights),
        1_000_000_000,
    )


def solution(mesh):
    placed = (
        P(("group", "gx"), "gy", "gz", None, None),
        P(("group", "gx"), "gy", "gz", None, None, None),
        P(None, ("group", "gx"), "gy", "gz", None),
        P(None, ("group", "gx"), "gy", "gz", None),
        P(("group", "gx"), "gy", "gz"),
        P(("group", "gx"), "gy", "gz", None, None),
        P(("group", "gx"), "gy", "gz", None),
        P(),
        P(),
        P(),
        P(),
        P(),
        P(),
        P(),
    )
    return jax.shard_map(
        body,
        mesh=mesh,
        in_specs=placed,
        out_specs=(
            P(("group", "gx"), "gy", "gz", None, None),
            P(None, ("group", "gx"), "gy", "gz", None),
            P(("group", "gx"), "gy", "gz", None, None),
            P(None, ("group", "gx"), "gy", "gz", None),
        ),
        check_vma=False,
    )
```

```python
import functools

import jax
import jax.numpy as jnp
from jax import lax
from jax.experimental import pallas as pl
from jax.experimental.pallas import tpu as pltpu
from jax.sharding import PartitionSpec as P

CAP = 8
F32 = jnp.float32
BF16 = jnp.bfloat16
I32 = jnp.int32
ROWS = 16
TILE = 256
CELLS = [(a, b) for a in range(2) for b in range(2)]
EDGE, NEAR, FAR, MIDDLE, FINAL, NODE_OLD, NODE_NEW, NODE_0, NODE_1, DECODE_0, DECODE_1 = range(11)

VMEM = pl.BlockSpec(memory_space=pltpu.VMEM)
SMEM = pl.BlockSpec(memory_space=pltpu.SMEM)
ANY = pl.BlockSpec(memory_space=pl.ANY)


def dot(left, right):
    return jnp.dot(left, right, preferred_element_type=F32)


def dot_nt(left, right):
    return lax.dot_general(left, right, (((1,), (1,)), ((), ())), preferred_element_type=F32)


def dot_tn(left, right):
    return lax.dot_general(left, right, (((0,), (0,)), ((), ())), preferred_element_type=F32)


def relu16(values):
    return jnp.maximum(values, 0.0).astype(BF16)


def norm(values, axis):
    scale = 1.0 / values.shape[axis]
    centred = values - jnp.sum(values, axis=axis, keepdims=True) * scale
    spread = jnp.sum(centred * centred, axis=axis, keepdims=True) * scale
    return centred * lax.rsqrt(spread + 1e-05)


def thirds(values):
    high = values.astype(BF16)
    rest = values - high.astype(F32)
    middle = rest.astype(BF16)
    low = (rest - middle.astype(F32)).astype(BF16)
    return jnp.concatenate([high, middle, low], axis=0)


def joined(values):
    rows = values.shape[0] // 3
    return values[:rows] + values[rows : 2 * rows] + values[2 * rows :]


def quotient(values, count):
    if count & (count - 1) == 0:
        return values >> (count.bit_length() - 1)
    return lax.div(values, jnp.full_like(values, count))


def flip(weights):
    return weights.astype(F32).T.astype(BF16)


def fetch(pairs, sems):
    copies = [pltpu.make_async_copy(src, dst, sems.at[i]) for i, (src, dst) in enumerate(pairs)]
    for copy in copies:
        copy.start()
    return copies


def encode(state, mask, inward, encoder_w, extent):
    width = state.shape[1]
    position = state[0:3]
    row = lax.broadcasted_iota(I32, (3, width), 0)
    size = jnp.where(row == 0, extent[0], jnp.where(row == 1, extent[1], extent[2]))
    features = jnp.concatenate(
        [
            state[3:9],
            jnp.clip(position, -1.0, 1.0),
            jnp.clip(size - position, -1.0, 1.0),
            jnp.zeros((4, width), F32),
        ],
        axis=0,
    )
    hidden = relu16(dot_tn(thirds(features), inward))
    hidden = relu16(dot(hidden, encoder_w[0]))
    column = jnp.broadcast_to(mask, (8, width)).T[:, 0:1]
    return (norm(dot(hidden, encoder_w[1]), 1) * column).astype(BF16)


def places(ids_low, ids_high, fold_y):
    plane = (ids_high * 43) >> 7
    ez = ids_high - plane * 3
    ey = plane & 3
    ex = plane >> 2
    if fold_y:
        row = jnp.where(ey == 1, 0, jnp.where(ey == 2, 1, 2))
    else:
        row = ey
    return ex * 4 + row, ids_low + jnp.where(ez == 1, 0, 128)


def pick(cells, place, key):
    width = cells[0][1].shape[0]
    chunk = 32
    window = jnp.concatenate(
        [ref[f : f + chunk] for f in range(0, width, chunk) for _, ref in cells], axis=0
    )
    key_rows = lax.broadcasted_iota(I32, (TILE, TILE), 0)
    picker = jnp.where(key_rows == key, 1.0, 0.0).astype(BF16)
    found = dot(window, picker).reshape(width // chunk, len(cells), chunk // 8, 8, TILE)
    where = jnp.broadcast_to(place, (8, TILE))
    parts = []
    for f in range(width // chunk):
        part = jnp.zeros((chunk // 8, 8, TILE), F32)
        for i, (column, _) in enumerate(cells):
            part = jnp.where((where == column)[None], found[f, i], part)
        parts.append(part.reshape(chunk, TILE))
    return jnp.concatenate(parts, axis=0)


def messages(cells, place, key, pre, middle_t, final_t, hidden_ref):
    for tile in range(place.shape[1] // TILE):
        at = slice(tile * TILE, (tile + 1) * TILE)
        hidden_ref[:, at] = relu16(pre(tile) + pick(cells, place[:, at], key[:, at]))
    hidden = relu16(dot(middle_t, hidden_ref[...]))
    return norm(dot(final_t, hidden), 0)


class Window:
    def __init__(self, fold_y, own_ref=None, rest_ref=None):
        self.row_count = 3 if fold_y else 4
        self.own_rows = (0, 1) if fold_y else (1, 2)
        self.outer_rows = (2,) if fold_y else (0, 3)
        self.own_ref, self.rest_ref = own_ref, rest_ref

    def own(self, ex, row):
        return (ex - 1) * 2 + self.own_rows.index(row)

    def side(self, ex, row):
        count = len(self.outer_rows)
        return 2 * self.row_count + (ex - 1) * count + self.outer_rows.index(row)

    def cells(self, columns):
        found = []
        for ex, row in columns:
            if ex in (1, 2) and row in self.own_rows:
                ref = self.own_ref.at[self.own(ex, row)]
            elif ex in (1, 2):
                ref = self.rest_ref.at[self.side(ex, row)]
            else:
                ref = self.rest_ref.at[(0 if ex == 0 else self.row_count) + row]
            found.append((ex * 4 + row, ref))
        return found


def slot_sum(message, step):
    total = message[:, :step]
    for at in range(step, message.shape[1], step):
        total = total + message[:, at : at + step]
    return total


def advance(pre, aggregate, latent_t, weights_ref, decoder_out):
    pre = pre + dot(weights_ref[NODE_NEW], aggregate)
    hidden = relu16(dot(weights_ref[NODE_0], relu16(pre)))
    updated = (latent_t + norm(dot(weights_ref[NODE_1], hidden), 0)).astype(BF16)
    hidden = relu16(dot(weights_ref[DECODE_0], updated))
    hidden = relu16(dot(weights_ref[DECODE_1], hidden))
    return dot(decoder_out, hidden)


def moved(position, velocity, acceleration):
    new_velocity = velocity + acceleration
    return jnp.concatenate([position + new_velocity, new_velocity, velocity], axis=0)


def ranks_kernel(
    sizes,
    fill_ref,
    owners_any,
    edge_w_any,
    node_in_any,
    node_w_any,
    decoder_w_any,
    decoder_out_any,
    encoder_in_any,
    encoder_w_any,
    latent_any,
    neighbours_any,
    positions_any,
    velocity_any,
    edge_any,
    weights_ref,
    decoder_out_ref,
    inward_ref,
    encoder_w_ref,
    placer_ref,
    masks_ref,
    alive_ref,
    latent_ref,
    neighbours_ref,
    positions_ref,
    velocity_ref,
    edge_ref,
    first_end_ref,
    second_end_ref,
    spread_ref,
    owners_ref,
    edge_w_ref,
    node_in_ref,
    node_w_ref,
    decoder_w_ref,
    encoder_in_ref,
    sems,
):
    count_x, count_y, count_z = sizes
    fold_y = count_y == 2
    copies = fetch(
        [
            (owners_any, owners_ref),
            (edge_w_any, edge_w_ref),
            (node_in_any, node_in_ref),
            (node_w_any, node_w_ref),
            (decoder_w_any, decoder_w_ref),
            (decoder_out_any, decoder_out_ref),
            (encoder_in_any, encoder_in_ref),
            (encoder_w_any, encoder_w_ref),
            (latent_any, latent_ref),
            (neighbours_any, neighbours_ref),
            (positions_any, positions_ref),
            (velocity_any, velocity_ref),
            (edge_any, edge_ref),
        ],
        sems,
    )
    copies[0].wait()
    index_x = lax.axis_index("gx")
    index_y = lax.axis_index("gy")
    index_z = lax.axis_index("gz")
    slots = owners_ref.shape[-1]
    width = node_in_ref.shape[-1]
    for a, b in CELLS:
        alive_ref[a, b] = jnp.where(
            lax.broadcasted_iota(I32, (1, slots), 1) < fill_ref[a, 0, b], 1.0, 0.0
        )

    lane = lax.broadcasted_iota(I32, (1, slots), 1)
    owner = jnp.concatenate([owners_ref[a, b] for a, b in CELLS], axis=1)
    alive = jnp.concatenate([jnp.where(lane < fill_ref[a, 0, b], 1, 0) for a, b in CELLS], axis=1)
    own_block = (index_x * count_y + index_y) * count_z + index_z
    stays = jnp.where((alive == 1) & (owner == own_block), 1.0, 0.0)
    moving = jnp.where((alive == 1) & (owner != own_block), 1, 0)
    owner_x = quotient(owner, count_y * count_z)
    rest = owner - owner_x * (count_y * count_z)
    owner_y = quotient(rest, count_z)
    owner_z = rest - owner_y * count_z
    step_y = owner_y - index_y
    side_y = jnp.where(step_y == 0, 0, 1) if fold_y else jnp.where(step_y < 0, 1, 2 * step_y)
    options_y = 2 if fold_y else 3
    group = ((owner_x - index_x + 1) * options_y + side_y) * 2 + jnp.where(owner_z == index_z, 0, 1)
    group_rows = (3 * options_y * 2 + 15) // 16 * 16
    particles = owner.shape[1]
    member = jnp.where(
        (lax.broadcasted_iota(I32, (group_rows, particles), 0) == group) & (moving == 1), 1.0, 0.0
    )
    triangle = jnp.where(
        lax.broadcasted_iota(I32, (slots, slots), 0) <= lax.broadcasted_iota(I32, (slots, slots), 1),
        1.0,
        0.0,
    ).astype(BF16)
    counted = []
    before = jnp.zeros((group_rows, 1), F32)
    for i in range(4):
        inside = member[:, i * slots : (i + 1) * slots]
        counted.append(dot(inside.astype(BF16), triangle) + before)
        before = before + jnp.sum(inside, axis=1, keepdims=True)
    counted = jnp.concatenate(counted, axis=1)
    rank = (jnp.sum(counted * member, axis=0, keepdims=True) - 1.0).astype(I32)
    column = jnp.where(moving == 1, group * CAP + rank, -1)
    movers = placer_ref.shape[0]
    placer_ref[...] = jnp.where(
        lax.broadcasted_iota(I32, (movers, particles), 0) == column, 1.0, 0.0
    ).astype(BF16)
    masks_ref[...] = jnp.concatenate(
        [stays, moving.astype(F32), jnp.zeros((6, particles), F32)], axis=0
    )

    spread_shape = spread_ref.shape
    line = lax.broadcasted_iota(I32, spread_shape, 0)
    from_group = line >> 3
    plane = from_group >> 1
    from_x = 1 - ((plane >> 1) if fold_y else ((plane * 43) >> 7))
    side_y = plane - (1 - from_x) * options_y
    if fold_y:
        from_y = jnp.where(side_y == 0, 0, jnp.where(index_y == 0, 1, -1))
    else:
        from_y = jnp.where(side_y == 0, 0, jnp.where(side_y == 1, 1, -1))
    from_z = jnp.where((from_group & 1) == 0, 0, jnp.where(index_z == 0, 1, -1))
    direction = (from_x + 1) * 9 + (from_y + 1) * 3 + from_z + 1
    direction = direction - jnp.where(direction > 13, 1, 0)
    column = direction * CAP + (line & 7)
    valid = (lax.broadcasted_iota(I32, spread_shape, 1) == column) & (
        (from_x != 0) | (from_y != 0) | (from_z != 0)
    )
    spread_ref[...] = jnp.where(valid, 1.0, 0.0).astype(BF16)

    for copy in copies[1:]:
        copy.wait()
    for i in range(5):
        weights_ref[i] = flip(edge_w_ref[i])
    weights_ref[NODE_OLD] = flip(node_in_ref[:width])
    weights_ref[NODE_NEW] = flip(node_in_ref[width:])
    for i in range(2):
        weights_ref[NODE_0 + i] = flip(node_w_ref[i])
        weights_ref[DECODE_0 + i] = flip(decoder_w_ref[i])
    inward = jnp.concatenate([encoder_in_ref[...].astype(F32), jnp.zeros((4, width), F32)], axis=0)
    inward = inward.astype(BF16)
    inward_ref[...] = jnp.concatenate([inward, inward, inward], axis=0)
    parity = index_x & 1
    for b in range(2):
        first_end_ref[b] = latent_ref[1 - parity, b, 0]
        second_end_ref[b] = latent_ref[parity, b, 0]


def prepare_kernel(
    sizes,
    latent_ref,
    own_zed,
    edge_ref,
    positions_ref,
    velocity_ref,
    neighbours_ref,
    weights_ref,
    placer_ref,
    masks_ref,
    far_ref,
    latent_t_ref,
    node_pre_ref,
    state_ref,
    mover_pre_ref,
    mover_place_ref,
    mover_key_ref,
    mover_node_pre_ref,
    mover_latent_ref,
    mover_state_ref,
):
    fold_y = sizes[1] == 2
    neighbour_count = edge_ref.shape[3]
    placer = placer_ref[...]
    movers, particles = placer.shape
    stays, moving = masks_ref[0:1], masks_ref[1:2]

    latent = jnp.concatenate([latent_ref[a, b, 0] for a, b in CELLS], axis=0)
    latent_t_ref[...] = latent.astype(F32).T
    node_pre_ref[...] = dot_nt(weights_ref[NODE_OLD], latent)

    def flat(ref, i):
        return jnp.concatenate([ref[i, a, b] for a, b in CELLS], axis=1)

    state = [flat(positions_ref, i) for i in range(3)] + [flat(velocity_ref, i) for i in range(3)]
    state_ref[...] = jnp.concatenate(state + [stays, jnp.zeros_like(stays)], axis=0)

    mover_latent = dot(placer, latent).astype(BF16)
    mover_latent_ref[...] = mover_latent.astype(F32).T
    mover_node_pre_ref[...] = dot_nt(weights_ref[NODE_OLD], mover_latent)
    near = dot_nt(weights_ref[NEAR], mover_latent)
    state = jnp.concatenate(state + [moving, jnp.zeros_like(stays)], axis=0)
    mover_state_ref[...] = joined(dot_nt(thirds(state), placer))
    ids = jnp.concatenate(
        [
            jnp.concatenate([neighbours_ref[a, b, k] for a, b in CELLS], axis=1)
            for k in range(neighbour_count)
        ],
        axis=0,
    )
    ids = jnp.concatenate([ids & 127, ids >> 7, jnp.zeros((8, particles), I32)], axis=0)
    ids = dot_nt(ids.astype(F32).astype(BF16), placer).astype(I32)
    place, key = places(ids[:neighbour_count], ids[neighbour_count : 2 * neighbour_count], fold_y)
    place = jnp.concatenate([place[k : k + 1] for k in range(neighbour_count)], axis=1)
    key = jnp.concatenate([key[k : k + 1] for k in range(neighbour_count)], axis=1)
    mover_place_ref[...] = place
    mover_key_ref[...] = key
    window = Window(fold_y, far_ref)
    columns = [(ex, row) for ex in (1, 2) for row in window.own_rows]
    for (ex, row), (a, b) in zip(columns, CELLS):
        pair = jnp.concatenate([latent_ref[a, b, 0], own_zed[a, b, 0]], axis=0)
        far_ref[window.own(ex, row)] = dot_nt(weights_ref[FAR], pair).astype(BF16)
    cells = window.cells(columns)
    step = TILE // movers
    near = jnp.concatenate([near] * step, axis=1)
    for tile in range(neighbour_count // step):
        edges = []
        for k in range(tile * step, (tile + 1) * step):
            rows = jnp.concatenate([edge_ref[a, b, 0, k] for a, b in CELLS], axis=0)
            edges.append(dot(placer, rows).astype(BF16))
        at = slice(tile * TILE, (tile + 1) * TILE)
        mover_pre_ref[:, at] = (
            dot_nt(weights_ref[EDGE], jnp.concatenate(edges, axis=0))
            + near
            + pick(cells, place[:, at], key[:, at])
        )


def movers_kernel(
    sizes,
    side_count,
    *refs,
):
    fold_y = sizes[1] == 2
    side_refs, refs = refs[:side_count], refs[side_count:]
    odd_ref, even_ref, refs = refs[0], refs[1], refs[2:]
    side_zeds, refs = refs[:side_count], refs[side_count:]
    odd_zed, even_zed, refs = refs[0], refs[1], refs[2:]
    (
        weights_ref,
        decoder_out_ref,
        pre_ref,
        place_ref,
        key_ref,
        node_pre_ref,
        latent_t_ref,
        state_ref,
        far_ref,
        bucket_ref,
        hidden_ref,
    ) = refs
    window = Window(fold_y, None, far_ref)
    row_count = window.row_count
    parity = lax.axis_index("gx") & 1
    far_t = weights_ref[FAR]

    def far(at, here, beside):
        pair = jnp.concatenate([here, beside], axis=0)
        far_ref[at] = dot_nt(far_t, pair).astype(BF16)

    for row in range(row_count):
        far((1 - parity) * row_count + row, even_ref[row], even_zed[row])
        far(parity * row_count + row, odd_ref[row], odd_zed[row])
    for side, row in enumerate(window.outer_rows):
        for ex in (1, 2):
            far(window.side(ex, row), side_refs[side][ex - 1], side_zeds[side][ex - 1])

    movers = state_ref.shape[1]
    columns = [(ex, row) for ex in (0, 3) for row in range(row_count)]
    columns += [(ex, row) for ex in (1, 2) for row in window.outer_rows]
    message = messages(
        window.cells(columns),
        place_ref[...],
        key_ref[...],
        lambda tile: pre_ref[:, tile * TILE : (tile + 1) * TILE],
        weights_ref[MIDDLE],
        weights_ref[FINAL],
        hidden_ref,
    )
    aggregate = slot_sum(message, movers).astype(BF16)
    acceleration = advance(
        node_pre_ref[...], aggregate, latent_t_ref[...], weights_ref, decoder_out_ref[...]
    )
    mask = state_ref[6:7]
    state = moved(state_ref[0:3], state_ref[3:6], acceleration) * mask
    bucket_ref[...] = jnp.concatenate([state, mask, jnp.zeros((ROWS - 10, movers), F32)], axis=0)


def edges_kernel(
    sizes,
    a,
    alive_ref,
    latent_ref,
    edge_ref,
    neighbours_ref,
    far_own_ref,
    far_rest_ref,
    weights_ref,
    total_ref,
    hidden_ref,
):
    fold_y = sizes[1] == 2
    window = Window(fold_y, far_own_ref, far_rest_ref)
    index_y = lax.axis_index("gy")
    alive_ref, latent_ref = alive_ref.at[a], latent_ref.at[a]
    edge_ref, neighbours_ref = edge_ref.at[a], neighbours_ref.at[a]
    slots, width = latent_ref.shape[-2:]
    neighbour_count = edge_ref.shape[2]
    for bt in range(2):
        if fold_y:
            b = index_y if bt == 0 else 1 - index_y
            rows = (0, 1) if bt == 0 else (0, 1, 2)
        else:
            b = bt
            rows = (bt, bt + 1, bt + 2)
        columns = [(ex, row) for ex in range(a, a + 3) for row in rows]
        near = dot_nt(weights_ref[NEAR], latent_ref[b, 0])
        near = jnp.concatenate([near, near], axis=1)
        ids = jnp.concatenate([neighbours_ref[b, k] for k in range(neighbour_count)], axis=1)
        place, key = places(ids & 127, ids >> 7, fold_y)

        def pre(tile, b=b, near=near):
            edges = jnp.concatenate([edge_ref[b, 0, 2 * tile], edge_ref[b, 0, 2 * tile + 1]], axis=0)
            return dot_nt(weights_ref[EDGE], edges) + near

        message = messages(
            window.cells(columns),
            place,
            key,
            pre,
            weights_ref[MIDDLE],
            weights_ref[FINAL],
            hidden_ref.at[bt],
        )
        total = jnp.where(alive_ref[b] > 0.5, slot_sum(message, slots), 0.0)
        total_ref[b] = total.astype(BF16)


def nodes_kernel(
    first_ref,
    second_ref,
    node_pre_ref,
    latent_t_ref,
    state_ref,
    weights_ref,
    decoder_out_ref,
    moved_ref,
):
    aggregate = jnp.concatenate([first_ref[0], first_ref[1], second_ref[0], second_ref[1]], axis=1)
    acceleration = advance(
        node_pre_ref[...], aggregate, latent_t_ref[...], weights_ref, decoder_out_ref[...]
    )
    state = moved(state_ref[0:3], state_ref[3:6], acceleration)
    moved_ref[...] = jnp.concatenate(
        [state, state_ref[6:7], jnp.zeros((ROWS - 10, state.shape[1]), F32)], axis=0
    )


def finish_kernel(
    sizes,
    moved_ref,
    own_ref,
    even_ref,
    odd_ref,
    own_zed,
    even_zed,
    odd_zed,
    spread_ref,
    inward_ref,
    encoder_w_ref,
    kept_latent_ref,
    kept_state_ref,
    arrived_latent_ref,
    arrived_state_ref,
):
    count_x, count_y, count_z = sizes
    extent = (2.0 * count_x, 2.0 * count_y, 1.0 * count_z)
    slots = kept_latent_ref.shape[-2]
    stays = moved_ref[9:10]
    kept = moved_ref[:9] * stays
    latents = encode(moved_ref[:9], stays, inward_ref[...], encoder_w_ref[...], extent)
    for i, (a, b) in enumerate(CELLS):
        kept_latent_ref[a, b, 0] = latents[i * slots : (i + 1) * slots]
        for j in range(9):
            kept_state_ref[j, a, b] = kept[j : j + 1, i * slots : (i + 1) * slots]
    fold_y = count_y == 2
    index_x = lax.axis_index("gx")
    options_y = 2 if fold_y else 3
    lanes = own_ref.shape[-1]
    group = lax.broadcasted_iota(I32, (ROWS, lanes), 1) >> 3
    even = (index_x & 1) == 0
    found = jnp.zeros((ROWS, lanes), F32)
    for source_x in (-1, 0, 1):
        for from_y in range(options_y):
            for from_z in range(2):
                if source_x == 0 and from_y == 0 and from_z == 0:
                    continue
                if from_z == 0:
                    own, first, second = own_ref, even_ref, odd_ref
                else:
                    own, first, second = own_zed, even_zed, odd_zed
                side_y = from_y if fold_y or from_y == 0 else 3 - from_y
                target = ((1 - source_x) * options_y + side_y) * 2 + from_z
                if source_x == 0:
                    tile = own[from_y]
                    there = group == target
                elif source_x == -1:
                    tile = jnp.where(even, second[from_y], first[from_y])
                    there = (group == target) & (index_x > 0)
                else:
                    tile = jnp.where(even, first[from_y], second[from_y])
                    there = (group == target) & (index_x < count_x - 1)
                found = jnp.where(there, tile, found)
    arrived = joined(dot(thirds(found), spread_ref[...]))
    for j in range(9):
        arrived_state_ref[j, 0, 0] = arrived[j : j + 1]
    arrived_latent_ref[0, 0, 0] = encode(
        arrived[:9], arrived[9:10], inward_ref[...], encoder_w_ref[...], extent
    )


def swap(values, axis):
    return lax.ppermute(values, axis, [(0, 1), (1, 0)])


def shift(values, axis, way):
    pairs = [(i, i + 1) for i in range(lax.axis_size(axis) - 1)]
    return lax.ppermute(values, axis, [(j, i) for i, j in pairs] if way else pairs)


def swap_x(values, first):
    count = lax.axis_size("gx")
    pairs = []
    for x in range(count):
        partner = x + 1 if (x - first) % 2 == 0 else x - 1
        for z in range(2):
            if 0 <= partner < count:
                pairs.append((x * 2 + z, partner * 2 + z))
            else:
                pairs.append((x * 2 + z, x * 2 + 1 - z))
    return lax.ppermute(values, ("gx", "gz"), pairs)


def call(kernel, name, in_specs, outs, scratch, operands, flops):
    return pl.pallas_call(
        kernel,
        out_shape=tuple(jax.ShapeDtypeStruct(shape, kind) for shape, kind in outs),
        in_specs=in_specs,
        out_specs=tuple(VMEM for _ in outs),
        scratch_shapes=scratch,
        compiler_params=pltpu.CompilerParams(vmem_limit_bytes=32 * 1024 * 1024),
        cost_estimate=pl.CostEstimate(flops=flops, bytes_accessed=0, transcendentals=0),
        name=name,
    )(*operands)


def in_hbm(array):
    return pltpu.with_memory_space_constraint(array, pltpu.HBM)


def like(array):
    return pltpu.VMEM(array.shape, array.dtype)


def body(
    node_latent,
    edge_latent,
    positions,
    velocity,
    fill,
    neighbours,
    owners,
    edge_weights,
    node_in,
    node_weights,
    decoder_weights,
    decoder_out,
    encoder_in,
    encoder_weights,
):
    sizes = tuple(lax.axis_size(axis) for axis in ("gx", "gy", "gz"))
    fold_y = sizes[1] == 2
    slots, width = node_latent.shape[-2:]
    neighbour_count = neighbours.shape[3]
    particles = 4 * slots
    options_y = 2 if fold_y else 3
    movers = (3 * options_y * 2 * CAP + 127) // 128 * 128
    rows = 3 if fold_y else 4
    fill = jnp.transpose(fill, (0, 2, 1))
    neighbours = neighbours.reshape(2, 2, neighbour_count, 1, slots)

    parity = lax.axis_index("gx") & 1
    cells = node_latent[:, :, 0]
    if fold_y:
        inner = 1 - lax.axis_index("gy")
        sides = [swap(lax.dynamic_index_in_dim(cells, inner, 1, keepdims=False), "gy")]
    else:
        sides = [shift(cells[:, 1], "gy", 0), shift(cells[:, 0], "gy", 1)]

    fetched = (node_latent, neighbours, positions, velocity, edge_latent)
    ranked = call(
        functools.partial(ranks_kernel, sizes),
        "ranks",
        [SMEM] + [ANY] * 13,
        [
            ((11, width, width), BF16),
            (decoder_out.shape, BF16),
            ((48, width), BF16),
            (encoder_weights.shape, BF16),
            ((movers, particles), BF16),
            ((8, particles), F32),
            ((2, 2, 1, slots), F32),
            *((array.shape, array.dtype) for array in fetched),
            ((2, slots, width), BF16),
            ((2, slots, width), BF16),
            ((movers, 26 * CAP), BF16),
        ],
        [
            like(owners),
            like(edge_weights),
            like(node_in),
            like(node_weights),
            like(decoder_weights),
            like(encoder_in),
            pltpu.SemaphoreType.DMA((13,)),
        ],
        [
            in_hbm(array)
            for array in (
                fill,
                owners,
                edge_weights,
                node_in,
                node_weights,
                decoder_weights,
                decoder_out,
                encoder_in,
                encoder_weights,
                *fetched,
            )
        ],
        500_000_000,
    )
    own_zed = swap(node_latent, "gz")
    sides, own_zed, ranked = lax.optimization_barrier((sides, own_zed, ranked))
    weights, decoder_out, inward, encoder_weights, placer, masks, alive, *ranked = ranked
    latent, neighbours, positions, velocity, edge_latent, *own_ends, spread = ranked

    def layer(a, own):
        outer = [lax.dynamic_index_in_dim(side, a, 0) for side in sides]
        parts = [own, outer[0]] if fold_y else [outer[0], own, outer[1]]
        return jnp.concatenate(parts, axis=0)

    ends = [swap_x(layer(parity, own_ends[1]), 1), swap_x(layer(1 - parity, own_ends[0]), 0)]
    zeds = [swap(part, "gz") for part in sides]
    prepared = call(
        functools.partial(prepare_kernel, sizes),
        "prepare",
        [VMEM] * 9,
        [
            ((4, width, 2 * slots), BF16),
            ((width, particles), F32),
            ((width, particles), F32),
            ((8, particles), F32),
            ((width, neighbour_count * movers), F32),
            ((1, neighbour_count * movers), I32),
            ((1, neighbour_count * movers), I32),
            ((width, movers), F32),
            ((width, movers), F32),
            ((8, movers), F32),
        ],
        [],
        (latent, own_zed, edge_latent, positions, velocity, neighbours, weights, placer, masks),
        500_000_000,
    )
    ends, zeds, prepared = lax.optimization_barrier((ends, zeds, prepared))
    (
        far_own,
        latent_t,
        node_pre,
        state,
        mover_pre,
        mover_place,
        mover_key,
        mover_node_pre,
        mover_latent,
        mover_state,
    ) = prepared
    halo = [*sides, *ends, *zeds, *(swap(part, "gz") for part in ends)]

    far_rest, bucket = call(
        functools.partial(movers_kernel, sizes, len(sides)),
        "movers",
        [VMEM] * (len(halo) + 8),
        [((4 * rows - 4, width, 2 * slots), BF16), ((ROWS, movers), F32)],
        [pltpu.VMEM((width, neighbour_count * movers), BF16)],
        (
            *halo,
            weights,
            decoder_out,
            mover_pre,
            mover_place,
            mover_key,
            mover_node_pre,
            mover_latent,
            mover_state,
        ),
        3_000_000_000,
    )

    def edges(a):
        return call(
            functools.partial(edges_kernel, sizes, a),
            "edges",
            [VMEM] * 7,
            [((2, width, slots), BF16)],
            [pltpu.VMEM((2, width, neighbour_count * slots), BF16)],
            (alive, latent, edge_latent, neighbours, far_own, far_rest, weights),
            4_000_000_000,
        )[0]

    first = edges(0)
    if fold_y:
        tiles = [swap(bucket, "gy")]
    else:
        tiles = [shift(bucket, "gy", 0), shift(bucket, "gy", 1)]
    tiles, first = lax.optimization_barrier((tiles, first))
    tiles = jnp.stack([bucket, *tiles], axis=0)
    second = edges(1)
    odd = swap_x(tiles, 1)
    sided = [swap_x(tiles, 0), odd]
    sided, second = lax.optimization_barrier((sided, second))
    tiles = [tiles, *sided]
    zeds = [swap(part, "gz") for part in tiles]
    state = call(
        nodes_kernel,
        "nodes",
        [VMEM] * 7,
        [((ROWS, particles), F32)],
        [],
        (first, second, node_pre, latent_t, state, weights, decoder_out),
        1_000_000_000,
    )[0]
    zeds, state = lax.optimization_barrier((zeds, state))
    return call(
        functools.partial(finish_kernel, sizes),
        "finish",
        [VMEM] * 10,
        [
            (node_latent.shape, BF16),
            ((9,) + node_latent.shape[:4], F32),
            ((1, 1, 1, 26 * CAP, width), BF16),
            ((9, 1, 1, 1, 26 * CAP), F32),
        ],
        [],
        (state, *tiles, *zeds, spread, inward, encoder_weights),
        1_000_000_000,
    )


def solution(mesh):
    placed = (
        P(("group", "gx"), "gy", "gz", None, None),
        P(("group", "gx"), "gy", "gz", None, None, None),
        P(None, ("group", "gx"), "gy", "gz", None),
        P(None, ("group", "gx"), "gy", "gz", None),
        P(("group", "gx"), "gy", "gz"),
        P(("group", "gx"), "gy", "gz", None, None),
        P(("group", "gx"), "gy", "gz", None),
        P(),
        P(),
        P(),
        P(),
        P(),
        P(),
        P(),
    )
    return jax.shard_map(
        body,
        mesh=mesh,
        in_specs=placed,
        out_specs=(
            P(("group", "gx"), "gy", "gz", None, None),
            P(None, ("group", "gx"), "gy", "gz", None),
            P(("group", "gx"), "gy", "gz", None, None),
            P(None, ("group", "gx"), "gy", "gz", None),
        ),
        check_vma=False,
    )
```

```python
import functools

import jax
import jax.numpy as jnp
from jax import lax
from jax.experimental import pallas as pl
from jax.experimental.pallas import tpu as pltpu
from jax.sharding import PartitionSpec as P

CAP = 8
F32 = jnp.float32
BF16 = jnp.bfloat16
I32 = jnp.int32
ROWS = 16
TILE = 256
CELLS = [(a, b) for a in range(2) for b in range(2)]
EDGE, NEAR, FAR, MIDDLE, FINAL, NODE_OLD, NODE_NEW, NODE_0, NODE_1, DECODE_0, DECODE_1 = range(11)

VMEM = pl.BlockSpec(memory_space=pltpu.VMEM)
SMEM = pl.BlockSpec(memory_space=pltpu.SMEM)
ANY = pl.BlockSpec(memory_space=pl.ANY)


def dot(left, right):
    return jnp.dot(left, right, preferred_element_type=F32)


def dot_nt(left, right):
    return lax.dot_general(left, right, (((1,), (1,)), ((), ())), preferred_element_type=F32)


def dot_tn(left, right):
    return lax.dot_general(left, right, (((0,), (0,)), ((), ())), preferred_element_type=F32)


def relu16(values):
    return jnp.maximum(values, 0.0).astype(BF16)


def norm(values, axis):
    scale = 1.0 / values.shape[axis]
    centred = values - jnp.sum(values, axis=axis, keepdims=True) * scale
    spread = jnp.sum(centred * centred, axis=axis, keepdims=True) * scale
    return centred * lax.rsqrt(spread + 1e-05)


def thirds(values):
    high = values.astype(BF16)
    rest = values - high.astype(F32)
    middle = rest.astype(BF16)
    low = (rest - middle.astype(F32)).astype(BF16)
    return jnp.concatenate([high, middle, low], axis=0)


def joined(values):
    rows = values.shape[0] // 3
    return values[:rows] + values[rows : 2 * rows] + values[2 * rows :]


def quotient(values, count):
    if count & (count - 1) == 0:
        return values >> (count.bit_length() - 1)
    return lax.div(values, jnp.full_like(values, count))


def flip(weights):
    return weights.astype(F32).T.astype(BF16)


def fetch(pairs, sems):
    copies = [pltpu.make_async_copy(src, dst, sems.at[i]) for i, (src, dst) in enumerate(pairs)]
    for copy in copies:
        copy.start()
    return copies


def encode(state, mask, inward, encoder_w, extent):
    width = state.shape[1]
    position = state[0:3]
    row = lax.broadcasted_iota(I32, (3, width), 0)
    size = jnp.where(row == 0, extent[0], jnp.where(row == 1, extent[1], extent[2]))
    features = jnp.concatenate(
        [
            state[3:9],
            jnp.clip(position, -1.0, 1.0),
            jnp.clip(size - position, -1.0, 1.0),
            jnp.zeros((4, width), F32),
        ],
        axis=0,
    )
    hidden = relu16(dot_tn(thirds(features), inward))
    hidden = relu16(dot(hidden, encoder_w[0]))
    column = jnp.broadcast_to(mask, (8, width)).T[:, 0:1]
    return (norm(dot(hidden, encoder_w[1]), 1) * column).astype(BF16)


def places(ids_low, ids_high, fold_y):
    plane = (ids_high * 43) >> 7
    ez = ids_high - plane * 3
    ey = plane & 3
    ex = plane >> 2
    if fold_y:
        row = jnp.where(ey == 1, 0, jnp.where(ey == 2, 1, 2))
    else:
        row = ey
    return ex * 4 + row, ids_low + jnp.where(ez == 1, 0, 128)


def pick(cells, place, key):
    width = cells[0][1].shape[0]
    chunk = 32
    window = jnp.concatenate(
        [ref[f : f + chunk] for f in range(0, width, chunk) for _, ref in cells], axis=0
    )
    key_rows = lax.broadcasted_iota(I32, (TILE, TILE), 0)
    picker = jnp.where(key_rows == key, 1.0, 0.0).astype(BF16)
    found = dot(window, picker).reshape(width // chunk, len(cells), chunk // 8, 8, TILE)
    where = jnp.broadcast_to(place, (8, TILE))
    parts = []
    for f in range(width // chunk):
        part = jnp.zeros((chunk // 8, 8, TILE), F32)
        for i, (column, _) in enumerate(cells):
            part = jnp.where((where == column)[None], found[f, i], part)
        parts.append(part.reshape(chunk, TILE))
    return jnp.concatenate(parts, axis=0)


def messages(cells, place, key, pre, middle_t, final_t, hidden_ref):
    for tile in range(place.shape[1] // TILE):
        at = slice(tile * TILE, (tile + 1) * TILE)
        hidden_ref[:, at] = relu16(pre(tile) + pick(cells, place[:, at], key[:, at]))
    hidden = relu16(dot(middle_t, hidden_ref[...]))
    return norm(dot(final_t, hidden), 0)


class Window:
    def __init__(self, fold_y, own_ref=None, rest_ref=None):
        self.row_count = 3 if fold_y else 4
        self.own_rows = (0, 1) if fold_y else (1, 2)
        self.outer_rows = (2,) if fold_y else (0, 3)
        self.own_ref, self.rest_ref = own_ref, rest_ref

    def own(self, ex, row):
        return (ex - 1) * 2 + self.own_rows.index(row)

    def side(self, ex, row):
        count = len(self.outer_rows)
        return 2 * self.row_count + (ex - 1) * count + self.outer_rows.index(row)

    def cells(self, columns):
        found = []
        for ex, row in columns:
            if ex in (1, 2) and row in self.own_rows:
                ref = self.own_ref.at[self.own(ex, row)]
            elif ex in (1, 2):
                ref = self.rest_ref.at[self.side(ex, row)]
            else:
                ref = self.rest_ref.at[(0 if ex == 0 else self.row_count) + row]
            found.append((ex * 4 + row, ref))
        return found


def slot_sum(message, step):
    total = message[:, :step]
    for at in range(step, message.shape[1], step):
        total = total + message[:, at : at + step]
    return total


def advance(pre, aggregate, latent_t, weights_ref, decoder_out):
    pre = pre + dot(weights_ref[NODE_NEW], aggregate)
    hidden = relu16(dot(weights_ref[NODE_0], relu16(pre)))
    updated = (latent_t + norm(dot(weights_ref[NODE_1], hidden), 0)).astype(BF16)
    hidden = relu16(dot(weights_ref[DECODE_0], updated))
    hidden = relu16(dot(weights_ref[DECODE_1], hidden))
    return dot(decoder_out, hidden)


def moved(position, velocity, acceleration):
    new_velocity = velocity + acceleration
    return jnp.concatenate([position + new_velocity, new_velocity, velocity], axis=0)


def cut_kernel(fold_y, latent_any, latent_ref, edge_ref, inner_ref, sems):
    end = 1 - lax.axis_index("gz")
    inner = 1 - lax.axis_index("gy") if fold_y else 0
    copies = fetch(
        [
            (latent_any, latent_ref),
            (latent_any.at[end], edge_ref),
            (latent_any.at[0, inner], inner_ref.at[0]),
            (latent_any.at[1, inner], inner_ref.at[1]),
        ],
        sems,
    )
    for copy in copies:
        copy.wait()


def ranks_kernel(
    sizes,
    fill_ref,
    owners_any,
    edge_w_any,
    node_in_any,
    node_w_any,
    decoder_w_any,
    decoder_out_any,
    encoder_in_any,
    encoder_w_any,
    neighbours_any,
    positions_any,
    velocity_any,
    edge_any,
    _,
    weights_ref,
    decoder_out_ref,
    inward_ref,
    encoder_w_ref,
    placer_ref,
    masks_ref,
    alive_ref,
    neighbours_ref,
    positions_ref,
    velocity_ref,
    edge_ref,
    spread_ref,
    owners_ref,
    edge_w_ref,
    node_in_ref,
    node_w_ref,
    decoder_w_ref,
    encoder_in_ref,
    sems,
):
    count_x, count_y, count_z = sizes
    fold_y = count_y == 2
    copies = fetch(
        [
            (owners_any, owners_ref),
            (edge_w_any, edge_w_ref),
            (node_in_any, node_in_ref),
            (node_w_any, node_w_ref),
            (decoder_w_any, decoder_w_ref),
            (decoder_out_any, decoder_out_ref),
            (encoder_in_any, encoder_in_ref),
            (encoder_w_any, encoder_w_ref),
            (neighbours_any, neighbours_ref),
            (positions_any, positions_ref),
            (velocity_any, velocity_ref),
            (edge_any, edge_ref),
        ],
        sems,
    )
    copies[0].wait()
    index_x = lax.axis_index("gx")
    index_y = lax.axis_index("gy")
    index_z = lax.axis_index("gz")
    slots = owners_ref.shape[-1]
    width = node_in_ref.shape[-1]
    for a, b in CELLS:
        alive_ref[a, b] = jnp.where(
            lax.broadcasted_iota(I32, (1, slots), 1) < fill_ref[a, 0, b], 1.0, 0.0
        )

    lane = lax.broadcasted_iota(I32, (1, slots), 1)
    owner = jnp.concatenate([owners_ref[a, b] for a, b in CELLS], axis=1)
    alive = jnp.concatenate([jnp.where(lane < fill_ref[a, 0, b], 1, 0) for a, b in CELLS], axis=1)
    own_block = (index_x * count_y + index_y) * count_z + index_z
    stays = jnp.where((alive == 1) & (owner == own_block), 1.0, 0.0)
    moving = jnp.where((alive == 1) & (owner != own_block), 1, 0)
    owner_x = quotient(owner, count_y * count_z)
    rest = owner - owner_x * (count_y * count_z)
    owner_y = quotient(rest, count_z)
    owner_z = rest - owner_y * count_z
    step_y = owner_y - index_y
    side_y = jnp.where(step_y == 0, 0, 1) if fold_y else jnp.where(step_y < 0, 1, 2 * step_y)
    options_y = 2 if fold_y else 3
    group = ((owner_x - index_x + 1) * options_y + side_y) * 2 + jnp.where(owner_z == index_z, 0, 1)
    group_rows = (3 * options_y * 2 + 15) // 16 * 16
    particles = owner.shape[1]
    member = jnp.where(
        (lax.broadcasted_iota(I32, (group_rows, particles), 0) == group) & (moving == 1), 1.0, 0.0
    )
    triangle = jnp.where(
        lax.broadcasted_iota(I32, (slots, slots), 0) <= lax.broadcasted_iota(I32, (slots, slots), 1),
        1.0,
        0.0,
    ).astype(BF16)
    counted = []
    before = jnp.zeros((group_rows, 1), F32)
    for i in range(4):
        inside = member[:, i * slots : (i + 1) * slots]
        counted.append(dot(inside.astype(BF16), triangle) + before)
        before = before + jnp.sum(inside, axis=1, keepdims=True)
    counted = jnp.concatenate(counted, axis=1)
    rank = (jnp.sum(counted * member, axis=0, keepdims=True) - 1.0).astype(I32)
    column = jnp.where(moving == 1, group * CAP + rank, -1)
    movers = placer_ref.shape[0]
    placer_ref[...] = jnp.where(
        lax.broadcasted_iota(I32, (movers, particles), 0) == column, 1.0, 0.0
    ).astype(BF16)
    masks_ref[...] = jnp.concatenate(
        [stays, moving.astype(F32), jnp.zeros((6, particles), F32)], axis=0
    )

    spread_shape = spread_ref.shape
    line = lax.broadcasted_iota(I32, spread_shape, 0)
    from_group = line >> 3
    plane = from_group >> 1
    from_x = 1 - ((plane >> 1) if fold_y else ((plane * 43) >> 7))
    side_y = plane - (1 - from_x) * options_y
    if fold_y:
        from_y = jnp.where(side_y == 0, 0, jnp.where(index_y == 0, 1, -1))
    else:
        from_y = jnp.where(side_y == 0, 0, jnp.where(side_y == 1, 1, -1))
    from_z = jnp.where((from_group & 1) == 0, 0, jnp.where(index_z == 0, 1, -1))
    direction = (from_x + 1) * 9 + (from_y + 1) * 3 + from_z + 1
    direction = direction - jnp.where(direction > 13, 1, 0)
    column = direction * CAP + (line & 7)
    valid = (lax.broadcasted_iota(I32, spread_shape, 1) == column) & (
        (from_x != 0) | (from_y != 0) | (from_z != 0)
    )
    spread_ref[...] = jnp.where(valid, 1.0, 0.0).astype(BF16)

    for copy in copies[1:]:
        copy.wait()
    for i in range(5):
        weights_ref[i] = flip(edge_w_ref[i])
    weights_ref[NODE_OLD] = flip(node_in_ref[:width])
    weights_ref[NODE_NEW] = flip(node_in_ref[width:])
    for i in range(2):
        weights_ref[NODE_0 + i] = flip(node_w_ref[i])
        weights_ref[DECODE_0 + i] = flip(decoder_w_ref[i])
    inward = jnp.concatenate([encoder_in_ref[...].astype(F32), jnp.zeros((4, width), F32)], axis=0)
    inward = inward.astype(BF16)
    inward_ref[...] = jnp.concatenate([inward, inward, inward], axis=0)


def prepare_kernel(
    sizes,
    latent_ref,
    own_zed,
    edge_ref,
    positions_ref,
    velocity_ref,
    neighbours_ref,
    weights_ref,
    placer_ref,
    masks_ref,
    far_ref,
    latent_t_ref,
    node_pre_ref,
    state_ref,
    mover_pre_ref,
    mover_place_ref,
    mover_key_ref,
    mover_node_pre_ref,
    mover_latent_ref,
    mover_state_ref,
):
    fold_y = sizes[1] == 2
    neighbour_count = edge_ref.shape[3]
    placer = placer_ref[...]
    movers, particles = placer.shape
    stays, moving = masks_ref[0:1], masks_ref[1:2]

    latent = jnp.concatenate([latent_ref[a, b, 0] for a, b in CELLS], axis=0)
    latent_t_ref[...] = latent.astype(F32).T
    node_pre_ref[...] = dot_nt(weights_ref[NODE_OLD], latent)

    def flat(ref, i):
        return jnp.concatenate([ref[i, a, b] for a, b in CELLS], axis=1)

    state = [flat(positions_ref, i) for i in range(3)] + [flat(velocity_ref, i) for i in range(3)]
    state_ref[...] = jnp.concatenate(state + [stays, jnp.zeros_like(stays)], axis=0)

    mover_latent = dot(placer, latent).astype(BF16)
    mover_latent_ref[...] = mover_latent.astype(F32).T
    mover_node_pre_ref[...] = dot_nt(weights_ref[NODE_OLD], mover_latent)
    near = dot_nt(weights_ref[NEAR], mover_latent)
    state = jnp.concatenate(state + [moving, jnp.zeros_like(stays)], axis=0)
    mover_state_ref[...] = joined(dot_nt(thirds(state), placer))
    ids = jnp.concatenate(
        [
            jnp.concatenate([neighbours_ref[a, b, k] for a, b in CELLS], axis=1)
            for k in range(neighbour_count)
        ],
        axis=0,
    )
    ids = jnp.concatenate([ids & 127, ids >> 7, jnp.zeros((8, particles), I32)], axis=0)
    ids = dot_nt(ids.astype(F32).astype(BF16), placer).astype(I32)
    place, key = places(ids[:neighbour_count], ids[neighbour_count : 2 * neighbour_count], fold_y)
    place = jnp.concatenate([place[k : k + 1] for k in range(neighbour_count)], axis=1)
    key = jnp.concatenate([key[k : k + 1] for k in range(neighbour_count)], axis=1)
    mover_place_ref[...] = place
    mover_key_ref[...] = key
    window = Window(fold_y, far_ref)
    columns = [(ex, row) for ex in (1, 2) for row in window.own_rows]
    for (ex, row), (a, b) in zip(columns, CELLS):
        pair = jnp.concatenate([latent_ref[a, b, 0], own_zed[a, b, 0]], axis=0)
        far_ref[window.own(ex, row)] = dot_nt(weights_ref[FAR], pair).astype(BF16)
    cells = window.cells(columns)
    step = TILE // movers
    near = jnp.concatenate([near] * step, axis=1)
    for tile in range(neighbour_count // step):
        edges = []
        for k in range(tile * step, (tile + 1) * step):
            rows = jnp.concatenate([edge_ref[a, b, 0, k] for a, b in CELLS], axis=0)
            edges.append(dot(placer, rows).astype(BF16))
        at = slice(tile * TILE, (tile + 1) * TILE)
        mover_pre_ref[:, at] = (
            dot_nt(weights_ref[EDGE], jnp.concatenate(edges, axis=0))
            + near
            + pick(cells, place[:, at], key[:, at])
        )


def movers_kernel(
    sizes,
    side_count,
    *refs,
):
    fold_y = sizes[1] == 2
    side_refs, refs = refs[:side_count], refs[side_count:]
    side_zeds, refs = refs[:side_count], refs[side_count:]
    mine_ref, other_ref, refs = refs[0], refs[1], refs[2:]
    (
        weights_ref,
        decoder_out_ref,
        pre_ref,
        place_ref,
        key_ref,
        node_pre_ref,
        latent_t_ref,
        state_ref,
        far_ref,
        bucket_ref,
        hidden_ref,
    ) = refs
    window = Window(fold_y, None, far_ref)
    row_count = window.row_count
    core = lax.axis_index("gz")
    far_t = weights_ref[FAR]

    def far(at, here, beside):
        pair = jnp.concatenate([here, beside], axis=0)
        far_ref[at] = dot_nt(far_t, pair).astype(BF16)

    for row in range(row_count):
        far((1 - core) * row_count + row, mine_ref[1, row], mine_ref[0, row])
        far(core * row_count + row, other_ref[0, row], other_ref[1, row])
    for side, row in enumerate(window.outer_rows):
        for ex in (1, 2):
            far(window.side(ex, row), side_refs[side][ex - 1], side_zeds[side][ex - 1])

    movers = state_ref.shape[1]
    columns = [(ex, row) for ex in (0, 3) for row in range(row_count)]
    columns += [(ex, row) for ex in (1, 2) for row in window.outer_rows]
    message = messages(
        window.cells(columns),
        place_ref[...],
        key_ref[...],
        lambda tile: pre_ref[:, tile * TILE : (tile + 1) * TILE],
        weights_ref[MIDDLE],
        weights_ref[FINAL],
        hidden_ref,
    )
    aggregate = slot_sum(message, movers).astype(BF16)
    acceleration = advance(
        node_pre_ref[...], aggregate, latent_t_ref[...], weights_ref, decoder_out_ref[...]
    )
    mask = state_ref[6:7]
    state = moved(state_ref[0:3], state_ref[3:6], acceleration) * mask
    bucket_ref[...] = jnp.concatenate([state, mask, jnp.zeros((ROWS - 10, movers), F32)], axis=0)


def edges_kernel(
    sizes,
    a,
    alive_ref,
    latent_ref,
    edge_ref,
    neighbours_ref,
    far_own_ref,
    far_rest_ref,
    weights_ref,
    total_ref,
    hidden_ref,
):
    fold_y = sizes[1] == 2
    window = Window(fold_y, far_own_ref, far_rest_ref)
    index_y = lax.axis_index("gy")
    alive_ref, latent_ref = alive_ref.at[a], latent_ref.at[a]
    edge_ref, neighbours_ref = edge_ref.at[a], neighbours_ref.at[a]
    slots, width = latent_ref.shape[-2:]
    neighbour_count = edge_ref.shape[2]
    for bt in range(2):
        if fold_y:
            b = index_y if bt == 0 else 1 - index_y
            rows = (0, 1) if bt == 0 else (0, 1, 2)
        else:
            b = bt
            rows = (bt, bt + 1, bt + 2)
        columns = [(ex, row) for ex in range(a, a + 3) for row in rows]
        near = dot_nt(weights_ref[NEAR], latent_ref[b, 0])
        near = jnp.concatenate([near, near], axis=1)
        ids = jnp.concatenate([neighbours_ref[b, k] for k in range(neighbour_count)], axis=1)
        place, key = places(ids & 127, ids >> 7, fold_y)

        def pre(tile, b=b, near=near):
            edges = jnp.concatenate([edge_ref[b, 0, 2 * tile], edge_ref[b, 0, 2 * tile + 1]], axis=0)
            return dot_nt(weights_ref[EDGE], edges) + near

        message = messages(
            window.cells(columns),
            place,
            key,
            pre,
            weights_ref[MIDDLE],
            weights_ref[FINAL],
            hidden_ref.at[bt],
        )
        total = jnp.where(alive_ref[b] > 0.5, slot_sum(message, slots), 0.0)
        total_ref[b] = total.astype(BF16)


def nodes_kernel(
    first_ref,
    second_ref,
    node_pre_ref,
    latent_t_ref,
    state_ref,
    weights_ref,
    decoder_out_ref,
    moved_ref,
):
    aggregate = jnp.concatenate([first_ref[0], first_ref[1], second_ref[0], second_ref[1]], axis=1)
    acceleration = advance(
        node_pre_ref[...], aggregate, latent_t_ref[...], weights_ref, decoder_out_ref[...]
    )
    state = moved(state_ref[0:3], state_ref[3:6], acceleration)
    moved_ref[...] = jnp.concatenate(
        [state, state_ref[6:7], jnp.zeros((ROWS - 10, state.shape[1]), F32)], axis=0
    )


def finish_kernel(
    sizes,
    moved_ref,
    own_ref,
    even_ref,
    odd_ref,
    own_zed,
    even_zed,
    odd_zed,
    spread_ref,
    inward_ref,
    encoder_w_ref,
    kept_latent_ref,
    kept_state_ref,
    arrived_latent_ref,
    arrived_state_ref,
):
    count_x, count_y, count_z = sizes
    extent = (2.0 * count_x, 2.0 * count_y, 1.0 * count_z)
    slots = kept_latent_ref.shape[-2]
    stays = moved_ref[9:10]
    kept = moved_ref[:9] * stays
    latents = encode(moved_ref[:9], stays, inward_ref[...], encoder_w_ref[...], extent)
    for i, (a, b) in enumerate(CELLS):
        kept_latent_ref[a, b, 0] = latents[i * slots : (i + 1) * slots]
        for j in range(9):
            kept_state_ref[j, a, b] = kept[j : j + 1, i * slots : (i + 1) * slots]
    fold_y = count_y == 2
    index_x = lax.axis_index("gx")
    options_y = 2 if fold_y else 3
    lanes = own_ref.shape[-1]
    group = lax.broadcasted_iota(I32, (ROWS, lanes), 1) >> 3
    even = (index_x & 1) == 0
    found = jnp.zeros((ROWS, lanes), F32)
    for source_x in (-1, 0, 1):
        for from_y in range(options_y):
            for from_z in range(2):
                if source_x == 0 and from_y == 0 and from_z == 0:
                    continue
                if from_z == 0:
                    own, first, second = own_ref, even_ref, odd_ref
                else:
                    own, first, second = own_zed, even_zed, odd_zed
                side_y = from_y if fold_y or from_y == 0 else 3 - from_y
                target = ((1 - source_x) * options_y + side_y) * 2 + from_z
                if source_x == 0:
                    tile = own[from_y]
                    there = group == target
                elif source_x == -1:
                    tile = jnp.where(even, second[from_y], first[from_y])
                    there = (group == target) & (index_x > 0)
                else:
                    tile = jnp.where(even, first[from_y], second[from_y])
                    there = (group == target) & (index_x < count_x - 1)
                found = jnp.where(there, tile, found)
    arrived = joined(dot(thirds(found), spread_ref[...]))
    for j in range(9):
        arrived_state_ref[j, 0, 0] = arrived[j : j + 1]
    arrived_latent_ref[0, 0, 0] = encode(
        arrived[:9], arrived[9:10], inward_ref[...], encoder_w_ref[...], extent
    )


def swap(values, axis):
    return lax.ppermute(values, axis, [(0, 1), (1, 0)])


def shift(values, axis, way):
    pairs = [(i, i + 1) for i in range(lax.axis_size(axis) - 1)]
    return lax.ppermute(values, axis, [(j, i) for i, j in pairs] if way else pairs)


def swap_x(values, first):
    count = lax.axis_size("gx")
    pairs = []
    for x in range(count):
        partner = x + 1 if (x - first) % 2 == 0 else x - 1
        for z in range(2):
            if 0 <= partner < count:
                pairs.append((x * 2 + z, partner * 2 + z))
            else:
                pairs.append((x * 2 + z, x * 2 + 1 - z))
    return lax.ppermute(values, ("gx", "gz"), pairs)


def swap_chips(values, cross):
    count_x, count_y, count_z = (lax.axis_size(axis) for axis in ("gx", "gy", "gz"))
    pairs = []
    for x in range(count_x):
        for y in range(count_y):
            for z in range(count_z):
                to_x = x + 1 - 2 * z
                if 0 <= to_x < count_x:
                    to = (to_x, y ^ 1 if cross else y, 1 - z)
                else:
                    to = (x, y ^ 1, z)
                pairs.append(((x * count_y + y) * count_z + z, (to[0] * count_y + to[1]) * count_z + to[2]))
    return lax.ppermute(values, ("gx", "gy", "gz"), pairs)


def call(kernel, name, in_specs, outs, scratch, operands, flops):
    return pl.pallas_call(
        kernel,
        out_shape=tuple(jax.ShapeDtypeStruct(shape, kind) for shape, kind in outs),
        in_specs=in_specs,
        out_specs=tuple(VMEM for _ in outs),
        scratch_shapes=scratch,
        compiler_params=pltpu.CompilerParams(vmem_limit_bytes=32 * 1024 * 1024),
        cost_estimate=pl.CostEstimate(flops=flops, bytes_accessed=0, transcendentals=0),
        name=name,
    )(*operands)


def in_hbm(array):
    return pltpu.with_memory_space_constraint(array, pltpu.HBM)


def like(array):
    return pltpu.VMEM(array.shape, array.dtype)


def body(
    node_latent,
    edge_latent,
    positions,
    velocity,
    fill,
    neighbours,
    owners,
    edge_weights,
    node_in,
    node_weights,
    decoder_weights,
    decoder_out,
    encoder_in,
    encoder_weights,
):
    sizes = tuple(lax.axis_size(axis) for axis in ("gx", "gy", "gz"))
    fold_y = sizes[1] == 2
    slots, width = node_latent.shape[-2:]
    neighbour_count = neighbours.shape[3]
    particles = 4 * slots
    options_y = 2 if fold_y else 3
    movers = (3 * options_y * 2 * CAP + 127) // 128 * 128
    rows = 3 if fold_y else 4
    fill = jnp.transpose(fill, (0, 2, 1))
    neighbours = neighbours.reshape(2, 2, neighbour_count, 1, slots)

    own_zed = swap(node_latent, "gz")
    latent, end, inner = call(
        functools.partial(cut_kernel, fold_y),
        "cut",
        [ANY],
        [
            (node_latent.shape, BF16),
            (node_latent.shape[1:], BF16),
            ((2, 1, slots, width), BF16),
        ],
        [pltpu.SemaphoreType.DMA((4,))],
        (in_hbm(node_latent),),
        1_000_000,
    )
    core = lax.axis_index("gz")
    if fold_y:
        sides = [swap(inner[:, 0], "gy")]
        row = 1 - lax.axis_index("gy")
        both = jnp.stack([end[:, 0], lax.dynamic_index_in_dim(own_zed[:, :, 0], 1 - core, 0, False)])
        corner = lax.dynamic_slice_in_dim(both, row, 1, axis=1)
        mine = [swap_chips(both, False), swap_chips(corner, True)]
    else:
        sides = [shift(latent[:, 1, 0], "gy", 0), shift(latent[:, 0, 0], "gy", 1)]
        side_zeds = [swap(part, "gz") for part in sides]
        layers = []
        for middle, outer in ((latent, sides), (own_zed, side_zeds)):
            parts = [outer[0][:, None], middle[:, :, 0], outer[1][:, None]]
            parts = [lax.dynamic_index_in_dim(part, 1 - core, 0, False) for part in parts]
            layers.append(jnp.concatenate(parts, axis=0))
        mine = [swap_chips(jnp.stack(layers), False)]

    fetched = (neighbours, positions, velocity, edge_latent)
    ranked = call(
        functools.partial(ranks_kernel, sizes),
        "ranks",
        [SMEM] + [ANY] * 13,
        [
            ((11, width, width), BF16),
            (decoder_out.shape, BF16),
            ((48, width), BF16),
            (encoder_weights.shape, BF16),
            ((movers, particles), BF16),
            ((8, particles), F32),
            ((2, 2, 1, slots), F32),
            *((array.shape, array.dtype) for array in fetched),
            ((movers, 26 * CAP), BF16),
        ],
        [
            like(owners),
            like(edge_weights),
            like(node_in),
            like(node_weights),
            like(decoder_weights),
            like(encoder_in),
            pltpu.SemaphoreType.DMA((12,)),
        ],
        [
            in_hbm(array)
            for array in (
                fill,
                owners,
                edge_weights,
                node_in,
                node_weights,
                decoder_weights,
                decoder_out,
                encoder_in,
                encoder_weights,
                *fetched,
            )
        ]
        + [own_zed],
        500_000_000,
    )
    sides, mine, ranked = lax.optimization_barrier((sides, mine, ranked))
    weights, decoder_out, inward, encoder_weights, placer, masks, alive, *ranked = ranked
    neighbours, positions, velocity, edge_latent, spread = ranked

    mine = jnp.concatenate(mine, axis=1)
    if fold_y:
        packed = jnp.concatenate([mine.reshape(-1, slots, width), sides[0]], axis=0)
    else:
        packed = mine.reshape(-1, slots, width)
    packed = swap(packed, "gz")
    prepared = call(
        functools.partial(prepare_kernel, sizes),
        "prepare",
        [VMEM] * 9,
        [
            ((4, width, 2 * slots), BF16),
            ((width, particles), F32),
            ((width, particles), F32),
            ((8, particles), F32),
            ((width, neighbour_count * movers), F32),
            ((1, neighbour_count * movers), I32),
            ((1, neighbour_count * movers), I32),
            ((width, movers), F32),
            ((width, movers), F32),
            ((8, movers), F32),
        ],
        [],
        (latent, own_zed, edge_latent, positions, velocity, neighbours, weights, placer, masks),
        500_000_000,
    )
    packed, prepared = lax.optimization_barrier((packed, prepared))
    cells = mine.shape[0] * mine.shape[1]
    if fold_y:
        side_zeds = [packed[cells:]]
    halo = [*sides, *side_zeds, mine, packed[:cells].reshape(mine.shape)]
    (
        far_own,
        latent_t,
        node_pre,
        state,
        mover_pre,
        mover_place,
        mover_key,
        mover_node_pre,
        mover_latent,
        mover_state,
    ) = prepared
    far_rest, bucket = call(
        functools.partial(movers_kernel, sizes, len(sides)),
        "movers",
        [VMEM] * (len(halo) + 8),
        [((4 * rows - 4, width, 2 * slots), BF16), ((ROWS, movers), F32)],
        [pltpu.VMEM((width, neighbour_count * movers), BF16)],
        (
            *halo,
            weights,
            decoder_out,
            mover_pre,
            mover_place,
            mover_key,
            mover_node_pre,
            mover_latent,
            mover_state,
        ),
        3_000_000_000,
    )

    def edges(a):
        return call(
            functools.partial(edges_kernel, sizes, a),
            "edges",
            [VMEM] * 7,
            [((2, width, slots), BF16)],
            [pltpu.VMEM((2, width, neighbour_count * slots), BF16)],
            (alive, latent, edge_latent, neighbours, far_own, far_rest, weights),
            4_000_000_000,
        )[0]

    first = edges(0)
    if fold_y:
        tiles = [swap(bucket, "gy")]
    else:
        tiles = [shift(bucket, "gy", 0), shift(bucket, "gy", 1)]
    tiles, first = lax.optimization_barrier((tiles, first))
    tiles = jnp.stack([bucket, *tiles], axis=0)
    second = edges(1)
    odd = swap_x(tiles, 1)
    sided = [swap_x(tiles, 0), odd]
    sided, second = lax.optimization_barrier((sided, second))
    tiles = [tiles, *sided]
    zeds = [swap(part, "gz") for part in tiles]
    state = call(
        nodes_kernel,
        "nodes",
        [VMEM] * 7,
        [((ROWS, particles), F32)],
        [],
        (first, second, node_pre, latent_t, state, weights, decoder_out),
        1_000_000_000,
    )[0]
    zeds, state = lax.optimization_barrier((zeds, state))
    return call(
        functools.partial(finish_kernel, sizes),
        "finish",
        [VMEM] * 10,
        [
            (node_latent.shape, BF16),
            ((9,) + node_latent.shape[:4], F32),
            ((1, 1, 1, 26 * CAP, width), BF16),
            ((9, 1, 1, 1, 26 * CAP), F32),
        ],
        [],
        (state, *tiles, *zeds, spread, inward, encoder_weights),
        1_000_000_000,
    )


def solution(mesh):
    placed = (
        P(("group", "gx"), "gy", "gz", None, None),
        P(("group", "gx"), "gy", "gz", None, None, None),
        P(None, ("group", "gx"), "gy", "gz", None),
        P(None, ("group", "gx"), "gy", "gz", None),
        P(("group", "gx"), "gy", "gz"),
        P(("group", "gx"), "gy", "gz", None, None),
        P(("group", "gx"), "gy", "gz", None),
        P(),
        P(),
        P(),
        P(),
        P(),
        P(),
        P(),
    )
    return jax.shard_map(
        body,
        mesh=mesh,
        in_specs=placed,
        out_specs=(
            P(("group", "gx"), "gy", "gz", None, None),
            P(None, ("group", "gx"), "gy", "gz", None),
            P(("group", "gx"), "gy", "gz", None, None),
            P(None, ("group", "gx"), "gy", "gz", None),
        ),
        check_vma=False,
    )
```

```python
import functools

import jax
import jax.numpy as jnp
from jax import lax
from jax.experimental import pallas as pl
from jax.experimental.pallas import tpu as pltpu
from jax.sharding import PartitionSpec as P

CAP = 8
F32 = jnp.float32
BF16 = jnp.bfloat16
I32 = jnp.int32
ROWS = 16
TILE = 256
CELLS = [(a, b) for a in range(2) for b in range(2)]
EDGE, NEAR, FAR, MIDDLE, FINAL, NODE_OLD, NODE_NEW, NODE_0, NODE_1, DECODE_0, DECODE_1 = range(11)

VMEM = pl.BlockSpec(memory_space=pltpu.VMEM)
SMEM = pl.BlockSpec(memory_space=pltpu.SMEM)
ANY = pl.BlockSpec(memory_space=pl.ANY)


def dot(left, right):
    return jnp.dot(left, right, preferred_element_type=F32)


def dot_nt(left, right):
    return lax.dot_general(left, right, (((1,), (1,)), ((), ())), preferred_element_type=F32)


def dot_tn(left, right):
    return lax.dot_general(left, right, (((0,), (0,)), ((), ())), preferred_element_type=F32)


def relu16(values):
    return jnp.maximum(values, 0.0).astype(BF16)


def norm(values, axis):
    scale = 1.0 / values.shape[axis]
    centred = values - jnp.sum(values, axis=axis, keepdims=True) * scale
    spread = jnp.sum(centred * centred, axis=axis, keepdims=True) * scale
    return centred * lax.rsqrt(spread + 1e-05)


def thirds(values):
    high = values.astype(BF16)
    rest = values - high.astype(F32)
    middle = rest.astype(BF16)
    low = (rest - middle.astype(F32)).astype(BF16)
    return jnp.concatenate([high, middle, low], axis=0)


def joined(values):
    rows = values.shape[0] // 3
    return values[:rows] + values[rows : 2 * rows] + values[2 * rows :]


def quotient(values, count):
    if count & (count - 1) == 0:
        return values >> (count.bit_length() - 1)
    return lax.div(values, jnp.full_like(values, count))


def flip(weights):
    return weights.astype(F32).T.astype(BF16)


def fetch(pairs, sems):
    copies = [pltpu.make_async_copy(src, dst, sems.at[i]) for i, (src, dst) in enumerate(pairs)]
    for copy in copies:
        copy.start()
    return copies


def encode(state, mask, inward, encoder_w, extent):
    width = state.shape[1]
    position = state[0:3]
    row = lax.broadcasted_iota(I32, (3, width), 0)
    size = jnp.where(row == 0, extent[0], jnp.where(row == 1, extent[1], extent[2]))
    features = jnp.concatenate(
        [
            state[3:9],
            jnp.clip(position, -1.0, 1.0),
            jnp.clip(size - position, -1.0, 1.0),
            jnp.zeros((4, width), F32),
        ],
        axis=0,
    )
    hidden = relu16(dot_tn(thirds(features), inward))
    hidden = relu16(dot(hidden, encoder_w[0]))
    column = jnp.broadcast_to(mask, (8, width)).T[:, 0:1]
    return (norm(dot(hidden, encoder_w[1]), 1) * column).astype(BF16)


def places(ids_low, ids_high, fold_y):
    plane = (ids_high * 43) >> 7
    ez = ids_high - plane * 3
    ey = plane & 3
    ex = plane >> 2
    if fold_y:
        row = jnp.where(ey == 1, 0, jnp.where(ey == 2, 1, 2))
    else:
        row = ey
    return ex * 4 + row, ids_low + jnp.where(ez == 1, 0, 128)


def pick(cells, place, key):
    width = cells[0][1].shape[0]
    chunk = 32
    window = jnp.concatenate(
        [ref[f : f + chunk] for f in range(0, width, chunk) for _, ref in cells], axis=0
    )
    key_rows = lax.broadcasted_iota(I32, (TILE, TILE), 0)
    picker = jnp.where(key_rows == key, 1.0, 0.0).astype(BF16)
    found = dot(window, picker).reshape(width // chunk, len(cells), chunk // 8, 8, TILE)
    where = jnp.broadcast_to(place, (8, TILE))
    parts = []
    for f in range(width // chunk):
        part = jnp.zeros((chunk // 8, 8, TILE), F32)
        for i, (column, _) in enumerate(cells):
            part = jnp.where((where == column)[None], found[f, i], part)
        parts.append(part.reshape(chunk, TILE))
    return jnp.concatenate(parts, axis=0)


def messages(cells, place, key, pre, middle_t, final_t, hidden_ref):
    for tile in range(place.shape[1] // TILE):
        at = slice(tile * TILE, (tile + 1) * TILE)
        hidden_ref[:, at] = relu16(pre(tile) + pick(cells, place[:, at], key[:, at]))
    hidden = relu16(dot(middle_t, hidden_ref[...]))
    return norm(dot(final_t, hidden), 0)


class Window:
    def __init__(self, fold_y, own_ref=None, rest_ref=None):
        self.row_count = 3 if fold_y else 4
        self.own_rows = (0, 1) if fold_y else (1, 2)
        self.outer_rows = (2,) if fold_y else (0, 3)
        self.own_ref, self.rest_ref = own_ref, rest_ref

    def own(self, ex, row):
        return (ex - 1) * 2 + self.own_rows.index(row)

    def side(self, ex, row):
        count = len(self.outer_rows)
        return 2 * self.row_count + (ex - 1) * count + self.outer_rows.index(row)

    def cells(self, columns):
        found = []
        for ex, row in columns:
            if ex in (1, 2) and row in self.own_rows:
                ref = self.own_ref.at[self.own(ex, row)]
            elif ex in (1, 2):
                ref = self.rest_ref.at[self.side(ex, row)]
            else:
                ref = self.rest_ref.at[(0 if ex == 0 else self.row_count) + row]
            found.append((ex * 4 + row, ref))
        return found


def slot_sum(message, step):
    total = message[:, :step]
    for at in range(step, message.shape[1], step):
        total = total + message[:, at : at + step]
    return total


def advance(pre, aggregate, latent_t, weights_ref, decoder_out):
    pre = pre + dot(weights_ref[NODE_NEW], aggregate)
    hidden = relu16(dot(weights_ref[NODE_0], relu16(pre)))
    updated = (latent_t + norm(dot(weights_ref[NODE_1], hidden), 0)).astype(BF16)
    hidden = relu16(dot(weights_ref[DECODE_0], updated))
    hidden = relu16(dot(weights_ref[DECODE_1], hidden))
    return dot(decoder_out, hidden)


def moved(position, velocity, acceleration):
    new_velocity = velocity + acceleration
    return jnp.concatenate([position + new_velocity, new_velocity, velocity], axis=0)


def cut_kernel(fold_y, latent_any, latent_ref, edge_ref, inner_ref, sems):
    end = 1 - lax.axis_index("gz")
    inner = 1 - lax.axis_index("gy") if fold_y else 0
    copies = fetch(
        [
            (latent_any, latent_ref),
            (latent_any.at[end], edge_ref),
            (latent_any.at[0, inner], inner_ref.at[0]),
            (latent_any.at[1, inner], inner_ref.at[1]),
        ],
        sems,
    )
    for copy in copies:
        copy.wait()


def ranks_kernel(
    sizes,
    fill_ref,
    owners_any,
    edge_w_any,
    node_in_any,
    node_w_any,
    decoder_w_any,
    decoder_out_any,
    encoder_in_any,
    encoder_w_any,
    neighbours_any,
    positions_any,
    velocity_any,
    edge_any,
    latent_ref,
    weights_ref,
    decoder_out_ref,
    inward_ref,
    encoder_w_ref,
    alive_ref,
    neighbours_ref,
    edge_ref,
    spread_ref,
    latent_t_ref,
    node_pre_ref,
    state_ref,
    mover_edge_ref,
    mover_place_ref,
    mover_key_ref,
    mover_near_ref,
    mover_node_pre_ref,
    mover_latent_ref,
    mover_state_ref,
    positions_ref,
    velocity_ref,
    owners_ref,
    edge_w_ref,
    node_in_ref,
    node_w_ref,
    decoder_w_ref,
    encoder_in_ref,
    sems,
):
    count_x, count_y, count_z = sizes
    fold_y = count_y == 2
    copies = fetch(
        [
            (owners_any, owners_ref),
            (edge_w_any, edge_w_ref),
            (node_in_any, node_in_ref),
            (node_w_any, node_w_ref),
            (decoder_w_any, decoder_w_ref),
            (decoder_out_any, decoder_out_ref),
            (encoder_in_any, encoder_in_ref),
            (encoder_w_any, encoder_w_ref),
            (neighbours_any, neighbours_ref),
            (positions_any, positions_ref),
            (velocity_any, velocity_ref),
            (edge_any, edge_ref),
        ],
        sems,
    )
    copies[0].wait()
    index_x = lax.axis_index("gx")
    index_y = lax.axis_index("gy")
    index_z = lax.axis_index("gz")
    slots = owners_ref.shape[-1]
    width = node_in_ref.shape[-1]
    for a, b in CELLS:
        alive_ref[a, b] = jnp.where(
            lax.broadcasted_iota(I32, (1, slots), 1) < fill_ref[a, 0, b], 1.0, 0.0
        )

    lane = lax.broadcasted_iota(I32, (1, slots), 1)
    owner = jnp.concatenate([owners_ref[a, b] for a, b in CELLS], axis=1)
    alive = jnp.concatenate([jnp.where(lane < fill_ref[a, 0, b], 1, 0) for a, b in CELLS], axis=1)
    own_block = (index_x * count_y + index_y) * count_z + index_z
    stays = jnp.where((alive == 1) & (owner == own_block), 1.0, 0.0)
    moving = jnp.where((alive == 1) & (owner != own_block), 1, 0)
    owner_x = quotient(owner, count_y * count_z)
    rest = owner - owner_x * (count_y * count_z)
    owner_y = quotient(rest, count_z)
    owner_z = rest - owner_y * count_z
    step_y = owner_y - index_y
    side_y = jnp.where(step_y == 0, 0, 1) if fold_y else jnp.where(step_y < 0, 1, 2 * step_y)
    options_y = 2 if fold_y else 3
    group = ((owner_x - index_x + 1) * options_y + side_y) * 2 + jnp.where(owner_z == index_z, 0, 1)
    group_rows = (3 * options_y * 2 + 15) // 16 * 16
    particles = owner.shape[1]
    member = jnp.where(
        (lax.broadcasted_iota(I32, (group_rows, particles), 0) == group) & (moving == 1), 1.0, 0.0
    )
    triangle = jnp.where(
        lax.broadcasted_iota(I32, (slots, slots), 0) <= lax.broadcasted_iota(I32, (slots, slots), 1),
        1.0,
        0.0,
    ).astype(BF16)
    counted = []
    before = jnp.zeros((group_rows, 1), F32)
    for i in range(4):
        inside = member[:, i * slots : (i + 1) * slots]
        counted.append(dot(inside.astype(BF16), triangle) + before)
        before = before + jnp.sum(inside, axis=1, keepdims=True)
    counted = jnp.concatenate(counted, axis=1)
    rank = (jnp.sum(counted * member, axis=0, keepdims=True) - 1.0).astype(I32)
    column = jnp.where(moving == 1, group * CAP + rank, -1)
    movers = mover_state_ref.shape[1]
    placer = jnp.where(
        lax.broadcasted_iota(I32, (movers, particles), 0) == column, 1.0, 0.0
    ).astype(BF16)

    spread_shape = spread_ref.shape
    line = lax.broadcasted_iota(I32, spread_shape, 0)
    from_group = line >> 3
    plane = from_group >> 1
    from_x = 1 - ((plane >> 1) if fold_y else ((plane * 43) >> 7))
    side_y = plane - (1 - from_x) * options_y
    if fold_y:
        from_y = jnp.where(side_y == 0, 0, jnp.where(index_y == 0, 1, -1))
    else:
        from_y = jnp.where(side_y == 0, 0, jnp.where(side_y == 1, 1, -1))
    from_z = jnp.where((from_group & 1) == 0, 0, jnp.where(index_z == 0, 1, -1))
    direction = (from_x + 1) * 9 + (from_y + 1) * 3 + from_z + 1
    direction = direction - jnp.where(direction > 13, 1, 0)
    column = direction * CAP + (line & 7)
    valid = (lax.broadcasted_iota(I32, spread_shape, 1) == column) & (
        (from_x != 0) | (from_y != 0) | (from_z != 0)
    )
    spread_ref[...] = jnp.where(valid, 1.0, 0.0).astype(BF16)

    for copy in copies[1:-1]:
        copy.wait()
    for i in range(5):
        weights_ref[i] = flip(edge_w_ref[i])
    weights_ref[NODE_OLD] = flip(node_in_ref[:width])
    weights_ref[NODE_NEW] = flip(node_in_ref[width:])
    for i in range(2):
        weights_ref[NODE_0 + i] = flip(node_w_ref[i])
        weights_ref[DECODE_0 + i] = flip(decoder_w_ref[i])
    inward = jnp.concatenate([encoder_in_ref[...].astype(F32), jnp.zeros((4, width), F32)], axis=0)
    inward = inward.astype(BF16)
    inward_ref[...] = jnp.concatenate([inward, inward, inward], axis=0)

    latent = jnp.concatenate([latent_ref[a, b, 0] for a, b in CELLS], axis=0)
    latent_t_ref[...] = latent.astype(F32).T
    node_pre_ref[...] = dot_nt(weights_ref[NODE_OLD], latent)

    def flat(ref, i):
        return jnp.concatenate([ref[i, a, b] for a, b in CELLS], axis=1)

    state = [flat(positions_ref, i) for i in range(3)] + [flat(velocity_ref, i) for i in range(3)]
    state_ref[...] = jnp.concatenate(state + [stays, jnp.zeros_like(stays)], axis=0)

    mover_latent = dot(placer, latent).astype(BF16)
    mover_latent_ref[...] = mover_latent.astype(F32).T
    mover_node_pre_ref[...] = dot_nt(weights_ref[NODE_OLD], mover_latent)
    mover_near_ref[...] = dot_nt(weights_ref[NEAR], mover_latent)
    state = jnp.concatenate(state + [moving.astype(F32), jnp.zeros_like(stays)], axis=0)
    mover_state_ref[...] = joined(dot_nt(thirds(state), placer))
    neighbour_count = edge_ref.shape[3]
    ids = jnp.concatenate(
        [
            jnp.concatenate([neighbours_ref[a, b, k] for a, b in CELLS], axis=1)
            for k in range(neighbour_count)
        ],
        axis=0,
    )
    ids = jnp.concatenate([ids & 127, ids >> 7, jnp.zeros((8, particles), I32)], axis=0)
    ids = dot_nt(ids.astype(F32).astype(BF16), placer).astype(I32)
    place, key = places(ids[:neighbour_count], ids[neighbour_count : 2 * neighbour_count], fold_y)
    mover_place_ref[...] = jnp.concatenate([place[k : k + 1] for k in range(neighbour_count)], axis=1)
    mover_key_ref[...] = jnp.concatenate([key[k : k + 1] for k in range(neighbour_count)], axis=1)
    copies[-1].wait()
    for k in range(neighbour_count):
        rows = jnp.concatenate([edge_ref[a, b, 0, k] for a, b in CELLS], axis=0)
        mover_edge_ref[k] = dot(placer, rows).astype(BF16)


def prepare_kernel(
    sizes,
    latent_ref,
    own_zed,
    mine_ref,
    weights_ref,
    edge_ref,
    place_ref,
    key_ref,
    near_ref,
    far_ref,
    far_mine_ref,
    pre_ref,
):
    window = Window(sizes[1] == 2, far_ref)
    core = lax.axis_index("gz")
    far_t = weights_ref[FAR]
    columns = [(ex, row) for ex in (1, 2) for row in window.own_rows]
    for (ex, row), (a, b) in zip(columns, CELLS):
        pair = jnp.concatenate([latent_ref[a, b, 0], own_zed[a, b, 0]], axis=0)
        far_ref[window.own(ex, row)] = dot_nt(far_t, pair).astype(BF16)
    cells = window.cells(columns)
    for row in range(window.row_count):
        pair = jnp.concatenate([mine_ref[1, row], mine_ref[0, row]], axis=0)
        far_mine_ref[row] = dot_nt(far_t, pair).astype(BF16)
        cells.append((12 * (1 - core) + row, far_mine_ref.at[row]))
    neighbour_count, movers = edge_ref.shape[:2]
    step = TILE // movers
    near = jnp.concatenate([near_ref[...]] * step, axis=1)
    for tile in range(neighbour_count // step):
        edges = jnp.concatenate([edge_ref[k] for k in range(tile * step, (tile + 1) * step)], axis=0)
        at = slice(tile * TILE, (tile + 1) * TILE)
        pre_ref[:, at] = (
            dot_nt(weights_ref[EDGE], edges) + near + pick(cells, place_ref[:, at], key_ref[:, at])
        )


def movers_kernel(
    sizes,
    side_count,
    *refs,
):
    fold_y = sizes[1] == 2
    side_refs, refs = refs[:side_count], refs[side_count:]
    side_zeds, refs = refs[:side_count], refs[side_count:]
    other_ref, far_mine_ref, refs = refs[0], refs[1], refs[2:]
    (
        weights_ref,
        decoder_out_ref,
        pre_ref,
        place_ref,
        key_ref,
        node_pre_ref,
        latent_t_ref,
        state_ref,
        far_ref,
        bucket_ref,
        hidden_ref,
    ) = refs
    window = Window(fold_y, None, far_ref)
    row_count = window.row_count
    core = lax.axis_index("gz")
    far_t = weights_ref[FAR]

    def far(at, here, beside):
        pair = jnp.concatenate([here, beside], axis=0)
        far_ref[at] = dot_nt(far_t, pair).astype(BF16)

    for row in range(row_count):
        far(core * row_count + row, other_ref[0, row], other_ref[1, row])
    for side, row in enumerate(window.outer_rows):
        for ex in (1, 2):
            far(window.side(ex, row), side_refs[side][ex - 1], side_zeds[side][ex - 1])

    movers = state_ref.shape[1]
    for row in range(row_count):
        far_ref[(1 - core) * row_count + row] = far_mine_ref[row]
    cells = [(12 * core + row, far_ref.at[core * row_count + row]) for row in range(row_count)]
    cells += window.cells([(ex, row) for ex in (1, 2) for row in window.outer_rows])
    message = messages(
        cells,
        place_ref[...],
        key_ref[...],
        lambda tile: pre_ref[:, tile * TILE : (tile + 1) * TILE],
        weights_ref[MIDDLE],
        weights_ref[FINAL],
        hidden_ref,
    )
    aggregate = slot_sum(message, movers).astype(BF16)
    acceleration = advance(
        node_pre_ref[...], aggregate, latent_t_ref[...], weights_ref, decoder_out_ref[...]
    )
    mask = state_ref[6:7]
    state = moved(state_ref[0:3], state_ref[3:6], acceleration) * mask
    bucket_ref[...] = jnp.concatenate([state, mask, jnp.zeros((ROWS - 10, movers), F32)], axis=0)


def edges_kernel(
    sizes,
    a,
    alive_ref,
    latent_ref,
    edge_ref,
    neighbours_ref,
    far_own_ref,
    far_rest_ref,
    weights_ref,
    total_ref,
    hidden_ref,
):
    fold_y = sizes[1] == 2
    window = Window(fold_y, far_own_ref, far_rest_ref)
    index_y = lax.axis_index("gy")
    alive_ref, latent_ref = alive_ref.at[a], latent_ref.at[a]
    edge_ref, neighbours_ref = edge_ref.at[a], neighbours_ref.at[a]
    slots, width = latent_ref.shape[-2:]
    neighbour_count = edge_ref.shape[2]
    for bt in range(2):
        if fold_y:
            b = index_y if bt == 0 else 1 - index_y
            rows = (0, 1) if bt == 0 else (0, 1, 2)
        else:
            b = bt
            rows = (bt, bt + 1, bt + 2)
        columns = [(ex, row) for ex in range(a, a + 3) for row in rows]
        near = dot_nt(weights_ref[NEAR], latent_ref[b, 0])
        near = jnp.concatenate([near, near], axis=1)
        ids = jnp.concatenate([neighbours_ref[b, k] for k in range(neighbour_count)], axis=1)
        place, key = places(ids & 127, ids >> 7, fold_y)

        def pre(tile, b=b, near=near):
            edges = jnp.concatenate([edge_ref[b, 0, 2 * tile], edge_ref[b, 0, 2 * tile + 1]], axis=0)
            return dot_nt(weights_ref[EDGE], edges) + near

        message = messages(
            window.cells(columns),
            place,
            key,
            pre,
            weights_ref[MIDDLE],
            weights_ref[FINAL],
            hidden_ref.at[bt],
        )
        total = jnp.where(alive_ref[b] > 0.5, slot_sum(message, slots), 0.0)
        total_ref[b] = total.astype(BF16)


def nodes_kernel(
    first_ref,
    second_ref,
    node_pre_ref,
    latent_t_ref,
    state_ref,
    weights_ref,
    decoder_out_ref,
    moved_ref,
):
    aggregate = jnp.concatenate([first_ref[0], first_ref[1], second_ref[0], second_ref[1]], axis=1)
    acceleration = advance(
        node_pre_ref[...], aggregate, latent_t_ref[...], weights_ref, decoder_out_ref[...]
    )
    state = moved(state_ref[0:3], state_ref[3:6], acceleration)
    moved_ref[...] = jnp.concatenate(
        [state, state_ref[6:7], jnp.zeros((ROWS - 10, state.shape[1]), F32)], axis=0
    )


def finish_kernel(
    sizes,
    moved_ref,
    own_ref,
    odd_ref,
    even_ref,
    own_zed,
    odd_zed,
    even_zed,
    spread_ref,
    inward_ref,
    encoder_w_ref,
    kept_latent_ref,
    kept_state_ref,
    arrived_latent_ref,
    arrived_state_ref,
):
    count_x, count_y, count_z = sizes
    extent = (2.0 * count_x, 2.0 * count_y, 1.0 * count_z)
    slots = kept_latent_ref.shape[-2]
    stays = moved_ref[9:10]
    kept = moved_ref[:9] * stays
    latents = encode(moved_ref[:9], stays, inward_ref[...], encoder_w_ref[...], extent)
    for i, (a, b) in enumerate(CELLS):
        kept_latent_ref[a, b, 0] = latents[i * slots : (i + 1) * slots]
        for j in range(9):
            kept_state_ref[j, a, b] = kept[j : j + 1, i * slots : (i + 1) * slots]
    fold_y = count_y == 2
    index_x = lax.axis_index("gx")
    options_y = 2 if fold_y else 3
    lanes = own_ref.shape[-1]
    group = lax.broadcasted_iota(I32, (ROWS, lanes), 1) >> 3
    even = (index_x & 1) == 0
    found = jnp.zeros((ROWS, lanes), F32)
    for source_x in (-1, 0, 1):
        for from_y in range(options_y):
            for from_z in range(2):
                if source_x == 0 and from_y == 0 and from_z == 0:
                    continue
                if from_z == 0:
                    own, first, second = own_ref, even_ref, odd_ref
                else:
                    own, first, second = own_zed, even_zed, odd_zed
                side_y = from_y if fold_y or from_y == 0 else 3 - from_y
                target = ((1 - source_x) * options_y + side_y) * 2 + from_z
                if source_x == 0:
                    tile = own[from_y]
                    there = group == target
                elif source_x == -1:
                    tile = jnp.where(even, second[from_y], first[from_y])
                    there = (group == target) & (index_x > 0)
                else:
                    tile = jnp.where(even, first[from_y], second[from_y])
                    there = (group == target) & (index_x < count_x - 1)
                found = jnp.where(there, tile, found)
    arrived = joined(dot(thirds(found), spread_ref[...]))
    for j in range(9):
        arrived_state_ref[j, 0, 0] = arrived[j : j + 1]
    arrived_latent_ref[0, 0, 0] = encode(
        arrived[:9], arrived[9:10], inward_ref[...], encoder_w_ref[...], extent
    )


def swap(values, axis):
    return lax.ppermute(values, axis, [(0, 1), (1, 0)])


def shift(values, axis, way):
    pairs = [(i, i + 1) for i in range(lax.axis_size(axis) - 1)]
    return lax.ppermute(values, axis, [(j, i) for i, j in pairs] if way else pairs)


def swap_x(values, first):
    count = lax.axis_size("gx")
    pairs = []
    for x in range(count):
        partner = x + 1 if (x - first) % 2 == 0 else x - 1
        for z in range(2):
            if 0 <= partner < count:
                pairs.append((x * 2 + z, partner * 2 + z))
            else:
                pairs.append((x * 2 + z, x * 2 + 1 - z))
    return lax.ppermute(values, ("gx", "gz"), pairs)


def swap_chips(values, cross):
    count_x, count_y, count_z = (lax.axis_size(axis) for axis in ("gx", "gy", "gz"))
    pairs = []
    for x in range(count_x):
        for y in range(count_y):
            for z in range(count_z):
                to_x = x + 1 - 2 * z
                if 0 <= to_x < count_x:
                    to = (to_x, y ^ 1 if cross else y, 1 - z)
                else:
                    to = (x, y ^ 1, z)
                pairs.append(((x * count_y + y) * count_z + z, (to[0] * count_y + to[1]) * count_z + to[2]))
    return lax.ppermute(values, ("gx", "gy", "gz"), pairs)


def call(kernel, name, in_specs, outs, scratch, operands, flops):
    return pl.pallas_call(
        kernel,
        out_shape=tuple(jax.ShapeDtypeStruct(shape, kind) for shape, kind in outs),
        in_specs=in_specs,
        out_specs=tuple(VMEM for _ in outs),
        scratch_shapes=scratch,
        compiler_params=pltpu.CompilerParams(vmem_limit_bytes=32 * 1024 * 1024),
        cost_estimate=pl.CostEstimate(flops=flops, bytes_accessed=0, transcendentals=0),
        name=name,
    )(*operands)


def in_hbm(array):
    return pltpu.with_memory_space_constraint(array, pltpu.HBM)


def like(array):
    return pltpu.VMEM(array.shape, array.dtype)


def body(
    node_latent,
    edge_latent,
    positions,
    velocity,
    fill,
    neighbours,
    owners,
    edge_weights,
    node_in,
    node_weights,
    decoder_weights,
    decoder_out,
    encoder_in,
    encoder_weights,
):
    sizes = tuple(lax.axis_size(axis) for axis in ("gx", "gy", "gz"))
    fold_y = sizes[1] == 2
    slots, width = node_latent.shape[-2:]
    neighbour_count = neighbours.shape[3]
    particles = 4 * slots
    options_y = 2 if fold_y else 3
    movers = (3 * options_y * 2 * CAP + 127) // 128 * 128
    rows = 3 if fold_y else 4
    fill = jnp.transpose(fill, (0, 2, 1))
    neighbours = neighbours.reshape(2, 2, neighbour_count, 1, slots)

    own_zed = swap(node_latent, "gz")
    latent, end, inner = call(
        functools.partial(cut_kernel, fold_y),
        "cut",
        [ANY],
        [
            (node_latent.shape, BF16),
            (node_latent.shape[1:], BF16),
            ((2, 1, slots, width), BF16),
        ],
        [pltpu.SemaphoreType.DMA((4,))],
        (in_hbm(node_latent),),
        1_000_000,
    )
    core = lax.axis_index("gz")
    if fold_y:
        row = 1 - lax.axis_index("gy")
        both = jnp.stack([end[:, 0], lax.dynamic_index_in_dim(own_zed[:, :, 0], 1 - core, 0, False)])
        corner = lax.dynamic_slice_in_dim(both, row, 1, axis=1)
        mine = [swap_chips(both, False), swap_chips(corner, True)]
        inner, own_zed = lax.optimization_barrier((inner, own_zed))
        sides = [swap(inner[:, 0], "gy")]
    else:
        sides = [shift(latent[:, 1, 0], "gy", 0), shift(latent[:, 0, 0], "gy", 1)]
        side_zeds = [swap(part, "gz") for part in sides]
        layers = []
        for middle, outer in ((latent, sides), (own_zed, side_zeds)):
            parts = [outer[0][:, None], middle[:, :, 0], outer[1][:, None]]
            parts = [lax.dynamic_index_in_dim(part, 1 - core, 0, False) for part in parts]
            layers.append(jnp.concatenate(parts, axis=0))
        mine = [swap_chips(jnp.stack(layers), False)]

    ranked = call(
        functools.partial(ranks_kernel, sizes),
        "ranks",
        [SMEM] + [ANY] * 12 + [VMEM],
        [
            ((11, width, width), BF16),
            (decoder_out.shape, BF16),
            ((48, width), BF16),
            (encoder_weights.shape, BF16),
            ((2, 2, 1, slots), F32),
            (neighbours.shape, I32),
            (edge_latent.shape, BF16),
            ((movers, 26 * CAP), BF16),
            ((width, particles), F32),
            ((width, particles), F32),
            ((8, particles), F32),
            ((neighbour_count, movers, width), BF16),
            ((1, neighbour_count * movers), I32),
            ((1, neighbour_count * movers), I32),
            ((width, movers), F32),
            ((width, movers), F32),
            ((width, movers), F32),
            ((8, movers), F32),
        ],
        [
            like(positions),
            like(velocity),
            like(owners),
            like(edge_weights),
            like(node_in),
            like(node_weights),
            like(decoder_weights),
            like(encoder_in),
            pltpu.SemaphoreType.DMA((12,)),
        ],
        [
            in_hbm(array)
            for array in (
                fill,
                owners,
                edge_weights,
                node_in,
                node_weights,
                decoder_weights,
                decoder_out,
                encoder_in,
                encoder_weights,
                neighbours,
                positions,
                velocity,
                edge_latent,
            )
        ]
        + [latent],
        500_000_000,
    )
    sides, mine, ranked = lax.optimization_barrier((sides, mine, ranked))
    (
        weights,
        decoder_out,
        inward,
        encoder_weights,
        alive,
        neighbours,
        edge_latent,
        spread,
        latent_t,
        node_pre,
        state,
        mover_edges,
        mover_place,
        mover_key,
        mover_near,
        mover_node_pre,
        mover_latent,
        mover_state,
    ) = ranked
    mine = jnp.concatenate(mine, axis=1)
    if fold_y:
        packed = jnp.concatenate([mine.reshape(-1, slots, width), sides[0]], axis=0)
    else:
        packed = mine.reshape(-1, slots, width)
    packed = swap(packed, "gz")
    prepared = call(
        functools.partial(prepare_kernel, sizes),
        "prepare",
        [VMEM] * 8,
        [
            ((4, width, 2 * slots), BF16),
            ((rows, width, 2 * slots), BF16),
            ((width, neighbour_count * movers), F32),
        ],
        [],
        (latent, own_zed, mine, weights, mover_edges, mover_place, mover_key, mover_near),
        500_000_000,
    )
    packed, prepared = lax.optimization_barrier((packed, prepared))
    cells = mine.shape[0] * mine.shape[1]
    if fold_y:
        side_zeds = [packed[cells:]]
    far_own, far_mine, mover_pre = prepared
    halo = [*sides, *side_zeds, packed[:cells].reshape(mine.shape), far_mine]

    far_rest, bucket = call(
        functools.partial(movers_kernel, sizes, len(sides)),
        "movers",
        [VMEM] * (len(halo) + 8),
        [((4 * rows - 4, width, 2 * slots), BF16), ((ROWS, movers), F32)],
        [pltpu.VMEM((width, neighbour_count * movers), BF16)],
        (
            *halo,
            weights,
            decoder_out,
            mover_pre,
            mover_place,
            mover_key,
            mover_node_pre,
            mover_latent,
            mover_state,
        ),
        3_000_000_000,
    )

    def edges(a):
        return call(
            functools.partial(edges_kernel, sizes, a),
            "edges",
            [VMEM] * 7,
            [((2, width, slots), BF16)],
            [pltpu.VMEM((2, width, neighbour_count * slots), BF16)],
            (alive, latent, edge_latent, neighbours, far_own, far_rest, weights),
            4_000_000_000,
        )[0]

    first = edges(0)
    if fold_y:
        tiles = [swap(bucket, "gy")]
    else:
        tiles = [shift(bucket, "gy", 0), shift(bucket, "gy", 1)]
    tiles, first = lax.optimization_barrier((tiles, first))
    tiles = jnp.stack([bucket, *tiles], axis=0)
    second = edges(1)
    sided = [swap_x(tiles, 1), swap_x(tiles, 0)]
    sided, second = lax.optimization_barrier((sided, second))
    tiles = [tiles, *sided]
    zeds = [swap(part, "gz") for part in tiles]
    state = call(
        nodes_kernel,
        "nodes",
        [VMEM] * 7,
        [((ROWS, particles), F32)],
        [],
        (first, second, node_pre, latent_t, state, weights, decoder_out),
        1_000_000_000,
    )[0]
    zeds, state = lax.optimization_barrier((zeds, state))
    return call(
        functools.partial(finish_kernel, sizes),
        "finish",
        [VMEM] * 10,
        [
            (node_latent.shape, BF16),
            ((9,) + node_latent.shape[:4], F32),
            ((1, 1, 1, 26 * CAP, width), BF16),
            ((9, 1, 1, 1, 26 * CAP), F32),
        ],
        [],
        (state, *tiles, *zeds, spread, inward, encoder_weights),
        1_000_000_000,
    )


def solution(mesh):
    placed = (
        P(("group", "gx"), "gy", "gz", None, None),
        P(("group", "gx"), "gy", "gz", None, None, None),
        P(None, ("group", "gx"), "gy", "gz", None),
        P(None, ("group", "gx"), "gy", "gz", None),
        P(("group", "gx"), "gy", "gz"),
        P(("group", "gx"), "gy", "gz", None, None),
        P(("group", "gx"), "gy", "gz", None),
        P(),
        P(),
        P(),
        P(),
        P(),
        P(),
        P(),
    )
    return jax.shard_map(
        body,
        mesh=mesh,
        in_specs=placed,
        out_specs=(
            P(("group", "gx"), "gy", "gz", None, None),
            P(None, ("group", "gx"), "gy", "gz", None),
            P(("group", "gx"), "gy", "gz", None, None),
            P(None, ("group", "gx"), "gy", "gz", None),
        ),
        check_vma=False,
    )
```

```python
import functools

import jax
import jax.numpy as jnp
from jax import lax
from jax.experimental import pallas as pl
from jax.experimental.pallas import tpu as pltpu
from jax.sharding import PartitionSpec as P

CAP = 8
F32 = jnp.float32
BF16 = jnp.bfloat16
I32 = jnp.int32
ROWS = 16
TILE = 256
CELLS = [(a, b) for a in range(2) for b in range(2)]
EDGE, NEAR, FAR, MIDDLE, FINAL, NODE_OLD, NODE_NEW, NODE_0, NODE_1, DECODE_0, DECODE_1 = range(11)

VMEM = pl.BlockSpec(memory_space=pltpu.VMEM)
SMEM = pl.BlockSpec(memory_space=pltpu.SMEM)
ANY = pl.BlockSpec(memory_space=pl.ANY)


def dot(left, right):
    return jnp.dot(left, right, preferred_element_type=F32)


def dot_nt(left, right):
    return lax.dot_general(left, right, (((1,), (1,)), ((), ())), preferred_element_type=F32)


def dot_tn(left, right):
    return lax.dot_general(left, right, (((0,), (0,)), ((), ())), preferred_element_type=F32)


def relu16(values):
    return jnp.maximum(values, 0.0).astype(BF16)


def norm(values, axis):
    scale = 1.0 / values.shape[axis]
    centred = values - jnp.sum(values, axis=axis, keepdims=True) * scale
    spread = jnp.sum(centred * centred, axis=axis, keepdims=True) * scale
    return centred * lax.rsqrt(spread + 1e-05)


def thirds(values):
    high = values.astype(BF16)
    rest = values - high.astype(F32)
    middle = rest.astype(BF16)
    low = (rest - middle.astype(F32)).astype(BF16)
    return jnp.concatenate([high, middle, low], axis=0)


def joined(values):
    rows = values.shape[0] // 3
    return values[:rows] + values[rows : 2 * rows] + values[2 * rows :]


def quotient(values, count):
    if count & (count - 1) == 0:
        return values >> (count.bit_length() - 1)
    return lax.div(values, jnp.full_like(values, count))


def flip(weights):
    return weights.astype(F32).T.astype(BF16)


def fetch(pairs, sems):
    copies = [pltpu.make_async_copy(src, dst, sems.at[i]) for i, (src, dst) in enumerate(pairs)]
    for copy in copies:
        copy.start()
    return copies


def encode(state, mask, inward, encoder_w, extent):
    width = state.shape[1]
    position = state[0:3]
    row = lax.broadcasted_iota(I32, (3, width), 0)
    size = jnp.where(row == 0, extent[0], jnp.where(row == 1, extent[1], extent[2]))
    features = jnp.concatenate(
        [
            state[3:9],
            jnp.clip(position, -1.0, 1.0),
            jnp.clip(size - position, -1.0, 1.0),
            jnp.zeros((4, width), F32),
        ],
        axis=0,
    )
    hidden = relu16(dot_tn(thirds(features), inward))
    hidden = relu16(dot(hidden, encoder_w[0]))
    column = jnp.broadcast_to(mask, (8, width)).T[:, 0:1]
    return (norm(dot(hidden, encoder_w[1]), 1) * column).astype(BF16)


def places(ids_low, ids_high, fold_y):
    plane = (ids_high * 43) >> 7
    ez = ids_high - plane * 3
    ey = plane & 3
    ex = plane >> 2
    if fold_y:
        row = jnp.where(ey == 1, 0, jnp.where(ey == 2, 1, 2))
    else:
        row = ey
    return ex * 4 + row, ids_low + jnp.where(ez == 1, 0, 128)


def pick(cells, place, key):
    width = cells[0][1].shape[0]
    chunk = 32
    window = jnp.concatenate(
        [ref[f : f + chunk] for f in range(0, width, chunk) for _, ref in cells], axis=0
    )
    key_rows = lax.broadcasted_iota(I32, (TILE, TILE), 0).astype(F32).astype(BF16)
    key = jnp.broadcast_to(key.astype(F32), (16, TILE)).astype(BF16)
    same = key_rows.reshape(TILE // 16, 16, TILE) == key[None]
    picker = jnp.where(same, jnp.ones((), BF16), jnp.zeros((), BF16)).reshape(TILE, TILE)
    found = dot(window, picker).reshape(width // chunk, len(cells), chunk // 8, 8, TILE)
    where = jnp.broadcast_to(place, (8, TILE))
    parts = []
    for f in range(width // chunk):
        part = jnp.zeros((chunk // 8, 8, TILE), F32)
        for i, (column, _) in enumerate(cells):
            part = jnp.where((where == column)[None], found[f, i], part)
        parts.append(part.reshape(chunk, TILE))
    return jnp.concatenate(parts, axis=0)


def messages(cells, place, key, pre, middle_t, final_t, hidden_ref):
    for tile in range(place.shape[1] // TILE):
        at = slice(tile * TILE, (tile + 1) * TILE)
        hidden_ref[:, at] = relu16(pre(tile) + pick(cells, place[:, at], key[:, at]))
    hidden = relu16(dot(middle_t, hidden_ref[...]))
    return norm(dot(final_t, hidden), 0)


class Window:
    def __init__(self, fold_y, own_ref=None, rest_ref=None):
        self.row_count = 3 if fold_y else 4
        self.own_rows = (0, 1) if fold_y else (1, 2)
        self.outer_rows = (2,) if fold_y else (0, 3)
        self.own_ref, self.rest_ref = own_ref, rest_ref

    def own(self, ex, row):
        return (ex - 1) * 2 + self.own_rows.index(row)

    def side(self, ex, row):
        count = len(self.outer_rows)
        return 2 * self.row_count + (ex - 1) * count + self.outer_rows.index(row)

    def cells(self, columns):
        found = []
        for ex, row in columns:
            if ex in (1, 2) and row in self.own_rows:
                ref = self.own_ref.at[self.own(ex, row)]
            elif ex in (1, 2):
                ref = self.rest_ref.at[self.side(ex, row)]
            else:
                ref = self.rest_ref.at[(0 if ex == 0 else self.row_count) + row]
            found.append((ex * 4 + row, ref))
        return found


def slot_sum(message, step):
    total = message[:, :step]
    for at in range(step, message.shape[1], step):
        total = total + message[:, at : at + step]
    return total


def advance(pre, aggregate, latent_t, weights_ref, decoder_out):
    pre = pre + dot(weights_ref[NODE_NEW], aggregate)
    hidden = relu16(dot(weights_ref[NODE_0], relu16(pre)))
    updated = (latent_t + norm(dot(weights_ref[NODE_1], hidden), 0)).astype(BF16)
    hidden = relu16(dot(weights_ref[DECODE_0], updated))
    hidden = relu16(dot(weights_ref[DECODE_1], hidden))
    return dot(decoder_out, hidden)


def moved(position, velocity, acceleration):
    new_velocity = velocity + acceleration
    return jnp.concatenate([position + new_velocity, new_velocity, velocity], axis=0)


def cut_kernel(fold_y, latent_any, latent_ref, edge_ref, inner_ref, sems):
    end = 1 - lax.axis_index("gz")
    inner = 1 - lax.axis_index("gy") if fold_y else 0
    copies = fetch(
        [
            (latent_any, latent_ref),
            (latent_any.at[end], edge_ref),
            (latent_any.at[0, inner], inner_ref.at[0]),
            (latent_any.at[1, inner], inner_ref.at[1]),
        ],
        sems,
    )
    for copy in copies:
        copy.wait()


def ranks_kernel(
    sizes,
    fill_ref,
    owners_any,
    edge_w_any,
    node_in_any,
    node_w_any,
    decoder_w_any,
    decoder_out_any,
    encoder_in_any,
    encoder_w_any,
    neighbours_any,
    positions_any,
    velocity_any,
    edge_any,
    latent_ref,
    weights_ref,
    decoder_out_ref,
    inward_ref,
    encoder_w_ref,
    alive_ref,
    neighbours_ref,
    edge_ref,
    spread_ref,
    latent_t_ref,
    node_pre_ref,
    state_ref,
    mover_edge_ref,
    mover_place_ref,
    mover_key_ref,
    mover_near_ref,
    mover_node_pre_ref,
    mover_latent_ref,
    mover_state_ref,
    positions_ref,
    velocity_ref,
    owners_ref,
    edge_w_ref,
    node_in_ref,
    node_w_ref,
    decoder_w_ref,
    encoder_in_ref,
    sems,
):
    count_x, count_y, count_z = sizes
    fold_y = count_y == 2
    copies = fetch(
        [
            (owners_any, owners_ref),
            (edge_w_any, edge_w_ref),
            (node_in_any, node_in_ref),
            (node_w_any, node_w_ref),
            (decoder_w_any, decoder_w_ref),
            (decoder_out_any, decoder_out_ref),
            (encoder_in_any, encoder_in_ref),
            (encoder_w_any, encoder_w_ref),
            (neighbours_any, neighbours_ref),
            (positions_any, positions_ref),
            (velocity_any, velocity_ref),
            (edge_any, edge_ref),
        ],
        sems,
    )
    copies[0].wait()
    index_x = lax.axis_index("gx")
    index_y = lax.axis_index("gy")
    index_z = lax.axis_index("gz")
    slots = owners_ref.shape[-1]
    width = node_in_ref.shape[-1]
    for a, b in CELLS:
        alive_ref[a, b] = jnp.where(
            lax.broadcasted_iota(I32, (1, slots), 1) < fill_ref[a, 0, b], 1.0, 0.0
        )

    lane = lax.broadcasted_iota(I32, (1, slots), 1)
    owner = jnp.concatenate([owners_ref[a, b] for a, b in CELLS], axis=1)
    alive = jnp.concatenate([jnp.where(lane < fill_ref[a, 0, b], 1, 0) for a, b in CELLS], axis=1)
    own_block = (index_x * count_y + index_y) * count_z + index_z
    stays = jnp.where((alive == 1) & (owner == own_block), 1.0, 0.0)
    moving = jnp.where((alive == 1) & (owner != own_block), 1, 0)
    owner_x = quotient(owner, count_y * count_z)
    rest = owner - owner_x * (count_y * count_z)
    owner_y = quotient(rest, count_z)
    owner_z = rest - owner_y * count_z
    step_y = owner_y - index_y
    side_y = jnp.where(step_y == 0, 0, 1) if fold_y else jnp.where(step_y < 0, 1, 2 * step_y)
    options_y = 2 if fold_y else 3
    group = ((owner_x - index_x + 1) * options_y + side_y) * 2 + jnp.where(owner_z == index_z, 0, 1)
    group_rows = (3 * options_y * 2 + 15) // 16 * 16
    particles = owner.shape[1]
    member = jnp.where(
        (lax.broadcasted_iota(I32, (group_rows, particles), 0) == group) & (moving == 1), 1.0, 0.0
    )
    triangle = jnp.where(
        lax.broadcasted_iota(I32, (slots, slots), 0) <= lax.broadcasted_iota(I32, (slots, slots), 1),
        1.0,
        0.0,
    ).astype(BF16)
    counted = []
    before = jnp.zeros((group_rows, 1), F32)
    for i in range(4):
        inside = member[:, i * slots : (i + 1) * slots]
        counted.append(dot(inside.astype(BF16), triangle) + before)
        before = before + jnp.sum(inside, axis=1, keepdims=True)
    counted = jnp.concatenate(counted, axis=1)
    rank = (jnp.sum(counted * member, axis=0, keepdims=True) - 1.0).astype(I32)
    column = jnp.where(moving == 1, group * CAP + rank, -1)
    movers = mover_state_ref.shape[1]
    placer = jnp.where(
        lax.broadcasted_iota(I32, (movers, particles), 0) == column, 1.0, 0.0
    ).astype(BF16)

    spread_shape = spread_ref.shape
    line = lax.broadcasted_iota(I32, spread_shape, 0)
    from_group = line >> 3
    plane = from_group >> 1
    from_x = 1 - ((plane >> 1) if fold_y else ((plane * 43) >> 7))
    side_y = plane - (1 - from_x) * options_y
    if fold_y:
        from_y = jnp.where(side_y == 0, 0, jnp.where(index_y == 0, 1, -1))
    else:
        from_y = jnp.where(side_y == 0, 0, jnp.where(side_y == 1, 1, -1))
    from_z = jnp.where((from_group & 1) == 0, 0, jnp.where(index_z == 0, 1, -1))
    direction = (from_x + 1) * 9 + (from_y + 1) * 3 + from_z + 1
    direction = direction - jnp.where(direction > 13, 1, 0)
    column = direction * CAP + (line & 7)
    valid = (lax.broadcasted_iota(I32, spread_shape, 1) == column) & (
        (from_x != 0) | (from_y != 0) | (from_z != 0)
    )
    spread_ref[...] = jnp.where(valid, 1.0, 0.0).astype(BF16)

    for copy in copies[1:-1]:
        copy.wait()
    for i in range(5):
        weights_ref[i] = flip(edge_w_ref[i])
    weights_ref[NODE_OLD] = flip(node_in_ref[:width])
    weights_ref[NODE_NEW] = flip(node_in_ref[width:])
    for i in range(2):
        weights_ref[NODE_0 + i] = flip(node_w_ref[i])
        weights_ref[DECODE_0 + i] = flip(decoder_w_ref[i])
    inward = jnp.concatenate([encoder_in_ref[...].astype(F32), jnp.zeros((4, width), F32)], axis=0)
    inward = inward.astype(BF16)
    inward_ref[...] = jnp.concatenate([inward, inward, inward], axis=0)

    latent = jnp.concatenate([latent_ref[a, b, 0] for a, b in CELLS], axis=0)
    latent_t_ref[...] = latent.astype(F32).T
    node_pre_ref[...] = dot_nt(weights_ref[NODE_OLD], latent)

    def flat(ref, i):
        return jnp.concatenate([ref[i, a, b] for a, b in CELLS], axis=1)

    state = [flat(positions_ref, i) for i in range(3)] + [flat(velocity_ref, i) for i in range(3)]
    state_ref[...] = jnp.concatenate(state + [stays, jnp.zeros_like(stays)], axis=0)

    mover_latent = dot(placer, latent).astype(BF16)
    mover_latent_ref[...] = mover_latent.astype(F32).T
    mover_node_pre_ref[...] = dot_nt(weights_ref[NODE_OLD], mover_latent)
    mover_near_ref[...] = dot_nt(weights_ref[NEAR], mover_latent)
    state = jnp.concatenate(state + [moving.astype(F32), jnp.zeros_like(stays)], axis=0)
    mover_state_ref[...] = joined(dot_nt(thirds(state), placer))
    neighbour_count = edge_ref.shape[3]
    ids = jnp.concatenate(
        [
            jnp.concatenate([neighbours_ref[a, b, k] for a, b in CELLS], axis=1)
            for k in range(neighbour_count)
        ],
        axis=0,
    )
    ids = jnp.concatenate([ids & 127, ids >> 7, jnp.zeros((8, particles), I32)], axis=0)
    ids = dot_nt(ids.astype(F32).astype(BF16), placer).astype(I32)
    place, key = places(ids[:neighbour_count], ids[neighbour_count : 2 * neighbour_count], fold_y)
    mover_place_ref[...] = jnp.concatenate([place[k : k + 1] for k in range(neighbour_count)], axis=1)
    mover_key_ref[...] = jnp.concatenate([key[k : k + 1] for k in range(neighbour_count)], axis=1)
    copies[-1].wait()
    for k in range(neighbour_count):
        rows = jnp.concatenate([edge_ref[a, b, 0, k] for a, b in CELLS], axis=0)
        mover_edge_ref[k] = dot(placer, rows).astype(BF16)


def prepare_kernel(
    sizes,
    latent_ref,
    own_zed,
    mine_ref,
    weights_ref,
    edge_ref,
    place_ref,
    key_ref,
    near_ref,
    far_ref,
    far_mine_ref,
    pre_ref,
):
    window = Window(sizes[1] == 2, far_ref)
    core = lax.axis_index("gz")
    far_t = weights_ref[FAR]
    columns = [(ex, row) for ex in (1, 2) for row in window.own_rows]
    for (ex, row), (a, b) in zip(columns, CELLS):
        pair = jnp.concatenate([latent_ref[a, b, 0], own_zed[a, b, 0]], axis=0)
        far_ref[window.own(ex, row)] = dot_nt(far_t, pair).astype(BF16)
    cells = window.cells(columns)
    for row in range(window.row_count):
        pair = jnp.concatenate([mine_ref[1, row], mine_ref[0, row]], axis=0)
        far_mine_ref[row] = dot_nt(far_t, pair).astype(BF16)
        cells.append((12 * (1 - core) + row, far_mine_ref.at[row]))
    neighbour_count, movers = edge_ref.shape[:2]
    step = TILE // movers
    near = jnp.concatenate([near_ref[...]] * step, axis=1)
    for tile in range(neighbour_count // step):
        edges = jnp.concatenate([edge_ref[k] for k in range(tile * step, (tile + 1) * step)], axis=0)
        at = slice(tile * TILE, (tile + 1) * TILE)
        pre_ref[:, at] = (
            dot_nt(weights_ref[EDGE], edges) + near + pick(cells, place_ref[:, at], key_ref[:, at])
        )


def movers_kernel(
    sizes,
    side_count,
    *refs,
):
    fold_y = sizes[1] == 2
    side_refs, refs = refs[:side_count], refs[side_count:]
    side_zeds, refs = refs[:side_count], refs[side_count:]
    other_ref, far_mine_ref, refs = refs[0], refs[1], refs[2:]
    (
        weights_ref,
        decoder_out_ref,
        pre_ref,
        place_ref,
        key_ref,
        node_pre_ref,
        latent_t_ref,
        state_ref,
        far_ref,
        bucket_ref,
        hidden_ref,
    ) = refs
    window = Window(fold_y, None, far_ref)
    row_count = window.row_count
    core = lax.axis_index("gz")
    far_t = weights_ref[FAR]

    def far(at, here, beside):
        pair = jnp.concatenate([here, beside], axis=0)
        far_ref[at] = dot_nt(far_t, pair).astype(BF16)

    for row in range(row_count):
        far(core * row_count + row, other_ref[0, row], other_ref[1, row])
    for side, row in enumerate(window.outer_rows):
        for ex in (1, 2):
            far(window.side(ex, row), side_refs[side][ex - 1], side_zeds[side][ex - 1])

    movers = state_ref.shape[1]
    for row in range(row_count):
        far_ref[(1 - core) * row_count + row] = far_mine_ref[row]
    cells = [(12 * core + row, far_ref.at[core * row_count + row]) for row in range(row_count)]
    cells += window.cells([(ex, row) for ex in (1, 2) for row in window.outer_rows])
    message = messages(
        cells,
        place_ref[...],
        key_ref[...],
        lambda tile: pre_ref[:, tile * TILE : (tile + 1) * TILE],
        weights_ref[MIDDLE],
        weights_ref[FINAL],
        hidden_ref,
    )
    aggregate = slot_sum(message, movers).astype(BF16)
    acceleration = advance(
        node_pre_ref[...], aggregate, latent_t_ref[...], weights_ref, decoder_out_ref[...]
    )
    mask = state_ref[6:7]
    state = moved(state_ref[0:3], state_ref[3:6], acceleration) * mask
    bucket_ref[...] = jnp.concatenate([state, mask, jnp.zeros((ROWS - 10, movers), F32)], axis=0)


def edges_kernel(
    sizes,
    a,
    alive_ref,
    latent_ref,
    edge_ref,
    neighbours_ref,
    far_own_ref,
    far_rest_ref,
    weights_ref,
    total_ref,
    hidden_ref,
):
    fold_y = sizes[1] == 2
    window = Window(fold_y, far_own_ref, far_rest_ref)
    index_y = lax.axis_index("gy")
    alive_ref, latent_ref = alive_ref.at[a], latent_ref.at[a]
    edge_ref, neighbours_ref = edge_ref.at[a], neighbours_ref.at[a]
    slots, width = latent_ref.shape[-2:]
    neighbour_count = edge_ref.shape[2]
    for bt in range(2):
        if fold_y:
            b = index_y if bt == 0 else 1 - index_y
            rows = (0, 1) if bt == 0 else (0, 1, 2)
        else:
            b = bt
            rows = (bt, bt + 1, bt + 2)
        columns = [(ex, row) for ex in range(a, a + 3) for row in rows]
        near = dot_nt(weights_ref[NEAR], latent_ref[b, 0])
        near = jnp.concatenate([near, near], axis=1)
        ids = jnp.concatenate([neighbours_ref[b, k] for k in range(neighbour_count)], axis=1)
        place, key = places(ids & 127, ids >> 7, fold_y)

        def pre(tile, b=b, near=near):
            edges = jnp.concatenate([edge_ref[b, 0, 2 * tile], edge_ref[b, 0, 2 * tile + 1]], axis=0)
            return dot_nt(weights_ref[EDGE], edges) + near

        message = messages(
            window.cells(columns),
            place,
            key,
            pre,
            weights_ref[MIDDLE],
            weights_ref[FINAL],
            hidden_ref.at[bt],
        )
        total = jnp.where(alive_ref[b] > 0.5, slot_sum(message, slots), 0.0)
        total_ref[b] = total.astype(BF16)


def nodes_kernel(
    first_ref,
    second_ref,
    node_pre_ref,
    latent_t_ref,
    state_ref,
    weights_ref,
    decoder_out_ref,
    moved_ref,
):
    aggregate = jnp.concatenate([first_ref[0], first_ref[1], second_ref[0], second_ref[1]], axis=1)
    acceleration = advance(
        node_pre_ref[...], aggregate, latent_t_ref[...], weights_ref, decoder_out_ref[...]
    )
    state = moved(state_ref[0:3], state_ref[3:6], acceleration)
    moved_ref[...] = jnp.concatenate(
        [state, state_ref[6:7], jnp.zeros((ROWS - 10, state.shape[1]), F32)], axis=0
    )


def finish_kernel(
    sizes,
    moved_ref,
    own_ref,
    odd_ref,
    even_ref,
    own_zed,
    odd_zed,
    even_zed,
    spread_ref,
    inward_ref,
    encoder_w_ref,
    kept_latent_ref,
    kept_state_ref,
    arrived_latent_ref,
    arrived_state_ref,
):
    count_x, count_y, count_z = sizes
    extent = (2.0 * count_x, 2.0 * count_y, 1.0 * count_z)
    slots = kept_latent_ref.shape[-2]
    stays = moved_ref[9:10]
    kept = moved_ref[:9] * stays
    latents = encode(moved_ref[:9], stays, inward_ref[...], encoder_w_ref[...], extent)
    for i, (a, b) in enumerate(CELLS):
        kept_latent_ref[a, b, 0] = latents[i * slots : (i + 1) * slots]
        for j in range(9):
            kept_state_ref[j, a, b] = kept[j : j + 1, i * slots : (i + 1) * slots]
    fold_y = count_y == 2
    index_x = lax.axis_index("gx")
    options_y = 2 if fold_y else 3
    lanes = own_ref.shape[-1]
    group = lax.broadcasted_iota(I32, (ROWS, lanes), 1) >> 3
    even = (index_x & 1) == 0
    found = jnp.zeros((ROWS, lanes), F32)
    for source_x in (-1, 0, 1):
        for from_y in range(options_y):
            for from_z in range(2):
                if source_x == 0 and from_y == 0 and from_z == 0:
                    continue
                if from_z == 0:
                    own, first, second = own_ref, even_ref, odd_ref
                else:
                    own, first, second = own_zed, even_zed, odd_zed
                side_y = from_y if fold_y or from_y == 0 else 3 - from_y
                target = ((1 - source_x) * options_y + side_y) * 2 + from_z
                if source_x == 0:
                    tile = own[from_y]
                    there = group == target
                elif source_x == -1:
                    tile = jnp.where(even, second[from_y], first[from_y])
                    there = (group == target) & (index_x > 0)
                else:
                    tile = jnp.where(even, first[from_y], second[from_y])
                    there = (group == target) & (index_x < count_x - 1)
                found = jnp.where(there, tile, found)
    arrived = joined(dot(thirds(found), spread_ref[...]))
    for j in range(9):
        arrived_state_ref[j, 0, 0] = arrived[j : j + 1]
    arrived_latent_ref[0, 0, 0] = encode(
        arrived[:9], arrived[9:10], inward_ref[...], encoder_w_ref[...], extent
    )


def swap(values, axis):
    return lax.ppermute(values, axis, [(0, 1), (1, 0)])


def shift(values, axis, way):
    pairs = [(i, i + 1) for i in range(lax.axis_size(axis) - 1)]
    return lax.ppermute(values, axis, [(j, i) for i, j in pairs] if way else pairs)


def swap_x(values, first):
    count = lax.axis_size("gx")
    pairs = []
    for x in range(count):
        partner = x + 1 if (x - first) % 2 == 0 else x - 1
        for z in range(2):
            if 0 <= partner < count:
                pairs.append((x * 2 + z, partner * 2 + z))
            else:
                pairs.append((x * 2 + z, x * 2 + 1 - z))
    return lax.ppermute(values, ("gx", "gz"), pairs)


def swap_chips(values, cross):
    count_x, count_y, count_z = (lax.axis_size(axis) for axis in ("gx", "gy", "gz"))
    pairs = []
    for x in range(count_x):
        for y in range(count_y):
            for z in range(count_z):
                to_x = x + 1 - 2 * z
                if 0 <= to_x < count_x:
                    to = (to_x, y ^ 1 if cross else y, 1 - z)
                else:
                    to = (x, y ^ 1, z)
                pairs.append(((x * count_y + y) * count_z + z, (to[0] * count_y + to[1]) * count_z + to[2]))
    return lax.ppermute(values, ("gx", "gy", "gz"), pairs)


def call(kernel, name, in_specs, outs, scratch, operands, flops):
    return pl.pallas_call(
        kernel,
        out_shape=tuple(jax.ShapeDtypeStruct(shape, kind) for shape, kind in outs),
        in_specs=in_specs,
        out_specs=tuple(VMEM for _ in outs),
        scratch_shapes=scratch,
        compiler_params=pltpu.CompilerParams(vmem_limit_bytes=32 * 1024 * 1024),
        cost_estimate=pl.CostEstimate(flops=flops, bytes_accessed=0, transcendentals=0),
        name=name,
    )(*operands)


def in_hbm(array):
    return pltpu.with_memory_space_constraint(array, pltpu.HBM)


def like(array):
    return pltpu.VMEM(array.shape, array.dtype)


def body(
    node_latent,
    edge_latent,
    positions,
    velocity,
    fill,
    neighbours,
    owners,
    edge_weights,
    node_in,
    node_weights,
    decoder_weights,
    decoder_out,
    encoder_in,
    encoder_weights,
):
    sizes = tuple(lax.axis_size(axis) for axis in ("gx", "gy", "gz"))
    fold_y = sizes[1] == 2
    slots, width = node_latent.shape[-2:]
    neighbour_count = neighbours.shape[3]
    particles = 4 * slots
    options_y = 2 if fold_y else 3
    movers = (3 * options_y * 2 * CAP + 127) // 128 * 128
    rows = 3 if fold_y else 4
    fill = jnp.transpose(fill, (0, 2, 1))
    neighbours = neighbours.reshape(2, 2, neighbour_count, 1, slots)

    own_zed = swap(node_latent, "gz")
    latent, end, inner = call(
        functools.partial(cut_kernel, fold_y),
        "cut",
        [ANY],
        [
            (node_latent.shape, BF16),
            (node_latent.shape[1:], BF16),
            ((2, 1, slots, width), BF16),
        ],
        [pltpu.SemaphoreType.DMA((4,))],
        (in_hbm(node_latent),),
        1_000_000,
    )
    core = lax.axis_index("gz")
    if fold_y:
        row = 1 - lax.axis_index("gy")
        sides = [swap(inner[:, 0], "gy")]
        beside = lax.dynamic_index_in_dim(own_zed[:, :, 0], 1 - core, 0, False)
        corner = jnp.concatenate(
            [lax.dynamic_slice_in_dim(part, row, 1, 0) for part in (end[:, 0], beside)], axis=0
        )
        both = jnp.stack([end[:, 0], beside])
        corner = corner[:, None]
        mine = [swap_chips(corner, True), swap_chips(both, False)]
    else:
        sides = [shift(latent[:, 1, 0], "gy", 0), shift(latent[:, 0, 0], "gy", 1)]
        side_zeds = [swap(part, "gz") for part in sides]
        layers = []
        for middle, outer in ((latent, sides), (own_zed, side_zeds)):
            parts = [outer[0][:, None], middle[:, :, 0], outer[1][:, None]]
            parts = [lax.dynamic_index_in_dim(part, 1 - core, 0, False) for part in parts]
            layers.append(jnp.concatenate(parts, axis=0))
        mine = [swap_chips(jnp.stack(layers), False)]

    ranked = call(
        functools.partial(ranks_kernel, sizes),
        "ranks",
        [SMEM] + [ANY] * 12 + [VMEM],
        [
            ((11, width, width), BF16),
            (decoder_out.shape, BF16),
            ((48, width), BF16),
            (encoder_weights.shape, BF16),
            ((2, 2, 1, slots), F32),
            (neighbours.shape, I32),
            (edge_latent.shape, BF16),
            ((movers, 26 * CAP), BF16),
            ((width, particles), F32),
            ((width, particles), F32),
            ((8, particles), F32),
            ((neighbour_count, movers, width), BF16),
            ((1, neighbour_count * movers), I32),
            ((1, neighbour_count * movers), I32),
            ((width, movers), F32),
            ((width, movers), F32),
            ((width, movers), F32),
            ((8, movers), F32),
        ],
        [
            like(positions),
            like(velocity),
            like(owners),
            like(edge_weights),
            like(node_in),
            like(node_weights),
            like(decoder_weights),
            like(encoder_in),
            pltpu.SemaphoreType.DMA((12,)),
        ],
        [
            in_hbm(array)
            for array in (
                fill,
                owners,
                edge_weights,
                node_in,
                node_weights,
                decoder_weights,
                decoder_out,
                encoder_in,
                encoder_weights,
                neighbours,
                positions,
                velocity,
                edge_latent,
            )
        ]
        + [latent],
        5_000_000_000,
    )
    sides, mine, ranked = lax.optimization_barrier((sides, mine, ranked))
    (
        weights,
        decoder_out,
        inward,
        encoder_weights,
        alive,
        neighbours,
        edge_latent,
        spread,
        latent_t,
        node_pre,
        state,
        mover_edges,
        mover_place,
        mover_key,
        mover_near,
        mover_node_pre,
        mover_latent,
        mover_state,
    ) = ranked
    mine = jnp.concatenate(mine[::-1], axis=1)
    if fold_y:
        packed = jnp.concatenate([mine.reshape(-1, slots, width), sides[0]], axis=0)
    else:
        packed = mine.reshape(-1, slots, width)
    packed = swap(packed, "gz")
    prepared = call(
        functools.partial(prepare_kernel, sizes),
        "prepare",
        [VMEM] * 8,
        [
            ((4, width, 2 * slots), BF16),
            ((rows, width, 2 * slots), BF16),
            ((width, neighbour_count * movers), F32),
        ],
        [],
        (latent, own_zed, mine, weights, mover_edges, mover_place, mover_key, mover_near),
        5_000_000_000,
    )
    packed, prepared = lax.optimization_barrier((packed, prepared))
    cells = mine.shape[0] * mine.shape[1]
    if fold_y:
        side_zeds = [packed[cells:]]
    far_own, far_mine, mover_pre = prepared
    halo = [*sides, *side_zeds, packed[:cells].reshape(mine.shape), far_mine]

    far_rest, bucket = call(
        functools.partial(movers_kernel, sizes, len(sides)),
        "movers",
        [VMEM] * (len(halo) + 8),
        [((4 * rows - 4, width, 2 * slots), BF16), ((ROWS, movers), F32)],
        [pltpu.VMEM((width, neighbour_count * movers), BF16)],
        (
            *halo,
            weights,
            decoder_out,
            mover_pre,
            mover_place,
            mover_key,
            mover_node_pre,
            mover_latent,
            mover_state,
        ),
        3_000_000_000,
    )

    def edges(a):
        return call(
            functools.partial(edges_kernel, sizes, a),
            "edges",
            [VMEM] * 7,
            [((2, width, slots), BF16)],
            [pltpu.VMEM((2, width, neighbour_count * slots), BF16)],
            (alive, latent, edge_latent, neighbours, far_own, far_rest, weights),
            4_000_000_000,
        )[0]

    first = edges(0)
    if fold_y:
        tiles = [swap(bucket, "gy")]
    else:
        tiles = [shift(bucket, "gy", 0), shift(bucket, "gy", 1)]
    tiles, first = lax.optimization_barrier((tiles, first))
    tiles = jnp.stack([bucket, *tiles], axis=0)
    second = edges(1)
    sided = [swap_x(tiles, 1), swap_x(tiles, 0)]
    sided, second = lax.optimization_barrier((sided, second))
    tiles = [tiles, *sided]
    zeds = [swap(part, "gz") for part in tiles]
    state = call(
        nodes_kernel,
        "nodes",
        [VMEM] * 7,
        [((ROWS, particles), F32)],
        [],
        (first, second, node_pre, latent_t, state, weights, decoder_out),
        1_000_000_000,
    )[0]
    zeds, state = lax.optimization_barrier((zeds, state))
    return call(
        functools.partial(finish_kernel, sizes),
        "finish",
        [VMEM] * 10,
        [
            (node_latent.shape, BF16),
            ((9,) + node_latent.shape[:4], F32),
            ((1, 1, 1, 26 * CAP, width), BF16),
            ((9, 1, 1, 1, 26 * CAP), F32),
        ],
        [],
        (state, *tiles, *zeds, spread, inward, encoder_weights),
        1_000_000_000,
    )


def solution(mesh):
    placed = (
        P(("group", "gx"), "gy", "gz", None, None),
        P(("group", "gx"), "gy", "gz", None, None, None),
        P(None, ("group", "gx"), "gy", "gz", None),
        P(None, ("group", "gx"), "gy", "gz", None),
        P(("group", "gx"), "gy", "gz"),
        P(("group", "gx"), "gy", "gz", None, None),
        P(("group", "gx"), "gy", "gz", None),
        P(),
        P(),
        P(),
        P(),
        P(),
        P(),
        P(),
    )
    return jax.shard_map(
        body,
        mesh=mesh,
        in_specs=placed,
        out_specs=(
            P(("group", "gx"), "gy", "gz", None, None),
            P(None, ("group", "gx"), "gy", "gz", None),
            P(("group", "gx"), "gy", "gz", None, None),
            P(None, ("group", "gx"), "gy", "gz", None),
        ),
        check_vma=False,
    )
```

```python
import functools

import jax
import jax.numpy as jnp
from jax import lax
from jax.experimental import pallas as pl
from jax.experimental.pallas import tpu as pltpu
from jax.sharding import PartitionSpec as P

CAP = 8
F32 = jnp.float32
BF16 = jnp.bfloat16
I32 = jnp.int32
ROWS = 16
TILE = 256
CELLS = [(a, b) for a in range(2) for b in range(2)]
EDGE, NEAR, FAR, MIDDLE, FINAL, NODE_OLD, NODE_NEW, NODE_0, NODE_1, DECODE_0, DECODE_1 = range(11)

VMEM = pl.BlockSpec(memory_space=pltpu.VMEM)
SMEM = pl.BlockSpec(memory_space=pltpu.SMEM)
ANY = pl.BlockSpec(memory_space=pl.ANY)


def dot(left, right):
    return jnp.dot(left, right, preferred_element_type=F32)


def dot_nt(left, right):
    return lax.dot_general(left, right, (((1,), (1,)), ((), ())), preferred_element_type=F32)


def dot_tn(left, right):
    return lax.dot_general(left, right, (((0,), (0,)), ((), ())), preferred_element_type=F32)


def relu16(values):
    return jnp.maximum(values, 0.0).astype(BF16)


def norm(values, axis):
    scale = 1.0 / values.shape[axis]
    centred = values - jnp.sum(values, axis=axis, keepdims=True) * scale
    spread = jnp.sum(centred * centred, axis=axis, keepdims=True) * scale
    return centred * lax.rsqrt(spread + 1e-05)


def thirds(values):
    high = values.astype(BF16)
    rest = values - high.astype(F32)
    middle = rest.astype(BF16)
    low = (rest - middle.astype(F32)).astype(BF16)
    return jnp.concatenate([high, middle, low], axis=0)


def joined(values):
    rows = values.shape[0] // 3
    return values[:rows] + values[rows : 2 * rows] + values[2 * rows :]


def quotient(values, count):
    if count & (count - 1) == 0:
        return values >> (count.bit_length() - 1)
    return lax.div(values, jnp.full_like(values, count))


def flip(weights):
    return weights.astype(F32).T.astype(BF16)


def fetch(pairs, sems):
    copies = [pltpu.make_async_copy(src, dst, sems.at[i]) for i, (src, dst) in enumerate(pairs)]
    for copy in copies:
        copy.start()
    return copies


def encode(state, mask, inward, encoder_w, extent):
    width = state.shape[1]
    position = state[0:3]
    row = lax.broadcasted_iota(I32, (3, width), 0)
    size = jnp.where(row == 0, extent[0], jnp.where(row == 1, extent[1], extent[2]))
    features = jnp.concatenate(
        [
            state[3:9],
            jnp.clip(position, -1.0, 1.0),
            jnp.clip(size - position, -1.0, 1.0),
            jnp.zeros((4, width), F32),
        ],
        axis=0,
    )
    hidden = relu16(dot_tn(thirds(features), inward))
    hidden = relu16(dot(hidden, encoder_w[0]))
    column = jnp.broadcast_to(mask, (8, width)).T[:, 0:1]
    return (norm(dot(hidden, encoder_w[1]), 1) * column).astype(BF16)


def places(ids_low, ids_high, fold_y):
    plane = (ids_high * 43) >> 7
    ez = ids_high - plane * 3
    ey = plane & 3
    ex = plane >> 2
    if fold_y:
        row = jnp.where(ey == 1, 0, jnp.where(ey == 2, 1, 2))
    else:
        row = ey
    return ex * 4 + row, ids_low + jnp.where(ez == 1, 0, 128)


def pick(cells, place, key):
    width = cells[0][1].shape[0]
    chunk = 32
    window = jnp.concatenate(
        [ref[f : f + chunk] for f in range(0, width, chunk) for _, ref in cells], axis=0
    )
    key_rows = lax.broadcasted_iota(I32, (TILE, TILE), 0).astype(F32).astype(BF16)
    key = jnp.broadcast_to(key.astype(F32), (16, TILE)).astype(BF16)
    same = key_rows.reshape(TILE // 16, 16, TILE) == key[None]
    picker = jnp.where(same, jnp.ones((), BF16), jnp.zeros((), BF16)).reshape(TILE, TILE)
    found = dot(window, picker).reshape(width // chunk, len(cells), chunk // 8, 8, TILE)
    where = jnp.broadcast_to(place, (8, TILE))
    parts = []
    for f in range(width // chunk):
        part = jnp.zeros((chunk // 8, 8, TILE), F32)
        for i, (column, _) in enumerate(cells):
            part = jnp.where((where == column)[None], found[f, i], part)
        parts.append(part.reshape(chunk, TILE))
    return jnp.concatenate(parts, axis=0)


def messages(cells, place, key, pre, middle_t, final_t, hidden_ref):
    for tile in range(place.shape[1] // TILE):
        at = slice(tile * TILE, (tile + 1) * TILE)
        hidden_ref[:, at] = relu16(pre(tile) + pick(cells, place[:, at], key[:, at]))
    hidden = relu16(dot(middle_t, hidden_ref[...]))
    return norm(dot(final_t, hidden), 0)


class Window:
    def __init__(self, fold_y, own_ref=None, rest_ref=None):
        self.row_count = 3 if fold_y else 4
        self.own_rows = (0, 1) if fold_y else (1, 2)
        self.outer_rows = (2,) if fold_y else (0, 3)
        self.own_ref, self.rest_ref = own_ref, rest_ref

    def own(self, ex, row):
        return (ex - 1) * 2 + self.own_rows.index(row)

    def side(self, ex, row):
        count = len(self.outer_rows)
        return 2 * self.row_count + (ex - 1) * count + self.outer_rows.index(row)

    def cells(self, columns):
        found = []
        for ex, row in columns:
            if ex in (1, 2) and row in self.own_rows:
                ref = self.own_ref.at[self.own(ex, row)]
            elif ex in (1, 2):
                ref = self.rest_ref.at[self.side(ex, row)]
            else:
                ref = self.rest_ref.at[(0 if ex == 0 else self.row_count) + row]
            found.append((ex * 4 + row, ref))
        return found


def slot_sum(message, step):
    total = message[:, :step]
    for at in range(step, message.shape[1], step):
        total = total + message[:, at : at + step]
    return total


def advance(pre, aggregate, latent_t, weights_ref, decoder_out):
    pre = pre + dot(weights_ref[NODE_NEW], aggregate)
    hidden = relu16(dot(weights_ref[NODE_0], relu16(pre)))
    updated = (latent_t + norm(dot(weights_ref[NODE_1], hidden), 0)).astype(BF16)
    hidden = relu16(dot(weights_ref[DECODE_0], updated))
    hidden = relu16(dot(weights_ref[DECODE_1], hidden))
    return dot(decoder_out, hidden)


def moved(position, velocity, acceleration):
    new_velocity = velocity + acceleration
    return jnp.concatenate([position + new_velocity, new_velocity, velocity], axis=0)


def cut_kernel(fold_y, latent_any, latent_ref, edge_ref, inner_ref, sems):
    end = 1 - lax.axis_index("gz")
    inner = 1 - lax.axis_index("gy") if fold_y else 0
    copies = fetch(
        [
            (latent_any, latent_ref),
            (latent_any.at[end], edge_ref),
            (latent_any.at[0, inner], inner_ref.at[0]),
            (latent_any.at[1, inner], inner_ref.at[1]),
        ],
        sems,
    )
    for copy in copies:
        copy.wait()


def ranks_kernel(
    sizes,
    fill_ref,
    owners_any,
    edge_w_any,
    node_in_any,
    node_w_any,
    decoder_w_any,
    decoder_out_any,
    encoder_in_any,
    encoder_w_any,
    neighbours_any,
    positions_any,
    velocity_any,
    edge_any,
    latent_ref,
    weights_ref,
    decoder_out_ref,
    inward_ref,
    encoder_w_ref,
    alive_ref,
    neighbours_ref,
    edge_ref,
    spread_ref,
    latent_t_ref,
    node_pre_ref,
    state_ref,
    mover_edge_ref,
    mover_place_ref,
    mover_key_ref,
    mover_near_ref,
    mover_node_pre_ref,
    mover_latent_ref,
    mover_state_ref,
    positions_ref,
    velocity_ref,
    owners_ref,
    edge_w_ref,
    node_in_ref,
    node_w_ref,
    decoder_w_ref,
    encoder_in_ref,
    sems,
):
    count_x, count_y, count_z = sizes
    fold_y = count_y == 2
    copies = fetch(
        [
            (owners_any, owners_ref),
            (edge_w_any, edge_w_ref),
            (node_in_any, node_in_ref),
            (node_w_any, node_w_ref),
            (decoder_w_any, decoder_w_ref),
            (decoder_out_any, decoder_out_ref),
            (encoder_in_any, encoder_in_ref),
            (encoder_w_any, encoder_w_ref),
            (neighbours_any, neighbours_ref),
            (positions_any, positions_ref),
            (velocity_any, velocity_ref),
            (edge_any, edge_ref),
        ],
        sems,
    )
    copies[0].wait()
    index_x = lax.axis_index("gx")
    index_y = lax.axis_index("gy")
    index_z = lax.axis_index("gz")
    slots = owners_ref.shape[-1]
    width = node_in_ref.shape[-1]
    for a, b in CELLS:
        alive_ref[a, b] = jnp.where(
            lax.broadcasted_iota(I32, (1, slots), 1) < fill_ref[a, 0, b], 1.0, 0.0
        )

    lane = lax.broadcasted_iota(I32, (1, slots), 1)
    owner = jnp.concatenate([owners_ref[a, b] for a, b in CELLS], axis=1)
    alive = jnp.concatenate([jnp.where(lane < fill_ref[a, 0, b], 1, 0) for a, b in CELLS], axis=1)
    own_block = (index_x * count_y + index_y) * count_z + index_z
    stays = jnp.where((alive == 1) & (owner == own_block), 1.0, 0.0)
    moving = jnp.where((alive == 1) & (owner != own_block), 1, 0)
    owner_x = quotient(owner, count_y * count_z)
    rest = owner - owner_x * (count_y * count_z)
    owner_y = quotient(rest, count_z)
    owner_z = rest - owner_y * count_z
    step_y = owner_y - index_y
    side_y = jnp.where(step_y == 0, 0, 1) if fold_y else jnp.where(step_y < 0, 1, 2 * step_y)
    options_y = 2 if fold_y else 3
    group = ((owner_x - index_x + 1) * options_y + side_y) * 2 + jnp.where(owner_z == index_z, 0, 1)
    group_rows = (3 * options_y * 2 + 15) // 16 * 16
    particles = owner.shape[1]
    member = jnp.where(
        (lax.broadcasted_iota(I32, (group_rows, particles), 0) == group) & (moving == 1), 1.0, 0.0
    )
    triangle = jnp.where(
        lax.broadcasted_iota(I32, (slots, slots), 0) <= lax.broadcasted_iota(I32, (slots, slots), 1),
        1.0,
        0.0,
    ).astype(BF16)
    counted = []
    before = jnp.zeros((group_rows, 1), F32)
    for i in range(4):
        inside = member[:, i * slots : (i + 1) * slots]
        counted.append(dot(inside.astype(BF16), triangle) + before)
        before = before + jnp.sum(inside, axis=1, keepdims=True)
    counted = jnp.concatenate(counted, axis=1)
    rank = (jnp.sum(counted * member, axis=0, keepdims=True) - 1.0).astype(I32)
    column = jnp.where(moving == 1, group * CAP + rank, -1)
    movers = mover_state_ref.shape[1]
    placer = jnp.where(
        lax.broadcasted_iota(I32, (movers, particles), 0) == column, 1.0, 0.0
    ).astype(BF16)

    line = lax.broadcasted_iota(I32, spread_ref.shape, 1)
    direction = line >> 3
    direction = direction + jnp.where(direction > 12, 1, 0)
    plane = (direction * 57) >> 9
    from_z = direction - 3 * ((direction * 43) >> 7) - 1
    from_y = ((direction * 43) >> 7) - 3 * plane - 1
    if fold_y:
        side_y = jnp.where(from_y == 0, 0, 1)
        valid = (from_y == 0) | (from_y == 1 - 2 * index_y)
    else:
        side_y = jnp.where(from_y < 0, 2, from_y)
        valid = from_y < 2
    side_z = jnp.where(from_z == 0, 0, 1)
    valid = valid & ((from_z == 0) | (from_z == 1 - 2 * index_z)) & (line < 26 * CAP)
    target = ((2 - plane) * options_y + side_y) * 2 + side_z
    spread_ref[...] = jnp.where(valid, target * CAP + (line & 7), -1)

    for copy in copies[1:-1]:
        copy.wait()
    for i in range(5):
        weights_ref[i] = flip(edge_w_ref[i])
    weights_ref[NODE_OLD] = flip(node_in_ref[:width])
    weights_ref[NODE_NEW] = flip(node_in_ref[width:])
    for i in range(2):
        weights_ref[NODE_0 + i] = flip(node_w_ref[i])
        weights_ref[DECODE_0 + i] = flip(decoder_w_ref[i])
    inward = jnp.concatenate([encoder_in_ref[...].astype(F32), jnp.zeros((4, width), F32)], axis=0)
    inward = inward.astype(BF16)
    inward_ref[...] = jnp.concatenate([inward, inward, inward], axis=0)

    latent = jnp.concatenate([latent_ref[a, b, 0] for a, b in CELLS], axis=0)
    latent_t_ref[...] = latent.astype(F32).T
    node_pre_ref[...] = dot_nt(weights_ref[NODE_OLD], latent)

    def flat(ref, i):
        return jnp.concatenate([ref[i, a, b] for a, b in CELLS], axis=1)

    state = [flat(positions_ref, i) for i in range(3)] + [flat(velocity_ref, i) for i in range(3)]
    state_ref[...] = jnp.concatenate(state + [stays, jnp.zeros_like(stays)], axis=0)

    mover_latent = dot(placer, latent).astype(BF16)
    mover_latent_ref[...] = mover_latent.astype(F32).T
    mover_node_pre_ref[...] = dot_nt(weights_ref[NODE_OLD], mover_latent)
    mover_near_ref[...] = dot_nt(weights_ref[NEAR], mover_latent)
    state = jnp.concatenate(state + [moving.astype(F32), jnp.zeros_like(stays)], axis=0)
    mover_state_ref[...] = joined(dot_nt(thirds(state), placer))
    neighbour_count = edge_ref.shape[3]
    ids = jnp.concatenate(
        [
            jnp.concatenate([neighbours_ref[a, b, k] for a, b in CELLS], axis=1)
            for k in range(neighbour_count)
        ],
        axis=0,
    )
    ids = jnp.concatenate([ids & 127, ids >> 7, jnp.zeros((8, particles), I32)], axis=0)
    ids = dot_nt(ids.astype(F32).astype(BF16), placer).astype(I32)
    place, key = places(ids[:neighbour_count], ids[neighbour_count : 2 * neighbour_count], fold_y)
    mover_place_ref[...] = jnp.concatenate([place[k : k + 1] for k in range(neighbour_count)], axis=1)
    mover_key_ref[...] = jnp.concatenate([key[k : k + 1] for k in range(neighbour_count)], axis=1)
    copies[-1].wait()
    for k in range(neighbour_count):
        rows = jnp.concatenate([edge_ref[a, b, 0, k] for a, b in CELLS], axis=0)
        mover_edge_ref[k] = dot(placer, rows).astype(BF16)


def prepare_kernel(
    sizes,
    latent_ref,
    own_zed,
    mine_ref,
    weights_ref,
    edge_ref,
    place_ref,
    key_ref,
    near_ref,
    far_ref,
    far_mine_ref,
    pre_ref,
):
    window = Window(sizes[1] == 2, far_ref)
    core = lax.axis_index("gz")
    far_t = weights_ref[FAR]
    columns = [(ex, row) for ex in (1, 2) for row in window.own_rows]
    for (ex, row), (a, b) in zip(columns, CELLS):
        pair = jnp.concatenate([latent_ref[a, b, 0], own_zed[a, b, 0]], axis=0)
        far_ref[window.own(ex, row)] = dot_nt(far_t, pair).astype(BF16)
    cells = window.cells(columns)
    for row in range(window.row_count):
        pair = jnp.concatenate([mine_ref[1, row], mine_ref[0, row]], axis=0)
        far_mine_ref[row] = dot_nt(far_t, pair).astype(BF16)
        cells.append((12 * (1 - core) + row, far_mine_ref.at[row]))
    neighbour_count, movers = edge_ref.shape[:2]
    step = TILE // movers
    near = jnp.concatenate([near_ref[...]] * step, axis=1)
    for tile in range(neighbour_count // step):
        edges = jnp.concatenate([edge_ref[k] for k in range(tile * step, (tile + 1) * step)], axis=0)
        at = slice(tile * TILE, (tile + 1) * TILE)
        pre_ref[:, at] = (
            dot_nt(weights_ref[EDGE], edges) + near + pick(cells, place_ref[:, at], key_ref[:, at])
        )


def movers_kernel(
    sizes,
    side_count,
    *refs,
):
    fold_y = sizes[1] == 2
    side_refs, refs = refs[:side_count], refs[side_count:]
    side_zeds, refs = refs[:side_count], refs[side_count:]
    other_ref, far_mine_ref, refs = refs[0], refs[1], refs[2:]
    (
        weights_ref,
        decoder_out_ref,
        pre_ref,
        place_ref,
        key_ref,
        node_pre_ref,
        latent_t_ref,
        state_ref,
        far_ref,
        bucket_ref,
        hidden_ref,
    ) = refs
    window = Window(fold_y, None, far_ref)
    row_count = window.row_count
    core = lax.axis_index("gz")
    far_t = weights_ref[FAR]

    def far(at, here, beside):
        pair = jnp.concatenate([here, beside], axis=0)
        far_ref[at] = dot_nt(far_t, pair).astype(BF16)

    for row in range(row_count):
        far(core * row_count + row, other_ref[0, row], other_ref[1, row])
    for side, row in enumerate(window.outer_rows):
        for ex in (1, 2):
            far(window.side(ex, row), side_refs[side][ex - 1], side_zeds[side][ex - 1])

    movers = state_ref.shape[1]
    for row in range(row_count):
        far_ref[(1 - core) * row_count + row] = far_mine_ref[row]
    cells = [(12 * core + row, far_ref.at[core * row_count + row]) for row in range(row_count)]
    cells += window.cells([(ex, row) for ex in (1, 2) for row in window.outer_rows])
    message = messages(
        cells,
        place_ref[...],
        key_ref[...],
        lambda tile: pre_ref[:, tile * TILE : (tile + 1) * TILE],
        weights_ref[MIDDLE],
        weights_ref[FINAL],
        hidden_ref,
    )
    aggregate = slot_sum(message, movers).astype(BF16)
    acceleration = advance(
        node_pre_ref[...], aggregate, latent_t_ref[...], weights_ref, decoder_out_ref[...]
    )
    mask = state_ref[6:7]
    state = moved(state_ref[0:3], state_ref[3:6], acceleration) * mask
    bucket_ref[...] = jnp.concatenate([state, mask, jnp.zeros((ROWS - 10, movers), F32)], axis=0)


def edges_kernel(
    sizes,
    a,
    alive_ref,
    latent_ref,
    edge_ref,
    neighbours_ref,
    far_own_ref,
    far_rest_ref,
    weights_ref,
    total_ref,
    hidden_ref,
):
    fold_y = sizes[1] == 2
    window = Window(fold_y, far_own_ref, far_rest_ref)
    index_y = lax.axis_index("gy")
    alive_ref, latent_ref = alive_ref.at[a], latent_ref.at[a]
    edge_ref, neighbours_ref = edge_ref.at[a], neighbours_ref.at[a]
    slots, width = latent_ref.shape[-2:]
    neighbour_count = edge_ref.shape[2]
    for bt in range(2):
        if fold_y:
            b = index_y if bt == 0 else 1 - index_y
            rows = (0, 1) if bt == 0 else (0, 1, 2)
        else:
            b = bt
            rows = (bt, bt + 1, bt + 2)
        columns = [(ex, row) for ex in range(a, a + 3) for row in rows]
        near = dot_nt(weights_ref[NEAR], latent_ref[b, 0])
        near = jnp.concatenate([near, near], axis=1)
        ids = jnp.concatenate([neighbours_ref[b, k] for k in range(neighbour_count)], axis=1)
        place, key = places(ids & 127, ids >> 7, fold_y)

        def pre(tile, b=b, near=near):
            edges = jnp.concatenate([edge_ref[b, 0, 2 * tile], edge_ref[b, 0, 2 * tile + 1]], axis=0)
            return dot_nt(weights_ref[EDGE], edges) + near

        message = messages(
            window.cells(columns),
            place,
            key,
            pre,
            weights_ref[MIDDLE],
            weights_ref[FINAL],
            hidden_ref.at[bt],
        )
        total = jnp.where(alive_ref[b] > 0.5, slot_sum(message, slots), 0.0)
        total_ref[b] = total.astype(BF16)


def nodes_kernel(
    first_ref,
    second_ref,
    node_pre_ref,
    latent_t_ref,
    state_ref,
    weights_ref,
    decoder_out_ref,
    moved_ref,
):
    aggregate = jnp.concatenate([first_ref[0], first_ref[1], second_ref[0], second_ref[1]], axis=1)
    acceleration = advance(
        node_pre_ref[...], aggregate, latent_t_ref[...], weights_ref, decoder_out_ref[...]
    )
    state = moved(state_ref[0:3], state_ref[3:6], acceleration)
    moved_ref[...] = jnp.concatenate(
        [state, state_ref[6:7], jnp.zeros((ROWS - 10, state.shape[1]), F32)], axis=0
    )


def finish_kernel(
    sizes,
    moved_ref,
    tiles_ref,
    zeds_ref,
    spread_ref,
    inward_ref,
    encoder_w_ref,
    kept_latent_ref,
    kept_state_ref,
    arrived_latent_ref,
    arrived_state_ref,
):
    count_x, count_y, count_z = sizes
    extent = (2.0 * count_x, 2.0 * count_y, 1.0 * count_z)
    slots = kept_latent_ref.shape[-2]
    stays = moved_ref[9:10]
    kept = moved_ref[:9] * stays
    latents = encode(moved_ref[:9], stays, inward_ref[...], encoder_w_ref[...], extent)
    for i, (a, b) in enumerate(CELLS):
        kept_latent_ref[a, b, 0] = latents[i * slots : (i + 1) * slots]
        for j in range(9):
            kept_state_ref[j, a, b] = kept[j : j + 1, i * slots : (i + 1) * slots]
    fold_y = count_y == 2
    index_x = lax.axis_index("gx")
    options_y = 2 if fold_y else 3
    lanes = tiles_ref.shape[-1]
    group = lax.broadcasted_iota(I32, (ROWS, lanes), 1) >> 3
    even = (index_x & 1) == 0
    found = jnp.zeros((ROWS, lanes), F32)
    for source_x in (-1, 0, 1):
        for from_y in range(options_y):
            for from_z in range(2):
                if source_x == 0 and from_y == 0 and from_z == 0:
                    continue
                ref = tiles_ref if from_z == 0 else zeds_ref
                own, second, first = ref.at[0], ref.at[1], ref.at[2]
                side_y = from_y if fold_y or from_y == 0 else 3 - from_y
                target = ((1 - source_x) * options_y + side_y) * 2 + from_z
                if source_x == 0:
                    tile = own[from_y]
                    there = group == target
                elif source_x == -1:
                    tile = jnp.where(even, second[from_y], first[from_y])
                    there = (group == target) & (index_x > 0)
                else:
                    tile = jnp.where(even, first[from_y], second[from_y])
                    there = (group == target) & (index_x < count_x - 1)
                found = jnp.where(there, tile, found)
    halves = []
    for at in range(0, spread_ref.shape[1], 128):
        lane = jnp.broadcast_to(spread_ref[0:1, at : at + 128], (ROWS, 128))
        half = jnp.zeros((ROWS, 128), F32)
        for base in range(0, lanes, 128):
            index = jnp.clip(lane - base, 0, 127)
            there = (lane >= base) & (lane < base + 128)
            part = jnp.take_along_axis(found[:, base : base + 128], index, axis=1)
            half = jnp.where(there, part, half)
        halves.append(half)
    arrived = jnp.concatenate(halves, axis=1)[:, : 26 * CAP]
    for j in range(9):
        arrived_state_ref[j, 0, 0] = arrived[j : j + 1]
    arrived_latent_ref[0, 0, 0] = encode(
        arrived[:9], arrived[9:10], inward_ref[...], encoder_w_ref[...], extent
    )


def swap(values, axis):
    return lax.ppermute(values, axis, [(0, 1), (1, 0)])


def shift(values, axis, way):
    pairs = [(i, i + 1) for i in range(lax.axis_size(axis) - 1)]
    return lax.ppermute(values, axis, [(j, i) for i, j in pairs] if way else pairs)


def swap_x(values, first):
    count = lax.axis_size("gx")
    pairs = []
    for x in range(count):
        partner = x + 1 if (x - first) % 2 == 0 else x - 1
        for z in range(2):
            if 0 <= partner < count:
                pairs.append((x * 2 + z, partner * 2 + z))
            else:
                pairs.append((x * 2 + z, x * 2 + 1 - z))
    return lax.ppermute(values, ("gx", "gz"), pairs)


def swap_chips(values, cross):
    count_x, count_y, count_z = (lax.axis_size(axis) for axis in ("gx", "gy", "gz"))
    pairs = []
    for x in range(count_x):
        for y in range(count_y):
            for z in range(count_z):
                to_x = x + 1 - 2 * z
                if 0 <= to_x < count_x:
                    to = (to_x, y ^ 1 if cross else y, 1 - z)
                else:
                    to = (x, y ^ 1, z)
                pairs.append(((x * count_y + y) * count_z + z, (to[0] * count_y + to[1]) * count_z + to[2]))
    return lax.ppermute(values, ("gx", "gy", "gz"), pairs)


def call(kernel, name, in_specs, outs, scratch, operands, flops):
    return pl.pallas_call(
        kernel,
        out_shape=tuple(jax.ShapeDtypeStruct(shape, kind) for shape, kind in outs),
        in_specs=in_specs,
        out_specs=tuple(VMEM for _ in outs),
        scratch_shapes=scratch,
        compiler_params=pltpu.CompilerParams(vmem_limit_bytes=32 * 1024 * 1024),
        cost_estimate=pl.CostEstimate(flops=flops, bytes_accessed=0, transcendentals=0),
        name=name,
    )(*operands)


def in_hbm(array):
    return pltpu.with_memory_space_constraint(array, pltpu.HBM)


def like(array):
    return pltpu.VMEM(array.shape, array.dtype)


def body(
    node_latent,
    edge_latent,
    positions,
    velocity,
    fill,
    neighbours,
    owners,
    edge_weights,
    node_in,
    node_weights,
    decoder_weights,
    decoder_out,
    encoder_in,
    encoder_weights,
):
    sizes = tuple(lax.axis_size(axis) for axis in ("gx", "gy", "gz"))
    fold_y = sizes[1] == 2
    slots, width = node_latent.shape[-2:]
    neighbour_count = neighbours.shape[3]
    particles = 4 * slots
    options_y = 2 if fold_y else 3
    movers = (3 * options_y * 2 * CAP + 127) // 128 * 128
    rows = 3 if fold_y else 4
    fill = jnp.transpose(fill, (0, 2, 1))
    neighbours = neighbours.reshape(2, 2, neighbour_count, 1, slots)

    own_zed = swap(node_latent, "gz")
    latent, end, inner = call(
        functools.partial(cut_kernel, fold_y),
        "cut",
        [ANY],
        [
            (node_latent.shape, BF16),
            (node_latent.shape[1:], BF16),
            ((2, 1, slots, width), BF16),
        ],
        [pltpu.SemaphoreType.DMA((4,))],
        (in_hbm(node_latent),),
        1_000_000,
    )
    core = lax.axis_index("gz")
    if fold_y:
        row = 1 - lax.axis_index("gy")
        beside = lax.dynamic_index_in_dim(own_zed[:, :, 0], 1 - core, 0, False)
        corner = jnp.concatenate(
            [lax.dynamic_slice_in_dim(part, row, 1, 0) for part in (end[:, 0], beside)], axis=0
        )
        both = jnp.stack([end[:, 0], beside])
        corner, inner = lax.optimization_barrier((corner, inner))
        mine = [swap_chips(corner[:, None], True)]
        sides = [swap(inner[:, 0], "gy")]
        mine.append(swap_chips(both, False))
    else:
        sides = [shift(latent[:, 1, 0], "gy", 0), shift(latent[:, 0, 0], "gy", 1)]
        side_zeds = [swap(part, "gz") for part in sides]
        layers = []
        for middle, outer in ((latent, sides), (own_zed, side_zeds)):
            parts = [outer[0][:, None], middle[:, :, 0], outer[1][:, None]]
            parts = [lax.dynamic_index_in_dim(part, 1 - core, 0, False) for part in parts]
            layers.append(jnp.concatenate(parts, axis=0))
        mine = [swap_chips(jnp.stack(layers), False)]

    ranked = call(
        functools.partial(ranks_kernel, sizes),
        "ranks",
        [SMEM] + [ANY] * 12 + [VMEM],
        [
            ((11, width, width), BF16),
            (decoder_out.shape, BF16),
            ((48, width), BF16),
            (encoder_weights.shape, BF16),
            ((2, 2, 1, slots), F32),
            (neighbours.shape, I32),
            (edge_latent.shape, BF16),
            ((8, 256), I32),
            ((width, particles), F32),
            ((width, particles), F32),
            ((8, particles), F32),
            ((neighbour_count, movers, width), BF16),
            ((1, neighbour_count * movers), I32),
            ((1, neighbour_count * movers), I32),
            ((width, movers), F32),
            ((width, movers), F32),
            ((width, movers), F32),
            ((8, movers), F32),
        ],
        [
            like(positions),
            like(velocity),
            like(owners),
            like(edge_weights),
            like(node_in),
            like(node_weights),
            like(decoder_weights),
            like(encoder_in),
            pltpu.SemaphoreType.DMA((12,)),
        ],
        [
            in_hbm(array)
            for array in (
                fill,
                owners,
                edge_weights,
                node_in,
                node_weights,
                decoder_weights,
                decoder_out,
                encoder_in,
                encoder_weights,
                neighbours,
                positions,
                velocity,
                edge_latent,
            )
        ]
        + [latent],
        5_000_000_000,
    )
    mine, sides, ranked = lax.optimization_barrier((mine, sides, ranked))
    (
        weights,
        decoder_out,
        inward,
        encoder_weights,
        alive,
        neighbours,
        edge_latent,
        spread,
        latent_t,
        node_pre,
        state,
        mover_edges,
        mover_place,
        mover_key,
        mover_near,
        mover_node_pre,
        mover_latent,
        mover_state,
    ) = ranked
    mine = jnp.concatenate(mine[::-1], axis=1)
    if fold_y:
        packed = jnp.concatenate([mine.reshape(-1, slots, width), sides[0]], axis=0)
    else:
        packed = mine.reshape(-1, slots, width)
    packed = swap(packed, "gz")
    prepared = call(
        functools.partial(prepare_kernel, sizes),
        "prepare",
        [VMEM] * 8,
        [
            ((4, width, 2 * slots), BF16),
            ((rows, width, 2 * slots), BF16),
            ((width, neighbour_count * movers), F32),
        ],
        [],
        (latent, own_zed, mine, weights, mover_edges, mover_place, mover_key, mover_near),
        5_000_000_000,
    )
    packed, prepared = lax.optimization_barrier((packed, prepared))
    cells = mine.shape[0] * mine.shape[1]
    if fold_y:
        side_zeds = [packed[cells:]]
    far_own, far_mine, mover_pre = prepared
    halo = [*sides, *side_zeds, packed[:cells].reshape(mine.shape), far_mine]

    far_rest, bucket = call(
        functools.partial(movers_kernel, sizes, len(sides)),
        "movers",
        [VMEM] * (len(halo) + 8),
        [((4 * rows - 4, width, 2 * slots), BF16), ((ROWS, movers), F32)],
        [pltpu.VMEM((width, neighbour_count * movers), BF16)],
        (
            *halo,
            weights,
            decoder_out,
            mover_pre,
            mover_place,
            mover_key,
            mover_node_pre,
            mover_latent,
            mover_state,
        ),
        3_000_000_000,
    )

    def edges(a):
        return call(
            functools.partial(edges_kernel, sizes, a),
            "edges",
            [VMEM] * 7,
            [((2, width, slots), BF16)],
            [pltpu.VMEM((2, width, neighbour_count * slots), BF16)],
            (alive, latent, edge_latent, neighbours, far_own, far_rest, weights),
            4_000_000_000,
        )[0]

    first = edges(0)
    if fold_y:
        tiles = [swap(bucket, "gy")]
    else:
        tiles = [shift(bucket, "gy", 0), shift(bucket, "gy", 1)]
    tiles, first = lax.optimization_barrier((tiles, first))
    tiles = jnp.stack([bucket, *tiles], axis=0)
    second = edges(1)
    sided = [swap_x(tiles, 1), swap_x(tiles, 0)]
    sided, second = lax.optimization_barrier((sided, second))
    tiles = jnp.stack([tiles, *sided], axis=0)
    zeds = swap(tiles, "gz")
    state = call(
        nodes_kernel,
        "nodes",
        [VMEM] * 7,
        [((ROWS, particles), F32)],
        [],
        (first, second, node_pre, latent_t, state, weights, decoder_out),
        1_000_000_000,
    )[0]
    zeds, state = lax.optimization_barrier((zeds, state))
    return call(
        functools.partial(finish_kernel, sizes),
        "finish",
        [VMEM] * 6,
        [
            (node_latent.shape, BF16),
            ((9,) + node_latent.shape[:4], F32),
            ((1, 1, 1, 26 * CAP, width), BF16),
            ((9, 1, 1, 1, 26 * CAP), F32),
        ],
        [],
        (state, tiles, zeds, spread, inward, encoder_weights),
        1_000_000_000,
    )


def solution(mesh):
    placed = (
        P(("group", "gx"), "gy", "gz", None, None),
        P(("group", "gx"), "gy", "gz", None, None, None),
        P(None, ("group", "gx"), "gy", "gz", None),
        P(None, ("group", "gx"), "gy", "gz", None),
        P(("group", "gx"), "gy", "gz"),
        P(("group", "gx"), "gy", "gz", None, None),
        P(("group", "gx"), "gy", "gz", None),
        P(),
        P(),
        P(),
        P(),
        P(),
        P(),
        P(),
    )
    return jax.shard_map(
        body,
        mesh=mesh,
        in_specs=placed,
        out_specs=(
            P(("group", "gx"), "gy", "gz", None, None),
            P(None, ("group", "gx"), "gy", "gz", None),
            P(("group", "gx"), "gy", "gz", None, None),
            P(None, ("group", "gx"), "gy", "gz", None),
        ),
        check_vma=False,
    )
```

```python
import functools

import jax
import jax.numpy as jnp
from jax import lax
from jax.experimental import pallas as pl
from jax.experimental.pallas import tpu as pltpu
from jax.sharding import PartitionSpec as P

CAP = 8
F32 = jnp.float32
BF16 = jnp.bfloat16
I32 = jnp.int32
ROWS = 16
TILE = 256
CELLS = [(a, b) for a in range(2) for b in range(2)]
EDGE, NEAR, FAR, MIDDLE, FINAL, NODE_OLD, NODE_NEW, NODE_0, NODE_1, DECODE_0, DECODE_1 = range(11)

VMEM = pl.BlockSpec(memory_space=pltpu.VMEM)
SMEM = pl.BlockSpec(memory_space=pltpu.SMEM)
ANY = pl.BlockSpec(memory_space=pl.ANY)


def dot(left, right):
    return jnp.dot(left, right, preferred_element_type=F32)


def dot_nt(left, right):
    return lax.dot_general(left, right, (((1,), (1,)), ((), ())), preferred_element_type=F32)


def dot_tn(left, right):
    return lax.dot_general(left, right, (((0,), (0,)), ((), ())), preferred_element_type=F32)


def relu16(values):
    return jnp.maximum(values, 0.0).astype(BF16)


def norm(values, axis):
    scale = 1.0 / values.shape[axis]
    centred = values - jnp.sum(values, axis=axis, keepdims=True) * scale
    spread = jnp.sum(centred * centred, axis=axis, keepdims=True) * scale
    return centred * lax.rsqrt(spread + 1e-05)


def thirds(values):
    high = values.astype(BF16)
    rest = values - high.astype(F32)
    middle = rest.astype(BF16)
    low = (rest - middle.astype(F32)).astype(BF16)
    return jnp.concatenate([high, middle, low], axis=0)


def joined(values):
    rows = values.shape[0] // 3
    return values[:rows] + values[rows : 2 * rows] + values[2 * rows :]


def quotient(values, count):
    if count & (count - 1) == 0:
        return values >> (count.bit_length() - 1)
    return lax.div(values, jnp.full_like(values, count))


def flip(weights):
    return weights.astype(F32).T.astype(BF16)


def fetch(pairs, sems):
    copies = [pltpu.make_async_copy(src, dst, sems.at[i]) for i, (src, dst) in enumerate(pairs)]
    for copy in copies:
        copy.start()
    return copies


def encode(state, mask, inward, encoder_w, extent):
    width = state.shape[1]
    position = state[0:3]
    row = lax.broadcasted_iota(I32, (3, width), 0)
    size = jnp.where(row == 0, extent[0], jnp.where(row == 1, extent[1], extent[2]))
    features = jnp.concatenate(
        [
            state[3:9],
            jnp.clip(position, -1.0, 1.0),
            jnp.clip(size - position, -1.0, 1.0),
            jnp.zeros((4, width), F32),
        ],
        axis=0,
    )
    hidden = relu16(dot_tn(thirds(features), inward))
    hidden = relu16(dot(hidden, encoder_w[0]))
    column = jnp.broadcast_to(mask, (8, width)).T[:, 0:1]
    return (norm(dot(hidden, encoder_w[1]), 1) * column).astype(BF16)


def places(ids_low, ids_high, fold_y):
    plane = (ids_high * 43) >> 7
    ez = ids_high - plane * 3
    ey = plane & 3
    ex = plane >> 2
    if fold_y:
        row = jnp.where(ey == 1, 0, jnp.where(ey == 2, 1, 2))
    else:
        row = ey
    return ex * 4 + row, ids_low + jnp.where(ez == 1, 0, 128)


def pick(cells, place, key):
    width = cells[0][1].shape[0]
    chunk = 32
    window = jnp.concatenate(
        [ref[f : f + chunk] for f in range(0, width, chunk) for _, ref in cells], axis=0
    )
    key_rows = lax.broadcasted_iota(I32, (TILE, TILE), 0).astype(F32).astype(BF16)
    key = jnp.broadcast_to(key.astype(F32), (16, TILE)).astype(BF16)
    same = key_rows.reshape(TILE // 16, 16, TILE) == key[None]
    picker = jnp.where(same, jnp.ones((), BF16), jnp.zeros((), BF16)).reshape(TILE, TILE)
    found = dot(window, picker).reshape(width // chunk, len(cells), chunk // 8, 8, TILE)
    where = jnp.broadcast_to(place, (8, TILE))
    parts = []
    for f in range(width // chunk):
        part = jnp.zeros((chunk // 8, 8, TILE), F32)
        for i, (column, _) in enumerate(cells):
            part = jnp.where((where == column)[None], found[f, i], part)
        parts.append(part.reshape(chunk, TILE))
    return jnp.concatenate(parts, axis=0)


def messages(cells, place, key, pre, middle_t, final_t, hidden_ref):
    for tile in range(place.shape[1] // TILE):
        at = slice(tile * TILE, (tile + 1) * TILE)
        hidden_ref[:, at] = relu16(pre(tile) + pick(cells, place[:, at], key[:, at]))
    hidden = relu16(dot(middle_t, hidden_ref[...]))
    return norm(dot(final_t, hidden), 0)


class Window:
    def __init__(self, fold_y, own_ref=None, rest_ref=None):
        self.row_count = 3 if fold_y else 4
        self.own_rows = (0, 1) if fold_y else (1, 2)
        self.outer_rows = (2,) if fold_y else (0, 3)
        self.own_ref, self.rest_ref = own_ref, rest_ref

    def own_columns(self):
        return [(ex, row) for ex in (1, 2) for row in self.own_rows]

    def own(self, ex, row):
        return (ex - 1) * 2 + self.own_rows.index(row)

    def side(self, ex, row):
        count = len(self.outer_rows)
        return 2 * self.row_count + (ex - 1) * count + self.outer_rows.index(row)

    def cells(self, columns):
        found = []
        for ex, row in columns:
            if ex in (1, 2) and row in self.own_rows:
                ref = self.own_ref.at[self.own(ex, row)]
            elif ex in (1, 2):
                ref = self.rest_ref.at[self.side(ex, row)]
            else:
                ref = self.rest_ref.at[(0 if ex == 0 else self.row_count) + row]
            found.append((ex * 4 + row, ref))
        return found


def slot_sum(message, step):
    total = message[:, :step]
    for at in range(step, message.shape[1], step):
        total = total + message[:, at : at + step]
    return total


def advance(pre, aggregate, latent_t, weights_ref, decoder_out):
    pre = pre + dot(weights_ref[NODE_NEW], aggregate)
    hidden = relu16(dot(weights_ref[NODE_0], relu16(pre)))
    updated = (latent_t + norm(dot(weights_ref[NODE_1], hidden), 0)).astype(BF16)
    hidden = relu16(dot(weights_ref[DECODE_0], updated))
    hidden = relu16(dot(weights_ref[DECODE_1], hidden))
    return dot(decoder_out, hidden)


def moved(position, velocity, acceleration):
    new_velocity = velocity + acceleration
    return jnp.concatenate([position + new_velocity, new_velocity, velocity], axis=0)


def cut_kernel(latent_any, latent_ref, edge_ref, sems):
    end = 1 - lax.axis_index("gz")
    copies = fetch([(latent_any, latent_ref), (latent_any.at[end], edge_ref)], sems)
    for copy in copies:
        copy.wait()


def ranks_kernel(
    sizes,
    fill_ref,
    owners_any,
    edge_w_any,
    node_in_any,
    node_w_any,
    decoder_w_any,
    decoder_out_any,
    encoder_in_any,
    encoder_w_any,
    neighbours_any,
    positions_any,
    velocity_any,
    edge_any,
    latent_ref,
    own_zed,
    weights_ref,
    decoder_out_ref,
    inward_ref,
    encoder_w_ref,
    alive_ref,
    neighbours_ref,
    edge_ref,
    spread_ref,
    latent_t_ref,
    node_pre_ref,
    state_ref,
    mover_edge_ref,
    mover_place_ref,
    mover_key_ref,
    mover_near_ref,
    mover_node_pre_ref,
    mover_latent_ref,
    mover_state_ref,
    far_ref,
    early_ref,
    positions_ref,
    velocity_ref,
    owners_ref,
    edge_w_ref,
    node_in_ref,
    node_w_ref,
    decoder_w_ref,
    encoder_in_ref,
    sems,
):
    count_x, count_y, count_z = sizes
    fold_y = count_y == 2
    copies = fetch(
        [
            (owners_any, owners_ref),
            (edge_w_any, edge_w_ref),
            (node_in_any, node_in_ref),
            (node_w_any, node_w_ref),
            (decoder_w_any, decoder_w_ref),
            (decoder_out_any, decoder_out_ref),
            (encoder_in_any, encoder_in_ref),
            (encoder_w_any, encoder_w_ref),
            (neighbours_any, neighbours_ref),
            (positions_any, positions_ref),
            (velocity_any, velocity_ref),
            (edge_any, edge_ref),
        ],
        sems,
    )
    copies[0].wait()
    index_x = lax.axis_index("gx")
    index_y = lax.axis_index("gy")
    index_z = lax.axis_index("gz")
    slots = owners_ref.shape[-1]
    width = node_in_ref.shape[-1]
    for a, b in CELLS:
        alive_ref[a, b] = jnp.where(
            lax.broadcasted_iota(I32, (1, slots), 1) < fill_ref[a, 0, b], 1.0, 0.0
        )

    lane = lax.broadcasted_iota(I32, (1, slots), 1)
    owner = jnp.concatenate([owners_ref[a, b] for a, b in CELLS], axis=1)
    alive = jnp.concatenate([jnp.where(lane < fill_ref[a, 0, b], 1, 0) for a, b in CELLS], axis=1)
    own_block = (index_x * count_y + index_y) * count_z + index_z
    stays = jnp.where((alive == 1) & (owner == own_block), 1.0, 0.0)
    moving = jnp.where((alive == 1) & (owner != own_block), 1, 0)
    owner_x = quotient(owner, count_y * count_z)
    rest = owner - owner_x * (count_y * count_z)
    owner_y = quotient(rest, count_z)
    owner_z = rest - owner_y * count_z
    step_y = owner_y - index_y
    side_y = jnp.where(step_y == 0, 0, 1) if fold_y else jnp.where(step_y < 0, 1, 2 * step_y)
    options_y = 2 if fold_y else 3
    group = ((owner_x - index_x + 1) * options_y + side_y) * 2 + jnp.where(owner_z == index_z, 0, 1)
    group_rows = (3 * options_y * 2 + 15) // 16 * 16
    particles = owner.shape[1]
    member = jnp.where(
        (lax.broadcasted_iota(I32, (group_rows, particles), 0) == group) & (moving == 1), 1.0, 0.0
    )
    triangle = jnp.where(
        lax.broadcasted_iota(I32, (slots, slots), 0) <= lax.broadcasted_iota(I32, (slots, slots), 1),
        1.0,
        0.0,
    ).astype(BF16)
    counted = []
    before = jnp.zeros((group_rows, 1), F32)
    for i in range(4):
        inside = member[:, i * slots : (i + 1) * slots]
        counted.append(dot(inside.astype(BF16), triangle) + before)
        before = before + jnp.sum(inside, axis=1, keepdims=True)
    counted = jnp.concatenate(counted, axis=1)
    rank = (jnp.sum(counted * member, axis=0, keepdims=True) - 1.0).astype(I32)
    column = jnp.where(moving == 1, group * CAP + rank, -1)
    movers = mover_state_ref.shape[1]
    placer = jnp.where(
        lax.broadcasted_iota(I32, (movers, particles), 0) == column, 1.0, 0.0
    ).astype(BF16)

    line = lax.broadcasted_iota(I32, spread_ref.shape, 1)
    direction = line >> 3
    direction = direction + jnp.where(direction > 12, 1, 0)
    plane = (direction * 57) >> 9
    from_z = direction - 3 * ((direction * 43) >> 7) - 1
    from_y = ((direction * 43) >> 7) - 3 * plane - 1
    if fold_y:
        side_y = jnp.where(from_y == 0, 0, 1)
        valid = (from_y == 0) | (from_y == 1 - 2 * index_y)
    else:
        side_y = jnp.where(from_y < 0, 2, from_y)
        valid = from_y < 2
    side_z = jnp.where(from_z == 0, 0, 1)
    valid = valid & ((from_z == 0) | (from_z == 1 - 2 * index_z)) & (line < 26 * CAP)
    target = ((2 - plane) * options_y + side_y) * 2 + side_z
    spread_ref[...] = jnp.where(valid, target * CAP + (line & 7), -1)

    for copy in copies[1:-1]:
        copy.wait()
    for i in range(5):
        weights_ref[i] = flip(edge_w_ref[i])
    weights_ref[NODE_OLD] = flip(node_in_ref[:width])
    weights_ref[NODE_NEW] = flip(node_in_ref[width:])
    for i in range(2):
        weights_ref[NODE_0 + i] = flip(node_w_ref[i])
        weights_ref[DECODE_0 + i] = flip(decoder_w_ref[i])
    inward = jnp.concatenate([encoder_in_ref[...].astype(F32), jnp.zeros((4, width), F32)], axis=0)
    inward = inward.astype(BF16)
    inward_ref[...] = jnp.concatenate([inward, inward, inward], axis=0)

    latent = jnp.concatenate([latent_ref[a, b, 0] for a, b in CELLS], axis=0)
    latent_t_ref[...] = latent.astype(F32).T
    node_pre_ref[...] = dot_nt(weights_ref[NODE_OLD], latent)

    def flat(ref, i):
        return jnp.concatenate([ref[i, a, b] for a, b in CELLS], axis=1)

    state = [flat(positions_ref, i) for i in range(3)] + [flat(velocity_ref, i) for i in range(3)]
    state_ref[...] = jnp.concatenate(state + [stays, jnp.zeros_like(stays)], axis=0)

    mover_latent = dot(placer, latent).astype(BF16)
    mover_latent_ref[...] = mover_latent.astype(F32).T
    mover_node_pre_ref[...] = dot_nt(weights_ref[NODE_OLD], mover_latent)
    mover_near_ref[...] = dot_nt(weights_ref[NEAR], mover_latent)
    state = jnp.concatenate(state + [moving.astype(F32), jnp.zeros_like(stays)], axis=0)
    mover_state_ref[...] = joined(dot_nt(thirds(state), placer))
    neighbour_count = edge_ref.shape[3]
    ids = jnp.concatenate(
        [
            jnp.concatenate([neighbours_ref[a, b, k] for a, b in CELLS], axis=1)
            for k in range(neighbour_count)
        ],
        axis=0,
    )
    ids = jnp.concatenate([ids & 127, ids >> 7, jnp.zeros((8, particles), I32)], axis=0)
    ids = dot_nt(ids.astype(F32).astype(BF16), placer).astype(I32)
    place, key = places(ids[:neighbour_count], ids[neighbour_count : 2 * neighbour_count], fold_y)
    mover_place_ref[...] = jnp.concatenate([place[k : k + 1] for k in range(neighbour_count)], axis=1)
    mover_key_ref[...] = jnp.concatenate([key[k : k + 1] for k in range(neighbour_count)], axis=1)

    window = Window(fold_y, far_ref)
    for (ex, row), (a, b) in zip(window.own_columns(), CELLS):
        pair = jnp.concatenate([latent_ref[a, b, 0], own_zed[a, b, 0]], axis=0)
        far_ref[window.own(ex, row)] = dot_nt(weights_ref[FAR], pair).astype(BF16)
    cells = window.cells(window.own_columns())
    for a in range(2):
        b = 1 - index_y if fold_y else 1
        ids = jnp.concatenate([neighbours_ref[a, b, k] for k in range(neighbour_count)], axis=1)
        place, key = places(ids & 127, ids >> 7, fold_y)
        for tile in range(ids.shape[1] // TILE):
            at = slice(tile * TILE, (tile + 1) * TILE)
            early_ref[a, :, at] = pick(cells, place[:, at], key[:, at]).astype(BF16)

    copies[-1].wait()
    for k in range(neighbour_count):
        rows = jnp.concatenate([edge_ref[a, b, 0, k] for a, b in CELLS], axis=0)
        mover_edge_ref[k] = dot(placer, rows).astype(BF16)


def prepare_kernel(
    sizes,
    far_ref,
    mine_ref,
    weights_ref,
    edge_ref,
    place_ref,
    key_ref,
    near_ref,
    far_mine_ref,
    pre_ref,
):
    window = Window(sizes[1] == 2, far_ref)
    core = lax.axis_index("gz")
    far_t = weights_ref[FAR]
    cells = window.cells(window.own_columns())
    for row in range(window.row_count):
        pair = jnp.concatenate([mine_ref[1, row], mine_ref[0, row]], axis=0)
        far_mine_ref[row] = dot_nt(far_t, pair).astype(BF16)
        cells.append((12 * (1 - core) + row, far_mine_ref.at[row]))
    neighbour_count, movers = edge_ref.shape[:2]
    step = TILE // movers
    near = jnp.concatenate([near_ref[...]] * step, axis=1)
    for tile in range(neighbour_count // step):
        edges = jnp.concatenate([edge_ref[k] for k in range(tile * step, (tile + 1) * step)], axis=0)
        at = slice(tile * TILE, (tile + 1) * TILE)
        pre_ref[:, at] = (
            dot_nt(weights_ref[EDGE], edges) + near + pick(cells, place_ref[:, at], key_ref[:, at])
        )


def movers_kernel(
    sizes,
    side_count,
    *refs,
):
    fold_y = sizes[1] == 2
    side_refs, refs = refs[:side_count], refs[side_count:]
    side_zeds, refs = refs[:side_count], refs[side_count:]
    other_ref, far_mine_ref, refs = refs[0], refs[1], refs[2:]
    (
        weights_ref,
        decoder_out_ref,
        pre_ref,
        place_ref,
        key_ref,
        node_pre_ref,
        latent_t_ref,
        state_ref,
        far_ref,
        bucket_ref,
        hidden_ref,
    ) = refs
    window = Window(fold_y, None, far_ref)
    row_count = window.row_count
    core = lax.axis_index("gz")
    far_t = weights_ref[FAR]

    def far(at, here, beside):
        pair = jnp.concatenate([here, beside], axis=0)
        far_ref[at] = dot_nt(far_t, pair).astype(BF16)

    for row in range(row_count):
        far(core * row_count + row, other_ref[0, row], other_ref[1, row])
    for side, row in enumerate(window.outer_rows):
        for ex in (1, 2):
            far(window.side(ex, row), side_refs[side][ex - 1], side_zeds[side][ex - 1])

    movers = state_ref.shape[1]
    for row in range(row_count):
        far_ref[(1 - core) * row_count + row] = far_mine_ref[row]
    cells = [(12 * core + row, far_ref.at[core * row_count + row]) for row in range(row_count)]
    cells += window.cells([(ex, row) for ex in (1, 2) for row in window.outer_rows])
    message = messages(
        cells,
        place_ref[...],
        key_ref[...],
        lambda tile: pre_ref[:, tile * TILE : (tile + 1) * TILE],
        weights_ref[MIDDLE],
        weights_ref[FINAL],
        hidden_ref,
    )
    aggregate = slot_sum(message, movers).astype(BF16)
    acceleration = advance(
        node_pre_ref[...], aggregate, latent_t_ref[...], weights_ref, decoder_out_ref[...]
    )
    mask = state_ref[6:7]
    state = moved(state_ref[0:3], state_ref[3:6], acceleration) * mask
    bucket_ref[...] = jnp.concatenate([state, mask, jnp.zeros((ROWS - 10, movers), F32)], axis=0)


def edges_kernel(
    sizes,
    a,
    alive_ref,
    latent_ref,
    edge_ref,
    neighbours_ref,
    far_own_ref,
    far_rest_ref,
    early_ref,
    weights_ref,
    total_ref,
    hidden_ref,
):
    fold_y = sizes[1] == 2
    window = Window(fold_y, far_own_ref, far_rest_ref)
    index_y = lax.axis_index("gy")
    alive_ref, latent_ref = alive_ref.at[a], latent_ref.at[a]
    edge_ref, neighbours_ref = edge_ref.at[a], neighbours_ref.at[a]
    slots, width = latent_ref.shape[-2:]
    neighbour_count = edge_ref.shape[2]
    for bt in range(2):
        if fold_y:
            b = index_y if bt == 0 else 1 - index_y
            rows = (0, 1) if bt == 0 else (0, 1, 2)
        else:
            b = bt
            rows = (bt, bt + 1, bt + 2)
        columns = [(ex, row) for ex in range(a, a + 3) for row in rows]
        if bt == 1:
            columns = [column for column in columns if column not in window.own_columns()]
        near = dot_nt(weights_ref[NEAR], latent_ref[b, 0])
        near = jnp.concatenate([near, near], axis=1)
        ids = jnp.concatenate([neighbours_ref[b, k] for k in range(neighbour_count)], axis=1)
        place, key = places(ids & 127, ids >> 7, fold_y)

        def pre(tile, b=b, bt=bt, near=near):
            edges = jnp.concatenate([edge_ref[b, 0, 2 * tile], edge_ref[b, 0, 2 * tile + 1]], axis=0)
            terms = dot_nt(weights_ref[EDGE], edges) + near
            if bt == 1:
                terms = terms + early_ref[a, :, tile * TILE : (tile + 1) * TILE].astype(F32)
            return terms

        message = messages(
            window.cells(columns),
            place,
            key,
            pre,
            weights_ref[MIDDLE],
            weights_ref[FINAL],
            hidden_ref.at[bt],
        )
        total = jnp.where(alive_ref[b] > 0.5, slot_sum(message, slots), 0.0)
        total_ref[b] = total.astype(BF16)


def nodes_kernel(
    first_ref,
    second_ref,
    node_pre_ref,
    latent_t_ref,
    state_ref,
    weights_ref,
    decoder_out_ref,
    moved_ref,
):
    aggregate = jnp.concatenate([first_ref[0], first_ref[1], second_ref[0], second_ref[1]], axis=1)
    acceleration = advance(
        node_pre_ref[...], aggregate, latent_t_ref[...], weights_ref, decoder_out_ref[...]
    )
    state = moved(state_ref[0:3], state_ref[3:6], acceleration)
    moved_ref[...] = jnp.concatenate(
        [state, state_ref[6:7], jnp.zeros((ROWS - 10, state.shape[1]), F32)], axis=0
    )


def finish_kernel(
    sizes,
    moved_ref,
    tiles_ref,
    zeds_ref,
    spread_ref,
    inward_ref,
    encoder_w_ref,
    kept_latent_ref,
    kept_state_ref,
    arrived_latent_ref,
    arrived_state_ref,
):
    count_x, count_y, count_z = sizes
    extent = (2.0 * count_x, 2.0 * count_y, 1.0 * count_z)
    slots = kept_latent_ref.shape[-2]
    stays = moved_ref[9:10]
    kept = moved_ref[:9] * stays
    latents = encode(moved_ref[:9], stays, inward_ref[...], encoder_w_ref[...], extent)
    for i, (a, b) in enumerate(CELLS):
        kept_latent_ref[a, b, 0] = latents[i * slots : (i + 1) * slots]
        for j in range(9):
            kept_state_ref[j, a, b] = kept[j : j + 1, i * slots : (i + 1) * slots]
    fold_y = count_y == 2
    index_x = lax.axis_index("gx")
    options_y = 2 if fold_y else 3
    lanes = tiles_ref.shape[-1]
    group = lax.broadcasted_iota(I32, (ROWS, lanes), 1) >> 3
    even = (index_x & 1) == 0
    found = jnp.zeros((ROWS, lanes), F32)
    for source_x in (-1, 0, 1):
        for from_y in range(options_y):
            for from_z in range(2):
                if source_x == 0 and from_y == 0 and from_z == 0:
                    continue
                ref = tiles_ref if from_z == 0 else zeds_ref
                own, second, first = ref.at[0], ref.at[1], ref.at[2]
                side_y = from_y if fold_y or from_y == 0 else 3 - from_y
                target = ((1 - source_x) * options_y + side_y) * 2 + from_z
                if source_x == 0:
                    tile = own[from_y]
                    there = group == target
                elif source_x == -1:
                    tile = jnp.where(even, second[from_y], first[from_y])
                    there = (group == target) & (index_x > 0)
                else:
                    tile = jnp.where(even, first[from_y], second[from_y])
                    there = (group == target) & (index_x < count_x - 1)
                found = jnp.where(there, tile, found)
    halves = []
    for at in range(0, spread_ref.shape[1], 128):
        lane = jnp.broadcast_to(spread_ref[0:1, at : at + 128], (ROWS, 128))
        half = jnp.zeros((ROWS, 128), F32)
        for base in range(0, lanes, 128):
            index = jnp.clip(lane - base, 0, 127)
            there = (lane >= base) & (lane < base + 128)
            part = jnp.take_along_axis(found[:, base : base + 128], index, axis=1)
            half = jnp.where(there, part, half)
        halves.append(half)
    arrived = jnp.concatenate(halves, axis=1)[:, : 26 * CAP]
    for j in range(9):
        arrived_state_ref[j, 0, 0] = arrived[j : j + 1]
    arrived_latent_ref[0, 0, 0] = encode(
        arrived[:9], arrived[9:10], inward_ref[...], encoder_w_ref[...], extent
    )


def swap(values, axis):
    return lax.ppermute(values, axis, [(0, 1), (1, 0)])


def shift(values, axis, way):
    pairs = [(i, i + 1) for i in range(lax.axis_size(axis) - 1)]
    return lax.ppermute(values, axis, [(j, i) for i, j in pairs] if way else pairs)


def swap_x(values, first):
    count = lax.axis_size("gx")
    pairs = []
    for x in range(count):
        partner = x + 1 if (x - first) % 2 == 0 else x - 1
        for z in range(2):
            if 0 <= partner < count:
                pairs.append((x * 2 + z, partner * 2 + z))
            else:
                pairs.append((x * 2 + z, x * 2 + 1 - z))
    return lax.ppermute(values, ("gx", "gz"), pairs)


def swap_chips(values, cross):
    count_x, count_y, count_z = (lax.axis_size(axis) for axis in ("gx", "gy", "gz"))
    pairs = []
    for x in range(count_x):
        for y in range(count_y):
            for z in range(count_z):
                to_x = x + 1 - 2 * z
                if 0 <= to_x < count_x:
                    to = (to_x, y ^ 1 if cross else y, 1 - z)
                else:
                    to = (x, y ^ 1, z)
                pairs.append(((x * count_y + y) * count_z + z, (to[0] * count_y + to[1]) * count_z + to[2]))
    return lax.ppermute(values, ("gx", "gy", "gz"), pairs)


def call(kernel, name, in_specs, outs, scratch, operands, flops):
    return pl.pallas_call(
        kernel,
        out_shape=tuple(jax.ShapeDtypeStruct(shape, kind) for shape, kind in outs),
        in_specs=in_specs,
        out_specs=tuple(VMEM for _ in outs),
        scratch_shapes=scratch,
        compiler_params=pltpu.CompilerParams(vmem_limit_bytes=32 * 1024 * 1024),
        cost_estimate=pl.CostEstimate(flops=flops, bytes_accessed=0, transcendentals=0),
        name=name,
    )(*operands)


def in_hbm(array):
    return pltpu.with_memory_space_constraint(array, pltpu.HBM)


def like(array):
    return pltpu.VMEM(array.shape, array.dtype)


def body(
    node_latent,
    edge_latent,
    positions,
    velocity,
    fill,
    neighbours,
    owners,
    edge_weights,
    node_in,
    node_weights,
    decoder_weights,
    decoder_out,
    encoder_in,
    encoder_weights,
):
    sizes = tuple(lax.axis_size(axis) for axis in ("gx", "gy", "gz"))
    fold_y = sizes[1] == 2
    slots, width = node_latent.shape[-2:]
    neighbour_count = neighbours.shape[3]
    particles = 4 * slots
    options_y = 2 if fold_y else 3
    movers = (3 * options_y * 2 * CAP + 127) // 128 * 128
    rows = 3 if fold_y else 4
    fill = jnp.transpose(fill, (0, 2, 1))
    neighbours = neighbours.reshape(2, 2, neighbour_count, 1, slots)

    own_zed = swap(node_latent, "gz")
    if fold_y:
        sides = [swap(node_latent, "gy")]
    latent, end = call(
        cut_kernel,
        "cut",
        [ANY],
        [(node_latent.shape, BF16), (node_latent.shape[1:], BF16)],
        [pltpu.SemaphoreType.DMA((2,))],
        (in_hbm(node_latent),),
        1_000_000,
    )
    core = lax.axis_index("gz")
    if fold_y:
        row = 1 - lax.axis_index("gy")
        beside = lax.dynamic_index_in_dim(own_zed[:, :, 0], 1 - core, 0, False)
        corner = jnp.concatenate(
            [lax.dynamic_slice_in_dim(part, row, 1, 0) for part in (end[:, 0], beside)], axis=0
        )
        both = jnp.stack([end[:, 0], beside])
        mine = [swap_chips(corner[:, None], True), swap_chips(both, False)]
    else:
        sides = [shift(latent[:, 1, 0], "gy", 0), shift(latent[:, 0, 0], "gy", 1)]
        side_zeds = [swap(part, "gz") for part in sides]
        layers = []
        for middle, outer in ((latent, sides), (own_zed, side_zeds)):
            parts = [outer[0][:, None], middle[:, :, 0], outer[1][:, None]]
            parts = [lax.dynamic_index_in_dim(part, 1 - core, 0, False) for part in parts]
            layers.append(jnp.concatenate(parts, axis=0))
        mine = [swap_chips(jnp.stack(layers), False)]

    ranked = call(
        functools.partial(ranks_kernel, sizes),
        "ranks",
        [SMEM] + [ANY] * 12 + [VMEM] * 2,
        [
            ((11, width, width), BF16),
            (decoder_out.shape, BF16),
            ((48, width), BF16),
            (encoder_weights.shape, BF16),
            ((2, 2, 1, slots), F32),
            (neighbours.shape, I32),
            (edge_latent.shape, BF16),
            ((8, 256), I32),
            ((width, particles), F32),
            ((width, particles), F32),
            ((8, particles), F32),
            ((neighbour_count, movers, width), BF16),
            ((1, neighbour_count * movers), I32),
            ((1, neighbour_count * movers), I32),
            ((width, movers), F32),
            ((width, movers), F32),
            ((width, movers), F32),
            ((8, movers), F32),
            ((4, width, 2 * slots), BF16),
            ((2, width, neighbour_count * slots), BF16),
        ],
        [
            like(positions),
            like(velocity),
            like(owners),
            like(edge_weights),
            like(node_in),
            like(node_weights),
            like(decoder_weights),
            like(encoder_in),
            pltpu.SemaphoreType.DMA((12,)),
        ],
        [
            in_hbm(array)
            for array in (
                fill,
                owners,
                edge_weights,
                node_in,
                node_weights,
                decoder_weights,
                decoder_out,
                encoder_in,
                encoder_weights,
                neighbours,
                positions,
                velocity,
                edge_latent,
            )
        ]
        + [latent, own_zed],
        5_000_000_000,
    )
    mine, sides, ranked = lax.optimization_barrier((mine, sides, ranked))
    (
        weights,
        decoder_out,
        inward,
        encoder_weights,
        alive,
        neighbours,
        edge_latent,
        spread,
        latent_t,
        node_pre,
        state,
        mover_edges,
        mover_place,
        mover_key,
        mover_near,
        mover_node_pre,
        mover_latent,
        mover_state,
        far_own,
        early,
    ) = ranked
    mine = jnp.concatenate(mine[::-1], axis=1)
    if fold_y:
        sides = [lax.dynamic_index_in_dim(sides[0][:, :, 0], lax.axis_index("gy"), 1, False)]
        packed = jnp.concatenate([mine.reshape(-1, slots, width), sides[0]], axis=0)
    else:
        packed = mine.reshape(-1, slots, width)
    packed = swap(packed, "gz")
    prepared = call(
        functools.partial(prepare_kernel, sizes),
        "prepare",
        [VMEM] * 7,
        [((rows, width, 2 * slots), BF16), ((width, neighbour_count * movers), F32)],
        [],
        (far_own, mine, weights, mover_edges, mover_place, mover_key, mover_near),
        5_000_000_000,
    )
    packed, prepared = lax.optimization_barrier((packed, prepared))
    cells = mine.shape[0] * mine.shape[1]
    if fold_y:
        side_zeds = [packed[cells:]]
    far_mine, mover_pre = prepared
    halo = [*sides, *side_zeds, packed[:cells].reshape(mine.shape), far_mine]

    far_rest, bucket = call(
        functools.partial(movers_kernel, sizes, len(sides)),
        "movers",
        [VMEM] * (len(halo) + 8),
        [((4 * rows - 4, width, 2 * slots), BF16), ((ROWS, movers), F32)],
        [pltpu.VMEM((width, neighbour_count * movers), BF16)],
        (
            *halo,
            weights,
            decoder_out,
            mover_pre,
            mover_place,
            mover_key,
            mover_node_pre,
            mover_latent,
            mover_state,
        ),
        3_000_000_000,
    )

    def edges(a):
        return call(
            functools.partial(edges_kernel, sizes, a),
            "edges",
            [VMEM] * 8,
            [((2, width, slots), BF16)],
            [pltpu.VMEM((2, width, neighbour_count * slots), BF16)],
            (alive, latent, edge_latent, neighbours, far_own, far_rest, early, weights),
            4_000_000_000,
        )[0]

    first = edges(0)
    if fold_y:
        tiles = [swap(bucket, "gy")]
    else:
        tiles = [shift(bucket, "gy", 0), shift(bucket, "gy", 1)]
    tiles, first = lax.optimization_barrier((tiles, first))
    tiles = jnp.stack([bucket, *tiles], axis=0)
    second = edges(1)
    sided = [swap_x(tiles, 1), swap_x(tiles, 0)]
    sided, second = lax.optimization_barrier((sided, second))
    tiles = jnp.stack([tiles, *sided], axis=0)
    zeds = swap(tiles, "gz")
    state = call(
        nodes_kernel,
        "nodes",
        [VMEM] * 7,
        [((ROWS, particles), F32)],
        [],
        (first, second, node_pre, latent_t, state, weights, decoder_out),
        1_000_000_000,
    )[0]
    zeds, state = lax.optimization_barrier((zeds, state))
    return call(
        functools.partial(finish_kernel, sizes),
        "finish",
        [VMEM] * 6,
        [
            (node_latent.shape, BF16),
            ((9,) + node_latent.shape[:4], F32),
            ((1, 1, 1, 26 * CAP, width), BF16),
            ((9, 1, 1, 1, 26 * CAP), F32),
        ],
        [],
        (state, tiles, zeds, spread, inward, encoder_weights),
        1_000_000_000,
    )


def solution(mesh):
    placed = (
        P(("group", "gx"), "gy", "gz", None, None),
        P(("group", "gx"), "gy", "gz", None, None, None),
        P(None, ("group", "gx"), "gy", "gz", None),
        P(None, ("group", "gx"), "gy", "gz", None),
        P(("group", "gx"), "gy", "gz"),
        P(("group", "gx"), "gy", "gz", None, None),
        P(("group", "gx"), "gy", "gz", None),
        P(),
        P(),
        P(),
        P(),
        P(),
        P(),
        P(),
    )
    return jax.shard_map(
        body,
        mesh=mesh,
        in_specs=placed,
        out_specs=(
            P(("group", "gx"), "gy", "gz", None, None),
            P(None, ("group", "gx"), "gy", "gz", None),
            P(("group", "gx"), "gy", "gz", None, None),
            P(None, ("group", "gx"), "gy", "gz", None),
        ),
        check_vma=False,
    )
```

```python
import functools

import jax
import jax.numpy as jnp
from jax import lax
from jax.experimental import pallas as pl
from jax.experimental.pallas import tpu as pltpu
from jax.sharding import PartitionSpec as P

CAP = 8
F32 = jnp.float32
BF16 = jnp.bfloat16
I32 = jnp.int32
ROWS = 16
TILE = 256
CELLS = [(a, b) for a in range(2) for b in range(2)]
EDGE, NEAR, FAR, MIDDLE, FINAL, NODE_OLD, NODE_NEW, NODE_0, NODE_1, DECODE_0, DECODE_1 = range(11)

VMEM = pl.BlockSpec(memory_space=pltpu.VMEM)
SMEM = pl.BlockSpec(memory_space=pltpu.SMEM)
ANY = pl.BlockSpec(memory_space=pl.ANY)


def dot(left, right):
    return jnp.dot(left, right, preferred_element_type=F32)


def dot_nt(left, right):
    return lax.dot_general(left, right, (((1,), (1,)), ((), ())), preferred_element_type=F32)


def dot_tn(left, right):
    return lax.dot_general(left, right, (((0,), (0,)), ((), ())), preferred_element_type=F32)


def relu16(values):
    return jnp.maximum(values, 0.0).astype(BF16)


def norm(values, axis):
    scale = 1.0 / values.shape[axis]
    centred = values - jnp.sum(values, axis=axis, keepdims=True) * scale
    spread = jnp.sum(centred * centred, axis=axis, keepdims=True) * scale
    return centred * lax.rsqrt(spread + 1e-05)


def thirds(values):
    high = values.astype(BF16)
    rest = values - high.astype(F32)
    middle = rest.astype(BF16)
    low = (rest - middle.astype(F32)).astype(BF16)
    return jnp.concatenate([high, middle, low], axis=0)


def joined(values):
    rows = values.shape[0] // 3
    return values[:rows] + values[rows : 2 * rows] + values[2 * rows :]


def quotient(values, count):
    if count & (count - 1) == 0:
        return values >> (count.bit_length() - 1)
    return lax.div(values, jnp.full_like(values, count))


def flip(weights):
    return weights.astype(F32).T.astype(BF16)


def fetch(pairs, sems):
    copies = [pltpu.make_async_copy(src, dst, sems.at[i]) for i, (src, dst) in enumerate(pairs)]
    for copy in copies:
        copy.start()
    return copies


def encode(state, mask, inward, encoder_w, extent):
    width = state.shape[1]
    position = state[0:3]
    row = lax.broadcasted_iota(I32, (3, width), 0)
    size = jnp.where(row == 0, extent[0], jnp.where(row == 1, extent[1], extent[2]))
    features = jnp.concatenate(
        [
            state[3:9],
            jnp.clip(position, -1.0, 1.0),
            jnp.clip(size - position, -1.0, 1.0),
            jnp.zeros((4, width), F32),
        ],
        axis=0,
    )
    hidden = relu16(dot_tn(thirds(features), inward))
    hidden = relu16(dot(hidden, encoder_w[0]))
    column = jnp.broadcast_to(mask, (8, width)).T[:, 0:1]
    return (norm(dot(hidden, encoder_w[1]), 1) * column).astype(BF16)


def places(ids_low, ids_high, fold_y):
    plane = (ids_high * 43) >> 7
    ez = ids_high - plane * 3
    ey = plane & 3
    ex = plane >> 2
    if fold_y:
        row = jnp.where(ey == 1, 0, jnp.where(ey == 2, 1, 2))
    else:
        row = ey
    return ex * 4 + row, ids_low + jnp.where(ez == 1, 0, 128)


def pick(cells, place, key):
    width = cells[0][1].shape[0]
    chunk = 32
    window = jnp.concatenate(
        [ref[f : f + chunk] for f in range(0, width, chunk) for _, ref in cells], axis=0
    )
    key_rows = lax.broadcasted_iota(I32, (TILE, TILE), 0).astype(F32).astype(BF16)
    key = jnp.broadcast_to(key.astype(F32), (16, TILE)).astype(BF16)
    same = key_rows.reshape(TILE // 16, 16, TILE) == key[None]
    picker = jnp.where(same, jnp.ones((), BF16), jnp.zeros((), BF16)).reshape(TILE, TILE)
    found = dot(window, picker).reshape(width // chunk, len(cells), chunk // 8, 8, TILE)
    where = jnp.broadcast_to(place, (8, TILE))
    parts = []
    for f in range(width // chunk):
        part = jnp.zeros((chunk // 8, 8, TILE), F32)
        for i, (column, _) in enumerate(cells):
            part = jnp.where((where == column)[None], found[f, i], part)
        parts.append(part.reshape(chunk, TILE))
    return jnp.concatenate(parts, axis=0)


def messages(cells, place, key, pre, middle_t, final_t, hidden_ref):
    for tile in range(place.shape[1] // TILE):
        at = slice(tile * TILE, (tile + 1) * TILE)
        hidden_ref[:, at] = relu16(pre(tile) + pick(cells, place[:, at], key[:, at]))
    hidden = relu16(dot(middle_t, hidden_ref[...]))
    return norm(dot(final_t, hidden), 0)


class Window:
    def __init__(self, fold_y, own_ref=None, rest_ref=None):
        self.row_count = 3 if fold_y else 4
        self.own_rows = (0, 1) if fold_y else (1, 2)
        self.outer_rows = (2,) if fold_y else (0, 3)
        self.own_ref, self.rest_ref = own_ref, rest_ref

    def own_columns(self):
        return [(ex, row) for ex in (1, 2) for row in self.own_rows]

    def own(self, ex, row):
        return (ex - 1) * 2 + self.own_rows.index(row)

    def side(self, ex, row):
        count = len(self.outer_rows)
        return 2 * self.row_count + (ex - 1) * count + self.outer_rows.index(row)

    def cells(self, columns):
        found = []
        for ex, row in columns:
            if ex in (1, 2) and row in self.own_rows:
                ref = self.own_ref.at[self.own(ex, row)]
            elif ex in (1, 2):
                ref = self.rest_ref.at[self.side(ex, row)]
            else:
                ref = self.rest_ref.at[(0 if ex == 0 else self.row_count) + row]
            found.append((ex * 4 + row, ref))
        return found


def slot_sum(message, step):
    total = message[:, :step]
    for at in range(step, message.shape[1], step):
        total = total + message[:, at : at + step]
    return total


def advance(pre, aggregate, latent_t, weights_ref, decoder_out):
    pre = pre + dot(weights_ref[NODE_NEW], aggregate)
    hidden = relu16(dot(weights_ref[NODE_0], relu16(pre)))
    updated = (latent_t + norm(dot(weights_ref[NODE_1], hidden), 0)).astype(BF16)
    hidden = relu16(dot(weights_ref[DECODE_0], updated))
    hidden = relu16(dot(weights_ref[DECODE_1], hidden))
    return dot(decoder_out, hidden)


def moved(position, velocity, acceleration):
    new_velocity = velocity + acceleration
    return jnp.concatenate([position + new_velocity, new_velocity, velocity], axis=0)


def cut_kernel(count, fill_any, *refs):
    sources, refs = refs[:count], refs[count:]
    copied, (end_ref, alive_ref, fill_ref, sems) = refs[:count], refs[count:]
    end = 1 - lax.axis_index("gz")
    copies = fetch(
        [(fill_any, fill_ref), (sources[0].at[end], end_ref), *zip(sources, copied)], sems
    )
    copies[0].wait()
    lane = lax.broadcasted_iota(I32, alive_ref.shape[2:], 1)
    for a, b in CELLS:
        alive_ref[a, b] = jnp.where(lane < fill_ref[a, 0, b], 1.0, 0.0)
    for copy in copies[1:]:
        copy.wait()


def ranks_kernel(
    sizes,
    edge_any,
    latent_ref,
    own_zed,
    alive_ref,
    owners_ref,
    edge_w_ref,
    node_in_ref,
    node_w_ref,
    decoder_w_ref,
    encoder_in_ref,
    neighbours_ref,
    positions_ref,
    velocity_ref,
    weights_ref,
    inward_ref,
    edge_ref,
    spread_ref,
    latent_t_ref,
    node_pre_ref,
    state_ref,
    mover_edge_ref,
    mover_place_ref,
    mover_key_ref,
    mover_near_ref,
    mover_node_pre_ref,
    mover_latent_ref,
    mover_state_ref,
    far_ref,
    early_ref,
    sems,
):
    count_x, count_y, count_z = sizes
    fold_y = count_y == 2
    copies = fetch([(edge_any, edge_ref)], sems)
    index_x = lax.axis_index("gx")
    index_y = lax.axis_index("gy")
    index_z = lax.axis_index("gz")
    slots = owners_ref.shape[-1]
    width = node_in_ref.shape[-1]
    owner = jnp.concatenate([owners_ref[a, b] for a, b in CELLS], axis=1)
    alive = jnp.concatenate([alive_ref[a, b] for a, b in CELLS], axis=1)
    own_block = (index_x * count_y + index_y) * count_z + index_z
    stays = jnp.where((alive > 0.5) & (owner == own_block), 1.0, 0.0)
    moving = jnp.where((alive > 0.5) & (owner != own_block), 1, 0)
    owner_x = quotient(owner, count_y * count_z)
    rest = owner - owner_x * (count_y * count_z)
    owner_y = quotient(rest, count_z)
    owner_z = rest - owner_y * count_z
    step_y = owner_y - index_y
    side_y = jnp.where(step_y == 0, 0, 1) if fold_y else jnp.where(step_y < 0, 1, 2 * step_y)
    options_y = 2 if fold_y else 3
    group = ((owner_x - index_x + 1) * options_y + side_y) * 2 + jnp.where(owner_z == index_z, 0, 1)
    group_rows = (3 * options_y * 2 + 15) // 16 * 16
    particles = owner.shape[1]
    member = jnp.where(
        (lax.broadcasted_iota(I32, (group_rows, particles), 0) == group) & (moving == 1), 1.0, 0.0
    )
    triangle = jnp.where(
        lax.broadcasted_iota(I32, (slots, slots), 0) <= lax.broadcasted_iota(I32, (slots, slots), 1),
        1.0,
        0.0,
    ).astype(BF16)
    counted = []
    before = jnp.zeros((group_rows, 1), F32)
    for i in range(4):
        inside = member[:, i * slots : (i + 1) * slots]
        counted.append(dot(inside.astype(BF16), triangle) + before)
        before = before + jnp.sum(inside, axis=1, keepdims=True)
    counted = jnp.concatenate(counted, axis=1)
    rank = (jnp.sum(counted * member, axis=0, keepdims=True) - 1.0).astype(I32)
    column = jnp.where(moving == 1, group * CAP + rank, -1)
    movers = mover_state_ref.shape[1]
    placer = jnp.where(
        lax.broadcasted_iota(I32, (movers, particles), 0) == column, 1.0, 0.0
    ).astype(BF16)

    line = lax.broadcasted_iota(I32, spread_ref.shape, 1)
    direction = line >> 3
    direction = direction + jnp.where(direction > 12, 1, 0)
    plane = (direction * 57) >> 9
    from_z = direction - 3 * ((direction * 43) >> 7) - 1
    from_y = ((direction * 43) >> 7) - 3 * plane - 1
    if fold_y:
        side_y = jnp.where(from_y == 0, 0, 1)
        valid = (from_y == 0) | (from_y == 1 - 2 * index_y)
    else:
        side_y = jnp.where(from_y < 0, 2, from_y)
        valid = from_y < 2
    side_z = jnp.where(from_z == 0, 0, 1)
    valid = valid & ((from_z == 0) | (from_z == 1 - 2 * index_z)) & (line < 26 * CAP)
    target = ((2 - plane) * options_y + side_y) * 2 + side_z
    spread_ref[...] = jnp.where(valid, target * CAP + (line & 7), -1)

    for i in range(5):
        weights_ref[i] = flip(edge_w_ref[i])
    weights_ref[NODE_OLD] = flip(node_in_ref[:width])
    weights_ref[NODE_NEW] = flip(node_in_ref[width:])
    for i in range(2):
        weights_ref[NODE_0 + i] = flip(node_w_ref[i])
        weights_ref[DECODE_0 + i] = flip(decoder_w_ref[i])
    inward = jnp.concatenate([encoder_in_ref[...].astype(F32), jnp.zeros((4, width), F32)], axis=0)
    inward = inward.astype(BF16)
    inward_ref[...] = jnp.concatenate([inward, inward, inward], axis=0)

    latent = jnp.concatenate([latent_ref[a, b, 0] for a, b in CELLS], axis=0)
    latent_t_ref[...] = latent.astype(F32).T
    node_pre_ref[...] = dot_nt(weights_ref[NODE_OLD], latent)

    def flat(ref, i):
        return jnp.concatenate([ref[i, a, b] for a, b in CELLS], axis=1)

    state = [flat(positions_ref, i) for i in range(3)] + [flat(velocity_ref, i) for i in range(3)]
    state_ref[...] = jnp.concatenate(state + [stays, jnp.zeros_like(stays)], axis=0)

    mover_latent = dot(placer, latent).astype(BF16)
    mover_latent_ref[...] = mover_latent.astype(F32).T
    mover_node_pre_ref[...] = dot_nt(weights_ref[NODE_OLD], mover_latent)
    mover_near_ref[...] = dot_nt(weights_ref[NEAR], mover_latent)
    state = jnp.concatenate(state + [moving.astype(F32), jnp.zeros_like(stays)], axis=0)
    mover_state_ref[...] = joined(dot_nt(thirds(state), placer))
    neighbour_count = edge_ref.shape[3]
    ids = jnp.concatenate(
        [
            jnp.concatenate([neighbours_ref[a, b, k] for a, b in CELLS], axis=1)
            for k in range(neighbour_count)
        ],
        axis=0,
    )
    ids = jnp.concatenate([ids & 127, ids >> 7, jnp.zeros((8, particles), I32)], axis=0)
    ids = dot_nt(ids.astype(F32).astype(BF16), placer).astype(I32)
    place, key = places(ids[:neighbour_count], ids[neighbour_count : 2 * neighbour_count], fold_y)
    mover_place_ref[...] = jnp.concatenate([place[k : k + 1] for k in range(neighbour_count)], axis=1)
    mover_key_ref[...] = jnp.concatenate([key[k : k + 1] for k in range(neighbour_count)], axis=1)

    window = Window(fold_y, far_ref)
    for (ex, row), (a, b) in zip(window.own_columns(), CELLS):
        pair = jnp.concatenate([latent_ref[a, b, 0], own_zed[a, b, 0]], axis=0)
        far_ref[window.own(ex, row)] = dot_nt(weights_ref[FAR], pair).astype(BF16)
    cells = window.cells(window.own_columns())
    for a in range(2):
        b = 1 - index_y if fold_y else 1
        ids = jnp.concatenate([neighbours_ref[a, b, k] for k in range(neighbour_count)], axis=1)
        place, key = places(ids & 127, ids >> 7, fold_y)
        for tile in range(ids.shape[1] // TILE):
            at = slice(tile * TILE, (tile + 1) * TILE)
            early_ref[a, :, at] = pick(cells, place[:, at], key[:, at]).astype(BF16)

    copies[-1].wait()
    for k in range(neighbour_count):
        rows = jnp.concatenate([edge_ref[a, b, 0, k] for a, b in CELLS], axis=0)
        mover_edge_ref[k] = dot(placer, rows).astype(BF16)


def prepare_kernel(
    sizes,
    far_ref,
    mine_ref,
    weights_ref,
    edge_ref,
    place_ref,
    key_ref,
    near_ref,
    far_mine_ref,
    pre_ref,
):
    window = Window(sizes[1] == 2, far_ref)
    core = lax.axis_index("gz")
    far_t = weights_ref[FAR]
    cells = window.cells(window.own_columns())
    for row in range(window.row_count):
        pair = jnp.concatenate([mine_ref[1, row], mine_ref[0, row]], axis=0)
        far_mine_ref[row] = dot_nt(far_t, pair).astype(BF16)
        cells.append((12 * (1 - core) + row, far_mine_ref.at[row]))
    neighbour_count, movers = edge_ref.shape[:2]
    step = TILE // movers
    near = jnp.concatenate([near_ref[...]] * step, axis=1)
    for tile in range(neighbour_count // step):
        edges = jnp.concatenate([edge_ref[k] for k in range(tile * step, (tile + 1) * step)], axis=0)
        at = slice(tile * TILE, (tile + 1) * TILE)
        pre_ref[:, at] = (
            dot_nt(weights_ref[EDGE], edges) + near + pick(cells, place_ref[:, at], key_ref[:, at])
        )


def movers_kernel(
    sizes,
    side_count,
    *refs,
):
    fold_y = sizes[1] == 2
    side_refs, refs = refs[:side_count], refs[side_count:]
    side_zeds, refs = refs[:side_count], refs[side_count:]
    other_ref, far_mine_ref, refs = refs[0], refs[1], refs[2:]
    (
        weights_ref,
        decoder_out_ref,
        pre_ref,
        place_ref,
        key_ref,
        node_pre_ref,
        latent_t_ref,
        state_ref,
        far_ref,
        bucket_ref,
        hidden_ref,
    ) = refs
    window = Window(fold_y, None, far_ref)
    row_count = window.row_count
    core = lax.axis_index("gz")
    far_t = weights_ref[FAR]

    def far(at, here, beside):
        pair = jnp.concatenate([here, beside], axis=0)
        far_ref[at] = dot_nt(far_t, pair).astype(BF16)

    for row in range(row_count):
        far(core * row_count + row, other_ref[0, row], other_ref[1, row])
    for side, row in enumerate(window.outer_rows):
        for ex in (1, 2):
            far(window.side(ex, row), side_refs[side][ex - 1], side_zeds[side][ex - 1])

    movers = state_ref.shape[1]
    for row in range(row_count):
        far_ref[(1 - core) * row_count + row] = far_mine_ref[row]
    cells = [(12 * core + row, far_ref.at[core * row_count + row]) for row in range(row_count)]
    cells += window.cells([(ex, row) for ex in (1, 2) for row in window.outer_rows])
    message = messages(
        cells,
        place_ref[...],
        key_ref[...],
        lambda tile: pre_ref[:, tile * TILE : (tile + 1) * TILE],
        weights_ref[MIDDLE],
        weights_ref[FINAL],
        hidden_ref,
    )
    aggregate = slot_sum(message, movers).astype(BF16)
    acceleration = advance(
        node_pre_ref[...], aggregate, latent_t_ref[...], weights_ref, decoder_out_ref[...]
    )
    mask = state_ref[6:7]
    state = moved(state_ref[0:3], state_ref[3:6], acceleration) * mask
    bucket_ref[...] = jnp.concatenate([state, mask, jnp.zeros((ROWS - 10, movers), F32)], axis=0)


def edges_kernel(
    sizes,
    a,
    alive_ref,
    latent_ref,
    edge_ref,
    neighbours_ref,
    far_own_ref,
    far_rest_ref,
    early_ref,
    weights_ref,
    total_ref,
    hidden_ref,
):
    fold_y = sizes[1] == 2
    window = Window(fold_y, far_own_ref, far_rest_ref)
    index_y = lax.axis_index("gy")
    alive_ref, latent_ref = alive_ref.at[a], latent_ref.at[a]
    edge_ref, neighbours_ref = edge_ref.at[a], neighbours_ref.at[a]
    slots, width = latent_ref.shape[-2:]
    neighbour_count = edge_ref.shape[2]
    for bt in range(2):
        if fold_y:
            b = index_y if bt == 0 else 1 - index_y
            rows = (0, 1) if bt == 0 else (0, 1, 2)
        else:
            b = bt
            rows = (bt, bt + 1, bt + 2)
        columns = [(ex, row) for ex in range(a, a + 3) for row in rows]
        if bt == 1:
            columns = [column for column in columns if column not in window.own_columns()]
        near = dot_nt(weights_ref[NEAR], latent_ref[b, 0])
        near = jnp.concatenate([near, near], axis=1)
        ids = jnp.concatenate([neighbours_ref[b, k] for k in range(neighbour_count)], axis=1)
        place, key = places(ids & 127, ids >> 7, fold_y)

        def pre(tile, b=b, bt=bt, near=near):
            edges = jnp.concatenate([edge_ref[b, 0, 2 * tile], edge_ref[b, 0, 2 * tile + 1]], axis=0)
            terms = dot_nt(weights_ref[EDGE], edges) + near
            if bt == 1:
                terms = terms + early_ref[a, :, tile * TILE : (tile + 1) * TILE].astype(F32)
            return terms

        message = messages(
            window.cells(columns),
            place,
            key,
            pre,
            weights_ref[MIDDLE],
            weights_ref[FINAL],
            hidden_ref.at[bt],
        )
        total = jnp.where(alive_ref[b] > 0.5, slot_sum(message, slots), 0.0)
        total_ref[b] = total.astype(BF16)


def nodes_kernel(
    first_ref,
    second_ref,
    node_pre_ref,
    latent_t_ref,
    state_ref,
    weights_ref,
    decoder_out_ref,
    moved_ref,
):
    aggregate = jnp.concatenate([first_ref[0], first_ref[1], second_ref[0], second_ref[1]], axis=1)
    acceleration = advance(
        node_pre_ref[...], aggregate, latent_t_ref[...], weights_ref, decoder_out_ref[...]
    )
    state = moved(state_ref[0:3], state_ref[3:6], acceleration)
    moved_ref[...] = jnp.concatenate(
        [state, state_ref[6:7], jnp.zeros((ROWS - 10, state.shape[1]), F32)], axis=0
    )


def finish_kernel(sizes, moved_ref, zed_ref, *refs):
    count_x, count_y, count_z = sizes
    fold_y = count_y == 2
    options_y = 2 if fold_y else 3
    side_refs, refs = refs[: options_y - 1], refs[options_y - 1 :]
    if fold_y:
        cross_ref, end_ref, *refs = refs
    else:
        end_ref, *refs = refs
    (
        packed_ref,
        spread_ref,
        inward_ref,
        encoder_w_ref,
        kept_latent_ref,
        kept_state_ref,
        arrived_latent_ref,
        arrived_state_ref,
    ) = refs
    core = lax.axis_index("gz")

    def tile(source_x, from_y, from_z):
        if source_x == 0:
            if from_y == 0:
                return zed_ref[...]
            if fold_y:
                return packed_ref[4] if from_z else side_refs[0][...]
            return side_refs[from_y - 1][from_z]
        if fold_y:
            mine = (cross_ref if from_y else end_ref)[1 - from_z]
            other = packed_ref[(0 if from_y else 2) + from_z]
        else:
            mine = end_ref[1 - from_z, from_y]
            other = packed_ref[from_z, from_y]
        return jnp.where(core == (1 - source_x) // 2, mine, other)

    extent = (2.0 * count_x, 2.0 * count_y, 1.0 * count_z)
    slots = kept_latent_ref.shape[-2]
    stays = moved_ref[9:10]
    kept = moved_ref[:9] * stays
    latents = encode(moved_ref[:9], stays, inward_ref[...], encoder_w_ref[...], extent)
    for i, (a, b) in enumerate(CELLS):
        kept_latent_ref[a, b, 0] = latents[i * slots : (i + 1) * slots]
        for j in range(9):
            kept_state_ref[j, a, b] = kept[j : j + 1, i * slots : (i + 1) * slots]
    fold_y = count_y == 2
    index_x = lax.axis_index("gx")
    lanes = zed_ref.shape[-1]
    group = lax.broadcasted_iota(I32, (ROWS, lanes), 1) >> 3
    found = jnp.zeros((ROWS, lanes), F32)
    for source_x in (-1, 0, 1):
        for from_y in range(options_y):
            for from_z in range(2):
                if source_x == 0 and from_y == 0 and from_z == 0:
                    continue
                side_y = from_y if fold_y or from_y == 0 else 3 - from_y
                there = group == ((1 - source_x) * options_y + side_y) * 2 + from_z
                if source_x == -1:
                    there = there & (index_x > 0)
                elif source_x == 1:
                    there = there & (index_x < count_x - 1)
                found = jnp.where(there, tile(source_x, from_y, from_z), found)
    halves = []
    for at in range(0, spread_ref.shape[1], 128):
        lane = jnp.broadcast_to(spread_ref[0:1, at : at + 128], (ROWS, 128))
        half = jnp.zeros((ROWS, 128), F32)
        for base in range(0, lanes, 128):
            index = jnp.clip(lane - base, 0, 127)
            there = (lane >= base) & (lane < base + 128)
            part = jnp.take_along_axis(found[:, base : base + 128], index, axis=1)
            half = jnp.where(there, part, half)
        halves.append(half)
    arrived = jnp.concatenate(halves, axis=1)[:, : 26 * CAP]
    for j in range(9):
        arrived_state_ref[j, 0, 0] = arrived[j : j + 1]
    arrived_latent_ref[0, 0, 0] = encode(
        arrived[:9], arrived[9:10], inward_ref[...], encoder_w_ref[...], extent
    )


def swap(values, axis):
    return lax.ppermute(values, axis, [(0, 1), (1, 0)])


def shift(values, axis, way):
    pairs = [(i, i + 1) for i in range(lax.axis_size(axis) - 1)]
    return lax.ppermute(values, axis, [(j, i) for i, j in pairs] if way else pairs)


def swap_chips(values, cross):
    count_x, count_y, count_z = (lax.axis_size(axis) for axis in ("gx", "gy", "gz"))
    pairs = []
    for x in range(count_x):
        for y in range(count_y):
            for z in range(count_z):
                to_x = x + 1 - 2 * z
                if 0 <= to_x < count_x:
                    to = (to_x, y ^ 1 if cross else y, 1 - z)
                else:
                    to = (x, y ^ 1, z)
                pairs.append(((x * count_y + y) * count_z + z, (to[0] * count_y + to[1]) * count_z + to[2]))
    return lax.ppermute(values, ("gx", "gy", "gz"), pairs)


def call(kernel, name, in_specs, outs, scratch, operands, flops):
    return pl.pallas_call(
        kernel,
        out_shape=tuple(jax.ShapeDtypeStruct(shape, kind) for shape, kind in outs),
        in_specs=in_specs,
        out_specs=tuple(VMEM for _ in outs),
        scratch_shapes=scratch,
        compiler_params=pltpu.CompilerParams(vmem_limit_bytes=32 * 1024 * 1024),
        cost_estimate=pl.CostEstimate(flops=flops, bytes_accessed=0, transcendentals=0),
        name=name,
    )(*operands)


def in_hbm(array):
    return pltpu.with_memory_space_constraint(array, pltpu.HBM)


def like(array):
    return pltpu.VMEM(array.shape, array.dtype)


def body(
    node_latent,
    edge_latent,
    positions,
    velocity,
    fill,
    neighbours,
    owners,
    edge_weights,
    node_in,
    node_weights,
    decoder_weights,
    decoder_out,
    encoder_in,
    encoder_weights,
):
    sizes = tuple(lax.axis_size(axis) for axis in ("gx", "gy", "gz"))
    fold_y = sizes[1] == 2
    slots, width = node_latent.shape[-2:]
    neighbour_count = neighbours.shape[3]
    particles = 4 * slots
    options_y = 2 if fold_y else 3
    movers = (3 * options_y * 2 * CAP + 127) // 128 * 128
    rows = 3 if fold_y else 4
    fill = jnp.transpose(fill, (0, 2, 1))
    neighbours = neighbours.reshape(2, 2, neighbour_count, 1, slots)

    own_zed = swap(node_latent, "gz")
    if fold_y:
        sides = [swap(node_latent, "gy")]
    small = (
        node_latent,
        owners,
        edge_weights,
        node_in,
        node_weights,
        decoder_weights,
        encoder_in,
        neighbours,
        positions,
        velocity,
        decoder_out,
        encoder_weights,
    )
    *copied, end, alive = call(
        functools.partial(cut_kernel, len(small)),
        "cut",
        [ANY] * (len(small) + 1),
        [(array.shape, array.dtype) for array in small]
        + [(node_latent.shape[1:], BF16), ((2, 2, 1, slots), F32)],
        [pltpu.SMEM(fill.shape, I32), pltpu.SemaphoreType.DMA((len(small) + 2,))],
        [in_hbm(array) for array in (fill, *small)],
        1_000_000,
    )
    latent, *copied, decoder_out, encoder_weights = copied
    neighbours = copied[6]
    core = lax.axis_index("gz")
    if fold_y:
        row = 1 - lax.axis_index("gy")
        beside = lax.dynamic_index_in_dim(own_zed[:, :, 0], 1 - core, 0, False)
        corner = jnp.concatenate(
            [lax.dynamic_slice_in_dim(part, row, 1, 0) for part in (end[:, 0], beside)], axis=0
        )
        both = jnp.stack([end[:, 0], beside])
        mine = [swap_chips(corner[:, None], True), swap_chips(both, False)]
    else:
        sides = [shift(latent[:, 1, 0], "gy", 0), shift(latent[:, 0, 0], "gy", 1)]
        side_zeds = [swap(part, "gz") for part in sides]
        layers = []
        for middle, outer in ((latent, sides), (own_zed, side_zeds)):
            parts = [outer[0][:, None], middle[:, :, 0], outer[1][:, None]]
            parts = [lax.dynamic_index_in_dim(part, 1 - core, 0, False) for part in parts]
            layers.append(jnp.concatenate(parts, axis=0))
        mine = [swap_chips(jnp.stack(layers), False)]

    ranked = call(
        functools.partial(ranks_kernel, sizes),
        "ranks",
        [ANY] + [VMEM] * 12,
        [
            ((11, width, width), BF16),
            ((48, width), BF16),
            (edge_latent.shape, BF16),
            ((8, 256), I32),
            ((width, particles), F32),
            ((width, particles), F32),
            ((8, particles), F32),
            ((neighbour_count, movers, width), BF16),
            ((1, neighbour_count * movers), I32),
            ((1, neighbour_count * movers), I32),
            ((width, movers), F32),
            ((width, movers), F32),
            ((width, movers), F32),
            ((8, movers), F32),
            ((4, width, 2 * slots), BF16),
            ((2, width, neighbour_count * slots), BF16),
        ],
        [pltpu.SemaphoreType.DMA((1,))],
        (in_hbm(edge_latent), latent, own_zed, alive, *copied),
        5_000_000_000,
    )
    mine, sides, ranked = lax.optimization_barrier((mine, sides, ranked))
    (
        weights,
        inward,
        edge_latent,
        spread,
        latent_t,
        node_pre,
        state,
        mover_edges,
        mover_place,
        mover_key,
        mover_near,
        mover_node_pre,
        mover_latent,
        mover_state,
        far_own,
        early,
    ) = ranked
    mine = jnp.concatenate(mine[::-1], axis=1)
    if fold_y:
        sides = [lax.dynamic_index_in_dim(sides[0][:, :, 0], lax.axis_index("gy"), 1, False)]
        packed = jnp.concatenate([mine.reshape(-1, slots, width), sides[0]], axis=0)
    else:
        packed = mine.reshape(-1, slots, width)
    packed = swap(packed, "gz")
    prepared = call(
        functools.partial(prepare_kernel, sizes),
        "prepare",
        [VMEM] * 7,
        [((rows, width, 2 * slots), BF16), ((width, neighbour_count * movers), F32)],
        [],
        (far_own, mine, weights, mover_edges, mover_place, mover_key, mover_near),
        5_000_000_000,
    )
    packed, prepared = lax.optimization_barrier((packed, prepared))
    cells = mine.shape[0] * mine.shape[1]
    if fold_y:
        side_zeds = [packed[cells:]]
    far_mine, mover_pre = prepared
    halo = [*sides, *side_zeds, packed[:cells].reshape(mine.shape), far_mine]

    far_rest, bucket = call(
        functools.partial(movers_kernel, sizes, len(sides)),
        "movers",
        [VMEM] * (len(halo) + 8),
        [((4 * rows - 4, width, 2 * slots), BF16), ((ROWS, movers), F32)],
        [pltpu.VMEM((width, neighbour_count * movers), BF16)],
        (
            *halo,
            weights,
            decoder_out,
            mover_pre,
            mover_place,
            mover_key,
            mover_node_pre,
            mover_latent,
            mover_state,
        ),
        3_000_000_000,
    )

    def edges(a):
        return call(
            functools.partial(edges_kernel, sizes, a),
            "edges",
            [VMEM] * 8,
            [((2, width, slots), BF16)],
            [pltpu.VMEM((2, width, neighbour_count * slots), BF16)],
            (alive, latent, edge_latent, neighbours, far_own, far_rest, early, weights),
            4_000_000_000,
        )[0]

    zed = swap(bucket, "gz")
    if fold_y:
        sides = [swap(bucket, "gy")]
        zed, far_rest = lax.optimization_barrier((zed, far_rest))
        both = jnp.stack([bucket, zed])
        ends = [swap_chips(both, True), swap_chips(both, False)]
    else:
        both = jnp.stack([bucket, zed])
        sides = [shift(both, "gy", 0), shift(both, "gy", 1)]
        ends = [swap_chips(jnp.stack([both, *sides], axis=1), False)]
    first, second = edges(0), edges(1)
    sides, ends, first, second = lax.optimization_barrier((sides, ends, first, second))
    if fold_y:
        packed = swap(jnp.concatenate([*ends, sides[0][None]], axis=0), "gz")
    else:
        packed = swap(ends[0], "gz")
    state = call(
        nodes_kernel,
        "nodes",
        [VMEM] * 7,
        [((ROWS, particles), F32)],
        [],
        (first, second, node_pre, latent_t, state, weights, decoder_out),
        1_000_000_000,
    )[0]
    packed, state = lax.optimization_barrier((packed, state))
    return call(
        functools.partial(finish_kernel, sizes),
        "finish",
        [VMEM] * (len(sides) + len(ends) + 6),
        [
            (node_latent.shape, BF16),
            ((9,) + node_latent.shape[:4], F32),
            ((1, 1, 1, 26 * CAP, width), BF16),
            ((9, 1, 1, 1, 26 * CAP), F32),
        ],
        [],
        (state, zed, *sides, *ends, packed, spread, inward, encoder_weights),
        1_000_000_000,
    )


def solution(mesh):
    placed = (
        P(("group", "gx"), "gy", "gz", None, None),
        P(("group", "gx"), "gy", "gz", None, None, None),
        P(None, ("group", "gx"), "gy", "gz", None),
        P(None, ("group", "gx"), "gy", "gz", None),
        P(("group", "gx"), "gy", "gz"),
        P(("group", "gx"), "gy", "gz", None, None),
        P(("group", "gx"), "gy", "gz", None),
        P(),
        P(),
        P(),
        P(),
        P(),
        P(),
        P(),
    )
    return jax.shard_map(
        body,
        mesh=mesh,
        in_specs=placed,
        out_specs=(
            P(("group", "gx"), "gy", "gz", None, None),
            P(None, ("group", "gx"), "gy", "gz", None),
            P(("group", "gx"), "gy", "gz", None, None),
            P(None, ("group", "gx"), "gy", "gz", None),
        ),
        check_vma=False,
    )
```

```python
import functools

import jax
import jax.numpy as jnp
from jax import lax
from jax.experimental import pallas as pl
from jax.experimental.pallas import tpu as pltpu
from jax.sharding import PartitionSpec as P

CAP = 8
F32 = jnp.float32
BF16 = jnp.bfloat16
I32 = jnp.int32
ROWS = 16
TILE = 256
CELLS = [(a, b) for a in range(2) for b in range(2)]
EDGE, NEAR, FAR, MIDDLE, FINAL, NODE_OLD, NODE_NEW, NODE_0, NODE_1, DECODE_0, DECODE_1 = range(11)

VMEM = pl.BlockSpec(memory_space=pltpu.VMEM)
SMEM = pl.BlockSpec(memory_space=pltpu.SMEM)
ANY = pl.BlockSpec(memory_space=pl.ANY)


def dot(left, right):
    return jnp.dot(left, right, preferred_element_type=F32)


def dot_nt(left, right):
    return lax.dot_general(left, right, (((1,), (1,)), ((), ())), preferred_element_type=F32)


def dot_tn(left, right):
    return lax.dot_general(left, right, (((0,), (0,)), ((), ())), preferred_element_type=F32)


def relu16(values):
    return jnp.maximum(values, 0.0).astype(BF16)


def norm(values, axis):
    scale = 1.0 / values.shape[axis]
    centred = values - jnp.sum(values, axis=axis, keepdims=True) * scale
    spread = jnp.sum(centred * centred, axis=axis, keepdims=True) * scale
    return centred * lax.rsqrt(spread + 1e-05)


def thirds(values):
    high = values.astype(BF16)
    rest = values - high.astype(F32)
    middle = rest.astype(BF16)
    low = (rest - middle.astype(F32)).astype(BF16)
    return jnp.concatenate([high, middle, low], axis=0)


def joined(values):
    rows = values.shape[0] // 3
    return values[:rows] + values[rows : 2 * rows] + values[2 * rows :]


def quotient(values, count):
    if count & (count - 1) == 0:
        return values >> (count.bit_length() - 1)
    return lax.div(values, jnp.full_like(values, count))


def flip(weights):
    return weights.astype(F32).T.astype(BF16)


def fetch(pairs, sems):
    copies = [pltpu.make_async_copy(src, dst, sems.at[i]) for i, (src, dst) in enumerate(pairs)]
    for copy in copies:
        copy.start()
    return copies


def encode(state, mask, inward, encoder_w, extent):
    width = state.shape[1]
    position = state[0:3]
    row = lax.broadcasted_iota(I32, (3, width), 0)
    size = jnp.where(row == 0, extent[0], jnp.where(row == 1, extent[1], extent[2]))
    features = jnp.concatenate(
        [
            state[3:9],
            jnp.clip(position, -1.0, 1.0),
            jnp.clip(size - position, -1.0, 1.0),
            jnp.zeros((4, width), F32),
        ],
        axis=0,
    )
    hidden = relu16(dot_tn(thirds(features), inward))
    hidden = relu16(dot(hidden, encoder_w[0]))
    column = jnp.broadcast_to(mask, (8, width)).T[:, 0:1]
    return (norm(dot(hidden, encoder_w[1]), 1) * column).astype(BF16)


def places(ids_low, ids_high, fold_y):
    plane = (ids_high * 43) >> 7
    ez = ids_high - plane * 3
    ey = plane & 3
    ex = plane >> 2
    if fold_y:
        row = jnp.where(ey == 1, 0, jnp.where(ey == 2, 1, 2))
    else:
        row = ey
    return ex * 4 + row, ids_low + jnp.where(ez == 1, 0, 128)


def pick(cells, place, key):
    width = cells[0][1].shape[0]
    chunk = 32
    window = jnp.concatenate(
        [ref[f : f + chunk] for f in range(0, width, chunk) for _, ref in cells], axis=0
    )
    key_rows = lax.broadcasted_iota(I32, (TILE, TILE), 0).astype(F32).astype(BF16)
    key = jnp.broadcast_to(key.astype(F32), (16, TILE)).astype(BF16)
    same = key_rows.reshape(TILE // 16, 16, TILE) == key[None]
    picker = jnp.where(same, jnp.ones((), BF16), jnp.zeros((), BF16)).reshape(TILE, TILE)
    found = dot(window, picker).reshape(width // chunk, len(cells), chunk // 8, 8, TILE)
    where = jnp.broadcast_to(place, (8, TILE))
    parts = []
    for f in range(width // chunk):
        part = jnp.zeros((chunk // 8, 8, TILE), F32)
        for i, (column, _) in enumerate(cells):
            part = jnp.where((where == column)[None], found[f, i], part)
        parts.append(part.reshape(chunk, TILE))
    return jnp.concatenate(parts, axis=0)


def messages(cells, place, key, pre, middle_t, final_t, hidden_ref):
    for tile in range(place.shape[1] // TILE):
        at = slice(tile * TILE, (tile + 1) * TILE)
        hidden_ref[:, at] = relu16(pre(tile) + pick(cells, place[:, at], key[:, at]))
    hidden = relu16(dot(middle_t, hidden_ref[...]))
    return norm(dot(final_t, hidden), 0)


class Window:
    def __init__(self, fold_y, own_ref=None, rest_ref=None):
        self.row_count = 3 if fold_y else 4
        self.own_rows = (0, 1) if fold_y else (1, 2)
        self.outer_rows = (2,) if fold_y else (0, 3)
        self.own_ref, self.rest_ref = own_ref, rest_ref

    def own_columns(self):
        return [(ex, row) for ex in (1, 2) for row in self.own_rows]

    def own(self, ex, row):
        return (ex - 1) * 2 + self.own_rows.index(row)

    def side(self, ex, row):
        count = len(self.outer_rows)
        return 2 * self.row_count + (ex - 1) * count + self.outer_rows.index(row)

    def cells(self, columns):
        found = []
        for ex, row in columns:
            if ex in (1, 2) and row in self.own_rows:
                ref = self.own_ref.at[self.own(ex, row)]
            elif ex in (1, 2):
                ref = self.rest_ref.at[self.side(ex, row)]
            else:
                ref = self.rest_ref.at[(0 if ex == 0 else self.row_count) + row]
            found.append((ex * 4 + row, ref))
        return found


def slot_sum(message, step):
    total = message[:, :step]
    for at in range(step, message.shape[1], step):
        total = total + message[:, at : at + step]
    return total


def advance(pre, aggregate, latent_t, weights_ref, decoder_out):
    pre = pre + dot(weights_ref[NODE_NEW], aggregate)
    hidden = relu16(dot(weights_ref[NODE_0], relu16(pre)))
    updated = (latent_t + norm(dot(weights_ref[NODE_1], hidden), 0)).astype(BF16)
    hidden = relu16(dot(weights_ref[DECODE_0], updated))
    hidden = relu16(dot(weights_ref[DECODE_1], hidden))
    return dot(decoder_out, hidden)


def moved(position, velocity, acceleration):
    new_velocity = velocity + acceleration
    return jnp.concatenate([position + new_velocity, new_velocity, velocity], axis=0)


def cut_kernel(count, fill_any, *refs):
    sources, refs = refs[:count], refs[count:]
    copied, (end_ref, alive_ref, fill_ref, sems) = refs[:count], refs[count:]
    end = 1 - lax.axis_index("gz")
    copies = fetch(
        [(fill_any, fill_ref), (sources[0].at[end], end_ref), *zip(sources, copied)], sems
    )
    copies[0].wait()
    lane = lax.broadcasted_iota(I32, alive_ref.shape[2:], 1)
    for a, b in CELLS:
        alive_ref[a, b] = jnp.where(lane < fill_ref[a, 0, b], 1.0, 0.0)
    for copy in copies[1:]:
        copy.wait()


def ranks_kernel(
    sizes,
    edge_any,
    latent_ref,
    own_zed,
    alive_ref,
    owners_ref,
    edge_w_ref,
    node_in_ref,
    node_w_ref,
    decoder_w_ref,
    encoder_in_ref,
    neighbours_ref,
    positions_ref,
    velocity_ref,
    weights_ref,
    inward_ref,
    edge_ref,
    spread_ref,
    latent_t_ref,
    node_pre_ref,
    state_ref,
    mover_edge_ref,
    mover_place_ref,
    mover_key_ref,
    mover_near_ref,
    mover_node_pre_ref,
    mover_latent_ref,
    mover_state_ref,
    far_ref,
    early_ref,
    sems,
):
    count_x, count_y, count_z = sizes
    fold_y = count_y == 2
    copies = fetch([(edge_any, edge_ref)], sems)
    index_x = lax.axis_index("gx")
    index_y = lax.axis_index("gy")
    index_z = lax.axis_index("gz")
    slots = owners_ref.shape[-1]
    width = node_in_ref.shape[-1]
    owner = jnp.concatenate([owners_ref[a, b] for a, b in CELLS], axis=1)
    alive = jnp.concatenate([alive_ref[a, b] for a, b in CELLS], axis=1)
    own_block = (index_x * count_y + index_y) * count_z + index_z
    stays = jnp.where((alive > 0.5) & (owner == own_block), 1.0, 0.0)
    moving = jnp.where((alive > 0.5) & (owner != own_block), 1, 0)
    owner_x = quotient(owner, count_y * count_z)
    rest = owner - owner_x * (count_y * count_z)
    owner_y = quotient(rest, count_z)
    owner_z = rest - owner_y * count_z
    step_y = owner_y - index_y
    side_y = jnp.where(step_y == 0, 0, 1) if fold_y else jnp.where(step_y < 0, 1, 2 * step_y)
    options_y = 2 if fold_y else 3
    group = ((owner_x - index_x + 1) * options_y + side_y) * 2 + jnp.where(owner_z == index_z, 0, 1)
    group_rows = (3 * options_y * 2 + 15) // 16 * 16
    particles = owner.shape[1]
    member = jnp.where(
        (lax.broadcasted_iota(I32, (group_rows, particles), 0) == group) & (moving == 1), 1.0, 0.0
    )
    triangle = jnp.where(
        lax.broadcasted_iota(I32, (slots, slots), 0) <= lax.broadcasted_iota(I32, (slots, slots), 1),
        1.0,
        0.0,
    ).astype(BF16)
    counted = []
    before = jnp.zeros((group_rows, 1), F32)
    for i in range(4):
        inside = member[:, i * slots : (i + 1) * slots]
        counted.append(dot(inside.astype(BF16), triangle) + before)
        before = before + jnp.sum(inside, axis=1, keepdims=True)
    counted = jnp.concatenate(counted, axis=1)
    rank = (jnp.sum(counted * member, axis=0, keepdims=True) - 1.0).astype(I32)
    column = jnp.where(moving == 1, group * CAP + rank, -1)
    movers = mover_state_ref.shape[1]
    placer = jnp.where(
        lax.broadcasted_iota(I32, (movers, particles), 0) == column, 1.0, 0.0
    ).astype(BF16)

    line = lax.broadcasted_iota(I32, spread_ref.shape, 1)
    direction = line >> 3
    direction = direction + jnp.where(direction > 12, 1, 0)
    plane = (direction * 57) >> 9
    from_z = direction - 3 * ((direction * 43) >> 7) - 1
    from_y = ((direction * 43) >> 7) - 3 * plane - 1
    if fold_y:
        side_y = jnp.where(from_y == 0, 0, 1)
        valid = (from_y == 0) | (from_y == 1 - 2 * index_y)
    else:
        side_y = jnp.where(from_y < 0, 2, from_y)
        valid = from_y < 2
    side_z = jnp.where(from_z == 0, 0, 1)
    valid = valid & ((from_z == 0) | (from_z == 1 - 2 * index_z)) & (line < 26 * CAP)
    target = ((2 - plane) * options_y + side_y) * 2 + side_z
    spread_ref[...] = jnp.where(valid, target * CAP + (line & 7), -1)

    for i in range(5):
        weights_ref[i] = flip(edge_w_ref[i])
    weights_ref[NODE_OLD] = flip(node_in_ref[:width])
    weights_ref[NODE_NEW] = flip(node_in_ref[width:])
    for i in range(2):
        weights_ref[NODE_0 + i] = flip(node_w_ref[i])
        weights_ref[DECODE_0 + i] = flip(decoder_w_ref[i])
    inward = jnp.concatenate([encoder_in_ref[...].astype(F32), jnp.zeros((4, width), F32)], axis=0)
    inward = inward.astype(BF16)
    inward_ref[...] = jnp.concatenate([inward, inward, inward], axis=0)

    latent = jnp.concatenate([latent_ref[a, b, 0] for a, b in CELLS], axis=0)
    latent_t_ref[...] = latent.astype(F32).T
    node_pre_ref[...] = dot_nt(weights_ref[NODE_OLD], latent)

    def flat(ref, i):
        return jnp.concatenate([ref[i, a, b] for a, b in CELLS], axis=1)

    state = [flat(positions_ref, i) for i in range(3)] + [flat(velocity_ref, i) for i in range(3)]
    state_ref[...] = jnp.concatenate(state + [stays, jnp.zeros_like(stays)], axis=0)

    mover_latent = dot(placer, latent).astype(BF16)
    mover_latent_ref[...] = mover_latent.astype(F32).T
    mover_node_pre_ref[...] = dot_nt(weights_ref[NODE_OLD], mover_latent)
    mover_near_ref[...] = dot_nt(weights_ref[NEAR], mover_latent)
    state = jnp.concatenate(state + [moving.astype(F32), jnp.zeros_like(stays)], axis=0)
    mover_state_ref[...] = joined(dot_nt(thirds(state), placer))
    neighbour_count = edge_ref.shape[3]
    ids = jnp.concatenate(
        [
            jnp.concatenate([neighbours_ref[a, b, k] for a, b in CELLS], axis=1)
            for k in range(neighbour_count)
        ],
        axis=0,
    )
    ids = jnp.concatenate([ids & 127, ids >> 7, jnp.zeros((8, particles), I32)], axis=0)
    ids = dot_nt(ids.astype(F32).astype(BF16), placer).astype(I32)
    place, key = places(ids[:neighbour_count], ids[neighbour_count : 2 * neighbour_count], fold_y)
    mover_place_ref[...] = jnp.concatenate([place[k : k + 1] for k in range(neighbour_count)], axis=1)
    mover_key_ref[...] = jnp.concatenate([key[k : k + 1] for k in range(neighbour_count)], axis=1)

    window = Window(fold_y, far_ref)
    for (ex, row), (a, b) in zip(window.own_columns(), CELLS):
        pair = jnp.concatenate([latent_ref[a, b, 0], own_zed[a, b, 0]], axis=0)
        far_ref[window.own(ex, row)] = dot_nt(weights_ref[FAR], pair).astype(BF16)
    cells = window.cells(window.own_columns())
    for a, bt in CELLS:
        b = (index_y if bt == 0 else 1 - index_y) if fold_y else bt
        ids = jnp.concatenate([neighbours_ref[a, b, k] for k in range(neighbour_count)], axis=1)
        place, key = places(ids & 127, ids >> 7, fold_y)
        for tile in range(ids.shape[1] // TILE):
            at = slice(tile * TILE, (tile + 1) * TILE)
            early_ref[2 * a + bt, :, at] = pick(cells, place[:, at], key[:, at]).astype(BF16)

    copies[-1].wait()
    for k in range(neighbour_count):
        rows = jnp.concatenate([edge_ref[a, b, 0, k] for a, b in CELLS], axis=0)
        mover_edge_ref[k] = dot(placer, rows).astype(BF16)


def prepare_kernel(
    sizes,
    far_ref,
    mine_ref,
    weights_ref,
    edge_ref,
    place_ref,
    key_ref,
    near_ref,
    far_mine_ref,
    pre_ref,
):
    window = Window(sizes[1] == 2, far_ref)
    core = lax.axis_index("gz")
    far_t = weights_ref[FAR]
    cells = window.cells(window.own_columns())
    for row in range(window.row_count):
        pair = jnp.concatenate([mine_ref[1, row], mine_ref[0, row]], axis=0)
        far_mine_ref[row] = dot_nt(far_t, pair).astype(BF16)
        cells.append((12 * (1 - core) + row, far_mine_ref.at[row]))
    neighbour_count, movers = edge_ref.shape[:2]
    step = TILE // movers
    near = jnp.concatenate([near_ref[...]] * step, axis=1)
    for tile in range(neighbour_count // step):
        edges = jnp.concatenate([edge_ref[k] for k in range(tile * step, (tile + 1) * step)], axis=0)
        at = slice(tile * TILE, (tile + 1) * TILE)
        pre_ref[:, at] = (
            dot_nt(weights_ref[EDGE], edges) + near + pick(cells, place_ref[:, at], key_ref[:, at])
        )


def movers_kernel(
    sizes,
    side_count,
    *refs,
):
    fold_y = sizes[1] == 2
    side_refs, refs = refs[:side_count], refs[side_count:]
    side_zeds, refs = refs[:side_count], refs[side_count:]
    other_ref, far_mine_ref, refs = refs[0], refs[1], refs[2:]
    (
        weights_ref,
        decoder_out_ref,
        pre_ref,
        place_ref,
        key_ref,
        node_pre_ref,
        latent_t_ref,
        state_ref,
        far_ref,
        bucket_ref,
        hidden_ref,
    ) = refs
    window = Window(fold_y, None, far_ref)
    row_count = window.row_count
    core = lax.axis_index("gz")
    far_t = weights_ref[FAR]

    def far(at, here, beside):
        pair = jnp.concatenate([here, beside], axis=0)
        far_ref[at] = dot_nt(far_t, pair).astype(BF16)

    for row in range(row_count):
        far(core * row_count + row, other_ref[0, row], other_ref[1, row])
    for side, row in enumerate(window.outer_rows):
        for ex in (1, 2):
            far(window.side(ex, row), side_refs[side][ex - 1], side_zeds[side][ex - 1])

    movers = state_ref.shape[1]
    for row in range(row_count):
        far_ref[(1 - core) * row_count + row] = far_mine_ref[row]
    cells = [(12 * core + row, far_ref.at[core * row_count + row]) for row in range(row_count)]
    cells += window.cells([(ex, row) for ex in (1, 2) for row in window.outer_rows])
    message = messages(
        cells,
        place_ref[...],
        key_ref[...],
        lambda tile: pre_ref[:, tile * TILE : (tile + 1) * TILE],
        weights_ref[MIDDLE],
        weights_ref[FINAL],
        hidden_ref,
    )
    aggregate = slot_sum(message, movers).astype(BF16)
    acceleration = advance(
        node_pre_ref[...], aggregate, latent_t_ref[...], weights_ref, decoder_out_ref[...]
    )
    mask = state_ref[6:7]
    state = moved(state_ref[0:3], state_ref[3:6], acceleration) * mask
    bucket_ref[...] = jnp.concatenate([state, mask, jnp.zeros((ROWS - 10, movers), F32)], axis=0)


def edges_kernel(
    sizes,
    a,
    alive_ref,
    latent_ref,
    edge_ref,
    neighbours_ref,
    far_own_ref,
    far_rest_ref,
    early_ref,
    weights_ref,
    total_ref,
    hidden_ref,
):
    fold_y = sizes[1] == 2
    window = Window(fold_y, far_own_ref, far_rest_ref)
    index_y = lax.axis_index("gy")
    alive_ref, latent_ref = alive_ref.at[a], latent_ref.at[a]
    edge_ref, neighbours_ref = edge_ref.at[a], neighbours_ref.at[a]
    slots, width = latent_ref.shape[-2:]
    neighbour_count = edge_ref.shape[2]
    for bt in range(2):
        if fold_y:
            b = index_y if bt == 0 else 1 - index_y
            rows = (0, 1) if bt == 0 else (0, 1, 2)
        else:
            b = bt
            rows = (bt, bt + 1, bt + 2)
        columns = [(ex, row) for ex in range(a, a + 3) for row in rows]
        columns = [column for column in columns if column not in window.own_columns()]
        near = dot_nt(weights_ref[NEAR], latent_ref[b, 0])
        near = jnp.concatenate([near, near], axis=1)
        ids = jnp.concatenate([neighbours_ref[b, k] for k in range(neighbour_count)], axis=1)
        place, key = places(ids & 127, ids >> 7, fold_y)

        def pre(tile, b=b, bt=bt, near=near):
            edges = jnp.concatenate([edge_ref[b, 0, 2 * tile], edge_ref[b, 0, 2 * tile + 1]], axis=0)
            early = early_ref[2 * a + bt, :, tile * TILE : (tile + 1) * TILE]
            return dot_nt(weights_ref[EDGE], edges) + near + early.astype(F32)

        message = messages(
            window.cells(columns),
            place,
            key,
            pre,
            weights_ref[MIDDLE],
            weights_ref[FINAL],
            hidden_ref.at[bt],
        )
        total = jnp.where(alive_ref[b] > 0.5, slot_sum(message, slots), 0.0)
        total_ref[b] = total.astype(BF16)


def nodes_kernel(
    first_ref,
    second_ref,
    node_pre_ref,
    latent_t_ref,
    state_ref,
    weights_ref,
    decoder_out_ref,
    moved_ref,
):
    aggregate = jnp.concatenate([first_ref[0], first_ref[1], second_ref[0], second_ref[1]], axis=1)
    acceleration = advance(
        node_pre_ref[...], aggregate, latent_t_ref[...], weights_ref, decoder_out_ref[...]
    )
    state = moved(state_ref[0:3], state_ref[3:6], acceleration)
    moved_ref[...] = jnp.concatenate(
        [state, state_ref[6:7], jnp.zeros((ROWS - 10, state.shape[1]), F32)], axis=0
    )


def finish_kernel(sizes, moved_ref, zed_ref, *refs):
    count_x, count_y, count_z = sizes
    fold_y = count_y == 2
    options_y = 2 if fold_y else 3
    side_refs, refs = refs[: options_y - 1], refs[options_y - 1 :]
    if fold_y:
        cross_ref, end_ref, *refs = refs
    else:
        end_ref, *refs = refs
    (
        packed_ref,
        spread_ref,
        inward_ref,
        encoder_w_ref,
        kept_latent_ref,
        kept_state_ref,
        arrived_latent_ref,
        arrived_state_ref,
    ) = refs
    core = lax.axis_index("gz")

    def tile(source_x, from_y, from_z):
        if source_x == 0:
            if from_y == 0:
                return zed_ref[...]
            if fold_y:
                return packed_ref[4] if from_z else side_refs[0][...]
            return side_refs[from_y - 1][from_z]
        if fold_y:
            mine = (cross_ref if from_y else end_ref)[1 - from_z]
            other = packed_ref[(0 if from_y else 2) + from_z]
        else:
            mine = end_ref[1 - from_z, from_y]
            other = packed_ref[from_z, from_y]
        return jnp.where(core == (1 - source_x) // 2, mine, other)

    extent = (2.0 * count_x, 2.0 * count_y, 1.0 * count_z)
    slots = kept_latent_ref.shape[-2]
    stays = moved_ref[9:10]
    kept = moved_ref[:9] * stays
    latents = encode(moved_ref[:9], stays, inward_ref[...], encoder_w_ref[...], extent)
    for i, (a, b) in enumerate(CELLS):
        kept_latent_ref[a, b, 0] = latents[i * slots : (i + 1) * slots]
        for j in range(9):
            kept_state_ref[j, a, b] = kept[j : j + 1, i * slots : (i + 1) * slots]
    fold_y = count_y == 2
    index_x = lax.axis_index("gx")
    lanes = zed_ref.shape[-1]
    group = lax.broadcasted_iota(I32, (ROWS, lanes), 1) >> 3
    found = jnp.zeros((ROWS, lanes), F32)
    for source_x in (-1, 0, 1):
        for from_y in range(options_y):
            for from_z in range(2):
                if source_x == 0 and from_y == 0 and from_z == 0:
                    continue
                side_y = from_y if fold_y or from_y == 0 else 3 - from_y
                there = group == ((1 - source_x) * options_y + side_y) * 2 + from_z
                if source_x == -1:
                    there = there & (index_x > 0)
                elif source_x == 1:
                    there = there & (index_x < count_x - 1)
                found = jnp.where(there, tile(source_x, from_y, from_z), found)
    halves = []
    for at in range(0, spread_ref.shape[1], 128):
        lane = jnp.broadcast_to(spread_ref[0:1, at : at + 128], (ROWS, 128))
        half = jnp.zeros((ROWS, 128), F32)
        for base in range(0, lanes, 128):
            index = jnp.clip(lane - base, 0, 127)
            there = (lane >= base) & (lane < base + 128)
            part = jnp.take_along_axis(found[:, base : base + 128], index, axis=1)
            half = jnp.where(there, part, half)
        halves.append(half)
    arrived = jnp.concatenate(halves, axis=1)[:, : 26 * CAP]
    for j in range(9):
        arrived_state_ref[j, 0, 0] = arrived[j : j + 1]
    arrived_latent_ref[0, 0, 0] = encode(
        arrived[:9], arrived[9:10], inward_ref[...], encoder_w_ref[...], extent
    )


def swap(values, axis):
    return lax.ppermute(values, axis, [(0, 1), (1, 0)])


def shift(values, axis, way):
    pairs = [(i, i + 1) for i in range(lax.axis_size(axis) - 1)]
    return lax.ppermute(values, axis, [(j, i) for i, j in pairs] if way else pairs)


def swap_chips(values, cross):
    count_x, count_y, count_z = (lax.axis_size(axis) for axis in ("gx", "gy", "gz"))
    pairs = []
    for x in range(count_x):
        for y in range(count_y):
            for z in range(count_z):
                to_x = x + 1 - 2 * z
                if 0 <= to_x < count_x:
                    to = (to_x, y ^ 1 if cross else y, 1 - z)
                else:
                    to = (x, y ^ 1, z)
                pairs.append(((x * count_y + y) * count_z + z, (to[0] * count_y + to[1]) * count_z + to[2]))
    return lax.ppermute(values, ("gx", "gy", "gz"), pairs)


def call(kernel, name, in_specs, outs, scratch, operands, flops):
    return pl.pallas_call(
        kernel,
        out_shape=tuple(jax.ShapeDtypeStruct(shape, kind) for shape, kind in outs),
        in_specs=in_specs,
        out_specs=tuple(VMEM for _ in outs),
        scratch_shapes=scratch,
        compiler_params=pltpu.CompilerParams(vmem_limit_bytes=32 * 1024 * 1024),
        cost_estimate=pl.CostEstimate(flops=flops, bytes_accessed=0, transcendentals=0),
        name=name,
    )(*operands)


def in_hbm(array):
    return pltpu.with_memory_space_constraint(array, pltpu.HBM)


def like(array):
    return pltpu.VMEM(array.shape, array.dtype)


def body(
    node_latent,
    edge_latent,
    positions,
    velocity,
    fill,
    neighbours,
    owners,
    edge_weights,
    node_in,
    node_weights,
    decoder_weights,
    decoder_out,
    encoder_in,
    encoder_weights,
):
    sizes = tuple(lax.axis_size(axis) for axis in ("gx", "gy", "gz"))
    fold_y = sizes[1] == 2
    slots, width = node_latent.shape[-2:]
    neighbour_count = neighbours.shape[3]
    particles = 4 * slots
    options_y = 2 if fold_y else 3
    movers = (3 * options_y * 2 * CAP + 127) // 128 * 128
    rows = 3 if fold_y else 4
    fill = jnp.transpose(fill, (0, 2, 1))
    neighbours = neighbours.reshape(2, 2, neighbour_count, 1, slots)

    own_zed = swap(node_latent, "gz")
    if fold_y:
        sides = [swap(node_latent, "gy")]
    small = (node_latent,)
    *copied, end, alive = call(
        functools.partial(cut_kernel, len(small)),
        "cut",
        [ANY] * (len(small) + 1),
        [(array.shape, array.dtype) for array in small]
        + [(node_latent.shape[1:], BF16), ((2, 2, 1, slots), F32)],
        [pltpu.SMEM(fill.shape, I32), pltpu.SemaphoreType.DMA((len(small) + 2,))],
        [in_hbm(array) for array in (fill, *small)],
        5_000_000_000,
    )
    latent = copied[0]
    core = lax.axis_index("gz")
    if fold_y:
        row = 1 - lax.axis_index("gy")
        beside = lax.dynamic_index_in_dim(own_zed[:, :, 0], 1 - core, 0, False)
        corner = jnp.concatenate(
            [lax.dynamic_slice_in_dim(part, row, 1, 0) for part in (end[:, 0], beside)], axis=0
        )
        both = jnp.stack([end[:, 0], beside])
        mine = [swap_chips(corner[:, None], True), swap_chips(both, False)]
    else:
        sides = [shift(latent[:, 1, 0], "gy", 0), shift(latent[:, 0, 0], "gy", 1)]
        side_zeds = [swap(part, "gz") for part in sides]
        layers = []
        for middle, outer in ((latent, sides), (own_zed, side_zeds)):
            parts = [outer[0][:, None], middle[:, :, 0], outer[1][:, None]]
            parts = [lax.dynamic_index_in_dim(part, 1 - core, 0, False) for part in parts]
            layers.append(jnp.concatenate(parts, axis=0))
        mine = [swap_chips(jnp.stack(layers), False)]

    ranked = call(
        functools.partial(ranks_kernel, sizes),
        "ranks",
        [ANY] + [VMEM] * 12,
        [
            ((11, width, width), BF16),
            ((48, width), BF16),
            (edge_latent.shape, BF16),
            ((8, 256), I32),
            ((width, particles), F32),
            ((width, particles), F32),
            ((8, particles), F32),
            ((neighbour_count, movers, width), BF16),
            ((1, neighbour_count * movers), I32),
            ((1, neighbour_count * movers), I32),
            ((width, movers), F32),
            ((width, movers), F32),
            ((width, movers), F32),
            ((8, movers), F32),
            ((4, width, 2 * slots), BF16),
            ((4, width, neighbour_count * slots), BF16),
        ],
        [pltpu.SemaphoreType.DMA((1,))],
        (in_hbm(edge_latent), latent, own_zed, alive, owners, edge_weights, node_in, node_weights, decoder_weights, encoder_in, neighbours, positions, velocity),
        5_000_000_000,
    )
    mine, sides, ranked = lax.optimization_barrier((mine, sides, ranked))
    (
        weights,
        inward,
        edge_latent,
        spread,
        latent_t,
        node_pre,
        state,
        mover_edges,
        mover_place,
        mover_key,
        mover_near,
        mover_node_pre,
        mover_latent,
        mover_state,
        far_own,
        early,
    ) = ranked
    mine = jnp.concatenate(mine[::-1], axis=1)
    if fold_y:
        sides = [lax.dynamic_index_in_dim(sides[0][:, :, 0], lax.axis_index("gy"), 1, False)]
        packed = jnp.concatenate([mine.reshape(-1, slots, width), sides[0]], axis=0)
    else:
        packed = mine.reshape(-1, slots, width)
    packed = swap(packed, "gz")
    prepared = call(
        functools.partial(prepare_kernel, sizes),
        "prepare",
        [VMEM] * 7,
        [((rows, width, 2 * slots), BF16), ((width, neighbour_count * movers), F32)],
        [],
        (far_own, mine, weights, mover_edges, mover_place, mover_key, mover_near),
        5_000_000_000,
    )
    packed, prepared = lax.optimization_barrier((packed, prepared))
    cells = mine.shape[0] * mine.shape[1]
    if fold_y:
        side_zeds = [packed[cells:]]
    far_mine, mover_pre = prepared
    halo = [*sides, *side_zeds, packed[:cells].reshape(mine.shape), far_mine]

    far_rest, bucket = call(
        functools.partial(movers_kernel, sizes, len(sides)),
        "movers",
        [VMEM] * (len(halo) + 8),
        [((4 * rows - 4, width, 2 * slots), BF16), ((ROWS, movers), F32)],
        [pltpu.VMEM((width, neighbour_count * movers), BF16)],
        (
            *halo,
            weights,
            decoder_out,
            mover_pre,
            mover_place,
            mover_key,
            mover_node_pre,
            mover_latent,
            mover_state,
        ),
        3_000_000_000,
    )

    def edges(a):
        return call(
            functools.partial(edges_kernel, sizes, a),
            "edges",
            [VMEM] * 8,
            [((2, width, slots), BF16)],
            [pltpu.VMEM((2, width, neighbour_count * slots), BF16)],
            (alive, latent, edge_latent, neighbours, far_own, far_rest, early, weights),
            4_000_000_000,
        )[0]

    zed = swap(bucket, "gz")
    if fold_y:
        sides = [swap(bucket, "gy")]
        zed, far_rest = lax.optimization_barrier((zed, far_rest))
        both = jnp.stack([bucket, zed])
        ends = [swap_chips(both, True), swap_chips(both, False)]
    else:
        both = jnp.stack([bucket, zed])
        sides = [shift(both, "gy", 0), shift(both, "gy", 1)]
        ends = [swap_chips(jnp.stack([both, *sides], axis=1), False)]
    first, second = edges(0), edges(1)
    sides, ends, first, second = lax.optimization_barrier((sides, ends, first, second))
    if fold_y:
        packed = swap(jnp.concatenate([*ends, sides[0][None]], axis=0), "gz")
    else:
        packed = swap(ends[0], "gz")
    state = call(
        nodes_kernel,
        "nodes",
        [VMEM] * 7,
        [((ROWS, particles), F32)],
        [],
        (first, second, node_pre, latent_t, state, weights, decoder_out),
        1_000_000_000,
    )[0]
    packed, state = lax.optimization_barrier((packed, state))
    return call(
        functools.partial(finish_kernel, sizes),
        "finish",
        [VMEM] * (len(sides) + len(ends) + 6),
        [
            (node_latent.shape, BF16),
            ((9,) + node_latent.shape[:4], F32),
            ((1, 1, 1, 26 * CAP, width), BF16),
            ((9, 1, 1, 1, 26 * CAP), F32),
        ],
        [],
        (state, zed, *sides, *ends, packed, spread, inward, encoder_weights),
        1_000_000_000,
    )


def solution(mesh):
    placed = (
        P(("group", "gx"), "gy", "gz", None, None),
        P(("group", "gx"), "gy", "gz", None, None, None),
        P(None, ("group", "gx"), "gy", "gz", None),
        P(None, ("group", "gx"), "gy", "gz", None),
        P(("group", "gx"), "gy", "gz"),
        P(("group", "gx"), "gy", "gz", None, None),
        P(("group", "gx"), "gy", "gz", None),
        P(),
        P(),
        P(),
        P(),
        P(),
        P(),
        P(),
    )
    return jax.shard_map(
        body,
        mesh=mesh,
        in_specs=placed,
        out_specs=(
            P(("group", "gx"), "gy", "gz", None, None),
            P(None, ("group", "gx"), "gy", "gz", None),
            P(("group", "gx"), "gy", "gz", None, None),
            P(None, ("group", "gx"), "gy", "gz", None),
        ),
        check_vma=False,
    )
```

```python
import functools

import jax
import jax.numpy as jnp
from jax import lax
from jax.experimental import pallas as pl
from jax.experimental.pallas import tpu as pltpu
from jax.sharding import PartitionSpec as P

CAP = 8
F32 = jnp.float32
BF16 = jnp.bfloat16
I32 = jnp.int32
ROWS = 16
TILE = 256
CELLS = [(a, b) for a in range(2) for b in range(2)]
EDGE, NEAR, FAR, MIDDLE, FINAL, NODE_OLD, NODE_NEW, NODE_0, NODE_1, DECODE_0, DECODE_1 = range(11)

VMEM = pl.BlockSpec(memory_space=pltpu.VMEM)
SMEM = pl.BlockSpec(memory_space=pltpu.SMEM)
ANY = pl.BlockSpec(memory_space=pl.ANY)


def dot(left, right):
    return jnp.dot(left, right, preferred_element_type=F32)


def dot_nt(left, right):
    return lax.dot_general(left, right, (((1,), (1,)), ((), ())), preferred_element_type=F32)


def dot_tn(left, right):
    return lax.dot_general(left, right, (((0,), (0,)), ((), ())), preferred_element_type=F32)


def relu16(values):
    return jnp.maximum(values, 0.0).astype(BF16)


def norm(values, axis):
    scale = 1.0 / values.shape[axis]
    centred = values - jnp.sum(values, axis=axis, keepdims=True) * scale
    spread = jnp.sum(centred * centred, axis=axis, keepdims=True) * scale
    return centred * lax.rsqrt(spread + 1e-05)


def thirds(values):
    high = values.astype(BF16)
    rest = values - high.astype(F32)
    middle = rest.astype(BF16)
    low = (rest - middle.astype(F32)).astype(BF16)
    return jnp.concatenate([high, middle, low], axis=0)


def joined(values):
    rows = values.shape[0] // 3
    return values[:rows] + values[rows : 2 * rows] + values[2 * rows :]


def quotient(values, count):
    if count & (count - 1) == 0:
        return values >> (count.bit_length() - 1)
    return lax.div(values, jnp.full_like(values, count))


def flip(weights):
    return weights.astype(F32).T.astype(BF16)


def fetch(pairs, sems):
    copies = [pltpu.make_async_copy(src, dst, sems.at[i]) for i, (src, dst) in enumerate(pairs)]
    for copy in copies:
        copy.start()
    return copies


def encode(state, mask, inward, encoder_w, extent):
    width = state.shape[1]
    position = state[0:3]
    row = lax.broadcasted_iota(I32, (3, width), 0)
    size = jnp.where(row == 0, extent[0], jnp.where(row == 1, extent[1], extent[2]))
    features = jnp.concatenate(
        [
            state[3:9],
            jnp.clip(position, -1.0, 1.0),
            jnp.clip(size - position, -1.0, 1.0),
            jnp.zeros((4, width), F32),
        ],
        axis=0,
    )
    hidden = relu16(dot_tn(thirds(features), inward))
    hidden = relu16(dot(hidden, encoder_w[0]))
    column = jnp.broadcast_to(mask, (8, width)).T[:, 0:1]
    return (norm(dot(hidden, encoder_w[1]), 1) * column).astype(BF16)


def places(ids_low, ids_high, fold_y):
    plane = (ids_high * 43) >> 7
    ez = ids_high - plane * 3
    ey = plane & 3
    ex = plane >> 2
    if fold_y:
        row = jnp.where(ey == 1, 0, jnp.where(ey == 2, 1, 2))
    else:
        row = ey
    return ex * 4 + row, ids_low + jnp.where(ez == 1, 0, 128)


def pick(cells, place, key):
    width = cells[0][1].shape[0]
    chunk = 32
    window = jnp.concatenate(
        [ref[f : f + chunk] for f in range(0, width, chunk) for _, ref in cells], axis=0
    )
    key_rows = lax.broadcasted_iota(I32, (TILE, TILE), 0).astype(F32).astype(BF16)
    key = jnp.broadcast_to(key.astype(F32), (16, TILE)).astype(BF16)
    same = key_rows.reshape(TILE // 16, 16, TILE) == key[None]
    picker = jnp.where(same, jnp.ones((), BF16), jnp.zeros((), BF16)).reshape(TILE, TILE)
    found = dot(window, picker).reshape(width // chunk, len(cells), chunk // 8, 8, TILE)
    where = jnp.broadcast_to(place, (8, TILE))
    parts = []
    for f in range(width // chunk):
        part = jnp.zeros((chunk // 8, 8, TILE), F32)
        for i, (column, _) in enumerate(cells):
            part = jnp.where((where == column)[None], found[f, i], part)
        parts.append(part.reshape(chunk, TILE))
    return jnp.concatenate(parts, axis=0)


def messages(cells, place, key, pre, middle_t, final_t, hidden_ref):
    for tile in range(place.shape[1] // TILE):
        at = slice(tile * TILE, (tile + 1) * TILE)
        hidden_ref[:, at] = relu16(pre(tile) + pick(cells, place[:, at], key[:, at]))
    hidden = relu16(dot(middle_t, hidden_ref[...]))
    return norm(dot(final_t, hidden), 0)


class Window:
    def __init__(self, fold_y, own_ref=None, rest_ref=None):
        self.row_count = 3 if fold_y else 4
        self.own_rows = (0, 1) if fold_y else (1, 2)
        self.outer_rows = (2,) if fold_y else (0, 3)
        self.own_ref, self.rest_ref = own_ref, rest_ref

    def own_columns(self):
        return [(ex, row) for ex in (1, 2) for row in self.own_rows]

    def own(self, ex, row):
        return (ex - 1) * 2 + self.own_rows.index(row)

    def side(self, ex, row):
        count = len(self.outer_rows)
        return 2 * self.row_count + (ex - 1) * count + self.outer_rows.index(row)

    def cells(self, columns):
        found = []
        for ex, row in columns:
            if ex in (1, 2) and row in self.own_rows:
                ref = self.own_ref.at[self.own(ex, row)]
            elif ex in (1, 2):
                ref = self.rest_ref.at[self.side(ex, row)]
            else:
                ref = self.rest_ref.at[(0 if ex == 0 else self.row_count) + row]
            found.append((ex * 4 + row, ref))
        return found


def slot_sum(message, step):
    total = message[:, :step]
    for at in range(step, message.shape[1], step):
        total = total + message[:, at : at + step]
    return total


def advance(pre, aggregate, latent_t, weights_ref, decoder_out):
    pre = pre + dot(weights_ref[NODE_NEW], aggregate)
    hidden = relu16(dot(weights_ref[NODE_0], relu16(pre)))
    updated = (latent_t + norm(dot(weights_ref[NODE_1], hidden), 0)).astype(BF16)
    hidden = relu16(dot(weights_ref[DECODE_0], updated))
    hidden = relu16(dot(weights_ref[DECODE_1], hidden))
    return dot(decoder_out, hidden)


def moved(position, velocity, acceleration):
    new_velocity = velocity + acceleration
    return jnp.concatenate([position + new_velocity, new_velocity, velocity], axis=0)


def cut_kernel(count, fill_any, *refs):
    sources, refs = refs[:count], refs[count:]
    copied, (end_ref, alive_ref, fill_ref, sems) = refs[:count], refs[count:]
    end = 1 - lax.axis_index("gz")
    copies = fetch(
        [(fill_any, fill_ref), (sources[0].at[end], end_ref), *zip(sources, copied)], sems
    )
    copies[0].wait()
    lane = lax.broadcasted_iota(I32, alive_ref.shape[2:], 1)
    for a, b in CELLS:
        alive_ref[a, b] = jnp.where(lane < fill_ref[a, 0, b], 1.0, 0.0)
    for copy in copies[1:]:
        copy.wait()


def ranks_kernel(
    sizes,
    edge_ref,
    latent_ref,
    own_zed,
    alive_ref,
    owners_ref,
    edge_w_ref,
    node_in_ref,
    node_w_ref,
    decoder_w_ref,
    encoder_in_ref,
    neighbours_ref,
    positions_ref,
    velocity_ref,
    weights_ref,
    inward_ref,
    spread_ref,
    latent_t_ref,
    node_pre_ref,
    state_ref,
    mover_edge_ref,
    mover_place_ref,
    mover_key_ref,
    mover_near_ref,
    mover_node_pre_ref,
    mover_latent_ref,
    mover_state_ref,
    far_ref,
    pre_ref,
):
    count_x, count_y, count_z = sizes
    fold_y = count_y == 2
    index_x = lax.axis_index("gx")
    index_y = lax.axis_index("gy")
    index_z = lax.axis_index("gz")
    slots = owners_ref.shape[-1]
    width = node_in_ref.shape[-1]
    owner = jnp.concatenate([owners_ref[a, b] for a, b in CELLS], axis=1)
    alive = jnp.concatenate([alive_ref[a, b] for a, b in CELLS], axis=1)
    own_block = (index_x * count_y + index_y) * count_z + index_z
    stays = jnp.where((alive > 0.5) & (owner == own_block), 1.0, 0.0)
    moving = jnp.where((alive > 0.5) & (owner != own_block), 1, 0)
    owner_x = quotient(owner, count_y * count_z)
    rest = owner - owner_x * (count_y * count_z)
    owner_y = quotient(rest, count_z)
    owner_z = rest - owner_y * count_z
    step_y = owner_y - index_y
    side_y = jnp.where(step_y == 0, 0, 1) if fold_y else jnp.where(step_y < 0, 1, 2 * step_y)
    options_y = 2 if fold_y else 3
    group = ((owner_x - index_x + 1) * options_y + side_y) * 2 + jnp.where(owner_z == index_z, 0, 1)
    group_rows = (3 * options_y * 2 + 15) // 16 * 16
    particles = owner.shape[1]
    member = jnp.where(
        (lax.broadcasted_iota(I32, (group_rows, particles), 0) == group) & (moving == 1), 1.0, 0.0
    )
    triangle = jnp.where(
        lax.broadcasted_iota(I32, (slots, slots), 0) <= lax.broadcasted_iota(I32, (slots, slots), 1),
        1.0,
        0.0,
    ).astype(BF16)
    counted = []
    before = jnp.zeros((group_rows, 1), F32)
    for i in range(4):
        inside = member[:, i * slots : (i + 1) * slots]
        counted.append(dot(inside.astype(BF16), triangle) + before)
        before = before + jnp.sum(inside, axis=1, keepdims=True)
    counted = jnp.concatenate(counted, axis=1)
    rank = (jnp.sum(counted * member, axis=0, keepdims=True) - 1.0).astype(I32)
    column = jnp.where(moving == 1, group * CAP + rank, -1)
    movers = mover_state_ref.shape[1]
    placer = jnp.where(
        lax.broadcasted_iota(I32, (movers, particles), 0) == column, 1.0, 0.0
    ).astype(BF16)

    line = lax.broadcasted_iota(I32, spread_ref.shape, 1)
    direction = line >> 3
    direction = direction + jnp.where(direction > 12, 1, 0)
    plane = (direction * 57) >> 9
    from_z = direction - 3 * ((direction * 43) >> 7) - 1
    from_y = ((direction * 43) >> 7) - 3 * plane - 1
    if fold_y:
        side_y = jnp.where(from_y == 0, 0, 1)
        valid = (from_y == 0) | (from_y == 1 - 2 * index_y)
    else:
        side_y = jnp.where(from_y < 0, 2, from_y)
        valid = from_y < 2
    side_z = jnp.where(from_z == 0, 0, 1)
    valid = valid & ((from_z == 0) | (from_z == 1 - 2 * index_z)) & (line < 26 * CAP)
    target = ((2 - plane) * options_y + side_y) * 2 + side_z
    spread_ref[...] = jnp.where(valid, target * CAP + (line & 7), -1)

    for i in range(5):
        weights_ref[i] = flip(edge_w_ref[i])
    weights_ref[NODE_OLD] = flip(node_in_ref[:width])
    weights_ref[NODE_NEW] = flip(node_in_ref[width:])
    for i in range(2):
        weights_ref[NODE_0 + i] = flip(node_w_ref[i])
        weights_ref[DECODE_0 + i] = flip(decoder_w_ref[i])
    inward = jnp.concatenate([encoder_in_ref[...].astype(F32), jnp.zeros((4, width), F32)], axis=0)
    inward = inward.astype(BF16)
    inward_ref[...] = jnp.concatenate([inward, inward, inward], axis=0)

    latent = jnp.concatenate([latent_ref[a, b, 0] for a, b in CELLS], axis=0)
    latent_t_ref[...] = latent.astype(F32).T
    node_pre_ref[...] = dot_nt(weights_ref[NODE_OLD], latent)

    def flat(ref, i):
        return jnp.concatenate([ref[i, a, b] for a, b in CELLS], axis=1)

    state = [flat(positions_ref, i) for i in range(3)] + [flat(velocity_ref, i) for i in range(3)]
    state_ref[...] = jnp.concatenate(state + [stays, jnp.zeros_like(stays)], axis=0)

    mover_latent = dot(placer, latent).astype(BF16)
    mover_latent_ref[...] = mover_latent.astype(F32).T
    mover_node_pre_ref[...] = dot_nt(weights_ref[NODE_OLD], mover_latent)
    mover_near_ref[...] = dot_nt(weights_ref[NEAR], mover_latent)
    state = jnp.concatenate(state + [moving.astype(F32), jnp.zeros_like(stays)], axis=0)
    mover_state_ref[...] = joined(dot_nt(thirds(state), placer))
    neighbour_count = edge_ref.shape[3]
    ids = jnp.concatenate(
        [
            jnp.concatenate([neighbours_ref[a, b, k] for a, b in CELLS], axis=1)
            for k in range(neighbour_count)
        ],
        axis=0,
    )
    ids = jnp.concatenate([ids & 127, ids >> 7, jnp.zeros((8, particles), I32)], axis=0)
    ids = dot_nt(ids.astype(F32).astype(BF16), placer).astype(I32)
    place, key = places(ids[:neighbour_count], ids[neighbour_count : 2 * neighbour_count], fold_y)
    mover_place_ref[...] = jnp.concatenate([place[k : k + 1] for k in range(neighbour_count)], axis=1)
    mover_key_ref[...] = jnp.concatenate([key[k : k + 1] for k in range(neighbour_count)], axis=1)

    window = Window(fold_y, far_ref)
    for (ex, row), (a, b) in zip(window.own_columns(), CELLS):
        pair = jnp.concatenate([latent_ref[a, b, 0], own_zed[a, b, 0]], axis=0)
        far_ref[window.own(ex, row)] = dot_nt(weights_ref[FAR], pair).astype(BF16)
    cells = window.cells(window.own_columns())
    for a, bt in CELLS:
        b = (index_y if bt == 0 else 1 - index_y) if fold_y else bt
        ids = jnp.concatenate([neighbours_ref[a, b, k] for k in range(neighbour_count)], axis=1)
        place, key = places(ids & 127, ids >> 7, fold_y)
        near = dot_nt(weights_ref[NEAR], latent_ref[a, b, 0])
        near = jnp.concatenate([near, near], axis=1)
        for tile in range(ids.shape[1] // TILE):
            at = slice(tile * TILE, (tile + 1) * TILE)
            edges = [edge_ref[a, b, 0, k] for k in (2 * tile, 2 * tile + 1)]
            pre_ref[2 * a + bt, :, at] = (
                dot_nt(weights_ref[EDGE], jnp.concatenate(edges, axis=0))
                + near
                + pick(cells, place[:, at], key[:, at])
            )
    for k in range(neighbour_count):
        rows = jnp.concatenate([edge_ref[a, b, 0, k] for a, b in CELLS], axis=0)
        mover_edge_ref[k] = dot(placer, rows).astype(BF16)


def prepare_kernel(
    sizes,
    far_ref,
    mine_ref,
    weights_ref,
    edge_ref,
    place_ref,
    key_ref,
    near_ref,
    far_mine_ref,
    pre_ref,
):
    window = Window(sizes[1] == 2, far_ref)
    core = lax.axis_index("gz")
    far_t = weights_ref[FAR]
    cells = window.cells(window.own_columns())
    for row in range(window.row_count):
        pair = jnp.concatenate([mine_ref[1, row], mine_ref[0, row]], axis=0)
        far_mine_ref[row] = dot_nt(far_t, pair).astype(BF16)
        cells.append((12 * (1 - core) + row, far_mine_ref.at[row]))
    neighbour_count, movers = edge_ref.shape[:2]
    step = TILE // movers
    near = jnp.concatenate([near_ref[...]] * step, axis=1)
    for tile in range(neighbour_count // step):
        edges = jnp.concatenate([edge_ref[k] for k in range(tile * step, (tile + 1) * step)], axis=0)
        at = slice(tile * TILE, (tile + 1) * TILE)
        pre_ref[:, at] = (
            dot_nt(weights_ref[EDGE], edges) + near + pick(cells, place_ref[:, at], key_ref[:, at])
        )


def movers_kernel(
    sizes,
    side_count,
    *refs,
):
    fold_y = sizes[1] == 2
    side_refs, refs = refs[:side_count], refs[side_count:]
    side_zeds, refs = refs[:side_count], refs[side_count:]
    other_ref, far_mine_ref, refs = refs[0], refs[1], refs[2:]
    (
        weights_ref,
        decoder_out_ref,
        pre_ref,
        place_ref,
        key_ref,
        node_pre_ref,
        latent_t_ref,
        state_ref,
        far_ref,
        bucket_ref,
        hidden_ref,
    ) = refs
    window = Window(fold_y, None, far_ref)
    row_count = window.row_count
    core = lax.axis_index("gz")
    far_t = weights_ref[FAR]

    def far(at, here, beside):
        pair = jnp.concatenate([here, beside], axis=0)
        far_ref[at] = dot_nt(far_t, pair).astype(BF16)

    for row in range(row_count):
        far(core * row_count + row, other_ref[0, row], other_ref[1, row])
    for side, row in enumerate(window.outer_rows):
        for ex in (1, 2):
            far(window.side(ex, row), side_refs[side][ex - 1], side_zeds[side][ex - 1])

    movers = state_ref.shape[1]
    for row in range(row_count):
        far_ref[(1 - core) * row_count + row] = far_mine_ref[row]
    cells = [(12 * core + row, far_ref.at[core * row_count + row]) for row in range(row_count)]
    cells += window.cells([(ex, row) for ex in (1, 2) for row in window.outer_rows])
    message = messages(
        cells,
        place_ref[...],
        key_ref[...],
        lambda tile: pre_ref[:, tile * TILE : (tile + 1) * TILE],
        weights_ref[MIDDLE],
        weights_ref[FINAL],
        hidden_ref,
    )
    aggregate = slot_sum(message, movers).astype(BF16)
    acceleration = advance(
        node_pre_ref[...], aggregate, latent_t_ref[...], weights_ref, decoder_out_ref[...]
    )
    mask = state_ref[6:7]
    state = moved(state_ref[0:3], state_ref[3:6], acceleration) * mask
    bucket_ref[...] = jnp.concatenate([state, mask, jnp.zeros((ROWS - 10, movers), F32)], axis=0)


def edges_kernel(
    sizes,
    a,
    alive_ref,
    neighbours_ref,
    far_ref,
    pre_ref,
    weights_ref,
    total_ref,
    hidden_ref,
):
    fold_y = sizes[1] == 2
    window = Window(fold_y, None, far_ref)
    index_y = lax.axis_index("gy")
    alive_ref, neighbours_ref = alive_ref.at[a], neighbours_ref.at[a]
    slots = alive_ref.shape[-1]
    neighbour_count = neighbours_ref.shape[1]
    for bt in range(2):
        if fold_y:
            b = index_y if bt == 0 else 1 - index_y
            rows = (0, 1) if bt == 0 else (0, 1, 2)
        else:
            b = bt
            rows = (bt, bt + 1, bt + 2)
        columns = [(ex, row) for ex in range(a, a + 3) for row in rows]
        columns = [column for column in columns if column not in window.own_columns()]
        ids = jnp.concatenate([neighbours_ref[b, k] for k in range(neighbour_count)], axis=1)
        place, key = places(ids & 127, ids >> 7, fold_y)

        message = messages(
            window.cells(columns),
            place,
            key,
            lambda tile, i=2 * a + bt: pre_ref[i, :, tile * TILE : (tile + 1) * TILE],
            weights_ref[MIDDLE],
            weights_ref[FINAL],
            hidden_ref.at[bt],
        )
        total = jnp.where(alive_ref[b] > 0.5, slot_sum(message, slots), 0.0)
        total_ref[b] = total.astype(BF16)


def nodes_kernel(
    first_ref,
    second_ref,
    node_pre_ref,
    latent_t_ref,
    state_ref,
    weights_ref,
    decoder_out_ref,
    moved_ref,
):
    aggregate = jnp.concatenate([first_ref[0], first_ref[1], second_ref[0], second_ref[1]], axis=1)
    acceleration = advance(
        node_pre_ref[...], aggregate, latent_t_ref[...], weights_ref, decoder_out_ref[...]
    )
    state = moved(state_ref[0:3], state_ref[3:6], acceleration)
    moved_ref[...] = jnp.concatenate(
        [state, state_ref[6:7], jnp.zeros((ROWS - 10, state.shape[1]), F32)], axis=0
    )


def finish_kernel(sizes, moved_ref, zed_ref, *refs):
    count_x, count_y, count_z = sizes
    fold_y = count_y == 2
    options_y = 2 if fold_y else 3
    side_refs, refs = refs[: options_y - 1], refs[options_y - 1 :]
    if fold_y:
        cross_ref, end_ref, *refs = refs
    else:
        end_ref, *refs = refs
    (
        packed_ref,
        spread_ref,
        inward_ref,
        encoder_w_ref,
        kept_latent_ref,
        kept_state_ref,
        arrived_latent_ref,
        arrived_state_ref,
    ) = refs
    core = lax.axis_index("gz")

    def tile(source_x, from_y, from_z):
        if source_x == 0:
            if from_y == 0:
                return zed_ref[...]
            if fold_y:
                return packed_ref[4] if from_z else side_refs[0][...]
            return side_refs[from_y - 1][from_z]
        if fold_y:
            mine = (cross_ref if from_y else end_ref)[1 - from_z]
            other = packed_ref[(0 if from_y else 2) + from_z]
        else:
            mine = end_ref[1 - from_z, from_y]
            other = packed_ref[from_z, from_y]
        return jnp.where(core == (1 - source_x) // 2, mine, other)

    extent = (2.0 * count_x, 2.0 * count_y, 1.0 * count_z)
    slots = kept_latent_ref.shape[-2]
    stays = moved_ref[9:10]
    kept = moved_ref[:9] * stays
    latents = encode(moved_ref[:9], stays, inward_ref[...], encoder_w_ref[...], extent)
    for i, (a, b) in enumerate(CELLS):
        kept_latent_ref[a, b, 0] = latents[i * slots : (i + 1) * slots]
        for j in range(9):
            kept_state_ref[j, a, b] = kept[j : j + 1, i * slots : (i + 1) * slots]
    fold_y = count_y == 2
    index_x = lax.axis_index("gx")
    lanes = zed_ref.shape[-1]
    group = lax.broadcasted_iota(I32, (ROWS, lanes), 1) >> 3
    found = jnp.zeros((ROWS, lanes), F32)
    for source_x in (-1, 0, 1):
        for from_y in range(options_y):
            for from_z in range(2):
                if source_x == 0 and from_y == 0 and from_z == 0:
                    continue
                side_y = from_y if fold_y or from_y == 0 else 3 - from_y
                there = group == ((1 - source_x) * options_y + side_y) * 2 + from_z
                if source_x == -1:
                    there = there & (index_x > 0)
                elif source_x == 1:
                    there = there & (index_x < count_x - 1)
                found = jnp.where(there, tile(source_x, from_y, from_z), found)
    halves = []
    for at in range(0, spread_ref.shape[1], 128):
        lane = jnp.broadcast_to(spread_ref[0:1, at : at + 128], (ROWS, 128))
        half = jnp.zeros((ROWS, 128), F32)
        for base in range(0, lanes, 128):
            index = jnp.clip(lane - base, 0, 127)
            there = (lane >= base) & (lane < base + 128)
            part = jnp.take_along_axis(found[:, base : base + 128], index, axis=1)
            half = jnp.where(there, part, half)
        halves.append(half)
    arrived = jnp.concatenate(halves, axis=1)[:, : 26 * CAP]
    for j in range(9):
        arrived_state_ref[j, 0, 0] = arrived[j : j + 1]
    arrived_latent_ref[0, 0, 0] = encode(
        arrived[:9], arrived[9:10], inward_ref[...], encoder_w_ref[...], extent
    )


def swap(values, axis):
    return lax.ppermute(values, axis, [(0, 1), (1, 0)])


def shift(values, axis, way):
    pairs = [(i, i + 1) for i in range(lax.axis_size(axis) - 1)]
    return lax.ppermute(values, axis, [(j, i) for i, j in pairs] if way else pairs)


def swap_chips(values, cross):
    count_x, count_y, count_z = (lax.axis_size(axis) for axis in ("gx", "gy", "gz"))
    pairs = []
    for x in range(count_x):
        for y in range(count_y):
            for z in range(count_z):
                to_x = x + 1 - 2 * z
                if 0 <= to_x < count_x:
                    to = (to_x, y ^ 1 if cross else y, 1 - z)
                else:
                    to = (x, y ^ 1, z)
                pairs.append(((x * count_y + y) * count_z + z, (to[0] * count_y + to[1]) * count_z + to[2]))
    return lax.ppermute(values, ("gx", "gy", "gz"), pairs)


def call(kernel, name, in_specs, outs, scratch, operands, flops):
    return pl.pallas_call(
        kernel,
        out_shape=tuple(jax.ShapeDtypeStruct(shape, kind) for shape, kind in outs),
        in_specs=in_specs,
        out_specs=tuple(VMEM for _ in outs),
        scratch_shapes=scratch,
        compiler_params=pltpu.CompilerParams(vmem_limit_bytes=32 * 1024 * 1024),
        cost_estimate=pl.CostEstimate(flops=flops, bytes_accessed=0, transcendentals=0),
        name=name,
    )(*operands)


def in_hbm(array):
    return pltpu.with_memory_space_constraint(array, pltpu.HBM)


def like(array):
    return pltpu.VMEM(array.shape, array.dtype)


def body(
    node_latent,
    edge_latent,
    positions,
    velocity,
    fill,
    neighbours,
    owners,
    edge_weights,
    node_in,
    node_weights,
    decoder_weights,
    decoder_out,
    encoder_in,
    encoder_weights,
):
    sizes = tuple(lax.axis_size(axis) for axis in ("gx", "gy", "gz"))
    fold_y = sizes[1] == 2
    slots, width = node_latent.shape[-2:]
    neighbour_count = neighbours.shape[3]
    particles = 4 * slots
    options_y = 2 if fold_y else 3
    movers = (3 * options_y * 2 * CAP + 127) // 128 * 128
    rows = 3 if fold_y else 4
    fill = jnp.transpose(fill, (0, 2, 1))
    neighbours = neighbours.reshape(2, 2, neighbour_count, 1, slots)

    own_zed = swap(node_latent, "gz")
    if fold_y:
        sides = [swap(node_latent, "gy")]
    small = (node_latent,)
    *copied, end, alive = call(
        functools.partial(cut_kernel, len(small)),
        "cut",
        [ANY] * (len(small) + 1),
        [(array.shape, array.dtype) for array in small]
        + [(node_latent.shape[1:], BF16), ((2, 2, 1, slots), F32)],
        [pltpu.SMEM(fill.shape, I32), pltpu.SemaphoreType.DMA((len(small) + 2,))],
        [in_hbm(array) for array in (fill, *small)],
        5_000_000_000,
    )
    latent = copied[0]
    core = lax.axis_index("gz")
    if fold_y:
        row = 1 - lax.axis_index("gy")
        beside = lax.dynamic_index_in_dim(own_zed[:, :, 0], 1 - core, 0, False)
        both = jnp.stack([end[:, 0], beside])
        corner = lax.dynamic_slice_in_dim(both, row, 1, axis=1)
        mine = [swap_chips(both, False)]
        corner, both = lax.optimization_barrier((corner, both))
        mine.append(swap_chips(corner, True))
    else:
        sides = [shift(latent[:, 1, 0], "gy", 0), shift(latent[:, 0, 0], "gy", 1)]
        side_zeds = [swap(part, "gz") for part in sides]
        layers = []
        for middle, outer in ((latent, sides), (own_zed, side_zeds)):
            parts = [outer[0][:, None], middle[:, :, 0], outer[1][:, None]]
            parts = [lax.dynamic_index_in_dim(part, 1 - core, 0, False) for part in parts]
            layers.append(jnp.concatenate(parts, axis=0))
        mine = [swap_chips(jnp.stack(layers), False)]

    ranked = call(
        functools.partial(ranks_kernel, sizes),
        "ranks",
        [VMEM] * 13,
        [
            ((11, width, width), BF16),
            ((48, width), BF16),
            ((8, 256), I32),
            ((width, particles), F32),
            ((width, particles), F32),
            ((8, particles), F32),
            ((neighbour_count, movers, width), BF16),
            ((1, neighbour_count * movers), I32),
            ((1, neighbour_count * movers), I32),
            ((width, movers), F32),
            ((width, movers), F32),
            ((width, movers), F32),
            ((8, movers), F32),
            ((4, width, 2 * slots), BF16),
            ((4, width, neighbour_count * slots), F32),
        ],
        [],
        (edge_latent, latent, own_zed, alive, owners, edge_weights, node_in, node_weights, decoder_weights, encoder_in, neighbours, positions, velocity),
        5_000_000_000,
    )
    mine, sides, ranked = lax.optimization_barrier((mine, sides, ranked))
    (
        weights,
        inward,
        spread,
        latent_t,
        node_pre,
        state,
        mover_edges,
        mover_place,
        mover_key,
        mover_near,
        mover_node_pre,
        mover_latent,
        mover_state,
        far_own,
        edge_pre,
    ) = ranked
    mine = jnp.concatenate(mine, axis=1)
    if fold_y:
        sides = [lax.dynamic_index_in_dim(sides[0][:, :, 0], lax.axis_index("gy"), 1, False)]
        packed = jnp.concatenate([mine.reshape(-1, slots, width), sides[0]], axis=0)
    else:
        packed = mine.reshape(-1, slots, width)
    packed = swap(packed, "gz")
    prepared = call(
        functools.partial(prepare_kernel, sizes),
        "prepare",
        [VMEM] * 7,
        [((rows, width, 2 * slots), BF16), ((width, neighbour_count * movers), F32)],
        [],
        (far_own, mine, weights, mover_edges, mover_place, mover_key, mover_near),
        5_000_000_000,
    )
    packed, prepared = lax.optimization_barrier((packed, prepared))
    cells = mine.shape[0] * mine.shape[1]
    if fold_y:
        side_zeds = [packed[cells:]]
    far_mine, mover_pre = prepared
    halo = [*sides, *side_zeds, packed[:cells].reshape(mine.shape), far_mine]

    far_rest, bucket = call(
        functools.partial(movers_kernel, sizes, len(sides)),
        "movers",
        [VMEM] * (len(halo) + 8),
        [((4 * rows - 4, width, 2 * slots), BF16), ((ROWS, movers), F32)],
        [pltpu.VMEM((width, neighbour_count * movers), BF16)],
        (
            *halo,
            weights,
            decoder_out,
            mover_pre,
            mover_place,
            mover_key,
            mover_node_pre,
            mover_latent,
            mover_state,
        ),
        3_000_000_000,
    )

    def edges(a):
        return call(
            functools.partial(edges_kernel, sizes, a),
            "edges",
            [VMEM] * 5,
            [((2, width, slots), BF16)],
            [pltpu.VMEM((2, width, neighbour_count * slots), BF16)],
            (alive, neighbours, far_rest, edge_pre, weights),
            4_000_000_000,
        )[0]

    zed = swap(bucket, "gz")
    if fold_y:
        sides = [swap(bucket, "gy")]
        zed, far_rest = lax.optimization_barrier((zed, far_rest))
        both = jnp.stack([bucket, zed])
        ends = [swap_chips(both, True), swap_chips(both, False)]
    else:
        both = jnp.stack([bucket, zed])
        sides = [shift(both, "gy", 0), shift(both, "gy", 1)]
        ends = [swap_chips(jnp.stack([both, *sides], axis=1), False)]
    first, second = edges(0), edges(1)
    sides, ends, first, second = lax.optimization_barrier((sides, ends, first, second))
    if fold_y:
        packed = swap(jnp.concatenate([*ends, sides[0][None]], axis=0), "gz")
    else:
        packed = swap(ends[0], "gz")
    state = call(
        nodes_kernel,
        "nodes",
        [VMEM] * 7,
        [((ROWS, particles), F32)],
        [],
        (first, second, node_pre, latent_t, state, weights, decoder_out),
        1_000_000_000,
    )[0]
    packed, state = lax.optimization_barrier((packed, state))
    return call(
        functools.partial(finish_kernel, sizes),
        "finish",
        [VMEM] * (len(sides) + len(ends) + 6),
        [
            (node_latent.shape, BF16),
            ((9,) + node_latent.shape[:4], F32),
            ((1, 1, 1, 26 * CAP, width), BF16),
            ((9, 1, 1, 1, 26 * CAP), F32),
        ],
        [],
        (state, zed, *sides, *ends, packed, spread, inward, encoder_weights),
        1_000_000_000,
    )


def solution(mesh):
    placed = (
        P(("group", "gx"), "gy", "gz", None, None),
        P(("group", "gx"), "gy", "gz", None, None, None),
        P(None, ("group", "gx"), "gy", "gz", None),
        P(None, ("group", "gx"), "gy", "gz", None),
        P(("group", "gx"), "gy", "gz"),
        P(("group", "gx"), "gy", "gz", None, None),
        P(("group", "gx"), "gy", "gz", None),
        P(),
        P(),
        P(),
        P(),
        P(),
        P(),
        P(),
    )
    return jax.shard_map(
        body,
        mesh=mesh,
        in_specs=placed,
        out_specs=(
            P(("group", "gx"), "gy", "gz", None, None),
            P(None, ("group", "gx"), "gy", "gz", None),
            P(("group", "gx"), "gy", "gz", None, None),
            P(None, ("group", "gx"), "gy", "gz", None),
        ),
        check_vma=False,
    )
```

```python
import functools

import jax
import jax.numpy as jnp
from jax import lax
from jax.experimental import pallas as pl
from jax.experimental.pallas import tpu as pltpu
from jax.sharding import PartitionSpec as P

CAP = 8
F32 = jnp.float32
BF16 = jnp.bfloat16
I32 = jnp.int32
ROWS = 16
TILE = 256
CELLS = [(a, b) for a in range(2) for b in range(2)]
EDGE, NEAR, FAR, MIDDLE, FINAL, NODE_OLD, NODE_NEW, NODE_0, NODE_1, DECODE_0, DECODE_1 = range(11)

VMEM = pl.BlockSpec(memory_space=pltpu.VMEM)
SMEM = pl.BlockSpec(memory_space=pltpu.SMEM)
ANY = pl.BlockSpec(memory_space=pl.ANY)


def dot(left, right):
    return jnp.dot(left, right, preferred_element_type=F32)


def dot_nt(left, right):
    return lax.dot_general(left, right, (((1,), (1,)), ((), ())), preferred_element_type=F32)


def dot_tn(left, right):
    return lax.dot_general(left, right, (((0,), (0,)), ((), ())), preferred_element_type=F32)


def relu16(values):
    return jnp.maximum(values, 0.0).astype(BF16)


def norm(values, axis):
    scale = 1.0 / values.shape[axis]
    centred = values - jnp.sum(values, axis=axis, keepdims=True) * scale
    spread = jnp.sum(centred * centred, axis=axis, keepdims=True) * scale
    return centred * lax.rsqrt(spread + 1e-05)


def thirds(values):
    high = values.astype(BF16)
    rest = values - high.astype(F32)
    middle = rest.astype(BF16)
    low = (rest - middle.astype(F32)).astype(BF16)
    return jnp.concatenate([high, middle, low], axis=0)


def joined(values):
    rows = values.shape[0] // 3
    return values[:rows] + values[rows : 2 * rows] + values[2 * rows :]


def quotient(values, count):
    if count & (count - 1) == 0:
        return values >> (count.bit_length() - 1)
    return lax.div(values, jnp.full_like(values, count))


def flip(weights):
    return weights.astype(F32).T.astype(BF16)


def fetch(pairs, sems):
    copies = [pltpu.make_async_copy(src, dst, sems.at[i]) for i, (src, dst) in enumerate(pairs)]
    for copy in copies:
        copy.start()
    return copies


def encode(state, mask, inward, encoder_w, extent):
    width = state.shape[1]
    position = state[0:3]
    row = lax.broadcasted_iota(I32, (3, width), 0)
    size = jnp.where(row == 0, extent[0], jnp.where(row == 1, extent[1], extent[2]))
    features = jnp.concatenate(
        [
            state[3:9],
            jnp.clip(position, -1.0, 1.0),
            jnp.clip(size - position, -1.0, 1.0),
            jnp.zeros((4, width), F32),
        ],
        axis=0,
    )
    hidden = relu16(dot_tn(thirds(features), inward))
    hidden = relu16(dot(hidden, encoder_w[0]))
    column = jnp.broadcast_to(mask, (8, width)).T[:, 0:1]
    return (norm(dot(hidden, encoder_w[1]), 1) * column).astype(BF16)


def places(ids_low, ids_high, fold_y):
    plane = (ids_high * 43) >> 7
    ez = ids_high - plane * 3
    ey = plane & 3
    ex = plane >> 2
    if fold_y:
        row = jnp.where(ey == 1, 0, jnp.where(ey == 2, 1, 2))
    else:
        row = ey
    return ex * 4 + row, ids_low + jnp.where(ez == 1, 0, 128)


def pick(cells, place, key):
    width = cells[0][1].shape[0]
    chunk = 32
    window = jnp.concatenate(
        [ref[f : f + chunk] for f in range(0, width, chunk) for _, ref in cells], axis=0
    )
    key_rows = lax.broadcasted_iota(I32, (TILE, TILE), 0).astype(F32).astype(BF16)
    key = jnp.broadcast_to(key.astype(F32), (16, TILE)).astype(BF16)
    same = key_rows.reshape(TILE // 16, 16, TILE) == key[None]
    picker = jnp.where(same, jnp.ones((), BF16), jnp.zeros((), BF16)).reshape(TILE, TILE)
    found = dot(window, picker).reshape(width // chunk, len(cells), chunk // 8, 8, TILE)
    where = jnp.broadcast_to(place, (8, TILE))
    parts = []
    for f in range(width // chunk):
        part = jnp.zeros((chunk // 8, 8, TILE), F32)
        for i, (column, _) in enumerate(cells):
            part = jnp.where((where == column)[None], found[f, i], part)
        parts.append(part.reshape(chunk, TILE))
    return jnp.concatenate(parts, axis=0)


def messages(cells, place, key, pre, middle_t, final_t, hidden_ref):
    for tile in range(place.shape[1] // TILE):
        at = slice(tile * TILE, (tile + 1) * TILE)
        hidden_ref[:, at] = relu16(pre(tile) + pick(cells, place[:, at], key[:, at]))
    hidden = relu16(dot(middle_t, hidden_ref[...]))
    return norm(dot(final_t, hidden), 0)


class Window:
    def __init__(self, fold_y, own_ref=None, rest_ref=None):
        self.row_count = 3 if fold_y else 4
        self.own_rows = (0, 1) if fold_y else (1, 2)
        self.outer_rows = (2,) if fold_y else (0, 3)
        self.own_ref, self.rest_ref = own_ref, rest_ref

    def own_columns(self):
        return [(ex, row) for ex in (1, 2) for row in self.own_rows]

    def own(self, ex, row):
        return (ex - 1) * 2 + self.own_rows.index(row)

    def side(self, ex, row):
        count = len(self.outer_rows)
        return 2 * self.row_count + (ex - 1) * count + self.outer_rows.index(row)

    def cells(self, columns):
        found = []
        for ex, row in columns:
            if ex in (1, 2) and row in self.own_rows:
                ref = self.own_ref.at[self.own(ex, row)]
            elif ex in (1, 2):
                ref = self.rest_ref.at[self.side(ex, row)]
            else:
                ref = self.rest_ref.at[(0 if ex == 0 else self.row_count) + row]
            found.append((ex * 4 + row, ref))
        return found


def slot_sum(message, step):
    total = message[:, :step]
    for at in range(step, message.shape[1], step):
        total = total + message[:, at : at + step]
    return total


def advance(pre, aggregate, latent_t, weights_ref, decoder_out):
    pre = pre + dot(weights_ref[NODE_NEW], aggregate)
    hidden = relu16(dot(weights_ref[NODE_0], relu16(pre)))
    updated = (latent_t + norm(dot(weights_ref[NODE_1], hidden), 0)).astype(BF16)
    hidden = relu16(dot(weights_ref[DECODE_0], updated))
    hidden = relu16(dot(weights_ref[DECODE_1], hidden))
    return dot(decoder_out, hidden)


def moved(position, velocity, acceleration):
    new_velocity = velocity + acceleration
    return jnp.concatenate([position + new_velocity, new_velocity, velocity], axis=0)


def tables_kernel(fold_y, spread_ref):
    index_y = lax.axis_index("gy")
    index_z = lax.axis_index("gz")
    options_y = 2 if fold_y else 3
    line = lax.broadcasted_iota(I32, spread_ref.shape, 1)
    direction = line >> 3
    direction = direction + jnp.where(direction > 12, 1, 0)
    plane = (direction * 57) >> 9
    from_z = direction - 3 * ((direction * 43) >> 7) - 1
    from_y = ((direction * 43) >> 7) - 3 * plane - 1
    if fold_y:
        side_y = jnp.where(from_y == 0, 0, 1)
        valid = (from_y == 0) | (from_y == 1 - 2 * index_y)
    else:
        side_y = jnp.where(from_y < 0, 2, from_y)
        valid = from_y < 2
    side_z = jnp.where(from_z == 0, 0, 1)
    valid = valid & ((from_z == 0) | (from_z == 1 - 2 * index_z)) & (line < 26 * CAP)
    target = ((2 - plane) * options_y + side_y) * 2 + side_z
    spread_ref[...] = jnp.where(valid, target * CAP + (line & 7), -1)


def ranks_kernel(
    sizes,
    edge_ref,
    latent_ref,
    own_zed,
    fill_ref,
    owners_ref,
    edge_w_ref,
    node_in_ref,
    node_w_ref,
    decoder_w_ref,
    encoder_in_ref,
    neighbours_ref,
    positions_ref,
    velocity_ref,
    weights_ref,
    inward_ref,
    alive_ref,
    latent_t_ref,
    node_pre_ref,
    state_ref,
    mover_edge_ref,
    mover_place_ref,
    mover_key_ref,
    mover_near_ref,
    mover_node_pre_ref,
    mover_latent_ref,
    mover_state_ref,
    far_ref,
    pre_ref,
):
    count_x, count_y, count_z = sizes
    fold_y = count_y == 2
    index_x = lax.axis_index("gx")
    index_y = lax.axis_index("gy")
    index_z = lax.axis_index("gz")
    slots = owners_ref.shape[-1]
    width = node_in_ref.shape[-1]
    lane = lax.broadcasted_iota(I32, (1, slots), 1)
    for a, b in CELLS:
        fill = jnp.broadcast_to(fill_ref[a, :, b : b + 1], (1, slots))
        alive_ref[a, b] = jnp.where(lane < fill, 1.0, 0.0)

    owner = jnp.concatenate([owners_ref[a, b] for a, b in CELLS], axis=1)
    alive = jnp.concatenate([alive_ref[a, b] for a, b in CELLS], axis=1)
    own_block = (index_x * count_y + index_y) * count_z + index_z
    stays = jnp.where((alive > 0.5) & (owner == own_block), 1.0, 0.0)
    moving = jnp.where((alive > 0.5) & (owner != own_block), 1, 0)
    owner_x = quotient(owner, count_y * count_z)
    rest = owner - owner_x * (count_y * count_z)
    owner_y = quotient(rest, count_z)
    owner_z = rest - owner_y * count_z
    step_y = owner_y - index_y
    side_y = jnp.where(step_y == 0, 0, 1) if fold_y else jnp.where(step_y < 0, 1, 2 * step_y)
    options_y = 2 if fold_y else 3
    group = ((owner_x - index_x + 1) * options_y + side_y) * 2 + jnp.where(owner_z == index_z, 0, 1)
    group_rows = (3 * options_y * 2 + 15) // 16 * 16
    particles = owner.shape[1]
    member = jnp.where(
        (lax.broadcasted_iota(I32, (group_rows, particles), 0) == group) & (moving == 1), 1.0, 0.0
    )
    triangle = jnp.where(
        lax.broadcasted_iota(I32, (slots, slots), 0) <= lax.broadcasted_iota(I32, (slots, slots), 1),
        1.0,
        0.0,
    ).astype(BF16)
    counted = []
    before = jnp.zeros((group_rows, 1), F32)
    for i in range(4):
        inside = member[:, i * slots : (i + 1) * slots]
        counted.append(dot(inside.astype(BF16), triangle) + before)
        before = before + jnp.sum(inside, axis=1, keepdims=True)
    counted = jnp.concatenate(counted, axis=1)
    rank = (jnp.sum(counted * member, axis=0, keepdims=True) - 1.0).astype(I32)
    column = jnp.where(moving == 1, group * CAP + rank, -1)
    movers = mover_state_ref.shape[1]
    placer = jnp.where(
        lax.broadcasted_iota(I32, (movers, particles), 0) == column, 1.0, 0.0
    ).astype(BF16)

    for i in range(5):
        weights_ref[i] = flip(edge_w_ref[i])
    weights_ref[NODE_OLD] = flip(node_in_ref[:width])
    weights_ref[NODE_NEW] = flip(node_in_ref[width:])
    for i in range(2):
        weights_ref[NODE_0 + i] = flip(node_w_ref[i])
        weights_ref[DECODE_0 + i] = flip(decoder_w_ref[i])
    inward = jnp.concatenate([encoder_in_ref[...].astype(F32), jnp.zeros((4, width), F32)], axis=0)
    inward = inward.astype(BF16)
    inward_ref[...] = jnp.concatenate([inward, inward, inward], axis=0)

    latent = jnp.concatenate([latent_ref[a, b, 0] for a, b in CELLS], axis=0)
    latent_t_ref[...] = latent.astype(F32).T
    node_pre_ref[...] = dot_nt(weights_ref[NODE_OLD], latent)

    def flat(ref, i):
        return jnp.concatenate([ref[i, a, b] for a, b in CELLS], axis=1)

    state = [flat(positions_ref, i) for i in range(3)] + [flat(velocity_ref, i) for i in range(3)]
    state_ref[...] = jnp.concatenate(state + [stays, jnp.zeros_like(stays)], axis=0)

    mover_latent = dot(placer, latent).astype(BF16)
    mover_latent_ref[...] = mover_latent.astype(F32).T
    mover_node_pre_ref[...] = dot_nt(weights_ref[NODE_OLD], mover_latent)
    mover_near_ref[...] = dot_nt(weights_ref[NEAR], mover_latent)
    state = jnp.concatenate(state + [moving.astype(F32), jnp.zeros_like(stays)], axis=0)
    mover_state_ref[...] = joined(dot_nt(thirds(state), placer))
    neighbour_count = edge_ref.shape[3]
    ids = jnp.concatenate(
        [
            jnp.concatenate([neighbours_ref[a, b, k] for a, b in CELLS], axis=1)
            for k in range(neighbour_count)
        ],
        axis=0,
    )
    ids = jnp.concatenate([ids & 127, ids >> 7, jnp.zeros((8, particles), I32)], axis=0)
    ids = dot_nt(ids.astype(F32).astype(BF16), placer).astype(I32)
    place, key = places(ids[:neighbour_count], ids[neighbour_count : 2 * neighbour_count], fold_y)
    mover_place_ref[...] = jnp.concatenate([place[k : k + 1] for k in range(neighbour_count)], axis=1)
    mover_key_ref[...] = jnp.concatenate([key[k : k + 1] for k in range(neighbour_count)], axis=1)

    window = Window(fold_y, far_ref)
    for (ex, row), (a, b) in zip(window.own_columns(), CELLS):
        pair = jnp.concatenate([latent_ref[a, b, 0], own_zed[a, b, 0]], axis=0)
        far_ref[window.own(ex, row)] = dot_nt(weights_ref[FAR], pair).astype(BF16)
    cells = window.cells(window.own_columns())
    for a, bt in CELLS:
        b = (index_y if bt == 0 else 1 - index_y) if fold_y else bt
        ids = jnp.concatenate([neighbours_ref[a, b, k] for k in range(neighbour_count)], axis=1)
        place, key = places(ids & 127, ids >> 7, fold_y)
        near = dot_nt(weights_ref[NEAR], latent_ref[a, b, 0])
        near = jnp.concatenate([near, near], axis=1)
        for tile in range(ids.shape[1] // TILE):
            at = slice(tile * TILE, (tile + 1) * TILE)
            edges = [edge_ref[a, b, 0, k] for k in (2 * tile, 2 * tile + 1)]
            pre_ref[2 * a + bt, :, at] = (
                dot_nt(weights_ref[EDGE], jnp.concatenate(edges, axis=0))
                + near
                + pick(cells, place[:, at], key[:, at])
            )
    for k in range(neighbour_count):
        rows = jnp.concatenate([edge_ref[a, b, 0, k] for a, b in CELLS], axis=0)
        mover_edge_ref[k] = dot(placer, rows).astype(BF16)


def prepare_kernel(
    sizes,
    far_ref,
    mine_ref,
    weights_ref,
    edge_ref,
    place_ref,
    key_ref,
    near_ref,
    far_mine_ref,
    pre_ref,
):
    window = Window(sizes[1] == 2, far_ref)
    core = lax.axis_index("gz")
    far_t = weights_ref[FAR]
    cells = window.cells(window.own_columns())
    for row in range(window.row_count):
        pair = jnp.concatenate([mine_ref[1, row], mine_ref[0, row]], axis=0)
        far_mine_ref[row] = dot_nt(far_t, pair).astype(BF16)
        cells.append((12 * (1 - core) + row, far_mine_ref.at[row]))
    neighbour_count, movers = edge_ref.shape[:2]
    step = TILE // movers
    near = jnp.concatenate([near_ref[...]] * step, axis=1)
    for tile in range(neighbour_count // step):
        edges = jnp.concatenate([edge_ref[k] for k in range(tile * step, (tile + 1) * step)], axis=0)
        at = slice(tile * TILE, (tile + 1) * TILE)
        pre_ref[:, at] = (
            dot_nt(weights_ref[EDGE], edges) + near + pick(cells, place_ref[:, at], key_ref[:, at])
        )


def movers_kernel(
    sizes,
    side_count,
    *refs,
):
    fold_y = sizes[1] == 2
    side_refs, refs = refs[:side_count], refs[side_count:]
    side_zeds, refs = refs[:side_count], refs[side_count:]
    other_ref, far_mine_ref, refs = refs[0], refs[1], refs[2:]
    (
        weights_ref,
        decoder_out_ref,
        pre_ref,
        place_ref,
        key_ref,
        node_pre_ref,
        latent_t_ref,
        state_ref,
        far_ref,
        bucket_ref,
        hidden_ref,
    ) = refs
    window = Window(fold_y, None, far_ref)
    row_count = window.row_count
    core = lax.axis_index("gz")
    far_t = weights_ref[FAR]

    def far(at, here, beside):
        pair = jnp.concatenate([here, beside], axis=0)
        far_ref[at] = dot_nt(far_t, pair).astype(BF16)

    for row in range(row_count):
        far(core * row_count + row, other_ref[0, row], other_ref[1, row])
    for side, row in enumerate(window.outer_rows):
        for ex in (1, 2):
            far(window.side(ex, row), side_refs[side][ex - 1], side_zeds[side][ex - 1])

    movers = state_ref.shape[1]
    for row in range(row_count):
        far_ref[(1 - core) * row_count + row] = far_mine_ref[row]
    cells = [(12 * core + row, far_ref.at[core * row_count + row]) for row in range(row_count)]
    cells += window.cells([(ex, row) for ex in (1, 2) for row in window.outer_rows])
    message = messages(
        cells,
        place_ref[...],
        key_ref[...],
        lambda tile: pre_ref[:, tile * TILE : (tile + 1) * TILE],
        weights_ref[MIDDLE],
        weights_ref[FINAL],
        hidden_ref,
    )
    aggregate = slot_sum(message, movers).astype(BF16)
    acceleration = advance(
        node_pre_ref[...], aggregate, latent_t_ref[...], weights_ref, decoder_out_ref[...]
    )
    mask = state_ref[6:7]
    state = moved(state_ref[0:3], state_ref[3:6], acceleration) * mask
    bucket_ref[...] = jnp.concatenate([state, mask, jnp.zeros((ROWS - 10, movers), F32)], axis=0)


def edges_kernel(
    sizes,
    a,
    alive_ref,
    neighbours_ref,
    far_ref,
    pre_ref,
    weights_ref,
    total_ref,
    hidden_ref,
):
    fold_y = sizes[1] == 2
    window = Window(fold_y, None, far_ref)
    index_y = lax.axis_index("gy")
    alive_ref, neighbours_ref = alive_ref.at[a], neighbours_ref.at[a]
    slots = alive_ref.shape[-1]
    neighbour_count = neighbours_ref.shape[1]
    for bt in range(2):
        if fold_y:
            b = index_y if bt == 0 else 1 - index_y
            rows = (0, 1) if bt == 0 else (0, 1, 2)
        else:
            b = bt
            rows = (bt, bt + 1, bt + 2)
        columns = [(ex, row) for ex in range(a, a + 3) for row in rows]
        columns = [column for column in columns if column not in window.own_columns()]
        ids = jnp.concatenate([neighbours_ref[b, k] for k in range(neighbour_count)], axis=1)
        place, key = places(ids & 127, ids >> 7, fold_y)

        message = messages(
            window.cells(columns),
            place,
            key,
            lambda tile, i=2 * a + bt: pre_ref[i, :, tile * TILE : (tile + 1) * TILE],
            weights_ref[MIDDLE],
            weights_ref[FINAL],
            hidden_ref.at[bt],
        )
        total = jnp.where(alive_ref[b] > 0.5, slot_sum(message, slots), 0.0)
        total_ref[b] = total.astype(BF16)


def nodes_kernel(
    first_ref,
    second_ref,
    node_pre_ref,
    latent_t_ref,
    state_ref,
    weights_ref,
    decoder_out_ref,
    moved_ref,
):
    aggregate = jnp.concatenate([first_ref[0], first_ref[1], second_ref[0], second_ref[1]], axis=1)
    acceleration = advance(
        node_pre_ref[...], aggregate, latent_t_ref[...], weights_ref, decoder_out_ref[...]
    )
    state = moved(state_ref[0:3], state_ref[3:6], acceleration)
    moved_ref[...] = jnp.concatenate(
        [state, state_ref[6:7], jnp.zeros((ROWS - 10, state.shape[1]), F32)], axis=0
    )


def finish_kernel(sizes, moved_ref, zed_ref, *refs):
    count_x, count_y, count_z = sizes
    fold_y = count_y == 2
    options_y = 2 if fold_y else 3
    side_refs, refs = refs[: options_y - 1], refs[options_y - 1 :]
    if fold_y:
        cross_ref, end_ref, *refs = refs
    else:
        end_ref, *refs = refs
    (
        packed_ref,
        spread_ref,
        inward_ref,
        encoder_w_ref,
        kept_latent_ref,
        kept_state_ref,
        arrived_latent_ref,
        arrived_state_ref,
    ) = refs
    core = lax.axis_index("gz")

    def tile(source_x, from_y, from_z):
        if source_x == 0:
            if from_y == 0:
                return zed_ref[...]
            if fold_y:
                return packed_ref[4] if from_z else side_refs[0][...]
            return side_refs[from_y - 1][from_z]
        if fold_y:
            mine = (cross_ref if from_y else end_ref)[1 - from_z]
            other = packed_ref[(0 if from_y else 2) + from_z]
        else:
            mine = end_ref[1 - from_z, from_y]
            other = packed_ref[from_z, from_y]
        return jnp.where(core == (1 - source_x) // 2, mine, other)

    extent = (2.0 * count_x, 2.0 * count_y, 1.0 * count_z)
    slots = kept_latent_ref.shape[-2]
    stays = moved_ref[9:10]
    kept = moved_ref[:9] * stays
    latents = encode(moved_ref[:9], stays, inward_ref[...], encoder_w_ref[...], extent)
    for i, (a, b) in enumerate(CELLS):
        kept_latent_ref[a, b, 0] = latents[i * slots : (i + 1) * slots]
        for j in range(9):
            kept_state_ref[j, a, b] = kept[j : j + 1, i * slots : (i + 1) * slots]
    fold_y = count_y == 2
    index_x = lax.axis_index("gx")
    lanes = zed_ref.shape[-1]
    group = lax.broadcasted_iota(I32, (ROWS, lanes), 1) >> 3
    found = jnp.zeros((ROWS, lanes), F32)
    for source_x in (-1, 0, 1):
        for from_y in range(options_y):
            for from_z in range(2):
                if source_x == 0 and from_y == 0 and from_z == 0:
                    continue
                side_y = from_y if fold_y or from_y == 0 else 3 - from_y
                there = group == ((1 - source_x) * options_y + side_y) * 2 + from_z
                if source_x == -1:
                    there = there & (index_x > 0)
                elif source_x == 1:
                    there = there & (index_x < count_x - 1)
                found = jnp.where(there, tile(source_x, from_y, from_z), found)
    halves = []
    for at in range(0, spread_ref.shape[1], 128):
        lane = jnp.broadcast_to(spread_ref[0:1, at : at + 128], (ROWS, 128))
        half = jnp.zeros((ROWS, 128), F32)
        for base in range(0, lanes, 128):
            index = jnp.clip(lane - base, 0, 127)
            there = (lane >= base) & (lane < base + 128)
            part = jnp.take_along_axis(found[:, base : base + 128], index, axis=1)
            half = jnp.where(there, part, half)
        halves.append(half)
    arrived = jnp.concatenate(halves, axis=1)[:, : 26 * CAP]
    for j in range(9):
        arrived_state_ref[j, 0, 0] = arrived[j : j + 1]
    arrived_latent_ref[0, 0, 0] = encode(
        arrived[:9], arrived[9:10], inward_ref[...], encoder_w_ref[...], extent
    )


def swap(values, axis):
    return lax.ppermute(values, axis, [(0, 1), (1, 0)])


def shift(values, axis, way):
    pairs = [(i, i + 1) for i in range(lax.axis_size(axis) - 1)]
    return lax.ppermute(values, axis, [(j, i) for i, j in pairs] if way else pairs)


def swap_chips(values, cross):
    count_x, count_y, count_z = (lax.axis_size(axis) for axis in ("gx", "gy", "gz"))
    pairs = []
    for x in range(count_x):
        for y in range(count_y):
            for z in range(count_z):
                to_x = x + 1 - 2 * z
                if 0 <= to_x < count_x:
                    to = (to_x, y ^ 1 if cross else y, 1 - z)
                else:
                    to = (x, y ^ 1, z)
                pairs.append(((x * count_y + y) * count_z + z, (to[0] * count_y + to[1]) * count_z + to[2]))
    return lax.ppermute(values, ("gx", "gy", "gz"), pairs)


def call(kernel, name, in_specs, outs, scratch, operands, flops):
    return pl.pallas_call(
        kernel,
        out_shape=tuple(jax.ShapeDtypeStruct(shape, kind) for shape, kind in outs),
        in_specs=in_specs,
        out_specs=tuple(VMEM for _ in outs),
        scratch_shapes=scratch,
        compiler_params=pltpu.CompilerParams(vmem_limit_bytes=32 * 1024 * 1024),
        cost_estimate=pl.CostEstimate(flops=flops, bytes_accessed=0, transcendentals=0),
        name=name,
    )(*operands)


def in_hbm(array):
    return pltpu.with_memory_space_constraint(array, pltpu.HBM)


def like(array):
    return pltpu.VMEM(array.shape, array.dtype)


def body(
    node_latent,
    edge_latent,
    positions,
    velocity,
    fill,
    neighbours,
    owners,
    edge_weights,
    node_in,
    node_weights,
    decoder_weights,
    decoder_out,
    encoder_in,
    encoder_weights,
):
    sizes = tuple(lax.axis_size(axis) for axis in ("gx", "gy", "gz"))
    fold_y = sizes[1] == 2
    slots, width = node_latent.shape[-2:]
    neighbour_count = neighbours.shape[3]
    particles = 4 * slots
    options_y = 2 if fold_y else 3
    movers = (3 * options_y * 2 * CAP + 127) // 128 * 128
    rows = 3 if fold_y else 4
    fill = jnp.transpose(fill, (0, 2, 1))
    neighbours = neighbours.reshape(2, 2, neighbour_count, 1, slots)

    own_zed = swap(node_latent, "gz")
    if fold_y:
        sides = [swap(node_latent, "gy")]
    spread = call(
        functools.partial(tables_kernel, fold_y),
        "tables",
        [],
        [((8, 256), I32)],
        [],
        [],
        5_000_000_000,
    )[0]
    latent, spread = lax.optimization_barrier((node_latent, spread))
    core = lax.axis_index("gz")
    if fold_y:
        row = 1 - lax.axis_index("gy")
        end = lax.dynamic_index_in_dim(latent[:, :, 0], 1 - core, 0, False)
        beside = lax.dynamic_index_in_dim(own_zed[:, :, 0], 1 - core, 0, False)
        both = jnp.stack([end, beside])
        corner = lax.dynamic_slice_in_dim(both, row, 1, axis=1)
        mine = [swap_chips(both, False)]
        corner, both = lax.optimization_barrier((corner, both))
        mine.append(swap_chips(corner, True))
    else:
        sides = [shift(latent[:, 1, 0], "gy", 0), shift(latent[:, 0, 0], "gy", 1)]
        side_zeds = [swap(part, "gz") for part in sides]
        layers = []
        for middle, outer in ((latent, sides), (own_zed, side_zeds)):
            parts = [outer[0][:, None], middle[:, :, 0], outer[1][:, None]]
            parts = [lax.dynamic_index_in_dim(part, 1 - core, 0, False) for part in parts]
            layers.append(jnp.concatenate(parts, axis=0))
        mine = [swap_chips(jnp.stack(layers), False)]

    ranked = call(
        functools.partial(ranks_kernel, sizes),
        "ranks",
        [VMEM] * 13,
        [
            ((11, width, width), BF16),
            ((48, width), BF16),
            ((2, 2, 1, slots), F32),
            ((width, particles), F32),
            ((width, particles), F32),
            ((8, particles), F32),
            ((neighbour_count, movers, width), BF16),
            ((1, neighbour_count * movers), I32),
            ((1, neighbour_count * movers), I32),
            ((width, movers), F32),
            ((width, movers), F32),
            ((width, movers), F32),
            ((8, movers), F32),
            ((4, width, 2 * slots), BF16),
            ((4, width, neighbour_count * slots), F32),
        ],
        [],
        (edge_latent, latent, own_zed, fill, owners, edge_weights, node_in, node_weights, decoder_weights, encoder_in, neighbours, positions, velocity),
        5_000_000_000,
    )
    mine, sides, ranked = lax.optimization_barrier((mine, sides, ranked))
    (
        weights,
        inward,
        alive,
        latent_t,
        node_pre,
        state,
        mover_edges,
        mover_place,
        mover_key,
        mover_near,
        mover_node_pre,
        mover_latent,
        mover_state,
        far_own,
        edge_pre,
    ) = ranked
    mine = jnp.concatenate(mine, axis=1)
    if fold_y:
        sides = [lax.dynamic_index_in_dim(sides[0][:, :, 0], lax.axis_index("gy"), 1, False)]
        packed = jnp.concatenate([mine.reshape(-1, slots, width), sides[0]], axis=0)
    else:
        packed = mine.reshape(-1, slots, width)
    packed = swap(packed, "gz")
    prepared = call(
        functools.partial(prepare_kernel, sizes),
        "prepare",
        [VMEM] * 7,
        [((rows, width, 2 * slots), BF16), ((width, neighbour_count * movers), F32)],
        [],
        (far_own, mine, weights, mover_edges, mover_place, mover_key, mover_near),
        5_000_000_000,
    )
    packed, prepared = lax.optimization_barrier((packed, prepared))
    cells = mine.shape[0] * mine.shape[1]
    if fold_y:
        side_zeds = [packed[cells:]]
    far_mine, mover_pre = prepared
    halo = [*sides, *side_zeds, packed[:cells].reshape(mine.shape), far_mine]

    far_rest, bucket = call(
        functools.partial(movers_kernel, sizes, len(sides)),
        "movers",
        [VMEM] * (len(halo) + 8),
        [((4 * rows - 4, width, 2 * slots), BF16), ((ROWS, movers), F32)],
        [pltpu.VMEM((width, neighbour_count * movers), BF16)],
        (
            *halo,
            weights,
            decoder_out,
            mover_pre,
            mover_place,
            mover_key,
            mover_node_pre,
            mover_latent,
            mover_state,
        ),
        3_000_000_000,
    )

    def edges(a):
        return call(
            functools.partial(edges_kernel, sizes, a),
            "edges",
            [VMEM] * 5,
            [((2, width, slots), BF16)],
            [pltpu.VMEM((2, width, neighbour_count * slots), BF16)],
            (alive, neighbours, far_rest, edge_pre, weights),
            4_000_000_000,
        )[0]

    zed = swap(bucket, "gz")
    if fold_y:
        sides = [swap(bucket, "gy")]
        zed, far_rest = lax.optimization_barrier((zed, far_rest))
        both = jnp.stack([bucket, zed])
        ends = [swap_chips(both, True), swap_chips(both, False)]
    else:
        both = jnp.stack([bucket, zed])
        sides = [shift(both, "gy", 0), shift(both, "gy", 1)]
        ends = [swap_chips(jnp.stack([both, *sides], axis=1), False)]
    first, second = edges(0), edges(1)
    sides, ends, first, second = lax.optimization_barrier((sides, ends, first, second))
    if fold_y:
        packed = swap(jnp.concatenate([*ends, sides[0][None]], axis=0), "gz")
    else:
        packed = swap(ends[0], "gz")
    state = call(
        nodes_kernel,
        "nodes",
        [VMEM] * 7,
        [((ROWS, particles), F32)],
        [],
        (first, second, node_pre, latent_t, state, weights, decoder_out),
        1_000_000_000,
    )[0]
    packed, state = lax.optimization_barrier((packed, state))
    return call(
        functools.partial(finish_kernel, sizes),
        "finish",
        [VMEM] * (len(sides) + len(ends) + 6),
        [
            (node_latent.shape, BF16),
            ((9,) + node_latent.shape[:4], F32),
            ((1, 1, 1, 26 * CAP, width), BF16),
            ((9, 1, 1, 1, 26 * CAP), F32),
        ],
        [],
        (state, zed, *sides, *ends, packed, spread, inward, encoder_weights),
        1_000_000_000,
    )


def solution(mesh):
    placed = (
        P(("group", "gx"), "gy", "gz", None, None),
        P(("group", "gx"), "gy", "gz", None, None, None),
        P(None, ("group", "gx"), "gy", "gz", None),
        P(None, ("group", "gx"), "gy", "gz", None),
        P(("group", "gx"), "gy", "gz"),
        P(("group", "gx"), "gy", "gz", None, None),
        P(("group", "gx"), "gy", "gz", None),
        P(),
        P(),
        P(),
        P(),
        P(),
        P(),
        P(),
    )
    return jax.shard_map(
        body,
        mesh=mesh,
        in_specs=placed,
        out_specs=(
            P(("group", "gx"), "gy", "gz", None, None),
            P(None, ("group", "gx"), "gy", "gz", None),
            P(("group", "gx"), "gy", "gz", None, None),
            P(None, ("group", "gx"), "gy", "gz", None),
        ),
        check_vma=False,
    )
```

```python
import functools

import jax
import jax.numpy as jnp
from jax import lax
from jax.experimental import pallas as pl
from jax.experimental.pallas import tpu as pltpu
from jax.sharding import PartitionSpec as P

CAP = 8
F32 = jnp.float32
BF16 = jnp.bfloat16
I32 = jnp.int32
ROWS = 16
TILE = 256
CELLS = [(a, b) for a in range(2) for b in range(2)]
EDGE, NEAR, FAR, MIDDLE, FINAL, NODE_OLD, NODE_NEW, NODE_0, NODE_1, DECODE_0, DECODE_1 = range(11)

VMEM = pl.BlockSpec(memory_space=pltpu.VMEM)
SMEM = pl.BlockSpec(memory_space=pltpu.SMEM)
ANY = pl.BlockSpec(memory_space=pl.ANY)


def dot(left, right):
    return jnp.dot(left, right, preferred_element_type=F32)


def dot_nt(left, right):
    return lax.dot_general(left, right, (((1,), (1,)), ((), ())), preferred_element_type=F32)


def dot_tn(left, right):
    return lax.dot_general(left, right, (((0,), (0,)), ((), ())), preferred_element_type=F32)


def relu16(values):
    return jnp.maximum(values, 0.0).astype(BF16)


def norm(values, axis):
    scale = 1.0 / values.shape[axis]
    centred = values - jnp.sum(values, axis=axis, keepdims=True) * scale
    spread = jnp.sum(centred * centred, axis=axis, keepdims=True) * scale
    return centred * lax.rsqrt(spread + 1e-05)


def thirds(values):
    high = values.astype(BF16)
    rest = values - high.astype(F32)
    middle = rest.astype(BF16)
    low = (rest - middle.astype(F32)).astype(BF16)
    return jnp.concatenate([high, middle, low], axis=0)


def joined(values):
    rows = values.shape[0] // 3
    return values[:rows] + values[rows : 2 * rows] + values[2 * rows :]


def quotient(values, count):
    if count & (count - 1) == 0:
        return values >> (count.bit_length() - 1)
    return lax.div(values, jnp.full_like(values, count))


def flip(weights):
    return weights.astype(F32).T.astype(BF16)


def fetch(pairs, sems):
    copies = [pltpu.make_async_copy(src, dst, sems.at[i]) for i, (src, dst) in enumerate(pairs)]
    for copy in copies:
        copy.start()
    return copies


def encode(state, mask, inward, encoder_w, extent):
    width = state.shape[1]
    position = state[0:3]
    row = lax.broadcasted_iota(I32, (3, width), 0)
    size = jnp.where(row == 0, extent[0], jnp.where(row == 1, extent[1], extent[2]))
    features = jnp.concatenate(
        [
            state[3:9],
            jnp.clip(position, -1.0, 1.0),
            jnp.clip(size - position, -1.0, 1.0),
            jnp.zeros((4, width), F32),
        ],
        axis=0,
    )
    hidden = relu16(dot_tn(thirds(features), inward))
    hidden = relu16(dot(hidden, encoder_w[0]))
    column = jnp.broadcast_to(mask, (8, width)).T[:, 0:1]
    return (norm(dot(hidden, encoder_w[1]), 1) * column).astype(BF16)


def places(ids_low, ids_high, fold_y):
    plane = (ids_high * 43) >> 7
    ez = ids_high - plane * 3
    ey = plane & 3
    ex = plane >> 2
    if fold_y:
        row = jnp.where(ey == 1, 0, jnp.where(ey == 2, 1, 2))
    else:
        row = ey
    return ex * 4 + row, ids_low + jnp.where(ez == 1, 0, 128)


def pick(cells, place, key):
    width = cells[0][1].shape[0]
    chunk = 32
    window = jnp.concatenate(
        [ref[f : f + chunk] for f in range(0, width, chunk) for _, ref in cells], axis=0
    )
    key_rows = lax.broadcasted_iota(I32, (TILE, TILE), 0).astype(F32).astype(BF16)
    key = jnp.broadcast_to(key.astype(F32), (16, TILE)).astype(BF16)
    same = key_rows.reshape(TILE // 16, 16, TILE) == key[None]
    picker = jnp.where(same, jnp.ones((), BF16), jnp.zeros((), BF16)).reshape(TILE, TILE)
    found = dot(window, picker).reshape(width // chunk, len(cells), chunk // 8, 8, TILE)
    where = jnp.broadcast_to(place, (8, TILE))
    parts = []
    for f in range(width // chunk):
        part = jnp.zeros((chunk // 8, 8, TILE), F32)
        for i, (column, _) in enumerate(cells):
            part = jnp.where((where == column)[None], found[f, i], part)
        parts.append(part.reshape(chunk, TILE))
    return jnp.concatenate(parts, axis=0)


def messages(cells, place, key, pre, middle_t, final_t, hidden_ref):
    for tile in range(place.shape[1] // TILE):
        at = slice(tile * TILE, (tile + 1) * TILE)
        hidden_ref[:, at] = relu16(pre(tile) + pick(cells, place[:, at], key[:, at]))
    hidden = relu16(dot(middle_t, hidden_ref[...]))
    return norm(dot(final_t, hidden), 0)


class Window:
    def __init__(self, fold_y, own_ref=None, rest_ref=None):
        self.row_count = 3 if fold_y else 4
        self.own_rows = (0, 1) if fold_y else (1, 2)
        self.outer_rows = (2,) if fold_y else (0, 3)
        self.own_ref, self.rest_ref = own_ref, rest_ref

    def own_columns(self):
        return [(ex, row) for ex in (1, 2) for row in self.own_rows]

    def own(self, ex, row):
        return (ex - 1) * 2 + self.own_rows.index(row)

    def side(self, ex, row):
        count = len(self.outer_rows)
        return 2 * self.row_count + (ex - 1) * count + self.outer_rows.index(row)

    def cells(self, columns):
        found = []
        for ex, row in columns:
            if ex in (1, 2) and row in self.own_rows:
                ref = self.own_ref.at[self.own(ex, row)]
            elif ex in (1, 2):
                ref = self.rest_ref.at[self.side(ex, row)]
            else:
                ref = self.rest_ref.at[(0 if ex == 0 else self.row_count) + row]
            found.append((ex * 4 + row, ref))
        return found


def slot_sum(message, step):
    total = message[:, :step]
    for at in range(step, message.shape[1], step):
        total = total + message[:, at : at + step]
    return total


def advance(pre, aggregate, latent_t, weights_ref, decoder_out):
    pre = pre + dot(weights_ref[NODE_NEW], aggregate)
    hidden = relu16(dot(weights_ref[NODE_0], relu16(pre)))
    updated = (latent_t + norm(dot(weights_ref[NODE_1], hidden), 0)).astype(BF16)
    hidden = relu16(dot(weights_ref[DECODE_0], updated))
    hidden = relu16(dot(weights_ref[DECODE_1], hidden))
    return dot(decoder_out, hidden)


def moved(position, velocity, acceleration):
    new_velocity = velocity + acceleration
    return jnp.concatenate([position + new_velocity, new_velocity, velocity], axis=0)


def tables_kernel(fold_y, spread_ref):
    index_y = lax.axis_index("gy")
    index_z = lax.axis_index("gz")
    options_y = 2 if fold_y else 3
    line = lax.broadcasted_iota(I32, spread_ref.shape, 1)
    direction = line >> 3
    direction = direction + jnp.where(direction > 12, 1, 0)
    plane = (direction * 57) >> 9
    from_z = direction - 3 * ((direction * 43) >> 7) - 1
    from_y = ((direction * 43) >> 7) - 3 * plane - 1
    if fold_y:
        side_y = jnp.where(from_y == 0, 0, 1)
        valid = (from_y == 0) | (from_y == 1 - 2 * index_y)
    else:
        side_y = jnp.where(from_y < 0, 2, from_y)
        valid = from_y < 2
    side_z = jnp.where(from_z == 0, 0, 1)
    valid = valid & ((from_z == 0) | (from_z == 1 - 2 * index_z)) & (line < 26 * CAP)
    target = ((2 - plane) * options_y + side_y) * 2 + side_z
    spread_ref[...] = jnp.where(valid, target * CAP + (line & 7), -1)


def ranks_kernel(
    sizes,
    edge_ref,
    latent_ref,
    own_zed,
    fill_ref,
    owners_ref,
    edge_w_ref,
    node_in_ref,
    node_w_ref,
    decoder_w_ref,
    encoder_in_ref,
    neighbours_ref,
    positions_ref,
    velocity_ref,
    weights_ref,
    inward_ref,
    alive_ref,
    latent_t_ref,
    node_pre_ref,
    state_ref,
    mover_edge_ref,
    mover_place_ref,
    mover_key_ref,
    mover_near_ref,
    mover_node_pre_ref,
    mover_latent_ref,
    mover_state_ref,
    far_ref,
    pre_ref,
):
    count_x, count_y, count_z = sizes
    fold_y = count_y == 2
    index_x = lax.axis_index("gx")
    index_y = lax.axis_index("gy")
    index_z = lax.axis_index("gz")
    slots = owners_ref.shape[-1]
    width = node_in_ref.shape[-1]
    lane = lax.broadcasted_iota(I32, (1, slots), 1)
    for a, b in CELLS:
        fill = jnp.broadcast_to(fill_ref[a, :, b : b + 1], (1, slots))
        alive_ref[a, b] = jnp.where(lane < fill, 1.0, 0.0)

    owner = jnp.concatenate([owners_ref[a, b] for a, b in CELLS], axis=1)
    alive = jnp.concatenate([alive_ref[a, b] for a, b in CELLS], axis=1)
    own_block = (index_x * count_y + index_y) * count_z + index_z
    stays = jnp.where((alive > 0.5) & (owner == own_block), 1.0, 0.0)
    moving = jnp.where((alive > 0.5) & (owner != own_block), 1, 0)
    owner_x = quotient(owner, count_y * count_z)
    rest = owner - owner_x * (count_y * count_z)
    owner_y = quotient(rest, count_z)
    owner_z = rest - owner_y * count_z
    step_y = owner_y - index_y
    side_y = jnp.where(step_y == 0, 0, 1) if fold_y else jnp.where(step_y < 0, 1, 2 * step_y)
    options_y = 2 if fold_y else 3
    group = ((owner_x - index_x + 1) * options_y + side_y) * 2 + jnp.where(owner_z == index_z, 0, 1)
    group_rows = (3 * options_y * 2 + 15) // 16 * 16
    particles = owner.shape[1]
    member = jnp.where(
        (lax.broadcasted_iota(I32, (group_rows, particles), 0) == group) & (moving == 1), 1.0, 0.0
    )
    triangle = jnp.where(
        lax.broadcasted_iota(I32, (slots, slots), 0) <= lax.broadcasted_iota(I32, (slots, slots), 1),
        1.0,
        0.0,
    ).astype(BF16)
    counted = []
    before = jnp.zeros((group_rows, 1), F32)
    for i in range(4):
        inside = member[:, i * slots : (i + 1) * slots]
        counted.append(dot(inside.astype(BF16), triangle) + before)
        before = before + jnp.sum(inside, axis=1, keepdims=True)
    counted = jnp.concatenate(counted, axis=1)
    rank = (jnp.sum(counted * member, axis=0, keepdims=True) - 1.0).astype(I32)
    column = jnp.where(moving == 1, group * CAP + rank, -1)
    movers = mover_state_ref.shape[1]
    placer = jnp.where(
        lax.broadcasted_iota(I32, (movers, particles), 0) == column, 1.0, 0.0
    ).astype(BF16)

    for i in range(5):
        weights_ref[i] = flip(edge_w_ref[i])
    weights_ref[NODE_OLD] = flip(node_in_ref[:width])
    weights_ref[NODE_NEW] = flip(node_in_ref[width:])
    for i in range(2):
        weights_ref[NODE_0 + i] = flip(node_w_ref[i])
        weights_ref[DECODE_0 + i] = flip(decoder_w_ref[i])
    inward = jnp.concatenate([encoder_in_ref[...].astype(F32), jnp.zeros((4, width), F32)], axis=0)
    inward = inward.astype(BF16)
    inward_ref[...] = jnp.concatenate([inward, inward, inward], axis=0)

    latent = jnp.concatenate([latent_ref[a, b, 0] for a, b in CELLS], axis=0)
    latent_t_ref[...] = latent.astype(F32).T
    node_pre_ref[...] = dot_nt(weights_ref[NODE_OLD], latent)

    def flat(ref, i):
        return jnp.concatenate([ref[i, a, b] for a, b in CELLS], axis=1)

    state = [flat(positions_ref, i) for i in range(3)] + [flat(velocity_ref, i) for i in range(3)]
    state_ref[...] = jnp.concatenate(state + [stays, jnp.zeros_like(stays)], axis=0)

    mover_latent = dot(placer, latent).astype(BF16)
    mover_latent_ref[...] = mover_latent.astype(F32).T
    mover_node_pre_ref[...] = dot_nt(weights_ref[NODE_OLD], mover_latent)
    mover_near_ref[...] = dot_nt(weights_ref[NEAR], mover_latent)
    state = jnp.concatenate(state + [moving.astype(F32), jnp.zeros_like(stays)], axis=0)
    mover_state_ref[...] = joined(dot_nt(thirds(state), placer))
    neighbour_count = edge_ref.shape[3]
    ids = jnp.concatenate(
        [
            jnp.concatenate([neighbours_ref[a, b, k] for a, b in CELLS], axis=1)
            for k in range(neighbour_count)
        ],
        axis=0,
    )
    ids = jnp.concatenate([ids & 127, ids >> 7, jnp.zeros((8, particles), I32)], axis=0)
    ids = dot_nt(ids.astype(F32).astype(BF16), placer).astype(I32)
    place, key = places(ids[:neighbour_count], ids[neighbour_count : 2 * neighbour_count], fold_y)
    mover_place_ref[...] = jnp.concatenate([place[k : k + 1] for k in range(neighbour_count)], axis=1)
    mover_key_ref[...] = jnp.concatenate([key[k : k + 1] for k in range(neighbour_count)], axis=1)

    window = Window(fold_y, far_ref)
    for (ex, row), (a, b) in zip(window.own_columns(), CELLS):
        pair = jnp.concatenate([latent_ref[a, b, 0], own_zed[a, b, 0]], axis=0)
        far_ref[window.own(ex, row)] = dot_nt(weights_ref[FAR], pair).astype(BF16)
    cells = window.cells(window.own_columns())
    for a, bt in CELLS:
        b = (index_y if bt == 0 else 1 - index_y) if fold_y else bt
        ids = jnp.concatenate([neighbours_ref[a, b, k] for k in range(neighbour_count)], axis=1)
        place, key = places(ids & 127, ids >> 7, fold_y)
        near = dot_nt(weights_ref[NEAR], latent_ref[a, b, 0])
        near = jnp.concatenate([near, near], axis=1)
        for tile in range(ids.shape[1] // TILE):
            at = slice(tile * TILE, (tile + 1) * TILE)
            edges = [edge_ref[a, b, 0, k] for k in (2 * tile, 2 * tile + 1)]
            pre_ref[2 * a + bt, :, at] = (
                dot_nt(weights_ref[EDGE], jnp.concatenate(edges, axis=0))
                + near
                + pick(cells, place[:, at], key[:, at])
            )
    for k in range(neighbour_count):
        rows = jnp.concatenate([edge_ref[a, b, 0, k] for a, b in CELLS], axis=0)
        mover_edge_ref[k] = dot(placer, rows).astype(BF16)


def prepare_kernel(
    sizes,
    far_ref,
    mine_ref,
    weights_ref,
    edge_ref,
    place_ref,
    key_ref,
    near_ref,
    far_mine_ref,
    pre_ref,
):
    window = Window(sizes[1] == 2, far_ref)
    core = lax.axis_index("gz")
    far_t = weights_ref[FAR]
    cells = window.cells(window.own_columns())
    for row in range(window.row_count):
        pair = jnp.concatenate([mine_ref[1, row], mine_ref[0, row]], axis=0)
        far_mine_ref[row] = dot_nt(far_t, pair).astype(BF16)
        cells.append((12 * (1 - core) + row, far_mine_ref.at[row]))
    neighbour_count, movers = edge_ref.shape[:2]
    step = TILE // movers
    near = jnp.concatenate([near_ref[...]] * step, axis=1)
    for tile in range(neighbour_count // step):
        edges = jnp.concatenate([edge_ref[k] for k in range(tile * step, (tile + 1) * step)], axis=0)
        at = slice(tile * TILE, (tile + 1) * TILE)
        pre_ref[:, at] = (
            dot_nt(weights_ref[EDGE], edges) + near + pick(cells, place_ref[:, at], key_ref[:, at])
        )


def movers_kernel(
    sizes,
    side_count,
    *refs,
):
    fold_y = sizes[1] == 2
    side_refs, refs = refs[:side_count], refs[side_count:]
    side_zeds, refs = refs[:side_count], refs[side_count:]
    other_ref, far_mine_ref, refs = refs[0], refs[1], refs[2:]
    (
        weights_ref,
        decoder_out_ref,
        pre_ref,
        place_ref,
        key_ref,
        node_pre_ref,
        latent_t_ref,
        state_ref,
        far_ref,
        bucket_ref,
        hidden_ref,
    ) = refs
    window = Window(fold_y, None, far_ref)
    row_count = window.row_count
    core = lax.axis_index("gz")
    far_t = weights_ref[FAR]

    def far(at, here, beside):
        pair = jnp.concatenate([here, beside], axis=0)
        far_ref[at] = dot_nt(far_t, pair).astype(BF16)

    for row in range(row_count):
        far(core * row_count + row, other_ref[0, row], other_ref[1, row])
    for side, row in enumerate(window.outer_rows):
        for ex in (1, 2):
            far(window.side(ex, row), side_refs[side][ex - 1], side_zeds[side][ex - 1])

    movers = state_ref.shape[1]
    for row in range(row_count):
        far_ref[(1 - core) * row_count + row] = far_mine_ref[row]
    cells = [(12 * core + row, far_ref.at[core * row_count + row]) for row in range(row_count)]
    cells += window.cells([(ex, row) for ex in (1, 2) for row in window.outer_rows])
    message = messages(
        cells,
        place_ref[...],
        key_ref[...],
        lambda tile: pre_ref[:, tile * TILE : (tile + 1) * TILE],
        weights_ref[MIDDLE],
        weights_ref[FINAL],
        hidden_ref,
    )
    aggregate = slot_sum(message, movers).astype(BF16)
    acceleration = advance(
        node_pre_ref[...], aggregate, latent_t_ref[...], weights_ref, decoder_out_ref[...]
    )
    mask = state_ref[6:7]
    state = moved(state_ref[0:3], state_ref[3:6], acceleration) * mask
    bucket_ref[...] = jnp.concatenate([state, mask, jnp.zeros((ROWS - 10, movers), F32)], axis=0)


def edges_kernel(
    sizes,
    a,
    alive_ref,
    neighbours_ref,
    far_ref,
    pre_ref,
    weights_ref,
    total_ref,
    hidden_ref,
):
    fold_y = sizes[1] == 2
    window = Window(fold_y, None, far_ref)
    index_y = lax.axis_index("gy")
    alive_ref, neighbours_ref = alive_ref.at[a], neighbours_ref.at[a]
    slots = alive_ref.shape[-1]
    neighbour_count = neighbours_ref.shape[1]
    for bt in range(2):
        if fold_y:
            b = index_y if bt == 0 else 1 - index_y
            rows = (0, 1) if bt == 0 else (0, 1, 2)
        else:
            b = bt
            rows = (bt, bt + 1, bt + 2)
        columns = [(ex, row) for ex in range(a, a + 3) for row in rows]
        columns = [column for column in columns if column not in window.own_columns()]
        ids = jnp.concatenate([neighbours_ref[b, k] for k in range(neighbour_count)], axis=1)
        place, key = places(ids & 127, ids >> 7, fold_y)

        message = messages(
            window.cells(columns),
            place,
            key,
            lambda tile, i=2 * a + bt: pre_ref[i, :, tile * TILE : (tile + 1) * TILE],
            weights_ref[MIDDLE],
            weights_ref[FINAL],
            hidden_ref.at[bt],
        )
        total = jnp.where(alive_ref[b] > 0.5, slot_sum(message, slots), 0.0)
        total_ref[b] = total.astype(BF16)


def nodes_kernel(
    first_ref,
    second_ref,
    node_pre_ref,
    latent_t_ref,
    state_ref,
    weights_ref,
    decoder_out_ref,
    moved_ref,
):
    aggregate = jnp.concatenate([first_ref[0], first_ref[1], second_ref[0], second_ref[1]], axis=1)
    acceleration = advance(
        node_pre_ref[...], aggregate, latent_t_ref[...], weights_ref, decoder_out_ref[...]
    )
    state = moved(state_ref[0:3], state_ref[3:6], acceleration)
    moved_ref[...] = jnp.concatenate(
        [state, state_ref[6:7], jnp.zeros((ROWS - 10, state.shape[1]), F32)], axis=0
    )


def finish_kernel(sizes, moved_ref, zed_ref, *refs):
    count_x, count_y, count_z = sizes
    fold_y = count_y == 2
    options_y = 2 if fold_y else 3
    side_refs, refs = refs[: options_y - 1], refs[options_y - 1 :]
    if fold_y:
        cross_ref, end_ref, *refs = refs
    else:
        end_ref, *refs = refs
    (
        packed_ref,
        spread_ref,
        inward_ref,
        encoder_w_ref,
        kept_latent_ref,
        kept_state_ref,
        arrived_latent_ref,
        arrived_state_ref,
    ) = refs
    core = lax.axis_index("gz")

    def tile(source_x, from_y, from_z):
        if source_x == 0:
            if from_y == 0:
                return zed_ref[...]
            if fold_y:
                return packed_ref[4] if from_z else side_refs[0][...]
            return side_refs[from_y - 1][from_z]
        if fold_y:
            mine = (cross_ref if from_y else end_ref)[1 - from_z]
            other = packed_ref[(0 if from_y else 2) + from_z]
        else:
            mine = end_ref[1 - from_z, from_y]
            other = packed_ref[from_z, from_y]
        return jnp.where(core == (1 - source_x) // 2, mine, other)

    extent = (2.0 * count_x, 2.0 * count_y, 1.0 * count_z)
    slots = kept_latent_ref.shape[-2]
    stays = moved_ref[9:10]
    kept = moved_ref[:9] * stays
    latents = encode(moved_ref[:9], stays, inward_ref[...], encoder_w_ref[...], extent)
    for i, (a, b) in enumerate(CELLS):
        kept_latent_ref[a, b, 0] = latents[i * slots : (i + 1) * slots]
        for j in range(9):
            kept_state_ref[j, a, b] = kept[j : j + 1, i * slots : (i + 1) * slots]
    fold_y = count_y == 2
    index_x = lax.axis_index("gx")
    lanes = zed_ref.shape[-1]
    group = lax.broadcasted_iota(I32, (ROWS, lanes), 1) >> 3
    found = jnp.zeros((ROWS, lanes), F32)
    for source_x in (-1, 0, 1):
        for from_y in range(options_y):
            for from_z in range(2):
                if source_x == 0 and from_y == 0 and from_z == 0:
                    continue
                side_y = from_y if fold_y or from_y == 0 else 3 - from_y
                there = group == ((1 - source_x) * options_y + side_y) * 2 + from_z
                if source_x == -1:
                    there = there & (index_x > 0)
                elif source_x == 1:
                    there = there & (index_x < count_x - 1)
                found = jnp.where(there, tile(source_x, from_y, from_z), found)
    halves = []
    for at in range(0, spread_ref.shape[1], 128):
        lane = jnp.broadcast_to(spread_ref[0:1, at : at + 128], (ROWS, 128))
        half = jnp.zeros((ROWS, 128), F32)
        for base in range(0, lanes, 128):
            index = jnp.clip(lane - base, 0, 127)
            there = (lane >= base) & (lane < base + 128)
            part = jnp.take_along_axis(found[:, base : base + 128], index, axis=1)
            half = jnp.where(there, part, half)
        halves.append(half)
    arrived = jnp.concatenate(halves, axis=1)[:, : 26 * CAP]
    for j in range(9):
        arrived_state_ref[j, 0, 0] = arrived[j : j + 1]
    arrived_latent_ref[0, 0, 0] = encode(
        arrived[:9], arrived[9:10], inward_ref[...], encoder_w_ref[...], extent
    )


def swap(values, axis):
    return lax.ppermute(values, axis, [(0, 1), (1, 0)])


def shift(values, axis, way):
    pairs = [(i, i + 1) for i in range(lax.axis_size(axis) - 1)]
    return lax.ppermute(values, axis, [(j, i) for i, j in pairs] if way else pairs)


def swap_chips(values, cross):
    count_x, count_y, count_z = (lax.axis_size(axis) for axis in ("gx", "gy", "gz"))
    pairs = []
    for x in range(count_x):
        for y in range(count_y):
            for z in range(count_z):
                to_x = x + 1 - 2 * z
                if 0 <= to_x < count_x:
                    to = (to_x, y ^ 1 if cross else y, 1 - z)
                else:
                    to = (x, y, z)
                pairs.append(((x * count_y + y) * count_z + z, (to[0] * count_y + to[1]) * count_z + to[2]))
    return lax.ppermute(values, ("gx", "gy", "gz"), pairs)


def call(kernel, name, in_specs, outs, scratch, operands, flops):
    return pl.pallas_call(
        kernel,
        out_shape=tuple(jax.ShapeDtypeStruct(shape, kind) for shape, kind in outs),
        in_specs=in_specs,
        out_specs=tuple(VMEM for _ in outs),
        scratch_shapes=scratch,
        compiler_params=pltpu.CompilerParams(vmem_limit_bytes=32 * 1024 * 1024),
        cost_estimate=pl.CostEstimate(flops=flops, bytes_accessed=0, transcendentals=0),
        name=name,
    )(*operands)


def in_hbm(array):
    return pltpu.with_memory_space_constraint(array, pltpu.HBM)


def like(array):
    return pltpu.VMEM(array.shape, array.dtype)


def body(
    node_latent,
    edge_latent,
    positions,
    velocity,
    fill,
    neighbours,
    owners,
    edge_weights,
    node_in,
    node_weights,
    decoder_weights,
    decoder_out,
    encoder_in,
    encoder_weights,
):
    sizes = tuple(lax.axis_size(axis) for axis in ("gx", "gy", "gz"))
    fold_y = sizes[1] == 2
    slots, width = node_latent.shape[-2:]
    neighbour_count = neighbours.shape[3]
    particles = 4 * slots
    options_y = 2 if fold_y else 3
    movers = (3 * options_y * 2 * CAP + 127) // 128 * 128
    rows = 3 if fold_y else 4
    fill = jnp.transpose(fill, (0, 2, 1))
    neighbours = neighbours.reshape(2, 2, neighbour_count, 1, slots)

    own_zed = swap(node_latent, "gz")
    if fold_y:
        sides = [swap(node_latent, "gy")]
    spread = call(
        functools.partial(tables_kernel, fold_y),
        "tables",
        [],
        [((8, 256), I32)],
        [],
        [],
        5_000_000_000,
    )[0]
    latent, spread = lax.optimization_barrier((node_latent, spread))
    core = lax.axis_index("gz")
    if fold_y:
        row = 1 - lax.axis_index("gy")
        end = lax.dynamic_index_in_dim(latent[:, :, 0], 1 - core, 0, False)
        beside = lax.dynamic_index_in_dim(own_zed[:, :, 0], 1 - core, 0, False)
        both = jnp.stack([end, beside])
        corner = lax.dynamic_slice_in_dim(both, row, 1, axis=1)
        mine = [swap_chips(both, False)]
        corner, both = lax.optimization_barrier((corner, both))
        mine.append(swap_chips(corner, True))
    else:
        sides = [shift(latent[:, 1, 0], "gy", 0), shift(latent[:, 0, 0], "gy", 1)]
        side_zeds = [swap(part, "gz") for part in sides]
        layers = []
        for middle, outer in ((latent, sides), (own_zed, side_zeds)):
            parts = [outer[0][:, None], middle[:, :, 0], outer[1][:, None]]
            parts = [lax.dynamic_index_in_dim(part, 1 - core, 0, False) for part in parts]
            layers.append(jnp.concatenate(parts, axis=0))
        mine = [swap_chips(jnp.stack(layers), False)]

    ranked = call(
        functools.partial(ranks_kernel, sizes),
        "ranks",
        [VMEM] * 13,
        [
            ((11, width, width), BF16),
            ((48, width), BF16),
            ((2, 2, 1, slots), F32),
            ((width, particles), F32),
            ((width, particles), F32),
            ((8, particles), F32),
            ((neighbour_count, movers, width), BF16),
            ((1, neighbour_count * movers), I32),
            ((1, neighbour_count * movers), I32),
            ((width, movers), F32),
            ((width, movers), F32),
            ((width, movers), F32),
            ((8, movers), F32),
            ((4, width, 2 * slots), BF16),
            ((4, width, neighbour_count * slots), F32),
        ],
        [],
        (edge_latent, latent, own_zed, fill, owners, edge_weights, node_in, node_weights, decoder_weights, encoder_in, neighbours, positions, velocity),
        5_000_000_000,
    )
    mine, sides, ranked = lax.optimization_barrier((mine, sides, ranked))
    (
        weights,
        inward,
        alive,
        latent_t,
        node_pre,
        state,
        mover_edges,
        mover_place,
        mover_key,
        mover_near,
        mover_node_pre,
        mover_latent,
        mover_state,
        far_own,
        edge_pre,
    ) = ranked
    mine = jnp.concatenate(mine, axis=1)
    if fold_y:
        sides = [lax.dynamic_index_in_dim(sides[0][:, :, 0], lax.axis_index("gy"), 1, False)]
        packed = jnp.concatenate([mine.reshape(-1, slots, width), sides[0]], axis=0)
    else:
        packed = mine.reshape(-1, slots, width)
    packed = swap(packed, "gz")
    prepared = call(
        functools.partial(prepare_kernel, sizes),
        "prepare",
        [VMEM] * 7,
        [((rows, width, 2 * slots), BF16), ((width, neighbour_count * movers), F32)],
        [],
        (far_own, mine, weights, mover_edges, mover_place, mover_key, mover_near),
        5_000_000_000,
    )
    packed, prepared = lax.optimization_barrier((packed, prepared))
    cells = mine.shape[0] * mine.shape[1]
    if fold_y:
        side_zeds = [packed[cells:]]
    far_mine, mover_pre = prepared
    halo = [*sides, *side_zeds, packed[:cells].reshape(mine.shape), far_mine]

    far_rest, bucket = call(
        functools.partial(movers_kernel, sizes, len(sides)),
        "movers",
        [VMEM] * (len(halo) + 8),
        [((4 * rows - 4, width, 2 * slots), BF16), ((ROWS, movers), F32)],
        [pltpu.VMEM((width, neighbour_count * movers), BF16)],
        (
            *halo,
            weights,
            decoder_out,
            mover_pre,
            mover_place,
            mover_key,
            mover_node_pre,
            mover_latent,
            mover_state,
        ),
        3_000_000_000,
    )

    def edges(a):
        return call(
            functools.partial(edges_kernel, sizes, a),
            "edges",
            [VMEM] * 5,
            [((2, width, slots), BF16)],
            [pltpu.VMEM((2, width, neighbour_count * slots), BF16)],
            (alive, neighbours, far_rest, edge_pre, weights),
            4_000_000_000,
        )[0]

    zed = swap(bucket, "gz")
    if fold_y:
        sides = [swap(bucket, "gy")]
        zed, far_rest = lax.optimization_barrier((zed, far_rest))
        both = jnp.stack([bucket, zed])
        ends = [swap_chips(both, True), swap_chips(both, False)]
    else:
        both = jnp.stack([bucket, zed])
        sides = [shift(both, "gy", 0), shift(both, "gy", 1)]
        ends = [swap_chips(jnp.stack([both, *sides], axis=1), False)]
    first, second = edges(0), edges(1)
    sides, ends, first, second = lax.optimization_barrier((sides, ends, first, second))
    if fold_y:
        packed = swap(jnp.concatenate([*ends, sides[0][None]], axis=0), "gz")
    else:
        packed = swap(ends[0], "gz")
    state = call(
        nodes_kernel,
        "nodes",
        [VMEM] * 7,
        [((ROWS, particles), F32)],
        [],
        (first, second, node_pre, latent_t, state, weights, decoder_out),
        1_000_000_000,
    )[0]
    packed, state = lax.optimization_barrier((packed, state))
    return call(
        functools.partial(finish_kernel, sizes),
        "finish",
        [VMEM] * (len(sides) + len(ends) + 6),
        [
            (node_latent.shape, BF16),
            ((9,) + node_latent.shape[:4], F32),
            ((1, 1, 1, 26 * CAP, width), BF16),
            ((9, 1, 1, 1, 26 * CAP), F32),
        ],
        [],
        (state, zed, *sides, *ends, packed, spread, inward, encoder_weights),
        1_000_000_000,
    )


def solution(mesh):
    placed = (
        P(("group", "gx"), "gy", "gz", None, None),
        P(("group", "gx"), "gy", "gz", None, None, None),
        P(None, ("group", "gx"), "gy", "gz", None),
        P(None, ("group", "gx"), "gy", "gz", None),
        P(("group", "gx"), "gy", "gz"),
        P(("group", "gx"), "gy", "gz", None, None),
        P(("group", "gx"), "gy", "gz", None),
        P(),
        P(),
        P(),
        P(),
        P(),
        P(),
        P(),
    )
    return jax.shard_map(
        body,
        mesh=mesh,
        in_specs=placed,
        out_specs=(
            P(("group", "gx"), "gy", "gz", None, None),
            P(None, ("group", "gx"), "gy", "gz", None),
            P(("group", "gx"), "gy", "gz", None, None),
            P(None, ("group", "gx"), "gy", "gz", None),
        ),
        check_vma=False,
    )
```

```python
import functools
import itertools

import jax
import jax.numpy as jnp
from jax import lax
from jax.experimental import pallas as pl
from jax.experimental.pallas import tpu as pltpu
from jax.sharding import PartitionSpec as P

CAP = 8
F32 = jnp.float32
BF16 = jnp.bfloat16
I32 = jnp.int32
ROWS = 16
TILE = 256
CELLS = [(a, b) for a in range(2) for b in range(2)]
EDGE, NEAR, FAR, MIDDLE, FINAL, NODE_OLD, NODE_NEW, NODE_0, NODE_1, DECODE_0, DECODE_1 = range(11)

VMEM = pl.BlockSpec(memory_space=pltpu.VMEM)
SMEM = pl.BlockSpec(memory_space=pltpu.SMEM)
ANY = pl.BlockSpec(memory_space=pl.ANY)


def dot(left, right):
    return jnp.dot(left, right, preferred_element_type=F32)


def dot_nt(left, right):
    return lax.dot_general(left, right, (((1,), (1,)), ((), ())), preferred_element_type=F32)


def dot_tn(left, right):
    return lax.dot_general(left, right, (((0,), (0,)), ((), ())), preferred_element_type=F32)


def relu16(values):
    return jnp.maximum(values, 0.0).astype(BF16)


def norm(values, axis):
    scale = 1.0 / values.shape[axis]
    centred = values - jnp.sum(values, axis=axis, keepdims=True) * scale
    spread = jnp.sum(centred * centred, axis=axis, keepdims=True) * scale
    return centred * lax.rsqrt(spread + 1e-05)


def thirds(values):
    high = values.astype(BF16)
    rest = values - high.astype(F32)
    middle = rest.astype(BF16)
    low = (rest - middle.astype(F32)).astype(BF16)
    return jnp.concatenate([high, middle, low], axis=0)


def joined(values):
    rows = values.shape[0] // 3
    return values[:rows] + values[rows : 2 * rows] + values[2 * rows :]


def quotient(values, count):
    if count & (count - 1) == 0:
        return values >> (count.bit_length() - 1)
    return lax.div(values, jnp.full_like(values, count))


def flip(weights):
    return weights.astype(F32).T.astype(BF16)


def fetch(pairs, sems):
    copies = [pltpu.make_async_copy(src, dst, sems.at[i]) for i, (src, dst) in enumerate(pairs)]
    for copy in copies:
        copy.start()
    return copies


def encode(state, mask, inward, encoder_w, extent):
    width = state.shape[1]
    position = state[0:3]
    row = lax.broadcasted_iota(I32, (3, width), 0)
    size = jnp.where(row == 0, extent[0], jnp.where(row == 1, extent[1], extent[2]))
    features = jnp.concatenate(
        [
            state[3:9],
            jnp.clip(position, -1.0, 1.0),
            jnp.clip(size - position, -1.0, 1.0),
            jnp.zeros((4, width), F32),
        ],
        axis=0,
    )
    hidden = relu16(dot_tn(thirds(features), inward))
    hidden = relu16(dot(hidden, encoder_w[0]))
    column = jnp.broadcast_to(mask, (8, width)).T[:, 0:1]
    return (norm(dot(hidden, encoder_w[1]), 1) * column).astype(BF16)


def places(ids_low, ids_high, fold_y):
    plane = (ids_high * 43) >> 7
    ez = ids_high - plane * 3
    ey = plane & 3
    ex = plane >> 2
    if fold_y:
        row = jnp.where(ey == 1, 0, jnp.where(ey == 2, 1, 2))
    else:
        row = ey
    return ex * 4 + row, ids_low + jnp.where(ez == 1, 0, 128)


def pick(cells, place, key):
    width = cells[0][1].shape[0]
    chunk = 32
    window = jnp.concatenate(
        [ref[f : f + chunk] for f in range(0, width, chunk) for _, ref in cells], axis=0
    )
    key_rows = lax.broadcasted_iota(I32, (TILE, TILE), 0).astype(F32).astype(BF16)
    key = jnp.broadcast_to(key.astype(F32), (16, TILE)).astype(BF16)
    same = key_rows.reshape(TILE // 16, 16, TILE) == key[None]
    picker = jnp.where(same, jnp.ones((), BF16), jnp.zeros((), BF16)).reshape(TILE, TILE)
    found = dot(window, picker).reshape(width // chunk, len(cells), chunk // 8, 8, TILE)
    where = jnp.broadcast_to(place, (8, TILE))
    parts = []
    for f in range(width // chunk):
        part = jnp.zeros((chunk // 8, 8, TILE), F32)
        for i, (column, _) in enumerate(cells):
            part = jnp.where((where == column)[None], found[f, i], part)
        parts.append(part.reshape(chunk, TILE))
    return jnp.concatenate(parts, axis=0)


def messages(cells, place, key, pre, middle_t, final_t, hidden_ref):
    for tile in range(place.shape[1] // TILE):
        at = slice(tile * TILE, (tile + 1) * TILE)
        hidden_ref[:, at] = relu16(pre(tile) + pick(cells, place[:, at], key[:, at]))
    hidden = relu16(dot(middle_t, hidden_ref[...]))
    return norm(dot(final_t, hidden), 0)


class Window:
    def __init__(self, fold_y, own_ref=None, rest_ref=None):
        self.row_count = 3 if fold_y else 4
        self.own_rows = (0, 1) if fold_y else (1, 2)
        self.outer_rows = (2,) if fold_y else (0, 3)
        self.own_ref, self.rest_ref = own_ref, rest_ref

    def own_columns(self):
        return [(ex, row) for ex in (1, 2) for row in self.own_rows]

    def own(self, ex, row):
        return (ex - 1) * 2 + self.own_rows.index(row)

    def side(self, ex, row):
        count = len(self.outer_rows)
        return 2 * self.row_count + (ex - 1) * count + self.outer_rows.index(row)

    def cells(self, columns):
        found = []
        for ex, row in columns:
            if ex in (1, 2) and row in self.own_rows:
                ref = self.own_ref.at[self.own(ex, row)]
            elif ex in (1, 2):
                ref = self.rest_ref.at[self.side(ex, row)]
            else:
                ref = self.rest_ref.at[(0 if ex == 0 else self.row_count) + row]
            found.append((ex * 4 + row, ref))
        return found


def slot_sum(message, step):
    total = message[:, :step]
    for at in range(step, message.shape[1], step):
        total = total + message[:, at : at + step]
    return total


def advance(pre, aggregate, latent_t, weights_ref, decoder_out):
    pre = pre + dot(weights_ref[NODE_NEW], aggregate)
    hidden = relu16(dot(weights_ref[NODE_0], relu16(pre)))
    updated = (latent_t + norm(dot(weights_ref[NODE_1], hidden), 0)).astype(BF16)
    hidden = relu16(dot(weights_ref[DECODE_0], updated))
    hidden = relu16(dot(weights_ref[DECODE_1], hidden))
    return dot(decoder_out, hidden)


def moved(position, velocity, acceleration):
    new_velocity = velocity + acceleration
    return jnp.concatenate([position + new_velocity, new_velocity, velocity], axis=0)


def tables_kernel(fold_y, spread_ref):
    index_y = lax.axis_index("gy")
    index_z = lax.axis_index("gz")
    options_y = 2 if fold_y else 3
    line = lax.broadcasted_iota(I32, spread_ref.shape, 1)
    direction = line >> 3
    direction = direction + jnp.where(direction > 12, 1, 0)
    plane = (direction * 57) >> 9
    from_z = direction - 3 * ((direction * 43) >> 7) - 1
    from_y = ((direction * 43) >> 7) - 3 * plane - 1
    if fold_y:
        side_y = jnp.where(from_y == 0, 0, 1)
        valid = (from_y == 0) | (from_y == 1 - 2 * index_y)
    else:
        side_y = jnp.where(from_y < 0, 2, from_y)
        valid = from_y < 2
    side_z = jnp.where(from_z == 0, 0, 1)
    valid = valid & ((from_z == 0) | (from_z == 1 - 2 * index_z)) & (line < 26 * CAP)
    target = ((2 - plane) * options_y + side_y) * 2 + side_z
    spread_ref[...] = jnp.where(valid, target * CAP + (line & 7), -1)


def ranks_kernel(
    sizes,
    edge_ref,
    latent_ref,
    own_zed,
    fill_ref,
    owners_ref,
    edge_w_ref,
    node_in_ref,
    node_w_ref,
    decoder_w_ref,
    encoder_in_ref,
    neighbours_ref,
    positions_ref,
    velocity_ref,
    weights_ref,
    inward_ref,
    alive_ref,
    latent_t_ref,
    node_pre_ref,
    state_ref,
    mover_edge_ref,
    mover_place_ref,
    mover_key_ref,
    mover_near_ref,
    mover_node_pre_ref,
    mover_latent_ref,
    mover_state_ref,
    far_ref,
    pre_ref,
):
    count_x, count_y, count_z = sizes
    fold_y = count_y == 2
    index_x = lax.axis_index("gx")
    index_y = lax.axis_index("gy")
    index_z = lax.axis_index("gz")
    slots = owners_ref.shape[-1]
    width = node_in_ref.shape[-1]
    lane = lax.broadcasted_iota(I32, (1, slots), 1)
    for a, b in CELLS:
        fill = jnp.broadcast_to(fill_ref[a, :, b : b + 1], (1, slots))
        alive_ref[a, b] = jnp.where(lane < fill, 1.0, 0.0)

    owner = jnp.concatenate([owners_ref[a, b] for a, b in CELLS], axis=1)
    alive = jnp.concatenate([alive_ref[a, b] for a, b in CELLS], axis=1)
    own_block = (index_x * count_y + index_y) * count_z + index_z
    stays = jnp.where((alive > 0.5) & (owner == own_block), 1.0, 0.0)
    moving = jnp.where((alive > 0.5) & (owner != own_block), 1, 0)
    owner_x = quotient(owner, count_y * count_z)
    rest = owner - owner_x * (count_y * count_z)
    owner_y = quotient(rest, count_z)
    owner_z = rest - owner_y * count_z
    step_y = owner_y - index_y
    side_y = jnp.where(step_y == 0, 0, 1) if fold_y else jnp.where(step_y < 0, 1, 2 * step_y)
    options_y = 2 if fold_y else 3
    group = ((owner_x - index_x + 1) * options_y + side_y) * 2 + jnp.where(owner_z == index_z, 0, 1)
    group_rows = (3 * options_y * 2 + 15) // 16 * 16
    particles = owner.shape[1]
    member = jnp.where(
        (lax.broadcasted_iota(I32, (group_rows, particles), 0) == group) & (moving == 1), 1.0, 0.0
    )
    triangle = jnp.where(
        lax.broadcasted_iota(I32, (slots, slots), 0) <= lax.broadcasted_iota(I32, (slots, slots), 1),
        1.0,
        0.0,
    ).astype(BF16)
    counted = []
    before = jnp.zeros((group_rows, 1), F32)
    for i in range(4):
        inside = member[:, i * slots : (i + 1) * slots]
        counted.append(dot(inside.astype(BF16), triangle) + before)
        before = before + jnp.sum(inside, axis=1, keepdims=True)
    counted = jnp.concatenate(counted, axis=1)
    rank = (jnp.sum(counted * member, axis=0, keepdims=True) - 1.0).astype(I32)
    column = jnp.where(moving == 1, group * CAP + rank, -1)
    movers = mover_state_ref.shape[1]
    placer = jnp.where(
        lax.broadcasted_iota(I32, (movers, particles), 0) == column, 1.0, 0.0
    ).astype(BF16)

    for i in range(5):
        weights_ref[i] = flip(edge_w_ref[i])
    weights_ref[NODE_OLD] = flip(node_in_ref[:width])
    weights_ref[NODE_NEW] = flip(node_in_ref[width:])
    for i in range(2):
        weights_ref[NODE_0 + i] = flip(node_w_ref[i])
        weights_ref[DECODE_0 + i] = flip(decoder_w_ref[i])
    inward = jnp.concatenate([encoder_in_ref[...].astype(F32), jnp.zeros((4, width), F32)], axis=0)
    inward = inward.astype(BF16)
    inward_ref[...] = jnp.concatenate([inward, inward, inward], axis=0)

    latent = jnp.concatenate([latent_ref[a, b, 0] for a, b in CELLS], axis=0)
    latent_t_ref[...] = latent.astype(F32).T
    node_pre_ref[...] = dot_nt(weights_ref[NODE_OLD], latent)

    def flat(ref, i):
        return jnp.concatenate([ref[i, a, b] for a, b in CELLS], axis=1)

    state = [flat(positions_ref, i) for i in range(3)] + [flat(velocity_ref, i) for i in range(3)]
    state_ref[...] = jnp.concatenate(state + [stays, jnp.zeros_like(stays)], axis=0)

    mover_latent = dot(placer, latent).astype(BF16)
    mover_latent_ref[...] = mover_latent.astype(F32).T
    mover_node_pre_ref[...] = dot_nt(weights_ref[NODE_OLD], mover_latent)
    mover_near_ref[...] = dot_nt(weights_ref[NEAR], mover_latent)
    state = jnp.concatenate(state + [moving.astype(F32), jnp.zeros_like(stays)], axis=0)
    mover_state_ref[...] = joined(dot_nt(thirds(state), placer))
    neighbour_count = edge_ref.shape[3]
    ids = jnp.concatenate(
        [
            jnp.concatenate([neighbours_ref[a, b, k] for a, b in CELLS], axis=1)
            for k in range(neighbour_count)
        ],
        axis=0,
    )
    ids = jnp.concatenate([ids & 127, ids >> 7, jnp.zeros((8, particles), I32)], axis=0)
    ids = dot_nt(ids.astype(F32).astype(BF16), placer).astype(I32)
    place, key = places(ids[:neighbour_count], ids[neighbour_count : 2 * neighbour_count], fold_y)
    mover_place_ref[...] = jnp.concatenate([place[k : k + 1] for k in range(neighbour_count)], axis=1)
    mover_key_ref[...] = jnp.concatenate([key[k : k + 1] for k in range(neighbour_count)], axis=1)

    window = Window(fold_y, far_ref)
    for (ex, row), (a, b) in zip(window.own_columns(), CELLS):
        pair = jnp.concatenate([latent_ref[a, b, 0], own_zed[a, b, 0]], axis=0)
        far_ref[window.own(ex, row)] = dot_nt(weights_ref[FAR], pair).astype(BF16)
    cells = window.cells(window.own_columns())
    for a, bt in CELLS:
        b = (index_y if bt == 0 else 1 - index_y) if fold_y else bt
        ids = jnp.concatenate([neighbours_ref[a, b, k] for k in range(neighbour_count)], axis=1)
        place, key = places(ids & 127, ids >> 7, fold_y)
        near = dot_nt(weights_ref[NEAR], latent_ref[a, b, 0])
        near = jnp.concatenate([near, near], axis=1)
        for tile in range(ids.shape[1] // TILE):
            at = slice(tile * TILE, (tile + 1) * TILE)
            edges = [edge_ref[a, b, 0, k] for k in (2 * tile, 2 * tile + 1)]
            pre_ref[2 * a + bt, :, at] = (
                dot_nt(weights_ref[EDGE], jnp.concatenate(edges, axis=0))
                + near
                + pick(cells, place[:, at], key[:, at])
            )
    for k in range(neighbour_count):
        rows = jnp.concatenate([edge_ref[a, b, 0, k] for a, b in CELLS], axis=0)
        mover_edge_ref[k] = dot(placer, rows).astype(BF16)


def prepare_kernel(
    sizes,
    far_ref,
    mine_ref,
    weights_ref,
    edge_ref,
    place_ref,
    key_ref,
    near_ref,
    far_mine_ref,
    pre_ref,
):
    window = Window(sizes[1] == 2, far_ref)
    core = lax.axis_index("gz")
    far_t = weights_ref[FAR]
    cells = window.cells(window.own_columns())
    for row in range(window.row_count):
        pair = jnp.concatenate([mine_ref[1, row], mine_ref[0, row]], axis=0)
        far_mine_ref[row] = dot_nt(far_t, pair).astype(BF16)
        cells.append((12 * (1 - core) + row, far_mine_ref.at[row]))
    neighbour_count, movers = edge_ref.shape[:2]
    step = TILE // movers
    near = jnp.concatenate([near_ref[...]] * step, axis=1)
    for tile in range(neighbour_count // step):
        edges = jnp.concatenate([edge_ref[k] for k in range(tile * step, (tile + 1) * step)], axis=0)
        at = slice(tile * TILE, (tile + 1) * TILE)
        pre_ref[:, at] = (
            dot_nt(weights_ref[EDGE], edges) + near + pick(cells, place_ref[:, at], key_ref[:, at])
        )


def movers_kernel(
    sizes,
    side_count,
    *refs,
):
    fold_y = sizes[1] == 2
    side_refs, refs = refs[:side_count], refs[side_count:]
    side_zeds, refs = refs[:side_count], refs[side_count:]
    other_ref, far_mine_ref, refs = refs[0], refs[1], refs[2:]
    (
        weights_ref,
        decoder_out_ref,
        pre_ref,
        place_ref,
        key_ref,
        node_pre_ref,
        latent_t_ref,
        state_ref,
        far_ref,
        bucket_ref,
        hidden_ref,
    ) = refs
    window = Window(fold_y, None, far_ref)
    row_count = window.row_count
    core = lax.axis_index("gz")
    far_t = weights_ref[FAR]

    def far(at, here, beside):
        pair = jnp.concatenate([here, beside], axis=0)
        far_ref[at] = dot_nt(far_t, pair).astype(BF16)

    for row in range(row_count):
        far(core * row_count + row, other_ref[0, row], other_ref[1, row])
    for side, row in enumerate(window.outer_rows):
        for ex in (1, 2):
            far(window.side(ex, row), side_refs[side][ex - 1], side_zeds[side][ex - 1])

    movers = state_ref.shape[1]
    for row in range(row_count):
        far_ref[(1 - core) * row_count + row] = far_mine_ref[row]
    cells = [(12 * core + row, far_ref.at[core * row_count + row]) for row in range(row_count)]
    cells += window.cells([(ex, row) for ex in (1, 2) for row in window.outer_rows])
    message = messages(
        cells,
        place_ref[...],
        key_ref[...],
        lambda tile: pre_ref[:, tile * TILE : (tile + 1) * TILE],
        weights_ref[MIDDLE],
        weights_ref[FINAL],
        hidden_ref,
    )
    aggregate = slot_sum(message, movers).astype(BF16)
    acceleration = advance(
        node_pre_ref[...], aggregate, latent_t_ref[...], weights_ref, decoder_out_ref[...]
    )
    mask = state_ref[6:7]
    state = moved(state_ref[0:3], state_ref[3:6], acceleration) * mask
    bucket_ref[...] = jnp.concatenate([state, mask, jnp.zeros((ROWS - 10, movers), F32)], axis=0)


def edges_kernel(
    sizes,
    a,
    alive_ref,
    neighbours_ref,
    far_ref,
    pre_ref,
    weights_ref,
    total_ref,
    hidden_ref,
):
    fold_y = sizes[1] == 2
    window = Window(fold_y, None, far_ref)
    index_y = lax.axis_index("gy")
    alive_ref, neighbours_ref = alive_ref.at[a], neighbours_ref.at[a]
    slots = alive_ref.shape[-1]
    neighbour_count = neighbours_ref.shape[1]
    for bt in range(2):
        if fold_y:
            b = index_y if bt == 0 else 1 - index_y
            rows = (0, 1) if bt == 0 else (0, 1, 2)
        else:
            b = bt
            rows = (bt, bt + 1, bt + 2)
        columns = [(ex, row) for ex in range(a, a + 3) for row in rows]
        columns = [column for column in columns if column not in window.own_columns()]
        ids = jnp.concatenate([neighbours_ref[b, k] for k in range(neighbour_count)], axis=1)
        place, key = places(ids & 127, ids >> 7, fold_y)

        message = messages(
            window.cells(columns),
            place,
            key,
            lambda tile, i=2 * a + bt: pre_ref[i, :, tile * TILE : (tile + 1) * TILE],
            weights_ref[MIDDLE],
            weights_ref[FINAL],
            hidden_ref.at[bt],
        )
        total = jnp.where(alive_ref[b] > 0.5, slot_sum(message, slots), 0.0)
        total_ref[b] = total.astype(BF16)


def nodes_kernel(
    first_ref,
    second_ref,
    node_pre_ref,
    latent_t_ref,
    state_ref,
    weights_ref,
    decoder_out_ref,
    moved_ref,
):
    aggregate = jnp.concatenate([first_ref[0], first_ref[1], second_ref[0], second_ref[1]], axis=1)
    acceleration = advance(
        node_pre_ref[...], aggregate, latent_t_ref[...], weights_ref, decoder_out_ref[...]
    )
    state = moved(state_ref[0:3], state_ref[3:6], acceleration)
    moved_ref[...] = jnp.concatenate(
        [state, state_ref[6:7], jnp.zeros((ROWS - 10, state.shape[1]), F32)], axis=0
    )


def finish_kernel(sizes, moved_ref, zed_ref, *refs):
    count_x, count_y, count_z = sizes
    fold_y = count_y == 2
    options_y = 2 if fold_y else 3
    side_refs, refs = refs[: options_y - 1], refs[options_y - 1 :]
    if fold_y:
        cross_ref, end_ref, *refs = refs
    else:
        end_ref, *refs = refs
    (
        packed_ref,
        spread_ref,
        inward_ref,
        encoder_w_ref,
        kept_latent_ref,
        kept_state_ref,
        arrived_latent_ref,
        arrived_state_ref,
    ) = refs
    core = lax.axis_index("gz")

    def tile(source_x, from_y, from_z):
        if source_x == 0:
            if from_y == 0:
                return zed_ref[...]
            if fold_y:
                return packed_ref[4] if from_z else side_refs[0][...]
            return side_refs[from_y - 1][from_z]
        if fold_y:
            mine = (cross_ref if from_y else end_ref)[1 - from_z]
            other = packed_ref[(0 if from_y else 2) + from_z]
        else:
            mine = end_ref[1 - from_z, from_y]
            other = packed_ref[from_z, from_y]
        return jnp.where(core == (1 - source_x) // 2, mine, other)

    extent = (2.0 * count_x, 2.0 * count_y, 1.0 * count_z)
    slots = kept_latent_ref.shape[-2]
    stays = moved_ref[9:10]
    kept = moved_ref[:9] * stays
    latents = encode(moved_ref[:9], stays, inward_ref[...], encoder_w_ref[...], extent)
    for i, (a, b) in enumerate(CELLS):
        kept_latent_ref[a, b, 0] = latents[i * slots : (i + 1) * slots]
        for j in range(9):
            kept_state_ref[j, a, b] = kept[j : j + 1, i * slots : (i + 1) * slots]
    fold_y = count_y == 2
    index_x = lax.axis_index("gx")
    lanes = zed_ref.shape[-1]
    group = lax.broadcasted_iota(I32, (ROWS, lanes), 1) >> 3
    found = jnp.zeros((ROWS, lanes), F32)
    for source_x in (-1, 0, 1):
        for from_y in range(options_y):
            for from_z in range(2):
                if source_x == 0 and from_y == 0 and from_z == 0:
                    continue
                side_y = from_y if fold_y or from_y == 0 else 3 - from_y
                there = group == ((1 - source_x) * options_y + side_y) * 2 + from_z
                if source_x == -1:
                    there = there & (index_x > 0)
                elif source_x == 1:
                    there = there & (index_x < count_x - 1)
                found = jnp.where(there, tile(source_x, from_y, from_z), found)
    halves = []
    for at in range(0, spread_ref.shape[1], 128):
        lane = jnp.broadcast_to(spread_ref[0:1, at : at + 128], (ROWS, 128))
        half = jnp.zeros((ROWS, 128), F32)
        for base in range(0, lanes, 128):
            index = jnp.clip(lane - base, 0, 127)
            there = (lane >= base) & (lane < base + 128)
            part = jnp.take_along_axis(found[:, base : base + 128], index, axis=1)
            half = jnp.where(there, part, half)
        halves.append(half)
    arrived = jnp.concatenate(halves, axis=1)[:, : 26 * CAP]
    for j in range(9):
        arrived_state_ref[j, 0, 0] = arrived[j : j + 1]
    arrived_latent_ref[0, 0, 0] = encode(
        arrived[:9], arrived[9:10], inward_ref[...], encoder_w_ref[...], extent
    )


def swap(values, axis):
    return lax.ppermute(values, axis, [(0, 1), (1, 0)])


def shift(values, axis, way):
    pairs = [(i, i + 1) for i in range(lax.axis_size(axis) - 1)]
    return lax.ppermute(values, axis, [(j, i) for i, j in pairs] if way else pairs)


def swap_chips(values, cross):
    axes = ("group", "gx", "gy", "gz")
    counts = tuple(lax.axis_size(axis) for axis in axes)

    def number(place):
        total = 0
        for count, index in zip(counts, place):
            total = total * count + index
        return total

    pairs = []
    for place in itertools.product(*(range(count) for count in counts)):
        group, x, y, z = place
        to_x = x + 1 - 2 * z
        if 0 <= to_x < counts[1]:
            to = (group, to_x, y ^ 1 if cross else y, 1 - z)
        else:
            to = (group ^ 1, x, y, z)
        pairs.append((number(place), number(to)))
    return lax.ppermute(values, axes, pairs)


def call(kernel, name, in_specs, outs, scratch, operands, flops):
    return pl.pallas_call(
        kernel,
        out_shape=tuple(jax.ShapeDtypeStruct(shape, kind) for shape, kind in outs),
        in_specs=in_specs,
        out_specs=tuple(VMEM for _ in outs),
        scratch_shapes=scratch,
        compiler_params=pltpu.CompilerParams(vmem_limit_bytes=32 * 1024 * 1024),
        cost_estimate=pl.CostEstimate(flops=flops, bytes_accessed=0, transcendentals=0),
        name=name,
    )(*operands)


def in_hbm(array):
    return pltpu.with_memory_space_constraint(array, pltpu.HBM)


def like(array):
    return pltpu.VMEM(array.shape, array.dtype)


def body(
    node_latent,
    edge_latent,
    positions,
    velocity,
    fill,
    neighbours,
    owners,
    edge_weights,
    node_in,
    node_weights,
    decoder_weights,
    decoder_out,
    encoder_in,
    encoder_weights,
):
    sizes = tuple(lax.axis_size(axis) for axis in ("gx", "gy", "gz"))
    fold_y = sizes[1] == 2
    slots, width = node_latent.shape[-2:]
    neighbour_count = neighbours.shape[3]
    particles = 4 * slots
    options_y = 2 if fold_y else 3
    movers = (3 * options_y * 2 * CAP + 127) // 128 * 128
    rows = 3 if fold_y else 4
    fill = jnp.transpose(fill, (0, 2, 1))
    neighbours = neighbours.reshape(2, 2, neighbour_count, 1, slots)

    own_zed = swap(node_latent, "gz")
    if fold_y:
        sides = [swap(node_latent, "gy")]
    spread = call(
        functools.partial(tables_kernel, fold_y),
        "tables",
        [],
        [((8, 256), I32)],
        [],
        [],
        5_000_000_000,
    )[0]
    latent, spread = lax.optimization_barrier((node_latent, spread))
    core = lax.axis_index("gz")
    if fold_y:
        row = 1 - lax.axis_index("gy")
        end = lax.dynamic_index_in_dim(latent[:, :, 0], 1 - core, 0, False)
        beside = lax.dynamic_index_in_dim(own_zed[:, :, 0], 1 - core, 0, False)
        both = jnp.stack([end, beside])
        corner = lax.dynamic_slice_in_dim(both, row, 1, axis=1)
        mine = [swap_chips(both, False)]
        corner, both = lax.optimization_barrier((corner, both))
        mine.append(swap_chips(corner, True))
    else:
        sides = [shift(latent[:, 1, 0], "gy", 0), shift(latent[:, 0, 0], "gy", 1)]
        side_zeds = [swap(part, "gz") for part in sides]
        layers = []
        for middle, outer in ((latent, sides), (own_zed, side_zeds)):
            parts = [outer[0][:, None], middle[:, :, 0], outer[1][:, None]]
            parts = [lax.dynamic_index_in_dim(part, 1 - core, 0, False) for part in parts]
            layers.append(jnp.concatenate(parts, axis=0))
        mine = [swap_chips(jnp.stack(layers), False)]

    ranked = call(
        functools.partial(ranks_kernel, sizes),
        "ranks",
        [VMEM] * 13,
        [
            ((11, width, width), BF16),
            ((48, width), BF16),
            ((2, 2, 1, slots), F32),
            ((width, particles), F32),
            ((width, particles), F32),
            ((8, particles), F32),
            ((neighbour_count, movers, width), BF16),
            ((1, neighbour_count * movers), I32),
            ((1, neighbour_count * movers), I32),
            ((width, movers), F32),
            ((width, movers), F32),
            ((width, movers), F32),
            ((8, movers), F32),
            ((4, width, 2 * slots), BF16),
            ((4, width, neighbour_count * slots), F32),
        ],
        [],
        (edge_latent, latent, own_zed, fill, owners, edge_weights, node_in, node_weights, decoder_weights, encoder_in, neighbours, positions, velocity),
        5_000_000_000,
    )
    mine, sides, ranked = lax.optimization_barrier((mine, sides, ranked))
    (
        weights,
        inward,
        alive,
        latent_t,
        node_pre,
        state,
        mover_edges,
        mover_place,
        mover_key,
        mover_near,
        mover_node_pre,
        mover_latent,
        mover_state,
        far_own,
        edge_pre,
    ) = ranked
    mine = jnp.concatenate(mine, axis=1)
    if fold_y:
        sides = [lax.dynamic_index_in_dim(sides[0][:, :, 0], lax.axis_index("gy"), 1, False)]
        packed = jnp.concatenate([mine.reshape(-1, slots, width), sides[0]], axis=0)
    else:
        packed = mine.reshape(-1, slots, width)
    packed = swap(packed, "gz")
    prepared = call(
        functools.partial(prepare_kernel, sizes),
        "prepare",
        [VMEM] * 7,
        [((rows, width, 2 * slots), BF16), ((width, neighbour_count * movers), F32)],
        [],
        (far_own, mine, weights, mover_edges, mover_place, mover_key, mover_near),
        5_000_000_000,
    )
    packed, prepared = lax.optimization_barrier((packed, prepared))
    cells = mine.shape[0] * mine.shape[1]
    if fold_y:
        side_zeds = [packed[cells:]]
    far_mine, mover_pre = prepared
    halo = [*sides, *side_zeds, packed[:cells].reshape(mine.shape), far_mine]

    far_rest, bucket = call(
        functools.partial(movers_kernel, sizes, len(sides)),
        "movers",
        [VMEM] * (len(halo) + 8),
        [((4 * rows - 4, width, 2 * slots), BF16), ((ROWS, movers), F32)],
        [pltpu.VMEM((width, neighbour_count * movers), BF16)],
        (
            *halo,
            weights,
            decoder_out,
            mover_pre,
            mover_place,
            mover_key,
            mover_node_pre,
            mover_latent,
            mover_state,
        ),
        3_000_000_000,
    )

    def edges(a):
        return call(
            functools.partial(edges_kernel, sizes, a),
            "edges",
            [VMEM] * 5,
            [((2, width, slots), BF16)],
            [pltpu.VMEM((2, width, neighbour_count * slots), BF16)],
            (alive, neighbours, far_rest, edge_pre, weights),
            4_000_000_000,
        )[0]

    zed = swap(bucket, "gz")
    if fold_y:
        sides = [swap(bucket, "gy")]
        zed, far_rest = lax.optimization_barrier((zed, far_rest))
        both = jnp.stack([bucket, zed])
        ends = [swap_chips(both, True), swap_chips(both, False)]
    else:
        both = jnp.stack([bucket, zed])
        sides = [shift(both, "gy", 0), shift(both, "gy", 1)]
        ends = [swap_chips(jnp.stack([both, *sides], axis=1), False)]
    first, second = edges(0), edges(1)
    sides, ends, first, second = lax.optimization_barrier((sides, ends, first, second))
    if fold_y:
        packed = swap(jnp.concatenate([*ends, sides[0][None]], axis=0), "gz")
    else:
        packed = swap(ends[0], "gz")
    state = call(
        nodes_kernel,
        "nodes",
        [VMEM] * 7,
        [((ROWS, particles), F32)],
        [],
        (first, second, node_pre, latent_t, state, weights, decoder_out),
        1_000_000_000,
    )[0]
    packed, state = lax.optimization_barrier((packed, state))
    return call(
        functools.partial(finish_kernel, sizes),
        "finish",
        [VMEM] * (len(sides) + len(ends) + 6),
        [
            (node_latent.shape, BF16),
            ((9,) + node_latent.shape[:4], F32),
            ((1, 1, 1, 26 * CAP, width), BF16),
            ((9, 1, 1, 1, 26 * CAP), F32),
        ],
        [],
        (state, zed, *sides, *ends, packed, spread, inward, encoder_weights),
        1_000_000_000,
    )


def solution(mesh):
    placed = (
        P(("group", "gx"), "gy", "gz", None, None),
        P(("group", "gx"), "gy", "gz", None, None, None),
        P(None, ("group", "gx"), "gy", "gz", None),
        P(None, ("group", "gx"), "gy", "gz", None),
        P(("group", "gx"), "gy", "gz"),
        P(("group", "gx"), "gy", "gz", None, None),
        P(("group", "gx"), "gy", "gz", None),
        P(),
        P(),
        P(),
        P(),
        P(),
        P(),
        P(),
    )
    return jax.shard_map(
        body,
        mesh=mesh,
        in_specs=placed,
        out_specs=(
            P(("group", "gx"), "gy", "gz", None, None),
            P(None, ("group", "gx"), "gy", "gz", None),
            P(("group", "gx"), "gy", "gz", None, None),
            P(None, ("group", "gx"), "gy", "gz", None),
        ),
        check_vma=False,
    )
```

```python
import functools
import itertools

import jax
import jax.numpy as jnp
from jax import lax
from jax.experimental import pallas as pl
from jax.experimental.pallas import tpu as pltpu
from jax.sharding import PartitionSpec as P

CAP = 8
F32 = jnp.float32
BF16 = jnp.bfloat16
I32 = jnp.int32
ROWS = 16
TILE = 256
CELLS = [(a, b) for a in range(2) for b in range(2)]
EDGE, NEAR, FAR, MIDDLE, FINAL, NODE_OLD, NODE_NEW, NODE_0, NODE_1, DECODE_0, DECODE_1 = range(11)

VMEM = pl.BlockSpec(memory_space=pltpu.VMEM)
SMEM = pl.BlockSpec(memory_space=pltpu.SMEM)
ANY = pl.BlockSpec(memory_space=pl.ANY)


def dot(left, right):
    return jnp.dot(left, right, preferred_element_type=F32)


def dot_nt(left, right):
    return lax.dot_general(left, right, (((1,), (1,)), ((), ())), preferred_element_type=F32)


def dot_tn(left, right):
    return lax.dot_general(left, right, (((0,), (0,)), ((), ())), preferred_element_type=F32)


def relu16(values):
    return jnp.maximum(values, 0.0).astype(BF16)


def norm(values, axis):
    scale = 1.0 / values.shape[axis]
    centred = values - jnp.sum(values, axis=axis, keepdims=True) * scale
    spread = jnp.sum(centred * centred, axis=axis, keepdims=True) * scale
    return centred * lax.rsqrt(spread + 1e-05)


def thirds(values):
    high = values.astype(BF16)
    rest = values - high.astype(F32)
    middle = rest.astype(BF16)
    low = (rest - middle.astype(F32)).astype(BF16)
    return jnp.concatenate([high, middle, low], axis=0)


def joined(values):
    rows = values.shape[0] // 3
    return values[:rows] + values[rows : 2 * rows] + values[2 * rows :]


def quotient(values, count):
    if count & (count - 1) == 0:
        return values >> (count.bit_length() - 1)
    return lax.div(values, jnp.full_like(values, count))


def flip(weights):
    return weights.astype(F32).T.astype(BF16)


def fetch(pairs, sems):
    copies = [pltpu.make_async_copy(src, dst, sems.at[i]) for i, (src, dst) in enumerate(pairs)]
    for copy in copies:
        copy.start()
    return copies


def encode(state, mask, inward, encoder_w, extent):
    width = state.shape[1]
    position = state[0:3]
    row = lax.broadcasted_iota(I32, (3, width), 0)
    size = jnp.where(row == 0, extent[0], jnp.where(row == 1, extent[1], extent[2]))
    features = jnp.concatenate(
        [
            state[3:9],
            jnp.clip(position, -1.0, 1.0),
            jnp.clip(size - position, -1.0, 1.0),
            jnp.zeros((4, width), F32),
        ],
        axis=0,
    )
    hidden = relu16(dot_tn(thirds(features), inward))
    hidden = relu16(dot(hidden, encoder_w[0]))
    column = jnp.broadcast_to(mask, (8, width)).T[:, 0:1]
    return (norm(dot(hidden, encoder_w[1]), 1) * column).astype(BF16)


def places(ids_low, ids_high, fold_y):
    plane = (ids_high * 43) >> 7
    ez = ids_high - plane * 3
    ey = plane & 3
    ex = plane >> 2
    if fold_y:
        row = jnp.where(ey == 1, 0, jnp.where(ey == 2, 1, 2))
    else:
        row = ey
    return ex * 4 + row, ids_low + jnp.where(ez == 1, 0, 128)


def pick(cells, place, key):
    width = cells[0][1].shape[0]
    chunk = 32
    window = jnp.concatenate(
        [ref[f : f + chunk] for f in range(0, width, chunk) for _, ref in cells], axis=0
    )
    key_rows = lax.broadcasted_iota(I32, (TILE, TILE), 0).astype(F32).astype(BF16)
    key = jnp.broadcast_to(key.astype(F32), (16, TILE)).astype(BF16)
    same = key_rows.reshape(TILE // 16, 16, TILE) == key[None]
    picker = jnp.where(same, jnp.ones((), BF16), jnp.zeros((), BF16)).reshape(TILE, TILE)
    found = dot(window, picker).reshape(width // chunk, len(cells), chunk // 8, 8, TILE)
    where = jnp.broadcast_to(place, (8, TILE))
    parts = []
    for f in range(width // chunk):
        part = jnp.zeros((chunk // 8, 8, TILE), F32)
        for i, (column, _) in enumerate(cells):
            part = jnp.where((where == column)[None], found[f, i], part)
        parts.append(part.reshape(chunk, TILE))
    return jnp.concatenate(parts, axis=0)


def messages(cells, place, key, pre, middle_t, final_t, hidden_ref):
    for tile in range(place.shape[1] // TILE):
        at = slice(tile * TILE, (tile + 1) * TILE)
        hidden_ref[:, at] = relu16(pre(tile) + pick(cells, place[:, at], key[:, at]))
    hidden = relu16(dot(middle_t, hidden_ref[...]))
    return norm(dot(final_t, hidden), 0)


class Window:
    def __init__(self, fold_y, own_ref=None, rest_ref=None):
        self.row_count = 3 if fold_y else 4
        self.own_rows = (0, 1) if fold_y else (1, 2)
        self.outer_rows = (2,) if fold_y else (0, 3)
        self.own_ref, self.rest_ref = own_ref, rest_ref

    def own_columns(self):
        return [(ex, row) for ex in (1, 2) for row in self.own_rows]

    def own(self, ex, row):
        return (ex - 1) * 2 + self.own_rows.index(row)

    def side(self, ex, row):
        count = len(self.outer_rows)
        return 2 * self.row_count + (ex - 1) * count + self.outer_rows.index(row)

    def cells(self, columns):
        found = []
        for ex, row in columns:
            if ex in (1, 2) and row in self.own_rows:
                ref = self.own_ref.at[self.own(ex, row)]
            elif ex in (1, 2):
                ref = self.rest_ref.at[self.side(ex, row)]
            else:
                ref = self.rest_ref.at[(0 if ex == 0 else self.row_count) + row]
            found.append((ex * 4 + row, ref))
        return found


def slot_sum(message, step):
    total = message[:, :step]
    for at in range(step, message.shape[1], step):
        total = total + message[:, at : at + step]
    return total


def advance(pre, aggregate, latent_t, weights_ref, decoder_out):
    pre = pre + dot(weights_ref[NODE_NEW], aggregate)
    hidden = relu16(dot(weights_ref[NODE_0], relu16(pre)))
    updated = (latent_t + norm(dot(weights_ref[NODE_1], hidden), 0)).astype(BF16)
    hidden = relu16(dot(weights_ref[DECODE_0], updated))
    hidden = relu16(dot(weights_ref[DECODE_1], hidden))
    return dot(decoder_out, hidden)


def moved(position, velocity, acceleration):
    new_velocity = velocity + acceleration
    return jnp.concatenate([position + new_velocity, new_velocity, velocity], axis=0)


def tables_kernel(fold_y, spread_ref):
    index_y = lax.axis_index("gy")
    index_z = lax.axis_index("gz")
    options_y = 2 if fold_y else 3
    line = lax.broadcasted_iota(I32, spread_ref.shape, 1)
    direction = line >> 3
    direction = direction + jnp.where(direction > 12, 1, 0)
    plane = (direction * 57) >> 9
    from_z = direction - 3 * ((direction * 43) >> 7) - 1
    from_y = ((direction * 43) >> 7) - 3 * plane - 1
    if fold_y:
        side_y = jnp.where(from_y == 0, 0, 1)
        valid = (from_y == 0) | (from_y == 1 - 2 * index_y)
    else:
        side_y = jnp.where(from_y < 0, 2, from_y)
        valid = from_y < 2
    side_z = jnp.where(from_z == 0, 0, 1)
    valid = valid & ((from_z == 0) | (from_z == 1 - 2 * index_z)) & (line < 26 * CAP)
    target = ((2 - plane) * options_y + side_y) * 2 + side_z
    spread_ref[...] = jnp.where(valid, target * CAP + (line & 7), -1)


def ranks_kernel(
    sizes,
    edge_ref,
    latent_ref,
    own_zed,
    fill_ref,
    owners_ref,
    edge_w_ref,
    node_in_ref,
    node_w_ref,
    decoder_w_ref,
    encoder_in_ref,
    neighbours_ref,
    positions_ref,
    velocity_ref,
    weights_ref,
    inward_ref,
    alive_ref,
    latent_t_ref,
    node_pre_ref,
    state_ref,
    mover_edge_ref,
    mover_place_ref,
    mover_key_ref,
    mover_near_ref,
    mover_node_pre_ref,
    mover_latent_ref,
    mover_state_ref,
    far_ref,
    pre_ref,
):
    count_x, count_y, count_z = sizes
    fold_y = count_y == 2
    index_x = lax.axis_index("gx")
    index_y = lax.axis_index("gy")
    index_z = lax.axis_index("gz")
    slots = owners_ref.shape[-1]
    width = node_in_ref.shape[-1]
    lane = lax.broadcasted_iota(I32, (1, slots), 1)
    for a, b in CELLS:
        fill = jnp.broadcast_to(fill_ref[a, :, b : b + 1], (1, slots))
        alive_ref[a, b] = jnp.where(lane < fill, 1.0, 0.0)

    owner = jnp.concatenate([owners_ref[a, b] for a, b in CELLS], axis=1)
    alive = jnp.concatenate([alive_ref[a, b] for a, b in CELLS], axis=1)
    own_block = (index_x * count_y + index_y) * count_z + index_z
    stays = jnp.where((alive > 0.5) & (owner == own_block), 1.0, 0.0)
    moving = jnp.where((alive > 0.5) & (owner != own_block), 1, 0)
    owner_x = quotient(owner, count_y * count_z)
    rest = owner - owner_x * (count_y * count_z)
    owner_y = quotient(rest, count_z)
    owner_z = rest - owner_y * count_z
    step_y = owner_y - index_y
    side_y = jnp.where(step_y == 0, 0, 1) if fold_y else jnp.where(step_y < 0, 1, 2 * step_y)
    options_y = 2 if fold_y else 3
    group = ((owner_x - index_x + 1) * options_y + side_y) * 2 + jnp.where(owner_z == index_z, 0, 1)
    group_rows = (3 * options_y * 2 + 15) // 16 * 16
    particles = owner.shape[1]
    member = jnp.where(
        (lax.broadcasted_iota(I32, (group_rows, particles), 0) == group) & (moving == 1), 1.0, 0.0
    )
    triangle = jnp.where(
        lax.broadcasted_iota(I32, (slots, slots), 0) <= lax.broadcasted_iota(I32, (slots, slots), 1),
        1.0,
        0.0,
    ).astype(BF16)
    counted = []
    before = jnp.zeros((group_rows, 1), F32)
    for i in range(4):
        inside = member[:, i * slots : (i + 1) * slots]
        counted.append(dot(inside.astype(BF16), triangle) + before)
        before = before + jnp.sum(inside, axis=1, keepdims=True)
    counted = jnp.concatenate(counted, axis=1)
    rank = (jnp.sum(counted * member, axis=0, keepdims=True) - 1.0).astype(I32)
    column = jnp.where(moving == 1, group * CAP + rank, -1)
    movers = mover_state_ref.shape[1]
    placer = jnp.where(
        lax.broadcasted_iota(I32, (movers, particles), 0) == column, 1.0, 0.0
    ).astype(BF16)

    for i in range(5):
        weights_ref[i] = flip(edge_w_ref[i])
    weights_ref[NODE_OLD] = flip(node_in_ref[:width])
    weights_ref[NODE_NEW] = flip(node_in_ref[width:])
    for i in range(2):
        weights_ref[NODE_0 + i] = flip(node_w_ref[i])
        weights_ref[DECODE_0 + i] = flip(decoder_w_ref[i])
    inward = jnp.concatenate([encoder_in_ref[...].astype(F32), jnp.zeros((4, width), F32)], axis=0)
    inward = inward.astype(BF16)
    inward_ref[...] = jnp.concatenate([inward, inward, inward], axis=0)

    latent = jnp.concatenate([latent_ref[a, b, 0] for a, b in CELLS], axis=0)
    latent_t_ref[...] = latent.astype(F32).T
    node_pre_ref[...] = dot_nt(weights_ref[NODE_OLD], latent)

    def flat(ref, i):
        return jnp.concatenate([ref[i, a, b] for a, b in CELLS], axis=1)

    state = [flat(positions_ref, i) for i in range(3)] + [flat(velocity_ref, i) for i in range(3)]
    state_ref[...] = jnp.concatenate(state + [stays, jnp.zeros_like(stays)], axis=0)

    mover_latent = dot(placer, latent).astype(BF16)
    mover_latent_ref[...] = mover_latent.astype(F32).T
    mover_node_pre_ref[...] = dot_nt(weights_ref[NODE_OLD], mover_latent)
    mover_near_ref[...] = dot_nt(weights_ref[NEAR], mover_latent)
    state = jnp.concatenate(state + [moving.astype(F32), jnp.zeros_like(stays)], axis=0)
    mover_state_ref[...] = joined(dot_nt(thirds(state), placer))
    neighbour_count = edge_ref.shape[3]
    ids = jnp.concatenate(
        [
            jnp.concatenate([neighbours_ref[a, b, k] for a, b in CELLS], axis=1)
            for k in range(neighbour_count)
        ],
        axis=0,
    )
    ids = jnp.concatenate([ids & 127, ids >> 7, jnp.zeros((8, particles), I32)], axis=0)
    ids = dot_nt(ids.astype(F32).astype(BF16), placer).astype(I32)
    place, key = places(ids[:neighbour_count], ids[neighbour_count : 2 * neighbour_count], fold_y)
    mover_place_ref[...] = jnp.concatenate([place[k : k + 1] for k in range(neighbour_count)], axis=1)
    mover_key_ref[...] = jnp.concatenate([key[k : k + 1] for k in range(neighbour_count)], axis=1)

    window = Window(fold_y, far_ref)
    for (ex, row), (a, b) in zip(window.own_columns(), CELLS):
        pair = jnp.concatenate([latent_ref[a, b, 0], own_zed[a, b, 0]], axis=0)
        far_ref[window.own(ex, row)] = dot_nt(weights_ref[FAR], pair).astype(BF16)
    cells = window.cells(window.own_columns())
    for a, bt in CELLS:
        b = (index_y if bt == 0 else 1 - index_y) if fold_y else bt
        ids = jnp.concatenate([neighbours_ref[a, b, k] for k in range(neighbour_count)], axis=1)
        place, key = places(ids & 127, ids >> 7, fold_y)
        near = dot_nt(weights_ref[NEAR], latent_ref[a, b, 0])
        near = jnp.concatenate([near, near], axis=1)
        for tile in range(ids.shape[1] // TILE):
            at = slice(tile * TILE, (tile + 1) * TILE)
            edges = [edge_ref[a, b, 0, k] for k in (2 * tile, 2 * tile + 1)]
            pre_ref[2 * a + bt, :, at] = (
                dot_nt(weights_ref[EDGE], jnp.concatenate(edges, axis=0))
                + near
                + pick(cells, place[:, at], key[:, at])
            )
    for k in range(neighbour_count):
        rows = jnp.concatenate([edge_ref[a, b, 0, k] for a, b in CELLS], axis=0)
        mover_edge_ref[k] = dot(placer, rows).astype(BF16)


def prepare_kernel(
    sizes,
    far_ref,
    mine_ref,
    weights_ref,
    edge_ref,
    place_ref,
    key_ref,
    near_ref,
    far_mine_ref,
    pre_ref,
):
    window = Window(sizes[1] == 2, far_ref)
    core = lax.axis_index("gz")
    far_t = weights_ref[FAR]
    cells = window.cells(window.own_columns())
    for row in range(window.row_count):
        pair = jnp.concatenate([mine_ref[1, row], mine_ref[0, row]], axis=0)
        far_mine_ref[row] = dot_nt(far_t, pair).astype(BF16)
        cells.append((12 * (1 - core) + row, far_mine_ref.at[row]))
    neighbour_count, movers = edge_ref.shape[:2]
    step = TILE // movers
    near = jnp.concatenate([near_ref[...]] * step, axis=1)
    for tile in range(neighbour_count // step):
        edges = jnp.concatenate([edge_ref[k] for k in range(tile * step, (tile + 1) * step)], axis=0)
        at = slice(tile * TILE, (tile + 1) * TILE)
        pre_ref[:, at] = (
            dot_nt(weights_ref[EDGE], edges) + near + pick(cells, place_ref[:, at], key_ref[:, at])
        )


def movers_kernel(
    sizes,
    side_count,
    *refs,
):
    fold_y = sizes[1] == 2
    side_refs, refs = refs[:side_count], refs[side_count:]
    side_zeds, refs = refs[:side_count], refs[side_count:]
    other_ref, far_mine_ref, refs = refs[0], refs[1], refs[2:]
    (
        weights_ref,
        decoder_out_ref,
        pre_ref,
        place_ref,
        key_ref,
        node_pre_ref,
        latent_t_ref,
        state_ref,
        far_ref,
        bucket_ref,
        hidden_ref,
    ) = refs
    window = Window(fold_y, None, far_ref)
    row_count = window.row_count
    core = lax.axis_index("gz")
    far_t = weights_ref[FAR]

    def far(at, here, beside):
        pair = jnp.concatenate([here, beside], axis=0)
        far_ref[at] = dot_nt(far_t, pair).astype(BF16)

    for row in range(row_count):
        far(core * row_count + row, other_ref[0, row], other_ref[1, row])
    for side, row in enumerate(window.outer_rows):
        for ex in (1, 2):
            far(window.side(ex, row), side_refs[side][ex - 1], side_zeds[side][ex - 1])

    movers = state_ref.shape[1]
    for row in range(row_count):
        far_ref[(1 - core) * row_count + row] = far_mine_ref[row]
    cells = [(12 * core + row, far_ref.at[core * row_count + row]) for row in range(row_count)]
    cells += window.cells([(ex, row) for ex in (1, 2) for row in window.outer_rows])
    message = messages(
        cells,
        place_ref[...],
        key_ref[...],
        lambda tile: pre_ref[:, tile * TILE : (tile + 1) * TILE],
        weights_ref[MIDDLE],
        weights_ref[FINAL],
        hidden_ref,
    )
    aggregate = slot_sum(message, movers).astype(BF16)
    acceleration = advance(
        node_pre_ref[...], aggregate, latent_t_ref[...], weights_ref, decoder_out_ref[...]
    )
    mask = state_ref[6:7]
    state = moved(state_ref[0:3], state_ref[3:6], acceleration) * mask
    bucket_ref[...] = jnp.concatenate([state, mask, jnp.zeros((ROWS - 10, movers), F32)], axis=0)


def edges_kernel(
    sizes,
    alive_ref,
    neighbours_ref,
    far_ref,
    pre_ref,
    weights_ref,
    total_ref,
    hidden_ref,
):
    fold_y = sizes[1] == 2
    window = Window(fold_y, None, far_ref)
    index_y = lax.axis_index("gy")
    slots = alive_ref.shape[-1]
    neighbour_count = neighbours_ref.shape[2]
    for a, bt in CELLS:
        if fold_y:
            b = index_y if bt == 0 else 1 - index_y
            rows = (0, 1) if bt == 0 else (0, 1, 2)
        else:
            b = bt
            rows = (bt, bt + 1, bt + 2)
        columns = [(ex, row) for ex in range(a, a + 3) for row in rows]
        columns = [column for column in columns if column not in window.own_columns()]
        ids = jnp.concatenate([neighbours_ref[a, b, k] for k in range(neighbour_count)], axis=1)
        place, key = places(ids & 127, ids >> 7, fold_y)
        message = messages(
            window.cells(columns),
            place,
            key,
            lambda tile, i=2 * a + bt: pre_ref[i, :, tile * TILE : (tile + 1) * TILE],
            weights_ref[MIDDLE],
            weights_ref[FINAL],
            hidden_ref.at[2 * a + bt],
        )
        total = jnp.where(alive_ref[a, b] > 0.5, slot_sum(message, slots), 0.0)
        total_ref[2 * a + b] = total.astype(BF16)


def nodes_kernel(
    total_ref,
    node_pre_ref,
    latent_t_ref,
    state_ref,
    weights_ref,
    decoder_out_ref,
    moved_ref,
):
    aggregate = jnp.concatenate([total_ref[i] for i in range(4)], axis=1)
    acceleration = advance(
        node_pre_ref[...], aggregate, latent_t_ref[...], weights_ref, decoder_out_ref[...]
    )
    state = moved(state_ref[0:3], state_ref[3:6], acceleration)
    moved_ref[...] = jnp.concatenate(
        [state, state_ref[6:7], jnp.zeros((ROWS - 10, state.shape[1]), F32)], axis=0
    )


def finish_kernel(sizes, moved_ref, zed_ref, *refs):
    count_x, count_y, count_z = sizes
    fold_y = count_y == 2
    options_y = 2 if fold_y else 3
    side_refs, refs = refs[: options_y - 1], refs[options_y - 1 :]
    if fold_y:
        cross_ref, end_ref, *refs = refs
    else:
        end_ref, *refs = refs
    (
        packed_ref,
        spread_ref,
        inward_ref,
        encoder_w_ref,
        kept_latent_ref,
        kept_state_ref,
        arrived_latent_ref,
        arrived_state_ref,
    ) = refs
    core = lax.axis_index("gz")

    def tile(source_x, from_y, from_z):
        if source_x == 0:
            if from_y == 0:
                return zed_ref[...]
            if fold_y:
                return packed_ref[4] if from_z else side_refs[0][...]
            return side_refs[from_y - 1][from_z]
        if fold_y:
            mine = (cross_ref if from_y else end_ref)[1 - from_z]
            other = packed_ref[(0 if from_y else 2) + from_z]
        else:
            mine = end_ref[1 - from_z, from_y]
            other = packed_ref[from_z, from_y]
        return jnp.where(core == (1 - source_x) // 2, mine, other)

    extent = (2.0 * count_x, 2.0 * count_y, 1.0 * count_z)
    slots = kept_latent_ref.shape[-2]
    stays = moved_ref[9:10]
    kept = moved_ref[:9] * stays
    latents = encode(moved_ref[:9], stays, inward_ref[...], encoder_w_ref[...], extent)
    for i, (a, b) in enumerate(CELLS):
        kept_latent_ref[a, b, 0] = latents[i * slots : (i + 1) * slots]
        for j in range(9):
            kept_state_ref[j, a, b] = kept[j : j + 1, i * slots : (i + 1) * slots]
    fold_y = count_y == 2
    index_x = lax.axis_index("gx")
    lanes = zed_ref.shape[-1]
    group = lax.broadcasted_iota(I32, (ROWS, lanes), 1) >> 3
    found = jnp.zeros((ROWS, lanes), F32)
    for source_x in (-1, 0, 1):
        for from_y in range(options_y):
            for from_z in range(2):
                if source_x == 0 and from_y == 0 and from_z == 0:
                    continue
                side_y = from_y if fold_y or from_y == 0 else 3 - from_y
                there = group == ((1 - source_x) * options_y + side_y) * 2 + from_z
                if source_x == -1:
                    there = there & (index_x > 0)
                elif source_x == 1:
                    there = there & (index_x < count_x - 1)
                found = jnp.where(there, tile(source_x, from_y, from_z), found)
    halves = []
    for at in range(0, spread_ref.shape[1], 128):
        lane = jnp.broadcast_to(spread_ref[0:1, at : at + 128], (ROWS, 128))
        half = jnp.zeros((ROWS, 128), F32)
        for base in range(0, lanes, 128):
            index = jnp.clip(lane - base, 0, 127)
            there = (lane >= base) & (lane < base + 128)
            part = jnp.take_along_axis(found[:, base : base + 128], index, axis=1)
            half = jnp.where(there, part, half)
        halves.append(half)
    arrived = jnp.concatenate(halves, axis=1)[:, : 26 * CAP]
    for j in range(9):
        arrived_state_ref[j, 0, 0] = arrived[j : j + 1]
    arrived_latent_ref[0, 0, 0] = encode(
        arrived[:9], arrived[9:10], inward_ref[...], encoder_w_ref[...], extent
    )


def swap(values, axis):
    return lax.ppermute(values, axis, [(0, 1), (1, 0)])


def shift(values, axis, way):
    pairs = [(i, i + 1) for i in range(lax.axis_size(axis) - 1)]
    return lax.ppermute(values, axis, [(j, i) for i, j in pairs] if way else pairs)


def swap_chips(values, cross):
    axes = ("group", "gx", "gy", "gz")
    counts = tuple(lax.axis_size(axis) for axis in axes)

    def number(place):
        total = 0
        for count, index in zip(counts, place):
            total = total * count + index
        return total

    pairs = []
    for place in itertools.product(*(range(count) for count in counts)):
        group, x, y, z = place
        to_x = x + 1 - 2 * z
        if 0 <= to_x < counts[1]:
            to = (group, to_x, y ^ 1 if cross else y, 1 - z)
        else:
            to = (group ^ 1, x, y, z)
        pairs.append((number(place), number(to)))
    return lax.ppermute(values, axes, pairs)


def call(kernel, name, in_specs, outs, scratch, operands, flops):
    return pl.pallas_call(
        kernel,
        out_shape=tuple(jax.ShapeDtypeStruct(shape, kind) for shape, kind in outs),
        in_specs=in_specs,
        out_specs=tuple(VMEM for _ in outs),
        scratch_shapes=scratch,
        compiler_params=pltpu.CompilerParams(vmem_limit_bytes=32 * 1024 * 1024),
        cost_estimate=pl.CostEstimate(flops=flops, bytes_accessed=0, transcendentals=0),
        name=name,
    )(*operands)


def in_hbm(array):
    return pltpu.with_memory_space_constraint(array, pltpu.HBM)


def like(array):
    return pltpu.VMEM(array.shape, array.dtype)


def body(
    node_latent,
    edge_latent,
    positions,
    velocity,
    fill,
    neighbours,
    owners,
    edge_weights,
    node_in,
    node_weights,
    decoder_weights,
    decoder_out,
    encoder_in,
    encoder_weights,
):
    sizes = tuple(lax.axis_size(axis) for axis in ("gx", "gy", "gz"))
    fold_y = sizes[1] == 2
    slots, width = node_latent.shape[-2:]
    neighbour_count = neighbours.shape[3]
    particles = 4 * slots
    options_y = 2 if fold_y else 3
    movers = (3 * options_y * 2 * CAP + 127) // 128 * 128
    rows = 3 if fold_y else 4
    fill = jnp.transpose(fill, (0, 2, 1))
    neighbours = neighbours.reshape(2, 2, neighbour_count, 1, slots)

    own_zed = swap(node_latent, "gz")
    if fold_y:
        sides = [swap(node_latent, "gy")]
    spread = call(
        functools.partial(tables_kernel, fold_y),
        "tables",
        [],
        [((8, 256), I32)],
        [],
        [],
        5_000_000_000,
    )[0]
    latent, spread = lax.optimization_barrier((node_latent, spread))
    core = lax.axis_index("gz")
    if fold_y:
        row = 1 - lax.axis_index("gy")
        end = lax.dynamic_index_in_dim(latent[:, :, 0], 1 - core, 0, False)
        beside = lax.dynamic_index_in_dim(own_zed[:, :, 0], 1 - core, 0, False)
        both = jnp.stack([end, beside])
        corner = lax.dynamic_slice_in_dim(both, row, 1, axis=1)
        mine = [swap_chips(both, False)]
        corner, both = lax.optimization_barrier((corner, both))
        mine.append(swap_chips(corner, True))
    else:
        sides = [shift(latent[:, 1, 0], "gy", 0), shift(latent[:, 0, 0], "gy", 1)]
        side_zeds = [swap(part, "gz") for part in sides]
        layers = []
        for middle, outer in ((latent, sides), (own_zed, side_zeds)):
            parts = [outer[0][:, None], middle[:, :, 0], outer[1][:, None]]
            parts = [lax.dynamic_index_in_dim(part, 1 - core, 0, False) for part in parts]
            layers.append(jnp.concatenate(parts, axis=0))
        mine = [swap_chips(jnp.stack(layers), False)]

    ranked = call(
        functools.partial(ranks_kernel, sizes),
        "ranks",
        [VMEM] * 13,
        [
            ((11, width, width), BF16),
            ((48, width), BF16),
            ((2, 2, 1, slots), F32),
            ((width, particles), F32),
            ((width, particles), F32),
            ((8, particles), F32),
            ((neighbour_count, movers, width), BF16),
            ((1, neighbour_count * movers), I32),
            ((1, neighbour_count * movers), I32),
            ((width, movers), F32),
            ((width, movers), F32),
            ((width, movers), F32),
            ((8, movers), F32),
            ((4, width, 2 * slots), BF16),
            ((4, width, neighbour_count * slots), F32),
        ],
        [],
        (edge_latent, latent, own_zed, fill, owners, edge_weights, node_in, node_weights, decoder_weights, encoder_in, neighbours, positions, velocity),
        5_000_000_000,
    )
    mine, sides, ranked = lax.optimization_barrier((mine, sides, ranked))
    (
        weights,
        inward,
        alive,
        latent_t,
        node_pre,
        state,
        mover_edges,
        mover_place,
        mover_key,
        mover_near,
        mover_node_pre,
        mover_latent,
        mover_state,
        far_own,
        edge_pre,
    ) = ranked
    mine = jnp.concatenate(mine, axis=1)
    if fold_y:
        sides = [lax.dynamic_index_in_dim(sides[0][:, :, 0], lax.axis_index("gy"), 1, False)]
        packed = jnp.concatenate([mine.reshape(-1, slots, width), sides[0]], axis=0)
    else:
        packed = mine.reshape(-1, slots, width)
    packed = swap(packed, "gz")
    prepared = call(
        functools.partial(prepare_kernel, sizes),
        "prepare",
        [VMEM] * 7,
        [((rows, width, 2 * slots), BF16), ((width, neighbour_count * movers), F32)],
        [],
        (far_own, mine, weights, mover_edges, mover_place, mover_key, mover_near),
        5_000_000_000,
    )
    packed, prepared = lax.optimization_barrier((packed, prepared))
    cells = mine.shape[0] * mine.shape[1]
    if fold_y:
        side_zeds = [packed[cells:]]
    far_mine, mover_pre = prepared
    halo = [*sides, *side_zeds, packed[:cells].reshape(mine.shape), far_mine]

    far_rest, bucket = call(
        functools.partial(movers_kernel, sizes, len(sides)),
        "movers",
        [VMEM] * (len(halo) + 8),
        [((4 * rows - 4, width, 2 * slots), BF16), ((ROWS, movers), F32)],
        [pltpu.VMEM((width, neighbour_count * movers), BF16)],
        (
            *halo,
            weights,
            decoder_out,
            mover_pre,
            mover_place,
            mover_key,
            mover_node_pre,
            mover_latent,
            mover_state,
        ),
        3_000_000_000,
    )

    zed = swap(bucket, "gz")
    if fold_y:
        sides = [swap(bucket, "gy")]
        zed, far_rest = lax.optimization_barrier((zed, far_rest))
        both = jnp.stack([bucket, zed])
        ends = [swap_chips(both, True), swap_chips(both, False)]
    else:
        both = jnp.stack([bucket, zed])
        sides = [shift(both, "gy", 0), shift(both, "gy", 1)]
        ends = [swap_chips(jnp.stack([both, *sides], axis=1), False)]
    total = call(
        functools.partial(edges_kernel, sizes),
        "edges",
        [VMEM] * 5,
        [((4, width, slots), BF16)],
        [pltpu.VMEM((4, width, neighbour_count * slots), BF16)],
        (alive, neighbours, far_rest, edge_pre, weights),
        8_000_000_000,
    )[0]
    sides, ends, total = lax.optimization_barrier((sides, ends, total))
    if fold_y:
        packed = swap(jnp.concatenate([*ends, sides[0][None]], axis=0), "gz")
    else:
        packed = swap(ends[0], "gz")
    state = call(
        nodes_kernel,
        "nodes",
        [VMEM] * 6,
        [((ROWS, particles), F32)],
        [],
        (total, node_pre, latent_t, state, weights, decoder_out),
        1_000_000_000,
    )[0]
    packed, state = lax.optimization_barrier((packed, state))
    return call(
        functools.partial(finish_kernel, sizes),
        "finish",
        [VMEM] * (len(sides) + len(ends) + 6),
        [
            (node_latent.shape, BF16),
            ((9,) + node_latent.shape[:4], F32),
            ((1, 1, 1, 26 * CAP, width), BF16),
            ((9, 1, 1, 1, 26 * CAP), F32),
        ],
        [],
        (state, zed, *sides, *ends, packed, spread, inward, encoder_weights),
        1_000_000_000,
    )


def solution(mesh):
    placed = (
        P(("group", "gx"), "gy", "gz", None, None),
        P(("group", "gx"), "gy", "gz", None, None, None),
        P(None, ("group", "gx"), "gy", "gz", None),
        P(None, ("group", "gx"), "gy", "gz", None),
        P(("group", "gx"), "gy", "gz"),
        P(("group", "gx"), "gy", "gz", None, None),
        P(("group", "gx"), "gy", "gz", None),
        P(),
        P(),
        P(),
        P(),
        P(),
        P(),
        P(),
    )
    return jax.shard_map(
        body,
        mesh=mesh,
        in_specs=placed,
        out_specs=(
            P(("group", "gx"), "gy", "gz", None, None),
            P(None, ("group", "gx"), "gy", "gz", None),
            P(("group", "gx"), "gy", "gz", None, None),
            P(None, ("group", "gx"), "gy", "gz", None),
        ),
        check_vma=False,
    )
```

```python
import functools
import itertools

import jax
import jax.numpy as jnp
from jax import lax
from jax.experimental import pallas as pl
from jax.experimental.pallas import tpu as pltpu
from jax.sharding import PartitionSpec as P

CAP = 8
F32 = jnp.float32
BF16 = jnp.bfloat16
I32 = jnp.int32
ROWS = 16
TILE = 256
CELLS = [(a, b) for a in range(2) for b in range(2)]
EDGE, NEAR, FAR, MIDDLE, FINAL, NODE_OLD, NODE_NEW, NODE_0, NODE_1, DECODE_0, DECODE_1 = range(11)

VMEM = pl.BlockSpec(memory_space=pltpu.VMEM)
SMEM = pl.BlockSpec(memory_space=pltpu.SMEM)
ANY = pl.BlockSpec(memory_space=pl.ANY)


def dot(left, right):
    return jnp.dot(left, right, preferred_element_type=F32)


def dot_nt(left, right):
    return lax.dot_general(left, right, (((1,), (1,)), ((), ())), preferred_element_type=F32)


def dot_tn(left, right):
    return lax.dot_general(left, right, (((0,), (0,)), ((), ())), preferred_element_type=F32)


def relu16(values):
    return jnp.maximum(values, 0.0).astype(BF16)


def norm(values, axis):
    scale = 1.0 / values.shape[axis]
    centred = values - jnp.sum(values, axis=axis, keepdims=True) * scale
    spread = jnp.sum(centred * centred, axis=axis, keepdims=True) * scale
    return centred * lax.rsqrt(spread + 1e-05)


def thirds(values):
    high = values.astype(BF16)
    rest = values - high.astype(F32)
    middle = rest.astype(BF16)
    low = (rest - middle.astype(F32)).astype(BF16)
    return jnp.concatenate([high, middle, low], axis=0)


def joined(values):
    rows = values.shape[0] // 3
    return values[:rows] + values[rows : 2 * rows] + values[2 * rows :]


def quotient(values, count):
    if count & (count - 1) == 0:
        return values >> (count.bit_length() - 1)
    return lax.div(values, jnp.full_like(values, count))


def flip(weights):
    return weights.astype(F32).T.astype(BF16)


def fetch(pairs, sems):
    copies = [pltpu.make_async_copy(src, dst, sems.at[i]) for i, (src, dst) in enumerate(pairs)]
    for copy in copies:
        copy.start()
    return copies


def encode(state, mask, inward, encoder_w, extent):
    width = state.shape[1]
    position = state[0:3]
    row = lax.broadcasted_iota(I32, (3, width), 0)
    size = jnp.where(row == 0, extent[0], jnp.where(row == 1, extent[1], extent[2]))
    features = jnp.concatenate(
        [
            state[3:9],
            jnp.clip(position, -1.0, 1.0),
            jnp.clip(size - position, -1.0, 1.0),
            jnp.zeros((4, width), F32),
        ],
        axis=0,
    )
    hidden = relu16(dot_tn(thirds(features), inward))
    hidden = relu16(dot(hidden, encoder_w[0]))
    column = jnp.broadcast_to(mask, (8, width)).T[:, 0:1]
    return (norm(dot(hidden, encoder_w[1]), 1) * column).astype(BF16)


def places(ids_low, ids_high, fold_y):
    plane = (ids_high * 43) >> 7
    ez = ids_high - plane * 3
    ey = plane & 3
    ex = plane >> 2
    if fold_y:
        row = jnp.where(ey == 1, 0, jnp.where(ey == 2, 1, 2))
    else:
        row = ey
    return ex * 4 + row, ids_low + jnp.where(ez == 1, 0, 128)


def pick(cells, place, key):
    width = cells[0][1].shape[0]
    chunk = 32
    window = jnp.concatenate(
        [ref[f : f + chunk] for f in range(0, width, chunk) for _, ref in cells], axis=0
    )
    key_rows = lax.broadcasted_iota(I32, (TILE, TILE), 0).astype(F32).astype(BF16)
    key = jnp.broadcast_to(key.astype(F32), (16, TILE)).astype(BF16)
    same = key_rows.reshape(TILE // 16, 16, TILE) == key[None]
    picker = jnp.where(same, jnp.ones((), BF16), jnp.zeros((), BF16)).reshape(TILE, TILE)
    found = dot(window, picker).reshape(width // chunk, len(cells), chunk // 8, 8, TILE)
    where = jnp.broadcast_to(place, (8, TILE))
    parts = []
    for f in range(width // chunk):
        part = jnp.zeros((chunk // 8, 8, TILE), F32)
        for i, (column, _) in enumerate(cells):
            part = jnp.where((where == column)[None], found[f, i], part)
        parts.append(part.reshape(chunk, TILE))
    return jnp.concatenate(parts, axis=0)


def messages(cells, place, key, pre, middle_t, final_t, hidden_ref):
    for tile in range(place.shape[1] // TILE):
        at = slice(tile * TILE, (tile + 1) * TILE)
        terms = pre(tile)
        if cells:
            terms = terms + pick(cells, place[:, at], key[:, at])
        hidden_ref[:, at] = relu16(terms)
    hidden = relu16(dot(middle_t, hidden_ref[...]))
    return norm(dot(final_t, hidden), 0)


class Window:
    def __init__(self, fold_y, own_ref=None, rest_ref=None):
        self.row_count = 3 if fold_y else 4
        self.own_rows = (0, 1) if fold_y else (1, 2)
        self.outer_rows = (2,) if fold_y else (0, 3)
        self.own_ref, self.rest_ref = own_ref, rest_ref

    def rows(self, bt):
        if self.row_count == 3:
            return (0, 1, 2)[: 2 + bt]
        return (bt, bt + 1, bt + 2)

    def own_columns(self):
        return [(ex, row) for ex in (1, 2) for row in self.own_rows]

    def own(self, ex, row):
        return (ex - 1) * 2 + self.own_rows.index(row)

    def side(self, ex, row):
        count = len(self.outer_rows)
        return 2 * self.row_count + (ex - 1) * count + self.outer_rows.index(row)

    def cells(self, columns):
        found = []
        for ex, row in columns:
            if ex in (1, 2) and row in self.own_rows:
                ref = self.own_ref.at[self.own(ex, row)]
            elif ex in (1, 2):
                ref = self.rest_ref.at[self.side(ex, row)]
            else:
                ref = self.rest_ref.at[(0 if ex == 0 else self.row_count) + row]
            found.append((ex * 4 + row, ref))
        return found


def slot_sum(message, step):
    total = message[:, :step]
    for at in range(step, message.shape[1], step):
        total = total + message[:, at : at + step]
    return total


def advance(pre, aggregate, latent_t, weights_ref, decoder_out):
    pre = pre + dot(weights_ref[NODE_NEW], aggregate)
    hidden = relu16(dot(weights_ref[NODE_0], relu16(pre)))
    updated = (latent_t + norm(dot(weights_ref[NODE_1], hidden), 0)).astype(BF16)
    hidden = relu16(dot(weights_ref[DECODE_0], updated))
    hidden = relu16(dot(weights_ref[DECODE_1], hidden))
    return dot(decoder_out, hidden)


def moved(position, velocity, acceleration):
    new_velocity = velocity + acceleration
    return jnp.concatenate([position + new_velocity, new_velocity, velocity], axis=0)


def tables_kernel(fold_y, spread_ref):
    index_y = lax.axis_index("gy")
    index_z = lax.axis_index("gz")
    options_y = 2 if fold_y else 3
    line = lax.broadcasted_iota(I32, spread_ref.shape, 1)
    direction = line >> 3
    direction = direction + jnp.where(direction > 12, 1, 0)
    plane = (direction * 57) >> 9
    from_z = direction - 3 * ((direction * 43) >> 7) - 1
    from_y = ((direction * 43) >> 7) - 3 * plane - 1
    if fold_y:
        side_y = jnp.where(from_y == 0, 0, 1)
        valid = (from_y == 0) | (from_y == 1 - 2 * index_y)
    else:
        side_y = jnp.where(from_y < 0, 2, from_y)
        valid = from_y < 2
    side_z = jnp.where(from_z == 0, 0, 1)
    valid = valid & ((from_z == 0) | (from_z == 1 - 2 * index_z)) & (line < 26 * CAP)
    target = ((2 - plane) * options_y + side_y) * 2 + side_z
    spread_ref[...] = jnp.where(valid, target * CAP + (line & 7), -1)


def ranks_kernel(
    sizes,
    edge_ref,
    latent_ref,
    own_zed,
    fill_ref,
    owners_ref,
    edge_w_ref,
    node_in_ref,
    node_w_ref,
    decoder_w_ref,
    encoder_in_ref,
    neighbours_ref,
    positions_ref,
    velocity_ref,
    weights_ref,
    inward_ref,
    alive_ref,
    latent_t_ref,
    node_pre_ref,
    state_ref,
    mover_edge_ref,
    mover_place_ref,
    mover_key_ref,
    mover_near_ref,
    mover_node_pre_ref,
    mover_latent_ref,
    mover_state_ref,
    far_ref,
    pre_ref,
):
    count_x, count_y, count_z = sizes
    fold_y = count_y == 2
    index_x = lax.axis_index("gx")
    index_y = lax.axis_index("gy")
    index_z = lax.axis_index("gz")
    slots = owners_ref.shape[-1]
    width = node_in_ref.shape[-1]
    lane = lax.broadcasted_iota(I32, (1, slots), 1)
    for a, b in CELLS:
        fill = jnp.broadcast_to(fill_ref[a, :, b : b + 1], (1, slots))
        alive_ref[a, b] = jnp.where(lane < fill, 1.0, 0.0)

    owner = jnp.concatenate([owners_ref[a, b] for a, b in CELLS], axis=1)
    alive = jnp.concatenate([alive_ref[a, b] for a, b in CELLS], axis=1)
    own_block = (index_x * count_y + index_y) * count_z + index_z
    stays = jnp.where((alive > 0.5) & (owner == own_block), 1.0, 0.0)
    moving = jnp.where((alive > 0.5) & (owner != own_block), 1, 0)
    owner_x = quotient(owner, count_y * count_z)
    rest = owner - owner_x * (count_y * count_z)
    owner_y = quotient(rest, count_z)
    owner_z = rest - owner_y * count_z
    step_y = owner_y - index_y
    side_y = jnp.where(step_y == 0, 0, 1) if fold_y else jnp.where(step_y < 0, 1, 2 * step_y)
    options_y = 2 if fold_y else 3
    group = ((owner_x - index_x + 1) * options_y + side_y) * 2 + jnp.where(owner_z == index_z, 0, 1)
    group_rows = (3 * options_y * 2 + 15) // 16 * 16
    particles = owner.shape[1]
    member = jnp.where(
        (lax.broadcasted_iota(I32, (group_rows, particles), 0) == group) & (moving == 1), 1.0, 0.0
    )
    triangle = jnp.where(
        lax.broadcasted_iota(I32, (slots, slots), 0) <= lax.broadcasted_iota(I32, (slots, slots), 1),
        1.0,
        0.0,
    ).astype(BF16)
    counted = []
    before = jnp.zeros((group_rows, 1), F32)
    for i in range(4):
        inside = member[:, i * slots : (i + 1) * slots]
        counted.append(dot(inside.astype(BF16), triangle) + before)
        before = before + jnp.sum(inside, axis=1, keepdims=True)
    counted = jnp.concatenate(counted, axis=1)
    rank = (jnp.sum(counted * member, axis=0, keepdims=True) - 1.0).astype(I32)
    column = jnp.where(moving == 1, group * CAP + rank, -1)
    movers = mover_state_ref.shape[1]
    placer = jnp.where(
        lax.broadcasted_iota(I32, (movers, particles), 0) == column, 1.0, 0.0
    ).astype(BF16)

    for i in range(5):
        weights_ref[i] = flip(edge_w_ref[i])
    weights_ref[NODE_OLD] = flip(node_in_ref[:width])
    weights_ref[NODE_NEW] = flip(node_in_ref[width:])
    for i in range(2):
        weights_ref[NODE_0 + i] = flip(node_w_ref[i])
        weights_ref[DECODE_0 + i] = flip(decoder_w_ref[i])
    inward = jnp.concatenate([encoder_in_ref[...].astype(F32), jnp.zeros((4, width), F32)], axis=0)
    inward = inward.astype(BF16)
    inward_ref[...] = jnp.concatenate([inward, inward, inward], axis=0)

    latent = jnp.concatenate([latent_ref[a, b, 0] for a, b in CELLS], axis=0)
    latent_t_ref[...] = latent.astype(F32).T
    node_pre_ref[...] = dot_nt(weights_ref[NODE_OLD], latent)

    def flat(ref, i):
        return jnp.concatenate([ref[i, a, b] for a, b in CELLS], axis=1)

    state = [flat(positions_ref, i) for i in range(3)] + [flat(velocity_ref, i) for i in range(3)]
    state_ref[...] = jnp.concatenate(state + [stays, jnp.zeros_like(stays)], axis=0)

    mover_latent = dot(placer, latent).astype(BF16)
    mover_latent_ref[...] = mover_latent.astype(F32).T
    mover_node_pre_ref[...] = dot_nt(weights_ref[NODE_OLD], mover_latent)
    mover_near_ref[...] = dot_nt(weights_ref[NEAR], mover_latent)
    state = jnp.concatenate(state + [moving.astype(F32), jnp.zeros_like(stays)], axis=0)
    mover_state_ref[...] = joined(dot_nt(thirds(state), placer))
    neighbour_count = edge_ref.shape[3]
    ids = jnp.concatenate(
        [
            jnp.concatenate([neighbours_ref[a, b, k] for a, b in CELLS], axis=1)
            for k in range(neighbour_count)
        ],
        axis=0,
    )
    ids = jnp.concatenate([ids & 127, ids >> 7, jnp.zeros((8, particles), I32)], axis=0)
    ids = dot_nt(ids.astype(F32).astype(BF16), placer).astype(I32)
    place, key = places(ids[:neighbour_count], ids[neighbour_count : 2 * neighbour_count], fold_y)
    mover_place_ref[...] = jnp.concatenate([place[k : k + 1] for k in range(neighbour_count)], axis=1)
    mover_key_ref[...] = jnp.concatenate([key[k : k + 1] for k in range(neighbour_count)], axis=1)

    window = Window(fold_y, far_ref)
    for (ex, row), (a, b) in zip(window.own_columns(), CELLS):
        pair = jnp.concatenate([latent_ref[a, b, 0], own_zed[a, b, 0]], axis=0)
        far_ref[window.own(ex, row)] = dot_nt(weights_ref[FAR], pair).astype(BF16)
    cells = window.cells(window.own_columns())
    for a, bt in CELLS:
        b = (index_y if bt == 0 else 1 - index_y) if fold_y else bt
        ids = jnp.concatenate([neighbours_ref[a, b, k] for k in range(neighbour_count)], axis=1)
        place, key = places(ids & 127, ids >> 7, fold_y)
        near = dot_nt(weights_ref[NEAR], latent_ref[a, b, 0])
        near = jnp.concatenate([near, near], axis=1)
        for tile in range(ids.shape[1] // TILE):
            at = slice(tile * TILE, (tile + 1) * TILE)
            edges = [edge_ref[a, b, 0, k] for k in (2 * tile, 2 * tile + 1)]
            pre_ref[2 * a + bt, :, at] = (
                dot_nt(weights_ref[EDGE], jnp.concatenate(edges, axis=0))
                + near
                + pick(cells, place[:, at], key[:, at])
            )
    for k in range(neighbour_count):
        rows = jnp.concatenate([edge_ref[a, b, 0, k] for a, b in CELLS], axis=0)
        mover_edge_ref[k] = dot(placer, rows).astype(BF16)


def prepare_kernel(
    sizes,
    far_ref,
    mine_ref,
    weights_ref,
    edge_ref,
    place_ref,
    key_ref,
    near_ref,
    neighbours_ref,
    edge_pre_ref,
    far_mine_ref,
    pre_ref,
    border_ref,
):
    window = Window(sizes[1] == 2, far_ref)
    core = lax.axis_index("gz")
    far_t = weights_ref[FAR]
    cells = window.cells(window.own_columns())
    for row in range(window.row_count):
        pair = jnp.concatenate([mine_ref[1, row], mine_ref[0, row]], axis=0)
        far_mine_ref[row] = dot_nt(far_t, pair).astype(BF16)
        cells.append((12 * (1 - core) + row, far_mine_ref.at[row]))
    neighbour_count, movers = edge_ref.shape[:2]
    step = TILE // movers
    near = jnp.concatenate([near_ref[...]] * step, axis=1)
    for tile in range(neighbour_count // step):
        edges = jnp.concatenate([edge_ref[k] for k in range(tile * step, (tile + 1) * step)], axis=0)
        at = slice(tile * TILE, (tile + 1) * TILE)
        pre_ref[:, at] = (
            dot_nt(weights_ref[EDGE], edges) + near + pick(cells, place_ref[:, at], key_ref[:, at])
        )

    a = 1 - core
    b = lax.axis_index("gy") if sizes[1] == 2 else 0
    side = [(12 * a + row, far_mine_ref.at[row]) for row in window.rows(0)]
    ids = jnp.concatenate([neighbours_ref[a, b, k] for k in range(neighbour_count)], axis=1)
    place, key = places(ids & 127, ids >> 7, sizes[1] == 2)
    for tile in range(ids.shape[1] // TILE):
        at = slice(tile * TILE, (tile + 1) * TILE)
        border_ref[:, at] = edge_pre_ref[2 * a, :, at] + pick(side, place[:, at], key[:, at])


def movers_kernel(
    sizes,
    side_count,
    *refs,
):
    fold_y = sizes[1] == 2
    side_refs, refs = refs[:side_count], refs[side_count:]
    side_zeds, refs = refs[:side_count], refs[side_count:]
    other_ref, far_mine_ref, refs = refs[0], refs[1], refs[2:]
    (
        weights_ref,
        decoder_out_ref,
        pre_ref,
        place_ref,
        key_ref,
        node_pre_ref,
        latent_t_ref,
        state_ref,
        far_ref,
        bucket_ref,
        hidden_ref,
    ) = refs
    window = Window(fold_y, None, far_ref)
    row_count = window.row_count
    core = lax.axis_index("gz")
    far_t = weights_ref[FAR]

    def far(at, here, beside):
        pair = jnp.concatenate([here, beside], axis=0)
        far_ref[at] = dot_nt(far_t, pair).astype(BF16)

    for row in range(row_count):
        far(core * row_count + row, other_ref[0, row], other_ref[1, row])
    for side, row in enumerate(window.outer_rows):
        for ex in (1, 2):
            far(window.side(ex, row), side_refs[side][ex - 1], side_zeds[side][ex - 1])

    movers = state_ref.shape[1]
    for row in range(row_count):
        far_ref[(1 - core) * row_count + row] = far_mine_ref[row]
    cells = [(12 * core + row, far_ref.at[core * row_count + row]) for row in range(row_count)]
    cells += window.cells([(ex, row) for ex in (1, 2) for row in window.outer_rows])
    message = messages(
        cells,
        place_ref[...],
        key_ref[...],
        lambda tile: pre_ref[:, tile * TILE : (tile + 1) * TILE],
        weights_ref[MIDDLE],
        weights_ref[FINAL],
        hidden_ref,
    )
    aggregate = slot_sum(message, movers).astype(BF16)
    acceleration = advance(
        node_pre_ref[...], aggregate, latent_t_ref[...], weights_ref, decoder_out_ref[...]
    )
    mask = state_ref[6:7]
    state = moved(state_ref[0:3], state_ref[3:6], acceleration) * mask
    bucket_ref[...] = jnp.concatenate([state, mask, jnp.zeros((ROWS - 10, movers), F32)], axis=0)


def edges_kernel(
    sizes,
    alive_ref,
    neighbours_ref,
    far_ref,
    pre_ref,
    border_ref,
    weights_ref,
    total_ref,
    hidden_ref,
):
    fold_y = sizes[1] == 2
    window = Window(fold_y, None, far_ref)
    index_y = lax.axis_index("gy")
    slots = alive_ref.shape[-1]
    neighbour_count = neighbours_ref.shape[2]
    core = lax.axis_index("gz")
    for other, bt in CELLS:
        a = core if other else 1 - core
        b = (index_y if bt == 0 else 1 - index_y) if fold_y else bt
        rows = window.rows(bt)
        cells = window.cells([(ex, row) for ex in (1, 2) for row in rows if row in window.outer_rows])
        picked = other == 0 and bt == 0
        if not picked:
            cells += [(12 * a + row, far_ref.at[a * window.row_count + row]) for row in rows]
        ids = jnp.concatenate([neighbours_ref[a, b, k] for k in range(neighbour_count)], axis=1)
        place, key = places(ids & 127, ids >> 7, fold_y)

        def pre(tile, picked=picked, i=2 * a + bt):
            at = slice(tile * TILE, (tile + 1) * TILE)
            return border_ref[:, at] if picked else pre_ref[i, :, at]

        message = messages(
            cells,
            place,
            key,
            pre,
            weights_ref[MIDDLE],
            weights_ref[FINAL],
            hidden_ref.at[2 * other + bt],
        )
        total = jnp.where(alive_ref[a, b] > 0.5, slot_sum(message, slots), 0.0)
        total_ref[2 * a + b] = total.astype(BF16)


def nodes_kernel(
    total_ref,
    node_pre_ref,
    latent_t_ref,
    state_ref,
    weights_ref,
    decoder_out_ref,
    moved_ref,
):
    aggregate = jnp.concatenate([total_ref[i] for i in range(4)], axis=1)
    acceleration = advance(
        node_pre_ref[...], aggregate, latent_t_ref[...], weights_ref, decoder_out_ref[...]
    )
    state = moved(state_ref[0:3], state_ref[3:6], acceleration)
    moved_ref[...] = jnp.concatenate(
        [state, state_ref[6:7], jnp.zeros((ROWS - 10, state.shape[1]), F32)], axis=0
    )


def finish_kernel(sizes, moved_ref, zed_ref, *refs):
    count_x, count_y, count_z = sizes
    fold_y = count_y == 2
    options_y = 2 if fold_y else 3
    side_refs, refs = refs[: options_y - 1], refs[options_y - 1 :]
    if fold_y:
        cross_ref, end_ref, *refs = refs
    else:
        end_ref, *refs = refs
    (
        packed_ref,
        spread_ref,
        inward_ref,
        encoder_w_ref,
        kept_latent_ref,
        kept_state_ref,
        arrived_latent_ref,
        arrived_state_ref,
    ) = refs
    core = lax.axis_index("gz")

    def tile(source_x, from_y, from_z):
        if source_x == 0:
            if from_y == 0:
                return zed_ref[...]
            if fold_y:
                return packed_ref[4] if from_z else side_refs[0][...]
            return side_refs[from_y - 1][from_z]
        if fold_y:
            mine = (cross_ref if from_y else end_ref)[1 - from_z]
            other = packed_ref[(0 if from_y else 2) + from_z]
        else:
            mine = end_ref[1 - from_z, from_y]
            other = packed_ref[from_z, from_y]
        return jnp.where(core == (1 - source_x) // 2, mine, other)

    extent = (2.0 * count_x, 2.0 * count_y, 1.0 * count_z)
    slots = kept_latent_ref.shape[-2]
    stays = moved_ref[9:10]
    kept = moved_ref[:9] * stays
    latents = encode(moved_ref[:9], stays, inward_ref[...], encoder_w_ref[...], extent)
    for i, (a, b) in enumerate(CELLS):
        kept_latent_ref[a, b, 0] = latents[i * slots : (i + 1) * slots]
        for j in range(9):
            kept_state_ref[j, a, b] = kept[j : j + 1, i * slots : (i + 1) * slots]
    fold_y = count_y == 2
    index_x = lax.axis_index("gx")
    lanes = zed_ref.shape[-1]
    group = lax.broadcasted_iota(I32, (ROWS, lanes), 1) >> 3
    found = jnp.zeros((ROWS, lanes), F32)
    for source_x in (-1, 0, 1):
        for from_y in range(options_y):
            for from_z in range(2):
                if source_x == 0 and from_y == 0 and from_z == 0:
                    continue
                side_y = from_y if fold_y or from_y == 0 else 3 - from_y
                there = group == ((1 - source_x) * options_y + side_y) * 2 + from_z
                if source_x == -1:
                    there = there & (index_x > 0)
                elif source_x == 1:
                    there = there & (index_x < count_x - 1)
                found = jnp.where(there, tile(source_x, from_y, from_z), found)
    halves = []
    for at in range(0, spread_ref.shape[1], 128):
        lane = jnp.broadcast_to(spread_ref[0:1, at : at + 128], (ROWS, 128))
        half = jnp.zeros((ROWS, 128), F32)
        for base in range(0, lanes, 128):
            index = jnp.clip(lane - base, 0, 127)
            there = (lane >= base) & (lane < base + 128)
            part = jnp.take_along_axis(found[:, base : base + 128], index, axis=1)
            half = jnp.where(there, part, half)
        halves.append(half)
    arrived = jnp.concatenate(halves, axis=1)[:, : 26 * CAP]
    for j in range(9):
        arrived_state_ref[j, 0, 0] = arrived[j : j + 1]
    arrived_latent_ref[0, 0, 0] = encode(
        arrived[:9], arrived[9:10], inward_ref[...], encoder_w_ref[...], extent
    )


def swap(values, axis):
    return lax.ppermute(values, axis, [(0, 1), (1, 0)])


def shift(values, axis, way):
    pairs = [(i, i + 1) for i in range(lax.axis_size(axis) - 1)]
    return lax.ppermute(values, axis, [(j, i) for i, j in pairs] if way else pairs)


def swap_chips(values, cross):
    axes = ("group", "gx", "gy", "gz")
    counts = tuple(lax.axis_size(axis) for axis in axes)

    def number(place):
        total = 0
        for count, index in zip(counts, place):
            total = total * count + index
        return total

    pairs = []
    for place in itertools.product(*(range(count) for count in counts)):
        group, x, y, z = place
        to_x = x + 1 - 2 * z
        if 0 <= to_x < counts[1]:
            to = (group, to_x, y ^ 1 if cross else y, 1 - z)
        else:
            to = (group ^ 1, x, y, z)
        pairs.append((number(place), number(to)))
    return lax.ppermute(values, axes, pairs)


def call(kernel, name, in_specs, outs, scratch, operands, flops):
    return pl.pallas_call(
        kernel,
        out_shape=tuple(jax.ShapeDtypeStruct(shape, kind) for shape, kind in outs),
        in_specs=in_specs,
        out_specs=tuple(VMEM for _ in outs),
        scratch_shapes=scratch,
        compiler_params=pltpu.CompilerParams(vmem_limit_bytes=32 * 1024 * 1024),
        cost_estimate=pl.CostEstimate(flops=flops, bytes_accessed=0, transcendentals=0),
        name=name,
    )(*operands)


def in_hbm(array):
    return pltpu.with_memory_space_constraint(array, pltpu.HBM)


def like(array):
    return pltpu.VMEM(array.shape, array.dtype)


def body(
    node_latent,
    edge_latent,
    positions,
    velocity,
    fill,
    neighbours,
    owners,
    edge_weights,
    node_in,
    node_weights,
    decoder_weights,
    decoder_out,
    encoder_in,
    encoder_weights,
):
    sizes = tuple(lax.axis_size(axis) for axis in ("gx", "gy", "gz"))
    fold_y = sizes[1] == 2
    slots, width = node_latent.shape[-2:]
    neighbour_count = neighbours.shape[3]
    particles = 4 * slots
    options_y = 2 if fold_y else 3
    movers = (3 * options_y * 2 * CAP + 127) // 128 * 128
    rows = 3 if fold_y else 4
    fill = jnp.transpose(fill, (0, 2, 1))
    neighbours = neighbours.reshape(2, 2, neighbour_count, 1, slots)

    own_zed = swap(node_latent, "gz")
    if fold_y:
        sides = [swap(node_latent, "gy")]
    spread = call(
        functools.partial(tables_kernel, fold_y),
        "tables",
        [],
        [((8, 256), I32)],
        [],
        [],
        5_000_000_000,
    )[0]
    latent, spread = lax.optimization_barrier((node_latent, spread))
    core = lax.axis_index("gz")
    if fold_y:
        row = 1 - lax.axis_index("gy")
        end = lax.dynamic_index_in_dim(latent[:, :, 0], 1 - core, 0, False)
        beside = lax.dynamic_index_in_dim(own_zed[:, :, 0], 1 - core, 0, False)
        both = jnp.stack([end, beside])
        corner = lax.dynamic_slice_in_dim(both, row, 1, axis=1)
        mine = [swap_chips(both, False)]
        corner, both = lax.optimization_barrier((corner, both))
        mine.append(swap_chips(corner, True))
    else:
        sides = [shift(latent[:, 1, 0], "gy", 0), shift(latent[:, 0, 0], "gy", 1)]
        side_zeds = [swap(part, "gz") for part in sides]
        layers = []
        for middle, outer in ((latent, sides), (own_zed, side_zeds)):
            parts = [outer[0][:, None], middle[:, :, 0], outer[1][:, None]]
            parts = [lax.dynamic_index_in_dim(part, 1 - core, 0, False) for part in parts]
            layers.append(jnp.concatenate(parts, axis=0))
        mine = [swap_chips(jnp.stack(layers), False)]

    ranked = call(
        functools.partial(ranks_kernel, sizes),
        "ranks",
        [VMEM] * 13,
        [
            ((11, width, width), BF16),
            ((48, width), BF16),
            ((2, 2, 1, slots), F32),
            ((width, particles), F32),
            ((width, particles), F32),
            ((8, particles), F32),
            ((neighbour_count, movers, width), BF16),
            ((1, neighbour_count * movers), I32),
            ((1, neighbour_count * movers), I32),
            ((width, movers), F32),
            ((width, movers), F32),
            ((width, movers), F32),
            ((8, movers), F32),
            ((4, width, 2 * slots), BF16),
            ((4, width, neighbour_count * slots), F32),
        ],
        [],
        (edge_latent, latent, own_zed, fill, owners, edge_weights, node_in, node_weights, decoder_weights, encoder_in, neighbours, positions, velocity),
        5_000_000_000,
    )
    mine, sides, ranked = lax.optimization_barrier((mine, sides, ranked))
    (
        weights,
        inward,
        alive,
        latent_t,
        node_pre,
        state,
        mover_edges,
        mover_place,
        mover_key,
        mover_near,
        mover_node_pre,
        mover_latent,
        mover_state,
        far_own,
        edge_pre,
    ) = ranked
    mine = jnp.concatenate(mine, axis=1)
    if fold_y:
        sides = [lax.dynamic_index_in_dim(sides[0][:, :, 0], lax.axis_index("gy"), 1, False)]
        packed = jnp.concatenate([mine.reshape(-1, slots, width), sides[0]], axis=0)
    else:
        packed = mine.reshape(-1, slots, width)
    packed = swap(packed, "gz")
    prepared = call(
        functools.partial(prepare_kernel, sizes),
        "prepare",
        [VMEM] * 9,
        [
            ((rows, width, 2 * slots), BF16),
            ((width, neighbour_count * movers), F32),
            ((width, neighbour_count * slots), F32),
        ],
        [],
        (
            far_own,
            mine,
            weights,
            mover_edges,
            mover_place,
            mover_key,
            mover_near,
            neighbours,
            edge_pre,
        ),
        5_000_000_000,
    )
    packed, prepared = lax.optimization_barrier((packed, prepared))
    cells = mine.shape[0] * mine.shape[1]
    if fold_y:
        side_zeds = [packed[cells:]]
    far_mine, mover_pre, border = prepared
    halo = [*sides, *side_zeds, packed[:cells].reshape(mine.shape), far_mine]

    far_rest, bucket = call(
        functools.partial(movers_kernel, sizes, len(sides)),
        "movers",
        [VMEM] * (len(halo) + 8),
        [((4 * rows - 4, width, 2 * slots), BF16), ((ROWS, movers), F32)],
        [pltpu.VMEM((width, neighbour_count * movers), BF16)],
        (
            *halo,
            weights,
            decoder_out,
            mover_pre,
            mover_place,
            mover_key,
            mover_node_pre,
            mover_latent,
            mover_state,
        ),
        3_000_000_000,
    )

    zed = swap(bucket, "gz")
    if fold_y:
        sides = [swap(bucket, "gy")]
        zed, far_rest = lax.optimization_barrier((zed, far_rest))
        both = jnp.stack([bucket, zed])
        ends = [swap_chips(both, True), swap_chips(both, False)]
    else:
        both = jnp.stack([bucket, zed])
        sides = [shift(both, "gy", 0), shift(both, "gy", 1)]
        ends = [swap_chips(jnp.stack([both, *sides], axis=1), False)]
    total = call(
        functools.partial(edges_kernel, sizes),
        "edges",
        [VMEM] * 6,
        [((4, width, slots), BF16)],
        [pltpu.VMEM((4, width, neighbour_count * slots), BF16)],
        (alive, neighbours, far_rest, edge_pre, border, weights),
        8_000_000_000,
    )[0]
    sides, ends, total = lax.optimization_barrier((sides, ends, total))
    if fold_y:
        packed = swap(jnp.concatenate([*ends, sides[0][None]], axis=0), "gz")
    else:
        packed = swap(ends[0], "gz")
    state = call(
        nodes_kernel,
        "nodes",
        [VMEM] * 6,
        [((ROWS, particles), F32)],
        [],
        (total, node_pre, latent_t, state, weights, decoder_out),
        1_000_000_000,
    )[0]
    packed, state = lax.optimization_barrier((packed, state))
    return call(
        functools.partial(finish_kernel, sizes),
        "finish",
        [VMEM] * (len(sides) + len(ends) + 6),
        [
            (node_latent.shape, BF16),
            ((9,) + node_latent.shape[:4], F32),
            ((1, 1, 1, 26 * CAP, width), BF16),
            ((9, 1, 1, 1, 26 * CAP), F32),
        ],
        [],
        (state, zed, *sides, *ends, packed, spread, inward, encoder_weights),
        1_000_000_000,
    )


def solution(mesh):
    placed = (
        P(("group", "gx"), "gy", "gz", None, None),
        P(("group", "gx"), "gy", "gz", None, None, None),
        P(None, ("group", "gx"), "gy", "gz", None),
        P(None, ("group", "gx"), "gy", "gz", None),
        P(("group", "gx"), "gy", "gz"),
        P(("group", "gx"), "gy", "gz", None, None),
        P(("group", "gx"), "gy", "gz", None),
        P(),
        P(),
        P(),
        P(),
        P(),
        P(),
        P(),
    )
    return jax.shard_map(
        body,
        mesh=mesh,
        in_specs=placed,
        out_specs=(
            P(("group", "gx"), "gy", "gz", None, None),
            P(None, ("group", "gx"), "gy", "gz", None),
            P(("group", "gx"), "gy", "gz", None, None),
            P(None, ("group", "gx"), "gy", "gz", None),
        ),
        check_vma=False,
    )
```

```python
import functools
import itertools

import jax
import jax.numpy as jnp
from jax import lax
from jax.experimental import pallas as pl
from jax.experimental.pallas import tpu as pltpu
from jax.sharding import PartitionSpec as P

CAP = 8
F32 = jnp.float32
BF16 = jnp.bfloat16
I32 = jnp.int32
ROWS = 16
TILE = 256
CELLS = [(a, b) for a in range(2) for b in range(2)]
EDGE, NEAR, FAR, MIDDLE, FINAL, NODE_OLD, NODE_NEW, NODE_0, NODE_1, DECODE_0, DECODE_1 = range(11)

VMEM = pl.BlockSpec(memory_space=pltpu.VMEM)
SMEM = pl.BlockSpec(memory_space=pltpu.SMEM)
ANY = pl.BlockSpec(memory_space=pl.ANY)


def dot(left, right):
    return jnp.dot(left, right, preferred_element_type=F32)


def dot_nt(left, right):
    return lax.dot_general(left, right, (((1,), (1,)), ((), ())), preferred_element_type=F32)


def dot_tn(left, right):
    return lax.dot_general(left, right, (((0,), (0,)), ((), ())), preferred_element_type=F32)


def relu16(values):
    return jnp.maximum(values, 0.0).astype(BF16)


def norm(values, axis):
    scale = 1.0 / values.shape[axis]
    centred = values - jnp.sum(values, axis=axis, keepdims=True) * scale
    spread = jnp.sum(centred * centred, axis=axis, keepdims=True) * scale
    return centred * lax.rsqrt(spread + 1e-05)


def thirds(values):
    high = values.astype(BF16)
    rest = values - high.astype(F32)
    middle = rest.astype(BF16)
    low = (rest - middle.astype(F32)).astype(BF16)
    return jnp.concatenate([high, middle, low], axis=0)


def joined(values):
    rows = values.shape[0] // 3
    return values[:rows] + values[rows : 2 * rows] + values[2 * rows :]


def quotient(values, count):
    if count & (count - 1) == 0:
        return values >> (count.bit_length() - 1)
    return lax.div(values, jnp.full_like(values, count))


def flip(weights):
    return weights.astype(F32).T.astype(BF16)


def fetch(pairs, sems):
    copies = [pltpu.make_async_copy(src, dst, sems.at[i]) for i, (src, dst) in enumerate(pairs)]
    for copy in copies:
        copy.start()
    return copies


def encode_first(state, inward, extent):
    width = state.shape[1]
    position = state[0:3]
    row = lax.broadcasted_iota(I32, (3, width), 0)
    size = jnp.where(row == 0, extent[0], jnp.where(row == 1, extent[1], extent[2]))
    features = jnp.concatenate(
        [
            state[3:9],
            jnp.clip(position, -1.0, 1.0),
            jnp.clip(size - position, -1.0, 1.0),
            jnp.zeros((4, width), F32),
        ],
        axis=0,
    )
    return relu16(dot_tn(thirds(features), inward))


def encode_rest(hidden, mask, encoder_w):
    width = hidden.shape[0]
    hidden = relu16(dot(hidden, encoder_w[0]))
    column = jnp.broadcast_to(mask, (8, width)).T[:, 0:1]
    return (norm(dot(hidden, encoder_w[1]), 1) * column).astype(BF16)


def places(ids_low, ids_high, fold_y):
    plane = (ids_high * 43) >> 7
    ez = ids_high - plane * 3
    ey = plane & 3
    ex = plane >> 2
    if fold_y:
        row = jnp.where(ey == 1, 0, jnp.where(ey == 2, 1, 2))
    else:
        row = ey
    return ex * 4 + row, ids_low + jnp.where(ez == 1, 0, 128)


def pick(cells, place, key):
    width = cells[0][1].shape[0]
    chunk = 32
    window = jnp.concatenate(
        [ref[f : f + chunk] for f in range(0, width, chunk) for _, ref in cells], axis=0
    )
    key_rows = lax.broadcasted_iota(I32, (TILE, TILE), 0).astype(F32).astype(BF16)
    key = jnp.broadcast_to(key.astype(F32), (16, TILE)).astype(BF16)
    same = key_rows.reshape(TILE // 16, 16, TILE) == key[None]
    picker = jnp.where(same, jnp.ones((), BF16), jnp.zeros((), BF16)).reshape(TILE, TILE)
    found = dot(window, picker).reshape(width // chunk, len(cells), chunk // 8, 8, TILE)
    where = jnp.broadcast_to(place, (8, TILE))
    parts = []
    for f in range(width // chunk):
        part = jnp.zeros((chunk // 8, 8, TILE), F32)
        for i, (column, _) in enumerate(cells):
            part = jnp.where((where == column)[None], found[f, i], part)
        parts.append(part.reshape(chunk, TILE))
    return jnp.concatenate(parts, axis=0)


def messages(cells, place, key, pre, middle_t, final_t, hidden_ref):
    for tile in range(place.shape[1] // TILE):
        at = slice(tile * TILE, (tile + 1) * TILE)
        terms = pre(tile)
        if cells:
            terms = terms + pick(cells, place[:, at], key[:, at])
        hidden_ref[:, at] = relu16(terms)
    hidden = relu16(dot(middle_t, hidden_ref[...]))
    return norm(dot(final_t, hidden), 0)


class Window:
    def __init__(self, fold_y, own_ref=None, rest_ref=None):
        self.row_count = 3 if fold_y else 4
        self.own_rows = (0, 1) if fold_y else (1, 2)
        self.outer_rows = (2,) if fold_y else (0, 3)
        self.own_ref, self.rest_ref = own_ref, rest_ref

    def rows(self, bt):
        if self.row_count == 3:
            return (0, 1, 2)[: 2 + bt]
        return (bt, bt + 1, bt + 2)

    def own_columns(self):
        return [(ex, row) for ex in (1, 2) for row in self.own_rows]

    def own(self, ex, row):
        return (ex - 1) * 2 + self.own_rows.index(row)

    def side(self, ex, row):
        count = len(self.outer_rows)
        return 2 * self.row_count + (ex - 1) * count + self.outer_rows.index(row)

    def cells(self, columns):
        found = []
        for ex, row in columns:
            if ex in (1, 2) and row in self.own_rows:
                ref = self.own_ref.at[self.own(ex, row)]
            elif ex in (1, 2):
                ref = self.rest_ref.at[self.side(ex, row)]
            else:
                ref = self.rest_ref.at[(0 if ex == 0 else self.row_count) + row]
            found.append((ex * 4 + row, ref))
        return found


def slot_sum(message, step):
    total = message[:, :step]
    for at in range(step, message.shape[1], step):
        total = total + message[:, at : at + step]
    return total


def advance(pre, aggregate, latent_t, weights_ref, decoder_out):
    pre = pre + dot(weights_ref[NODE_NEW], aggregate)
    hidden = relu16(dot(weights_ref[NODE_0], relu16(pre)))
    updated = (latent_t + norm(dot(weights_ref[NODE_1], hidden), 0)).astype(BF16)
    hidden = relu16(dot(weights_ref[DECODE_0], updated))
    hidden = relu16(dot(weights_ref[DECODE_1], hidden))
    return dot(decoder_out, hidden)


def moved(position, velocity, acceleration):
    new_velocity = velocity + acceleration
    return jnp.concatenate([position + new_velocity, new_velocity, velocity], axis=0)


def tables_kernel(fold_y, spread_ref):
    index_y = lax.axis_index("gy")
    index_z = lax.axis_index("gz")
    options_y = 2 if fold_y else 3
    line = lax.broadcasted_iota(I32, spread_ref.shape, 1)
    direction = line >> 3
    direction = direction + jnp.where(direction > 12, 1, 0)
    plane = (direction * 57) >> 9
    from_z = direction - 3 * ((direction * 43) >> 7) - 1
    from_y = ((direction * 43) >> 7) - 3 * plane - 1
    if fold_y:
        side_y = jnp.where(from_y == 0, 0, 1)
        valid = (from_y == 0) | (from_y == 1 - 2 * index_y)
    else:
        side_y = jnp.where(from_y < 0, 2, from_y)
        valid = from_y < 2
    side_z = jnp.where(from_z == 0, 0, 1)
    valid = valid & ((from_z == 0) | (from_z == 1 - 2 * index_z)) & (line < 26 * CAP)
    target = ((2 - plane) * options_y + side_y) * 2 + side_z
    spread_ref[...] = jnp.where(valid, target * CAP + (line & 7), -1)


def ranks_kernel(
    sizes,
    edge_ref,
    latent_ref,
    own_zed,
    fill_ref,
    owners_ref,
    edge_w_ref,
    node_in_ref,
    node_w_ref,
    decoder_w_ref,
    encoder_in_ref,
    neighbours_ref,
    positions_ref,
    velocity_ref,
    weights_ref,
    inward_ref,
    alive_ref,
    latent_t_ref,
    node_pre_ref,
    state_ref,
    mover_edge_ref,
    mover_place_ref,
    mover_key_ref,
    mover_near_ref,
    mover_node_pre_ref,
    mover_latent_ref,
    mover_state_ref,
    far_ref,
    pre_ref,
):
    count_x, count_y, count_z = sizes
    fold_y = count_y == 2
    index_x = lax.axis_index("gx")
    index_y = lax.axis_index("gy")
    index_z = lax.axis_index("gz")
    slots = owners_ref.shape[-1]
    width = node_in_ref.shape[-1]
    lane = lax.broadcasted_iota(I32, (1, slots), 1)
    for a, b in CELLS:
        fill = jnp.broadcast_to(fill_ref[a, :, b : b + 1], (1, slots))
        alive_ref[a, b] = jnp.where(lane < fill, 1.0, 0.0)

    owner = jnp.concatenate([owners_ref[a, b] for a, b in CELLS], axis=1)
    alive = jnp.concatenate([alive_ref[a, b] for a, b in CELLS], axis=1)
    own_block = (index_x * count_y + index_y) * count_z + index_z
    stays = jnp.where((alive > 0.5) & (owner == own_block), 1.0, 0.0)
    moving = jnp.where((alive > 0.5) & (owner != own_block), 1, 0)
    owner_x = quotient(owner, count_y * count_z)
    rest = owner - owner_x * (count_y * count_z)
    owner_y = quotient(rest, count_z)
    owner_z = rest - owner_y * count_z
    step_y = owner_y - index_y
    side_y = jnp.where(step_y == 0, 0, 1) if fold_y else jnp.where(step_y < 0, 1, 2 * step_y)
    options_y = 2 if fold_y else 3
    group = ((owner_x - index_x + 1) * options_y + side_y) * 2 + jnp.where(owner_z == index_z, 0, 1)
    group_rows = (3 * options_y * 2 + 15) // 16 * 16
    particles = owner.shape[1]
    member = jnp.where(
        (lax.broadcasted_iota(I32, (group_rows, particles), 0) == group) & (moving == 1), 1.0, 0.0
    )
    triangle = jnp.where(
        lax.broadcasted_iota(I32, (slots, slots), 0) <= lax.broadcasted_iota(I32, (slots, slots), 1),
        1.0,
        0.0,
    ).astype(BF16)
    counted = []
    before = jnp.zeros((group_rows, 1), F32)
    for i in range(4):
        inside = member[:, i * slots : (i + 1) * slots]
        counted.append(dot(inside.astype(BF16), triangle) + before)
        before = before + jnp.sum(inside, axis=1, keepdims=True)
    counted = jnp.concatenate(counted, axis=1)
    rank = (jnp.sum(counted * member, axis=0, keepdims=True) - 1.0).astype(I32)
    column = jnp.where(moving == 1, group * CAP + rank, -1)
    movers = mover_state_ref.shape[1]
    placer = jnp.where(
        lax.broadcasted_iota(I32, (movers, particles), 0) == column, 1.0, 0.0
    ).astype(BF16)

    for i in range(5):
        weights_ref[i] = flip(edge_w_ref[i])
    weights_ref[NODE_OLD] = flip(node_in_ref[:width])
    weights_ref[NODE_NEW] = flip(node_in_ref[width:])
    for i in range(2):
        weights_ref[NODE_0 + i] = flip(node_w_ref[i])
        weights_ref[DECODE_0 + i] = flip(decoder_w_ref[i])
    inward = jnp.concatenate([encoder_in_ref[...].astype(F32), jnp.zeros((4, width), F32)], axis=0)
    inward = inward.astype(BF16)
    inward_ref[...] = jnp.concatenate([inward, inward, inward], axis=0)

    latent = jnp.concatenate([latent_ref[a, b, 0] for a, b in CELLS], axis=0)
    latent_t_ref[...] = latent.astype(F32).T
    node_pre_ref[...] = dot_nt(weights_ref[NODE_OLD], latent)

    def flat(ref, i):
        return jnp.concatenate([ref[i, a, b] for a, b in CELLS], axis=1)

    state = [flat(positions_ref, i) for i in range(3)] + [flat(velocity_ref, i) for i in range(3)]
    state_ref[...] = jnp.concatenate(state + [stays, jnp.zeros_like(stays)], axis=0)

    mover_latent = dot(placer, latent).astype(BF16)
    mover_latent_ref[...] = mover_latent.astype(F32).T
    mover_node_pre_ref[...] = dot_nt(weights_ref[NODE_OLD], mover_latent)
    mover_near_ref[...] = dot_nt(weights_ref[NEAR], mover_latent)
    state = jnp.concatenate(state + [moving.astype(F32), jnp.zeros_like(stays)], axis=0)
    mover_state_ref[...] = joined(dot_nt(thirds(state), placer))
    neighbour_count = edge_ref.shape[3]
    ids = jnp.concatenate(
        [
            jnp.concatenate([neighbours_ref[a, b, k] for a, b in CELLS], axis=1)
            for k in range(neighbour_count)
        ],
        axis=0,
    )
    ids = jnp.concatenate([ids & 127, ids >> 7, jnp.zeros((8, particles), I32)], axis=0)
    ids = dot_nt(ids.astype(F32).astype(BF16), placer).astype(I32)
    place, key = places(ids[:neighbour_count], ids[neighbour_count : 2 * neighbour_count], fold_y)
    mover_place_ref[...] = jnp.concatenate([place[k : k + 1] for k in range(neighbour_count)], axis=1)
    mover_key_ref[...] = jnp.concatenate([key[k : k + 1] for k in range(neighbour_count)], axis=1)

    window = Window(fold_y, far_ref)
    for (ex, row), (a, b) in zip(window.own_columns(), CELLS):
        pair = jnp.concatenate([latent_ref[a, b, 0], own_zed[a, b, 0]], axis=0)
        far_ref[window.own(ex, row)] = dot_nt(weights_ref[FAR], pair).astype(BF16)
    cells = window.cells(window.own_columns())
    for a, bt in CELLS:
        b = (index_y if bt == 0 else 1 - index_y) if fold_y else bt
        ids = jnp.concatenate([neighbours_ref[a, b, k] for k in range(neighbour_count)], axis=1)
        place, key = places(ids & 127, ids >> 7, fold_y)
        near = dot_nt(weights_ref[NEAR], latent_ref[a, b, 0])
        near = jnp.concatenate([near, near], axis=1)
        for tile in range(ids.shape[1] // TILE):
            at = slice(tile * TILE, (tile + 1) * TILE)
            edges = [edge_ref[a, b, 0, k] for k in (2 * tile, 2 * tile + 1)]
            pre_ref[2 * a + bt, :, at] = (
                dot_nt(weights_ref[EDGE], jnp.concatenate(edges, axis=0))
                + near
                + pick(cells, place[:, at], key[:, at])
            )
    for k in range(neighbour_count):
        rows = jnp.concatenate([edge_ref[a, b, 0, k] for a, b in CELLS], axis=0)
        mover_edge_ref[k] = dot(placer, rows).astype(BF16)


def prepare_kernel(
    sizes,
    far_ref,
    mine_ref,
    weights_ref,
    edge_ref,
    place_ref,
    key_ref,
    near_ref,
    neighbours_ref,
    edge_pre_ref,
    far_mine_ref,
    pre_ref,
    border_ref,
):
    window = Window(sizes[1] == 2, far_ref)
    core = lax.axis_index("gz")
    far_t = weights_ref[FAR]
    cells = window.cells(window.own_columns())
    for row in range(window.row_count):
        pair = jnp.concatenate([mine_ref[1, row], mine_ref[0, row]], axis=0)
        far_mine_ref[row] = dot_nt(far_t, pair).astype(BF16)
        cells.append((12 * (1 - core) + row, far_mine_ref.at[row]))
    neighbour_count, movers = edge_ref.shape[:2]
    step = TILE // movers
    near = jnp.concatenate([near_ref[...]] * step, axis=1)
    for tile in range(neighbour_count // step):
        edges = jnp.concatenate([edge_ref[k] for k in range(tile * step, (tile + 1) * step)], axis=0)
        at = slice(tile * TILE, (tile + 1) * TILE)
        pre_ref[:, at] = (
            dot_nt(weights_ref[EDGE], edges) + near + pick(cells, place_ref[:, at], key_ref[:, at])
        )

    a = 1 - core
    b = lax.axis_index("gy") if sizes[1] == 2 else 0
    side = [(12 * a + row, far_mine_ref.at[row]) for row in window.rows(0)]
    ids = jnp.concatenate([neighbours_ref[a, b, k] for k in range(neighbour_count)], axis=1)
    place, key = places(ids & 127, ids >> 7, sizes[1] == 2)
    for tile in range(ids.shape[1] // TILE):
        at = slice(tile * TILE, (tile + 1) * TILE)
        border_ref[:, at] = edge_pre_ref[2 * a, :, at] + pick(side, place[:, at], key[:, at])


def movers_kernel(
    sizes,
    side_count,
    *refs,
):
    fold_y = sizes[1] == 2
    side_refs, refs = refs[:side_count], refs[side_count:]
    side_zeds, refs = refs[:side_count], refs[side_count:]
    other_ref, far_mine_ref, refs = refs[0], refs[1], refs[2:]
    (
        weights_ref,
        decoder_out_ref,
        pre_ref,
        place_ref,
        key_ref,
        node_pre_ref,
        latent_t_ref,
        state_ref,
        far_ref,
        bucket_ref,
        hidden_ref,
    ) = refs
    window = Window(fold_y, None, far_ref)
    row_count = window.row_count
    core = lax.axis_index("gz")
    far_t = weights_ref[FAR]

    def far(at, here, beside):
        pair = jnp.concatenate([here, beside], axis=0)
        far_ref[at] = dot_nt(far_t, pair).astype(BF16)

    for row in range(row_count):
        far(core * row_count + row, other_ref[0, row], other_ref[1, row])
    for side, row in enumerate(window.outer_rows):
        for ex in (1, 2):
            far(window.side(ex, row), side_refs[side][ex - 1], side_zeds[side][ex - 1])

    movers = state_ref.shape[1]
    for row in range(row_count):
        far_ref[(1 - core) * row_count + row] = far_mine_ref[row]
    cells = [(12 * core + row, far_ref.at[core * row_count + row]) for row in range(row_count)]
    cells += window.cells([(ex, row) for ex in (1, 2) for row in window.outer_rows])
    message = messages(
        cells,
        place_ref[...],
        key_ref[...],
        lambda tile: pre_ref[:, tile * TILE : (tile + 1) * TILE],
        weights_ref[MIDDLE],
        weights_ref[FINAL],
        hidden_ref,
    )
    aggregate = slot_sum(message, movers).astype(BF16)
    acceleration = advance(
        node_pre_ref[...], aggregate, latent_t_ref[...], weights_ref, decoder_out_ref[...]
    )
    mask = state_ref[6:7]
    state = moved(state_ref[0:3], state_ref[3:6], acceleration) * mask
    bucket_ref[...] = jnp.concatenate([state, mask, jnp.zeros((ROWS - 10, movers), F32)], axis=0)


def edges_kernel(
    sizes,
    alive_ref,
    neighbours_ref,
    far_ref,
    pre_ref,
    border_ref,
    weights_ref,
    total_ref,
    hidden_ref,
):
    fold_y = sizes[1] == 2
    window = Window(fold_y, None, far_ref)
    index_y = lax.axis_index("gy")
    slots = alive_ref.shape[-1]
    neighbour_count = neighbours_ref.shape[2]
    core = lax.axis_index("gz")
    for other, bt in CELLS:
        a = core if other else 1 - core
        b = (index_y if bt == 0 else 1 - index_y) if fold_y else bt
        rows = window.rows(bt)
        cells = window.cells([(ex, row) for ex in (1, 2) for row in rows if row in window.outer_rows])
        picked = other == 0 and bt == 0
        if not picked:
            cells += [(12 * a + row, far_ref.at[a * window.row_count + row]) for row in rows]
        ids = jnp.concatenate([neighbours_ref[a, b, k] for k in range(neighbour_count)], axis=1)
        place, key = places(ids & 127, ids >> 7, fold_y)

        def pre(tile, picked=picked, i=2 * a + bt):
            at = slice(tile * TILE, (tile + 1) * TILE)
            return border_ref[:, at] if picked else pre_ref[i, :, at]

        message = messages(
            cells,
            place,
            key,
            pre,
            weights_ref[MIDDLE],
            weights_ref[FINAL],
            hidden_ref.at[2 * other + bt],
        )
        total = jnp.where(alive_ref[a, b] > 0.5, slot_sum(message, slots), 0.0)
        total_ref[2 * a + b] = total.astype(BF16)


def nodes_kernel(
    sizes,
    total_ref,
    node_pre_ref,
    latent_t_ref,
    state_ref,
    weights_ref,
    decoder_out_ref,
    inward_ref,
    moved_ref,
    hidden_ref,
):
    aggregate = jnp.concatenate([total_ref[i] for i in range(4)], axis=1)
    acceleration = advance(
        node_pre_ref[...], aggregate, latent_t_ref[...], weights_ref, decoder_out_ref[...]
    )
    state = moved(state_ref[0:3], state_ref[3:6], acceleration)
    moved_ref[...] = jnp.concatenate(
        [state, state_ref[6:7], jnp.zeros((ROWS - 10, state.shape[1]), F32)], axis=0
    )
    extent = (2.0 * sizes[0], 2.0 * sizes[1], 1.0 * sizes[2])
    hidden_ref[...] = encode_first(state, inward_ref[...], extent)


def finish_kernel(sizes, moved_ref, hidden_ref, zed_ref, *refs):
    count_x, count_y, count_z = sizes
    fold_y = count_y == 2
    options_y = 2 if fold_y else 3
    side_refs, refs = refs[: options_y - 1], refs[options_y - 1 :]
    if fold_y:
        cross_ref, end_ref, *refs = refs
    else:
        end_ref, *refs = refs
    (
        packed_ref,
        spread_ref,
        inward_ref,
        encoder_w_ref,
        kept_latent_ref,
        kept_state_ref,
        arrived_latent_ref,
        arrived_state_ref,
    ) = refs
    core = lax.axis_index("gz")

    def tile(source_x, from_y, from_z):
        if source_x == 0:
            if from_y == 0:
                return zed_ref[...]
            if fold_y:
                return packed_ref[4] if from_z else side_refs[0][...]
            return side_refs[from_y - 1][from_z]
        if fold_y:
            mine = (cross_ref if from_y else end_ref)[1 - from_z]
            other = packed_ref[(0 if from_y else 2) + from_z]
        else:
            mine = end_ref[1 - from_z, from_y]
            other = packed_ref[from_z, from_y]
        return jnp.where(core == (1 - source_x) // 2, mine, other)

    extent = (2.0 * count_x, 2.0 * count_y, 1.0 * count_z)
    slots = kept_latent_ref.shape[-2]
    stays = moved_ref[9:10]
    kept = moved_ref[:9] * stays
    latents = encode_rest(hidden_ref[...], stays, encoder_w_ref[...])
    for i, (a, b) in enumerate(CELLS):
        kept_latent_ref[a, b, 0] = latents[i * slots : (i + 1) * slots]
        for j in range(9):
            kept_state_ref[j, a, b] = kept[j : j + 1, i * slots : (i + 1) * slots]
    fold_y = count_y == 2
    index_x = lax.axis_index("gx")
    lanes = zed_ref.shape[-1]
    group = lax.broadcasted_iota(I32, (ROWS, lanes), 1) >> 3
    found = jnp.zeros((ROWS, lanes), F32)
    for source_x in (-1, 0, 1):
        for from_y in range(options_y):
            for from_z in range(2):
                if source_x == 0 and from_y == 0 and from_z == 0:
                    continue
                side_y = from_y if fold_y or from_y == 0 else 3 - from_y
                there = group == ((1 - source_x) * options_y + side_y) * 2 + from_z
                if source_x == -1:
                    there = there & (index_x > 0)
                elif source_x == 1:
                    there = there & (index_x < count_x - 1)
                found = jnp.where(there, tile(source_x, from_y, from_z), found)
    halves = []
    for at in range(0, spread_ref.shape[1], 128):
        lane = jnp.broadcast_to(spread_ref[0:1, at : at + 128], (ROWS, 128))
        half = jnp.zeros((ROWS, 128), F32)
        for base in range(0, lanes, 128):
            index = jnp.clip(lane - base, 0, 127)
            there = (lane >= base) & (lane < base + 128)
            part = jnp.take_along_axis(found[:, base : base + 128], index, axis=1)
            half = jnp.where(there, part, half)
        halves.append(half)
    arrived = jnp.concatenate(halves, axis=1)[:, : 26 * CAP]
    for j in range(9):
        arrived_state_ref[j, 0, 0] = arrived[j : j + 1]
    hidden = encode_first(arrived[:9], inward_ref[...], extent)
    arrived_latent_ref[0, 0, 0] = encode_rest(hidden, arrived[9:10], encoder_w_ref[...])


def swap(values, axis):
    return lax.ppermute(values, axis, [(0, 1), (1, 0)])


def shift(values, axis, way):
    pairs = [(i, i + 1) for i in range(lax.axis_size(axis) - 1)]
    return lax.ppermute(values, axis, [(j, i) for i, j in pairs] if way else pairs)


def swap_chips(values, cross):
    axes = ("group", "gx", "gy", "gz")
    counts = tuple(lax.axis_size(axis) for axis in axes)

    def number(place):
        total = 0
        for count, index in zip(counts, place):
            total = total * count + index
        return total

    pairs = []
    for place in itertools.product(*(range(count) for count in counts)):
        group, x, y, z = place
        to_x = x + 1 - 2 * z
        if 0 <= to_x < counts[1]:
            to = (group, to_x, y ^ 1 if cross else y, 1 - z)
        else:
            to = (group ^ 1, x, y, z)
        pairs.append((number(place), number(to)))
    return lax.ppermute(values, axes, pairs)


def call(kernel, name, in_specs, outs, scratch, operands, flops):
    return pl.pallas_call(
        kernel,
        out_shape=tuple(jax.ShapeDtypeStruct(shape, kind) for shape, kind in outs),
        in_specs=in_specs,
        out_specs=tuple(VMEM for _ in outs),
        scratch_shapes=scratch,
        compiler_params=pltpu.CompilerParams(vmem_limit_bytes=32 * 1024 * 1024),
        cost_estimate=pl.CostEstimate(flops=flops, bytes_accessed=0, transcendentals=0),
        name=name,
    )(*operands)


def in_hbm(array):
    return pltpu.with_memory_space_constraint(array, pltpu.HBM)


def like(array):
    return pltpu.VMEM(array.shape, array.dtype)


def body(
    node_latent,
    edge_latent,
    positions,
    velocity,
    fill,
    neighbours,
    owners,
    edge_weights,
    node_in,
    node_weights,
    decoder_weights,
    decoder_out,
    encoder_in,
    encoder_weights,
):
    sizes = tuple(lax.axis_size(axis) for axis in ("gx", "gy", "gz"))
    fold_y = sizes[1] == 2
    slots, width = node_latent.shape[-2:]
    neighbour_count = neighbours.shape[3]
    particles = 4 * slots
    options_y = 2 if fold_y else 3
    movers = (3 * options_y * 2 * CAP + 127) // 128 * 128
    rows = 3 if fold_y else 4
    fill = jnp.transpose(fill, (0, 2, 1))
    neighbours = neighbours.reshape(2, 2, neighbour_count, 1, slots)

    own_zed = swap(node_latent, "gz")
    if fold_y:
        sides = [swap(node_latent, "gy")]
    spread = call(
        functools.partial(tables_kernel, fold_y),
        "tables",
        [],
        [((8, 256), I32)],
        [],
        [],
        5_000_000_000,
    )[0]
    latent, spread = lax.optimization_barrier((node_latent, spread))
    core = lax.axis_index("gz")
    if fold_y:
        row = 1 - lax.axis_index("gy")
        end = lax.dynamic_index_in_dim(latent[:, :, 0], 1 - core, 0, False)
        beside = lax.dynamic_index_in_dim(own_zed[:, :, 0], 1 - core, 0, False)
        both = jnp.stack([end, beside])
        corner = lax.dynamic_slice_in_dim(both, row, 1, axis=1)
        mine = [swap_chips(both, False)]
        corner, both = lax.optimization_barrier((corner, both))
        mine.append(swap_chips(corner, True))
    else:
        sides = [shift(latent[:, 1, 0], "gy", 0), shift(latent[:, 0, 0], "gy", 1)]
        side_zeds = [swap(part, "gz") for part in sides]
        layers = []
        for middle, outer in ((latent, sides), (own_zed, side_zeds)):
            parts = [outer[0][:, None], middle[:, :, 0], outer[1][:, None]]
            parts = [lax.dynamic_index_in_dim(part, 1 - core, 0, False) for part in parts]
            layers.append(jnp.concatenate(parts, axis=0))
        mine = [swap_chips(jnp.stack(layers), False)]

    ranked = call(
        functools.partial(ranks_kernel, sizes),
        "ranks",
        [VMEM] * 13,
        [
            ((11, width, width), BF16),
            ((48, width), BF16),
            ((2, 2, 1, slots), F32),
            ((width, particles), F32),
            ((width, particles), F32),
            ((8, particles), F32),
            ((neighbour_count, movers, width), BF16),
            ((1, neighbour_count * movers), I32),
            ((1, neighbour_count * movers), I32),
            ((width, movers), F32),
            ((width, movers), F32),
            ((width, movers), F32),
            ((8, movers), F32),
            ((4, width, 2 * slots), BF16),
            ((4, width, neighbour_count * slots), F32),
        ],
        [],
        (edge_latent, latent, own_zed, fill, owners, edge_weights, node_in, node_weights, decoder_weights, encoder_in, neighbours, positions, velocity),
        5_000_000_000,
    )
    mine, sides, ranked = lax.optimization_barrier((mine, sides, ranked))
    (
        weights,
        inward,
        alive,
        latent_t,
        node_pre,
        state,
        mover_edges,
        mover_place,
        mover_key,
        mover_near,
        mover_node_pre,
        mover_latent,
        mover_state,
        far_own,
        edge_pre,
    ) = ranked
    mine = jnp.concatenate(mine, axis=1)
    if fold_y:
        sides = [lax.dynamic_index_in_dim(sides[0][:, :, 0], lax.axis_index("gy"), 1, False)]
        packed = jnp.concatenate([mine.reshape(-1, slots, width), sides[0]], axis=0)
    else:
        packed = mine.reshape(-1, slots, width)
    packed = swap(packed, "gz")
    prepared = call(
        functools.partial(prepare_kernel, sizes),
        "prepare",
        [VMEM] * 9,
        [
            ((rows, width, 2 * slots), BF16),
            ((width, neighbour_count * movers), F32),
            ((width, neighbour_count * slots), F32),
        ],
        [],
        (
            far_own,
            mine,
            weights,
            mover_edges,
            mover_place,
            mover_key,
            mover_near,
            neighbours,
            edge_pre,
        ),
        5_000_000_000,
    )
    packed, prepared = lax.optimization_barrier((packed, prepared))
    cells = mine.shape[0] * mine.shape[1]
    if fold_y:
        side_zeds = [packed[cells:]]
    far_mine, mover_pre, border = prepared
    halo = [*sides, *side_zeds, packed[:cells].reshape(mine.shape), far_mine]

    far_rest, bucket = call(
        functools.partial(movers_kernel, sizes, len(sides)),
        "movers",
        [VMEM] * (len(halo) + 8),
        [((4 * rows - 4, width, 2 * slots), BF16), ((ROWS, movers), F32)],
        [pltpu.VMEM((width, neighbour_count * movers), BF16)],
        (
            *halo,
            weights,
            decoder_out,
            mover_pre,
            mover_place,
            mover_key,
            mover_node_pre,
            mover_latent,
            mover_state,
        ),
        3_000_000_000,
    )

    zed = swap(bucket, "gz")
    if fold_y:
        sides = [swap(bucket, "gy")]
        zed, far_rest = lax.optimization_barrier((zed, far_rest))
        both = jnp.stack([bucket, zed])
        ends = [swap_chips(both, True), swap_chips(both, False)]
    else:
        both = jnp.stack([bucket, zed])
        sides = [shift(both, "gy", 0), shift(both, "gy", 1)]
        ends = [swap_chips(jnp.stack([both, *sides], axis=1), False)]
    total = call(
        functools.partial(edges_kernel, sizes),
        "edges",
        [VMEM] * 6,
        [((4, width, slots), BF16)],
        [pltpu.VMEM((4, width, neighbour_count * slots), BF16)],
        (alive, neighbours, far_rest, edge_pre, border, weights),
        8_000_000_000,
    )[0]
    sides, ends, total = lax.optimization_barrier((sides, ends, total))
    if fold_y:
        packed = swap(jnp.concatenate([*ends, sides[0][None]], axis=0), "gz")
    else:
        packed = swap(ends[0], "gz")
    state, hidden = call(
        functools.partial(nodes_kernel, sizes),
        "nodes",
        [VMEM] * 7,
        [((ROWS, particles), F32), ((particles, width), BF16)],
        [],
        (total, node_pre, latent_t, state, weights, decoder_out, inward),
        1_000_000_000,
    )
    packed, state, hidden = lax.optimization_barrier((packed, state, hidden))
    return call(
        functools.partial(finish_kernel, sizes),
        "finish",
        [VMEM] * (len(sides) + len(ends) + 7),
        [
            (node_latent.shape, BF16),
            ((9,) + node_latent.shape[:4], F32),
            ((1, 1, 1, 26 * CAP, width), BF16),
            ((9, 1, 1, 1, 26 * CAP), F32),
        ],
        [],
        (state, hidden, zed, *sides, *ends, packed, spread, inward, encoder_weights),
        1_000_000_000,
    )


def solution(mesh):
    placed = (
        P(("group", "gx"), "gy", "gz", None, None),
        P(("group", "gx"), "gy", "gz", None, None, None),
        P(None, ("group", "gx"), "gy", "gz", None),
        P(None, ("group", "gx"), "gy", "gz", None),
        P(("group", "gx"), "gy", "gz"),
        P(("group", "gx"), "gy", "gz", None, None),
        P(("group", "gx"), "gy", "gz", None),
        P(),
        P(),
        P(),
        P(),
        P(),
        P(),
        P(),
    )
    return jax.shard_map(
        body,
        mesh=mesh,
        in_specs=placed,
        out_specs=(
            P(("group", "gx"), "gy", "gz", None, None),
            P(None, ("group", "gx"), "gy", "gz", None),
            P(("group", "gx"), "gy", "gz", None, None),
            P(None, ("group", "gx"), "gy", "gz", None),
        ),
        check_vma=False,
    )
```

```python
import functools
import itertools

import jax
import jax.numpy as jnp
from jax import lax
from jax.experimental import pallas as pl
from jax.experimental.pallas import tpu as pltpu
from jax.sharding import PartitionSpec as P

CAP = 8
F32 = jnp.float32
BF16 = jnp.bfloat16
I32 = jnp.int32
ROWS = 16
TILE = 256
CELLS = [(a, b) for a in range(2) for b in range(2)]
EDGE, NEAR, FAR, MIDDLE, FINAL, NODE_OLD, NODE_NEW, NODE_0, NODE_1, DECODE_0, DECODE_1 = range(11)

VMEM = pl.BlockSpec(memory_space=pltpu.VMEM)
SMEM = pl.BlockSpec(memory_space=pltpu.SMEM)
ANY = pl.BlockSpec(memory_space=pl.ANY)


def dot(left, right):
    return jnp.dot(left, right, preferred_element_type=F32)


def dot_nt(left, right):
    return lax.dot_general(left, right, (((1,), (1,)), ((), ())), preferred_element_type=F32)


def dot_tn(left, right):
    return lax.dot_general(left, right, (((0,), (0,)), ((), ())), preferred_element_type=F32)


def relu16(values):
    return jnp.maximum(values, 0.0).astype(BF16)


def norm(values, axis):
    scale = 1.0 / values.shape[axis]
    centred = values - jnp.sum(values, axis=axis, keepdims=True) * scale
    spread = jnp.sum(centred * centred, axis=axis, keepdims=True) * scale
    return centred * lax.rsqrt(spread + 1e-05)


def thirds(values):
    high = values.astype(BF16)
    rest = values - high.astype(F32)
    middle = rest.astype(BF16)
    low = (rest - middle.astype(F32)).astype(BF16)
    return jnp.concatenate([high, middle, low], axis=0)


def joined(values):
    rows = values.shape[0] // 3
    return values[:rows] + values[rows : 2 * rows] + values[2 * rows :]


def quotient(values, count):
    if count & (count - 1) == 0:
        return values >> (count.bit_length() - 1)
    return lax.div(values, jnp.full_like(values, count))


def flip(weights):
    return weights.astype(F32).T.astype(BF16)


def fetch(pairs, sems):
    copies = [pltpu.make_async_copy(src, dst, sems.at[i]) for i, (src, dst) in enumerate(pairs)]
    for copy in copies:
        copy.start()
    return copies


def encode(state, mask, inward, encoder_w, extent):
    width = state.shape[1]
    position = state[0:3]
    row = lax.broadcasted_iota(I32, (3, width), 0)
    size = jnp.where(row == 0, extent[0], jnp.where(row == 1, extent[1], extent[2]))
    features = jnp.concatenate(
        [
            state[3:9],
            jnp.clip(position, -1.0, 1.0),
            jnp.clip(size - position, -1.0, 1.0),
            jnp.zeros((4, width), F32),
        ],
        axis=0,
    )
    hidden = relu16(dot_tn(thirds(features), inward))
    hidden = relu16(dot(hidden, encoder_w[0]))
    column = jnp.broadcast_to(mask, (8, width)).T[:, 0:1]
    return (norm(dot(hidden, encoder_w[1]), 1) * column).astype(BF16)


def places(ids_low, ids_high, fold_y):
    plane = (ids_high * 43) >> 7
    ez = ids_high - plane * 3
    ey = plane & 3
    ex = plane >> 2
    if fold_y:
        row = jnp.where(ey == 1, 0, jnp.where(ey == 2, 1, 2))
    else:
        row = ey
    return ex * 4 + row, ids_low + jnp.where(ez == 1, 0, 128)


def pick(cells, place, key):
    width = cells[0][1].shape[0]
    chunk = 32
    window = jnp.concatenate(
        [ref[f : f + chunk] for f in range(0, width, chunk) for _, ref in cells], axis=0
    )
    key_rows = lax.broadcasted_iota(I32, (TILE, TILE), 0).astype(F32).astype(BF16)
    key = jnp.broadcast_to(key.astype(F32), (16, TILE)).astype(BF16)
    same = key_rows.reshape(TILE // 16, 16, TILE) == key[None]
    picker = jnp.where(same, jnp.ones((), BF16), jnp.zeros((), BF16)).reshape(TILE, TILE)
    found = dot(window, picker).reshape(width // chunk, len(cells), chunk // 8, 8, TILE)
    where = jnp.broadcast_to(place, (8, TILE))
    parts = []
    for f in range(width // chunk):
        part = jnp.zeros((chunk // 8, 8, TILE), F32)
        for i, (column, _) in enumerate(cells):
            part = jnp.where((where == column)[None], found[f, i], part)
        parts.append(part.reshape(chunk, TILE))
    return jnp.concatenate(parts, axis=0)


def messages(cells, place, key, pre, middle_t, final_t, hidden_ref):
    for tile in range(place.shape[1] // TILE):
        at = slice(tile * TILE, (tile + 1) * TILE)
        terms = pre(tile)
        if cells:
            terms = terms + pick(cells, place[:, at], key[:, at])
        hidden_ref[:, at] = relu16(terms)
    hidden = relu16(dot(middle_t, hidden_ref[...]))
    return norm(dot(final_t, hidden), 0)


class Window:
    def __init__(self, fold_y, own_ref=None, rest_ref=None):
        self.row_count = 3 if fold_y else 4
        self.own_rows = (0, 1) if fold_y else (1, 2)
        self.outer_rows = (2,) if fold_y else (0, 3)
        self.own_ref, self.rest_ref = own_ref, rest_ref

    def rows(self, bt):
        if self.row_count == 3:
            return (0, 1, 2)[: 2 + bt]
        return (bt, bt + 1, bt + 2)

    def own_columns(self):
        return [(ex, row) for ex in (1, 2) for row in self.own_rows]

    def own(self, ex, row):
        return (ex - 1) * 2 + self.own_rows.index(row)

    def side(self, ex, row):
        count = len(self.outer_rows)
        return 2 * self.row_count + (ex - 1) * count + self.outer_rows.index(row)

    def cells(self, columns):
        found = []
        for ex, row in columns:
            if ex in (1, 2) and row in self.own_rows:
                ref = self.own_ref.at[self.own(ex, row)]
            elif ex in (1, 2):
                ref = self.rest_ref.at[self.side(ex, row)]
            else:
                ref = self.rest_ref.at[(0 if ex == 0 else self.row_count) + row]
            found.append((ex * 4 + row, ref))
        return found


def slot_sum(message, step):
    total = message[:, :step]
    for at in range(step, message.shape[1], step):
        total = total + message[:, at : at + step]
    return total


def advance(pre, aggregate, latent_t, weights_ref, decoder_out):
    pre = pre + dot(weights_ref[NODE_NEW], aggregate)
    hidden = relu16(dot(weights_ref[NODE_0], relu16(pre)))
    updated = (latent_t + norm(dot(weights_ref[NODE_1], hidden), 0)).astype(BF16)
    hidden = relu16(dot(weights_ref[DECODE_0], updated))
    hidden = relu16(dot(weights_ref[DECODE_1], hidden))
    return dot(decoder_out, hidden)


def moved(position, velocity, acceleration):
    new_velocity = velocity + acceleration
    return jnp.concatenate([position + new_velocity, new_velocity, velocity], axis=0)


def tables_kernel(fold_y, spread_ref):
    index_y = lax.axis_index("gy")
    index_z = lax.axis_index("gz")
    options_y = 2 if fold_y else 3
    line = lax.broadcasted_iota(I32, spread_ref.shape, 1)
    direction = line >> 3
    direction = direction + jnp.where(direction > 12, 1, 0)
    plane = (direction * 57) >> 9
    from_z = direction - 3 * ((direction * 43) >> 7) - 1
    from_y = ((direction * 43) >> 7) - 3 * plane - 1
    if fold_y:
        side_y = jnp.where(from_y == 0, 0, 1)
        valid = (from_y == 0) | (from_y == 1 - 2 * index_y)
    else:
        side_y = jnp.where(from_y < 0, 2, from_y)
        valid = from_y < 2
    side_z = jnp.where(from_z == 0, 0, 1)
    valid = valid & ((from_z == 0) | (from_z == 1 - 2 * index_z)) & (line < 26 * CAP)
    target = ((2 - plane) * options_y + side_y) * 2 + side_z
    spread_ref[...] = jnp.where(valid, target * CAP + (line & 7), -1)


def ranks_kernel(
    sizes,
    edge_ref,
    latent_ref,
    own_zed,
    fill_ref,
    owners_ref,
    edge_w_ref,
    node_in_ref,
    node_w_ref,
    decoder_w_ref,
    encoder_in_ref,
    neighbours_ref,
    positions_ref,
    velocity_ref,
    weights_ref,
    inward_ref,
    alive_ref,
    latent_t_ref,
    node_pre_ref,
    state_ref,
    mover_edge_ref,
    mover_place_ref,
    mover_key_ref,
    mover_near_ref,
    mover_node_pre_ref,
    mover_latent_ref,
    mover_state_ref,
    far_ref,
    pre_ref,
):
    count_x, count_y, count_z = sizes
    fold_y = count_y == 2
    index_x = lax.axis_index("gx")
    index_y = lax.axis_index("gy")
    index_z = lax.axis_index("gz")
    slots = owners_ref.shape[-1]
    width = node_in_ref.shape[-1]
    lane = lax.broadcasted_iota(I32, (1, slots), 1)
    for a, b in CELLS:
        fill = jnp.broadcast_to(fill_ref[a, :, b : b + 1], (1, slots))
        alive_ref[a, b] = jnp.where(lane < fill, 1.0, 0.0)

    owner = jnp.concatenate([owners_ref[a, b] for a, b in CELLS], axis=1)
    alive = jnp.concatenate([alive_ref[a, b] for a, b in CELLS], axis=1)
    own_block = (index_x * count_y + index_y) * count_z + index_z
    stays = jnp.where((alive > 0.5) & (owner == own_block), 1.0, 0.0)
    moving = jnp.where((alive > 0.5) & (owner != own_block), 1, 0)
    owner_x = quotient(owner, count_y * count_z)
    rest = owner - owner_x * (count_y * count_z)
    owner_y = quotient(rest, count_z)
    owner_z = rest - owner_y * count_z
    step_y = owner_y - index_y
    side_y = jnp.where(step_y == 0, 0, 1) if fold_y else jnp.where(step_y < 0, 1, 2 * step_y)
    options_y = 2 if fold_y else 3
    group = ((owner_x - index_x + 1) * options_y + side_y) * 2 + jnp.where(owner_z == index_z, 0, 1)
    group_rows = (3 * options_y * 2 + 15) // 16 * 16
    particles = owner.shape[1]
    member = jnp.where(
        (lax.broadcasted_iota(I32, (group_rows, particles), 0) == group) & (moving == 1), 1.0, 0.0
    )
    triangle = jnp.where(
        lax.broadcasted_iota(I32, (slots, slots), 0) <= lax.broadcasted_iota(I32, (slots, slots), 1),
        1.0,
        0.0,
    ).astype(BF16)
    counted = []
    before = jnp.zeros((group_rows, 1), F32)
    for i in range(4):
        inside = member[:, i * slots : (i + 1) * slots]
        counted.append(dot(inside.astype(BF16), triangle) + before)
        before = before + jnp.sum(inside, axis=1, keepdims=True)
    counted = jnp.concatenate(counted, axis=1)
    rank = (jnp.sum(counted * member, axis=0, keepdims=True) - 1.0).astype(I32)
    column = jnp.where(moving == 1, group * CAP + rank, -1)
    movers = mover_state_ref.shape[1]
    placer = jnp.where(
        lax.broadcasted_iota(I32, (movers, particles), 0) == column, 1.0, 0.0
    ).astype(BF16)

    for i in range(5):
        weights_ref[i] = flip(edge_w_ref[i])
    weights_ref[NODE_OLD] = flip(node_in_ref[:width])
    weights_ref[NODE_NEW] = flip(node_in_ref[width:])
    for i in range(2):
        weights_ref[NODE_0 + i] = flip(node_w_ref[i])
        weights_ref[DECODE_0 + i] = flip(decoder_w_ref[i])
    inward = jnp.concatenate([encoder_in_ref[...].astype(F32), jnp.zeros((4, width), F32)], axis=0)
    inward = inward.astype(BF16)
    inward_ref[...] = jnp.concatenate([inward, inward, inward], axis=0)

    latent = jnp.concatenate([latent_ref[a, b, 0] for a, b in CELLS], axis=0)
    latent_t_ref[...] = latent.astype(F32).T
    node_pre_ref[...] = dot_nt(weights_ref[NODE_OLD], latent)

    def flat(ref, i):
        return jnp.concatenate([ref[i, a, b] for a, b in CELLS], axis=1)

    state = [flat(positions_ref, i) for i in range(3)] + [flat(velocity_ref, i) for i in range(3)]
    state_ref[...] = jnp.concatenate(state + [stays, jnp.zeros_like(stays)], axis=0)

    mover_latent = dot(placer, latent).astype(BF16)
    mover_latent_ref[...] = mover_latent.astype(F32).T
    mover_node_pre_ref[...] = dot_nt(weights_ref[NODE_OLD], mover_latent)
    mover_near_ref[...] = dot_nt(weights_ref[NEAR], mover_latent)
    state = jnp.concatenate(state + [moving.astype(F32), jnp.zeros_like(stays)], axis=0)
    mover_state_ref[...] = joined(dot_nt(thirds(state), placer))
    neighbour_count = edge_ref.shape[3]
    ids = jnp.concatenate(
        [
            jnp.concatenate([neighbours_ref[a, b, k] for a, b in CELLS], axis=1)
            for k in range(neighbour_count)
        ],
        axis=0,
    )
    ids = jnp.concatenate([ids & 127, ids >> 7, jnp.zeros((8, particles), I32)], axis=0)
    ids = dot_nt(ids.astype(F32).astype(BF16), placer).astype(I32)
    place, key = places(ids[:neighbour_count], ids[neighbour_count : 2 * neighbour_count], fold_y)
    mover_place_ref[...] = jnp.concatenate([place[k : k + 1] for k in range(neighbour_count)], axis=1)
    mover_key_ref[...] = jnp.concatenate([key[k : k + 1] for k in range(neighbour_count)], axis=1)

    window = Window(fold_y, far_ref)
    for (ex, row), (a, b) in zip(window.own_columns(), CELLS):
        pair = jnp.concatenate([latent_ref[a, b, 0], own_zed[a, b, 0]], axis=0)
        far_ref[window.own(ex, row)] = dot_nt(weights_ref[FAR], pair).astype(BF16)
    cells = window.cells(window.own_columns())
    for a, bt in CELLS:
        b = (index_y if bt == 0 else 1 - index_y) if fold_y else bt
        ids = jnp.concatenate([neighbours_ref[a, b, k] for k in range(neighbour_count)], axis=1)
        place, key = places(ids & 127, ids >> 7, fold_y)
        near = dot_nt(weights_ref[NEAR], latent_ref[a, b, 0])
        near = jnp.concatenate([near, near], axis=1)
        for tile in range(ids.shape[1] // TILE):
            at = slice(tile * TILE, (tile + 1) * TILE)
            edges = [edge_ref[a, b, 0, k] for k in (2 * tile, 2 * tile + 1)]
            pre_ref[2 * a + bt, :, at] = (
                dot_nt(weights_ref[EDGE], jnp.concatenate(edges, axis=0))
                + near
                + pick(cells, place[:, at], key[:, at])
            )
    for k in range(neighbour_count):
        rows = jnp.concatenate([edge_ref[a, b, 0, k] for a, b in CELLS], axis=0)
        mover_edge_ref[k] = dot(placer, rows).astype(BF16)


def prepare_kernel(
    sizes,
    far_ref,
    mine_ref,
    weights_ref,
    edge_ref,
    place_ref,
    key_ref,
    near_ref,
    neighbours_ref,
    edge_pre_ref,
    far_mine_ref,
    pre_ref,
    border_ref,
):
    window = Window(sizes[1] == 2, far_ref)
    core = lax.axis_index("gz")
    far_t = weights_ref[FAR]
    cells = window.cells(window.own_columns())
    for row in range(window.row_count):
        pair = jnp.concatenate([mine_ref[1, row], mine_ref[0, row]], axis=0)
        far_mine_ref[row] = dot_nt(far_t, pair).astype(BF16)
        cells.append((12 * (1 - core) + row, far_mine_ref.at[row]))
    neighbour_count, movers = edge_ref.shape[:2]
    step = TILE // movers
    near = jnp.concatenate([near_ref[...]] * step, axis=1)
    for tile in range(neighbour_count // step):
        edges = jnp.concatenate([edge_ref[k] for k in range(tile * step, (tile + 1) * step)], axis=0)
        at = slice(tile * TILE, (tile + 1) * TILE)
        pre_ref[:, at] = (
            dot_nt(weights_ref[EDGE], edges) + near + pick(cells, place_ref[:, at], key_ref[:, at])
        )

    a = 1 - core
    b = lax.axis_index("gy") if sizes[1] == 2 else 0
    side = [(12 * a + row, far_mine_ref.at[row]) for row in window.rows(0)]
    ids = jnp.concatenate([neighbours_ref[a, b, k] for k in range(neighbour_count)], axis=1)
    place, key = places(ids & 127, ids >> 7, sizes[1] == 2)
    for tile in range(ids.shape[1] // TILE):
        at = slice(tile * TILE, (tile + 1) * TILE)
        border_ref[:, at] = edge_pre_ref[2 * a, :, at] + pick(side, place[:, at], key[:, at])


def movers_kernel(
    sizes,
    side_count,
    *refs,
):
    fold_y = sizes[1] == 2
    side_refs, refs = refs[:side_count], refs[side_count:]
    side_zeds, refs = refs[:side_count], refs[side_count:]
    other_ref, refs = refs[0], refs[1:]
    (
        weights_ref,
        decoder_out_ref,
        pre_ref,
        place_ref,
        key_ref,
        node_pre_ref,
        latent_t_ref,
        state_ref,
        far_ref,
        bucket_ref,
        hidden_ref,
    ) = refs
    window = Window(fold_y, None, far_ref)
    row_count = window.row_count
    core = lax.axis_index("gz")
    far_t = weights_ref[FAR]

    def far(at, here, beside):
        pair = jnp.concatenate([here, beside], axis=0)
        far_ref[at] = dot_nt(far_t, pair).astype(BF16)

    for row in range(row_count):
        far(core * row_count + row, other_ref[0, row], other_ref[1, row])
    for side, row in enumerate(window.outer_rows):
        for ex in (1, 2):
            far(window.side(ex, row), side_refs[side][ex - 1], side_zeds[side][ex - 1])

    movers = state_ref.shape[1]
    cells = [(12 * core + row, far_ref.at[core * row_count + row]) for row in range(row_count)]
    cells += window.cells([(ex, row) for ex in (1, 2) for row in window.outer_rows])
    message = messages(
        cells,
        place_ref[...],
        key_ref[...],
        lambda tile: pre_ref[:, tile * TILE : (tile + 1) * TILE],
        weights_ref[MIDDLE],
        weights_ref[FINAL],
        hidden_ref,
    )
    aggregate = slot_sum(message, movers).astype(BF16)
    acceleration = advance(
        node_pre_ref[...], aggregate, latent_t_ref[...], weights_ref, decoder_out_ref[...]
    )
    mask = state_ref[6:7]
    state = moved(state_ref[0:3], state_ref[3:6], acceleration) * mask
    bucket_ref[...] = jnp.concatenate([state, mask, jnp.zeros((ROWS - 10, movers), F32)], axis=0)


def edges_kernel(
    sizes,
    alive_ref,
    neighbours_ref,
    far_ref,
    far_mine_ref,
    pre_ref,
    border_ref,
    weights_ref,
    total_ref,
    hidden_ref,
):
    fold_y = sizes[1] == 2
    window = Window(fold_y, None, far_ref)
    index_y = lax.axis_index("gy")
    slots = alive_ref.shape[-1]
    neighbour_count = neighbours_ref.shape[2]
    core = lax.axis_index("gz")
    for other, bt in CELLS:
        a = core if other else 1 - core
        b = (index_y if bt == 0 else 1 - index_y) if fold_y else bt
        rows = window.rows(bt)
        cells = window.cells([(ex, row) for ex in (1, 2) for row in rows if row in window.outer_rows])
        picked = other == 0 and bt == 0
        if not picked:
            for row in rows:
                end = far_ref.at[a * window.row_count + row] if other else far_mine_ref.at[row]
                cells.append((12 * a + row, end))
        ids = jnp.concatenate([neighbours_ref[a, b, k] for k in range(neighbour_count)], axis=1)
        place, key = places(ids & 127, ids >> 7, fold_y)

        def pre(tile, picked=picked, i=2 * a + bt):
            at = slice(tile * TILE, (tile + 1) * TILE)
            return border_ref[:, at] if picked else pre_ref[i, :, at]

        message = messages(
            cells,
            place,
            key,
            pre,
            weights_ref[MIDDLE],
            weights_ref[FINAL],
            hidden_ref.at[2 * other + bt],
        )
        total = jnp.where(alive_ref[a, b] > 0.5, slot_sum(message, slots), 0.0)
        total_ref[2 * a + b] = total.astype(BF16)


def nodes_kernel(
    total_ref,
    node_pre_ref,
    latent_t_ref,
    state_ref,
    weights_ref,
    decoder_out_ref,
    moved_ref,
):
    aggregate = jnp.concatenate([total_ref[i] for i in range(4)], axis=1)
    acceleration = advance(
        node_pre_ref[...], aggregate, latent_t_ref[...], weights_ref, decoder_out_ref[...]
    )
    state = moved(state_ref[0:3], state_ref[3:6], acceleration)
    moved_ref[...] = jnp.concatenate(
        [state, state_ref[6:7], jnp.zeros((ROWS - 10, state.shape[1]), F32)], axis=0
    )


def finish_kernel(sizes, moved_ref, zed_ref, *refs):
    count_x, count_y, count_z = sizes
    fold_y = count_y == 2
    options_y = 2 if fold_y else 3
    side_refs, refs = refs[: options_y - 1], refs[options_y - 1 :]
    if fold_y:
        cross_ref, end_ref, *refs = refs
    else:
        end_ref, *refs = refs
    (
        packed_ref,
        spread_ref,
        inward_ref,
        encoder_w_ref,
        kept_latent_ref,
        kept_state_ref,
        arrived_latent_ref,
        arrived_state_ref,
    ) = refs
    core = lax.axis_index("gz")

    def tile(source_x, from_y, from_z):
        if source_x == 0:
            if from_y == 0:
                return zed_ref[...]
            if fold_y:
                return packed_ref[4] if from_z else side_refs[0][...]
            return side_refs[from_y - 1][from_z]
        if fold_y:
            mine = (cross_ref if from_y else end_ref)[1 - from_z]
            other = packed_ref[(0 if from_y else 2) + from_z]
        else:
            mine = end_ref[1 - from_z, from_y]
            other = packed_ref[from_z, from_y]
        return jnp.where(core == (1 - source_x) // 2, mine, other)

    extent = (2.0 * count_x, 2.0 * count_y, 1.0 * count_z)
    slots = kept_latent_ref.shape[-2]
    stays = moved_ref[9:10]
    kept = moved_ref[:9] * stays
    latents = encode(moved_ref[:9], stays, inward_ref[...], encoder_w_ref[...], extent)
    for i, (a, b) in enumerate(CELLS):
        kept_latent_ref[a, b, 0] = latents[i * slots : (i + 1) * slots]
        for j in range(9):
            kept_state_ref[j, a, b] = kept[j : j + 1, i * slots : (i + 1) * slots]
    fold_y = count_y == 2
    index_x = lax.axis_index("gx")
    lanes = zed_ref.shape[-1]
    group = lax.broadcasted_iota(I32, (ROWS, lanes), 1) >> 3
    found = jnp.zeros((ROWS, lanes), F32)
    for source_x in (-1, 0, 1):
        for from_y in range(options_y):
            for from_z in range(2):
                if source_x == 0 and from_y == 0 and from_z == 0:
                    continue
                side_y = from_y if fold_y or from_y == 0 else 3 - from_y
                there = group == ((1 - source_x) * options_y + side_y) * 2 + from_z
                if source_x == -1:
                    there = there & (index_x > 0)
                elif source_x == 1:
                    there = there & (index_x < count_x - 1)
                found = jnp.where(there, tile(source_x, from_y, from_z), found)
    halves = []
    for at in range(0, spread_ref.shape[1], 128):
        lane = jnp.broadcast_to(spread_ref[0:1, at : at + 128], (ROWS, 128))
        half = jnp.zeros((ROWS, 128), F32)
        for base in range(0, lanes, 128):
            index = jnp.clip(lane - base, 0, 127)
            there = (lane >= base) & (lane < base + 128)
            part = jnp.take_along_axis(found[:, base : base + 128], index, axis=1)
            half = jnp.where(there, part, half)
        halves.append(half)
    arrived = jnp.concatenate(halves, axis=1)[:, : 26 * CAP]
    for j in range(9):
        arrived_state_ref[j, 0, 0] = arrived[j : j + 1]
    arrived_latent_ref[0, 0, 0] = encode(
        arrived[:9], arrived[9:10], inward_ref[...], encoder_w_ref[...], extent
    )


def swap(values, axis):
    return lax.ppermute(values, axis, [(0, 1), (1, 0)])


def shift(values, axis, way):
    pairs = [(i, i + 1) for i in range(lax.axis_size(axis) - 1)]
    return lax.ppermute(values, axis, [(j, i) for i, j in pairs] if way else pairs)


def swap_chips(values, cross):
    axes = ("group", "gx", "gy", "gz")
    counts = tuple(lax.axis_size(axis) for axis in axes)

    def number(place):
        total = 0
        for count, index in zip(counts, place):
            total = total * count + index
        return total

    pairs = []
    for place in itertools.product(*(range(count) for count in counts)):
        group, x, y, z = place
        to_x = x + 1 - 2 * z
        if 0 <= to_x < counts[1]:
            to = (group, to_x, y ^ 1 if cross else y, 1 - z)
        else:
            to = (group ^ 1, x, y, z)
        pairs.append((number(place), number(to)))
    return lax.ppermute(values, axes, pairs)


def call(kernel, name, in_specs, outs, scratch, operands, flops):
    return pl.pallas_call(
        kernel,
        out_shape=tuple(jax.ShapeDtypeStruct(shape, kind) for shape, kind in outs),
        in_specs=in_specs,
        out_specs=tuple(VMEM for _ in outs),
        scratch_shapes=scratch,
        compiler_params=pltpu.CompilerParams(vmem_limit_bytes=32 * 1024 * 1024),
        cost_estimate=pl.CostEstimate(flops=flops, bytes_accessed=0, transcendentals=0),
        name=name,
    )(*operands)


def in_hbm(array):
    return pltpu.with_memory_space_constraint(array, pltpu.HBM)


def like(array):
    return pltpu.VMEM(array.shape, array.dtype)


def body(
    node_latent,
    edge_latent,
    positions,
    velocity,
    fill,
    neighbours,
    owners,
    edge_weights,
    node_in,
    node_weights,
    decoder_weights,
    decoder_out,
    encoder_in,
    encoder_weights,
):
    sizes = tuple(lax.axis_size(axis) for axis in ("gx", "gy", "gz"))
    fold_y = sizes[1] == 2
    slots, width = node_latent.shape[-2:]
    neighbour_count = neighbours.shape[3]
    particles = 4 * slots
    options_y = 2 if fold_y else 3
    movers = (3 * options_y * 2 * CAP + 127) // 128 * 128
    rows = 3 if fold_y else 4
    fill = jnp.transpose(fill, (0, 2, 1))
    neighbours = neighbours.reshape(2, 2, neighbour_count, 1, slots)

    own_zed = swap(node_latent, "gz")
    if fold_y:
        sides = [swap(node_latent, "gy")]
    spread = call(
        functools.partial(tables_kernel, fold_y),
        "tables",
        [],
        [((8, 256), I32)],
        [],
        [],
        5_000_000_000,
    )[0]
    latent, spread = lax.optimization_barrier((node_latent, spread))
    core = lax.axis_index("gz")
    if fold_y:
        row = 1 - lax.axis_index("gy")
        end = lax.dynamic_index_in_dim(latent[:, :, 0], 1 - core, 0, False)
        beside = lax.dynamic_index_in_dim(own_zed[:, :, 0], 1 - core, 0, False)
        both = jnp.stack([end, beside])
        corner = lax.dynamic_slice_in_dim(both, row, 1, axis=1)
        mine = [swap_chips(both, False)]
        corner, both = lax.optimization_barrier((corner, both))
        mine.append(swap_chips(corner, True))
    else:
        sides = [shift(latent[:, 1, 0], "gy", 0), shift(latent[:, 0, 0], "gy", 1)]
        side_zeds = [swap(part, "gz") for part in sides]
        layers = []
        for middle, outer in ((latent, sides), (own_zed, side_zeds)):
            parts = [outer[0][:, None], middle[:, :, 0], outer[1][:, None]]
            parts = [lax.dynamic_index_in_dim(part, 1 - core, 0, False) for part in parts]
            layers.append(jnp.concatenate(parts, axis=0))
        mine = [swap_chips(jnp.stack(layers), False)]

    ranked = call(
        functools.partial(ranks_kernel, sizes),
        "ranks",
        [VMEM] * 13,
        [
            ((11, width, width), BF16),
            ((48, width), BF16),
            ((2, 2, 1, slots), F32),
            ((width, particles), F32),
            ((width, particles), F32),
            ((8, particles), F32),
            ((neighbour_count, movers, width), BF16),
            ((1, neighbour_count * movers), I32),
            ((1, neighbour_count * movers), I32),
            ((width, movers), F32),
            ((width, movers), F32),
            ((width, movers), F32),
            ((8, movers), F32),
            ((4, width, 2 * slots), BF16),
            ((4, width, neighbour_count * slots), F32),
        ],
        [],
        (edge_latent, latent, own_zed, fill, owners, edge_weights, node_in, node_weights, decoder_weights, encoder_in, neighbours, positions, velocity),
        5_000_000_000,
    )
    mine, sides, ranked = lax.optimization_barrier((mine, sides, ranked))
    (
        weights,
        inward,
        alive,
        latent_t,
        node_pre,
        state,
        mover_edges,
        mover_place,
        mover_key,
        mover_near,
        mover_node_pre,
        mover_latent,
        mover_state,
        far_own,
        edge_pre,
    ) = ranked
    mine = jnp.concatenate(mine, axis=1)
    if fold_y:
        sides = [lax.dynamic_index_in_dim(sides[0][:, :, 0], lax.axis_index("gy"), 1, False)]
        packed = jnp.concatenate([mine.reshape(-1, slots, width), sides[0]], axis=0)
    else:
        packed = mine.reshape(-1, slots, width)
    packed = swap(packed, "gz")
    prepared = call(
        functools.partial(prepare_kernel, sizes),
        "prepare",
        [VMEM] * 9,
        [
            ((rows, width, 2 * slots), BF16),
            ((width, neighbour_count * movers), F32),
            ((width, neighbour_count * slots), F32),
        ],
        [],
        (
            far_own,
            mine,
            weights,
            mover_edges,
            mover_place,
            mover_key,
            mover_near,
            neighbours,
            edge_pre,
        ),
        5_000_000_000,
    )
    packed, prepared = lax.optimization_barrier((packed, prepared))
    cells = mine.shape[0] * mine.shape[1]
    if fold_y:
        side_zeds = [packed[cells:]]
    far_mine, mover_pre, border = prepared
    halo = [*sides, *side_zeds, packed[:cells].reshape(mine.shape)]

    far_rest, bucket = call(
        functools.partial(movers_kernel, sizes, len(sides)),
        "movers",
        [VMEM] * (len(halo) + 8),
        [((4 * rows - 4, width, 2 * slots), BF16), ((ROWS, movers), F32)],
        [pltpu.VMEM((width, neighbour_count * movers), BF16)],
        (
            *halo,
            weights,
            decoder_out,
            mover_pre,
            mover_place,
            mover_key,
            mover_node_pre,
            mover_latent,
            mover_state,
        ),
        3_000_000_000,
    )

    zed = swap(bucket, "gz")
    if fold_y:
        sides = [swap(bucket, "gy")]
        zed, far_rest = lax.optimization_barrier((zed, far_rest))
        both = jnp.stack([bucket, zed])
        ends = [swap_chips(both, True), swap_chips(both, False)]
    else:
        both = jnp.stack([bucket, zed])
        sides = [shift(both, "gy", 0), shift(both, "gy", 1)]
        ends = [swap_chips(jnp.stack([both, *sides], axis=1), False)]
    total = call(
        functools.partial(edges_kernel, sizes),
        "edges",
        [VMEM] * 7,
        [((4, width, slots), BF16)],
        [pltpu.VMEM((4, width, neighbour_count * slots), BF16)],
        (alive, neighbours, far_rest, far_mine, edge_pre, border, weights),
        8_000_000_000,
    )[0]
    sides, ends, total = lax.optimization_barrier((sides, ends, total))
    if fold_y:
        packed = swap(jnp.concatenate([*ends, sides[0][None]], axis=0), "gz")
    else:
        packed = swap(ends[0], "gz")
    state = call(
        nodes_kernel,
        "nodes",
        [VMEM] * 6,
        [((ROWS, particles), F32)],
        [],
        (total, node_pre, latent_t, state, weights, decoder_out),
        1_000_000_000,
    )[0]
    packed, state = lax.optimization_barrier((packed, state))
    return call(
        functools.partial(finish_kernel, sizes),
        "finish",
        [VMEM] * (len(sides) + len(ends) + 6),
        [
            (node_latent.shape, BF16),
            ((9,) + node_latent.shape[:4], F32),
            ((1, 1, 1, 26 * CAP, width), BF16),
            ((9, 1, 1, 1, 26 * CAP), F32),
        ],
        [],
        (state, zed, *sides, *ends, packed, spread, inward, encoder_weights),
        1_000_000_000,
    )


def solution(mesh):
    placed = (
        P(("group", "gx"), "gy", "gz", None, None),
        P(("group", "gx"), "gy", "gz", None, None, None),
        P(None, ("group", "gx"), "gy", "gz", None),
        P(None, ("group", "gx"), "gy", "gz", None),
        P(("group", "gx"), "gy", "gz"),
        P(("group", "gx"), "gy", "gz", None, None),
        P(("group", "gx"), "gy", "gz", None),
        P(),
        P(),
        P(),
        P(),
        P(),
        P(),
        P(),
    )
    return jax.shard_map(
        body,
        mesh=mesh,
        in_specs=placed,
        out_specs=(
            P(("group", "gx"), "gy", "gz", None, None),
            P(None, ("group", "gx"), "gy", "gz", None),
            P(("group", "gx"), "gy", "gz", None, None),
            P(None, ("group", "gx"), "gy", "gz", None),
        ),
        check_vma=False,
    )
```
